32 devices in a mesh: seq: 8 (over z, core), fsdp: 4 (over y, x).
Axes of the slice: x: 2, y: 2, z: 4, core: 2. Of those that a mesh axis runs over, the one named last changes fastest.
Arguments:
- tokens: bfloat16 [4, 1024, 2048], P('fsdp', 'seq'), may hold values from -6 to 6
- cotangent: bfloat16 [4, 1024, 2048], P('fsdp', 'seq'), may hold values from -6 to 6
- mix_gain: bfloat16 [2048], P(('seq', 'fsdp')), may hold values from 0.099609375 to 1.8984375
- lru_in_weight: bfloat16 [2048, 2560], P(('seq', 'fsdp')), may hold values from -0.125 to 0.125
- gelu_in_weight: bfloat16 [2048, 2560], P(('seq', 'fsdp')), may hold values from -0.125 to 0.125
- out_weight: bfloat16 [2560, 2048], P(('seq', 'fsdp')), may hold values from -0.3125 to 0.3125
- conv_weight: bfloat16 [2560, 4], P(('seq', 'fsdp')), may hold values from -3 to 3
- conv_bias: bfloat16 [2560], P(('seq', 'fsdp')), may hold values from -3 to 3
- recurrence_weight: bfloat16 [2560, 160], P(('seq', 'fsdp')), may hold values from -0.5 to 0.5
- recurrence_bias: bfloat16 [2560], P(('seq', 'fsdp')), may hold values from -3 to 3
- input_gate_weight: bfloat16 [2560, 160], P(('seq', 'fsdp')), may hold values from -0.5 to 0.5
- input_gate_bias: bfloat16 [2560], P(('seq', 'fsdp')), may hold values from -3 to 3
- decay_param: bfloat16 [2560], P(('seq', 'fsdp')), may hold values from 3 to 13
- mlp_gain: bfloat16 [2048], P(('seq', 'fsdp')), may hold values from 0.099609375 to 1.8984375
- gate_weight: bfloat16 [2048, 6144], P(('seq', 'fsdp')), may hold values from -0.125 to 0.125
- up_weight: bfloat16 [2048, 6144], P(('seq', 'fsdp')), may hold values from -0.125 to 0.125
- down_weight: bfloat16 [6144, 2048], P(('seq', 'fsdp')), may hold values from -0.109375 to 0.109375
Outputs:
- result: bfloat16 [4, 1024, 2048], P('fsdp', 'seq')
- tokens_grad: bfloat16 [4, 1024, 2048], P('fsdp', 'seq')
- mix_gain_grad: float32 [2048], P(('seq', 'fsdp'))
- lru_in_weight_grad: float32 [2048, 2560], P(('seq', 'fsdp'))
- gelu_in_weight_grad: float32 [2048, 2560], P(('seq', 'fsdp'))
- out_weight_grad: float32 [2560, 2048], P(('seq', 'fsdp'))
- conv_weight_grad: float32 [2560, 4], P(('seq', 'fsdp'))
- conv_bias_grad: float32 [2560], P(('seq', 'fsdp'))
- recurrence_weight_grad: float32 [2560, 160], P(('seq', 'fsdp'))
- recurrence_bias_grad: float32 [2560], P(('seq', 'fsdp'))
- input_gate_weight_grad: float32 [2560, 160], P(('seq', 'fsdp'))
- input_gate_bias_grad: float32 [2560], P(('seq', 'fsdp'))
- decay_param_grad: float32 [2560], P(('seq', 'fsdp'))
- mlp_gain_grad: float32 [2048], P(('seq', 'fsdp'))
- gate_weight_grad: float32 [2048, 6144], P(('seq', 'fsdp'))
- up_weight_grad: float32 [2048, 6144], P(('seq', 'fsdp'))
- down_weight_grad: float32 [6144, 2048], P(('seq', 'fsdp'))
The draws below stay inside these ranges and needn't reach their ends.
All inputs are finite; a program needn't handle non-finite values.
Results may differ from the reference program's by a relative error of at most 0.012.
Values may be sent and summed in bfloat16 or wider, within the bound.
A program may use at most 512 MiB of HBM per device.

```python
import jax
import jax.numpy as jnp
from jax import lax

D = 2048
W = 2560
FF = 6144
BLOCK = 160
CONV = 4
SEQS = 4
LENGTH = 1024


def draw_decay_param(key, part):
    key = jax.random.fold_in(key, 7)
    pick_key, slow_key, fast_key = jax.random.split(key, 3)
    share = 0.5
    chosen = jax.random.uniform(pick_key, (W,), jnp.float32) < share
    slow_low = jnp.log(0.1 / LENGTH)
    slow_high = jnp.log(0.5 / LENGTH)
    fast_high = jnp.log(0.03)
    slow_rate = jnp.exp(slow_low + (slow_high - slow_low) * jax.random.uniform(slow_key, (W,), jnp.float32))
    fast_rate = jnp.exp(slow_high + (fast_high - slow_high) * jax.random.uniform(fast_key, (W,), jnp.float32))
    rate = jnp.where(chosen, slow_rate, fast_rate)
    return (-jnp.log(jnp.expm1(rate))).astype(jnp.bfloat16)


def shard_levels(stream_key, dims, cuts, least, high):
    level = 1.0
    for position, parts in cuts:
        heights = jax.random.uniform(jax.random.fold_in(jax.random.fold_in(stream_key, 6), position), (parts,), jnp.float32, least / len(cuts), high / len(cuts))
        level = level * jnp.repeat(jnp.exp(heights), dims[position] // parts).reshape((-1,) + (1,) * (len(dims) - 1 - position))
    return level


def centred(own_key, extent, deviation, reach, pieces=(), dtype=jnp.bfloat16):
    entries = deviation * jax.random.normal(own_key, extent, jnp.float32)
    if pieces:
        entries = entries * shard_levels(own_key, extent, pieces, -0.22, 0.18)
    return jnp.clip(entries, -reach, reach).astype(dtype)


def setup_inputs(seed: int = 0) -> dict:
    splits = jax.random.split(jax.random.key(seed), 18)
    return {
        "tokens": centred(splits[0], (SEQS, LENGTH, D), 1.0, 6.0, ((0, 4), (1, 8))),
        "cotangent": centred(splits[1], (SEQS, LENGTH, D), 1.0, 6.0, ((0, 4), (1, 8))),
        "mix_gain": jnp.clip(1.0 + 0.18 * jax.random.normal(splits[2], (D,), jnp.float32), 0.099609375, 1.8984375).astype(jnp.bfloat16),
        "lru_in_weight": centred(splits[3], (D, W), D ** -0.5, 0.125, ((0, 32),)),
        "gelu_in_weight": centred(splits[4], (D, W), D ** -0.5, 0.125, ((0, 32),)),
        "out_weight": centred(splits[5], (W, D), (W // 8) ** -0.5, 0.3125, ((0, 32),)),
        "conv_weight": centred(splits[6], (W, CONV), CONV ** -0.5, 3.0, ((0, 32),)),
        "conv_bias": centred(splits[7], (W,), 0.5, 3.0, ((0, 32),)),
        "recurrence_weight": centred(splits[8], (W, BLOCK), BLOCK ** -0.5, 0.5, ((0, 32),)),
        "recurrence_bias": centred(splits[9], (W,), 0.5, 3.0, ((0, 32),)),
        "input_gate_weight": centred(splits[10], (W, BLOCK), BLOCK ** -0.5, 0.5, ((0, 32),)),
        "input_gate_bias": centred(splits[11], (W,), 0.5, 3.0, ((0, 32),)),
        "decay_param": draw_decay_param(jax.random.fold_in(splits[17], 71), 0),
        "mlp_gain": jnp.clip(1.0 + 0.18 * jax.random.normal(splits[13], (D,), jnp.float32), 0.099609375, 1.8984375).astype(jnp.bfloat16),
        "gate_weight": centred(splits[14], (D, FF), D ** -0.5, 0.125, ((0, 32),)),
        "up_weight": centred(splits[15], (D, FF), D ** -0.5, 0.125, ((0, 32),)),
        "down_weight": centred(splits[16], (FF, D), (FF // 2) ** -0.5, 0.109375, ((0, 32),)),
    }


EPSILON = 1e-06
RATE_SCALE = 8.0

@jax.custom_vjp
def low(v):
    return lax.optimization_barrier(v.astype(jnp.bfloat16)).astype(jnp.float32)

@jax.custom_vjp
def low_back(v):
    return v

def low_keep(v):
    return (low(v), None)

def low_pass(kept, grad):
    return (grad,)

def back_keep(v):
    return (v, None)

def back_low(kept, grad):
    return (low(grad),)
low.defvjp(low_keep, low_pass)
low_back.defvjp(back_keep, back_low)

def rms_scale(values, gain):
    scale = lax.rsqrt(lax.optimization_barrier(jnp.mean(values * values, axis=-1, keepdims=True)) + EPSILON)
    return values * scale * gain

def linear_pair(first, second):
    return (first[0] * second[0], second[0] * first[1] + second[1])

def coefficients(gate_pre, input_pre, inputs, gate_bias, input_bias, decay_param):
    recur_gate = jax.nn.sigmoid(gate_pre + gate_bias)
    input_gate = jax.nn.sigmoid(input_pre + input_bias)
    log_decay = -RATE_SCALE * recur_gate * jax.nn.softplus(-decay_param)
    factor = jnp.exp(log_decay)
    driving = jnp.sqrt(-jnp.expm1(2.0 * log_decay)) * input_gate * inputs
    return (factor, driving)

def convolve(extended, taps_weight, conv_bias, positions):
    summed = jnp.zeros_like(extended[:positions]) + conv_bias
    taps = taps_weight.shape[1]
    for offset in range(taps):
        summed = summed + taps_weight[:, offset] * extended[taps - 1 - offset:taps - 1 - offset + positions]
    return summed

def dense(left, right):
    return jnp.dot(left, right, precision=lax.Precision.HIGHEST)

def block_product(values, weight):
    row_count = values.shape[0]
    block_width = weight.shape[1]
    block_count = weight.shape[0] // block_width
    shaped = values.reshape(row_count, block_count, block_width)
    return jnp.einsum('tnk,nkj->tnj', shaped, weight.reshape(block_count, block_width, block_width), precision=lax.Precision.HIGHEST).reshape(row_count, block_count * block_width)

def forward(tokens, params):
    mix_gain, lru_in_weight, gelu_in_weight, out_weight, conv_weight, conv_bias, recurrence_weight, recurrence_bias, input_gate_weight, input_gate_bias, decay_param, mlp_gain, gate_weight, up_weight, down_weight = params
    normed = low(rms_scale(tokens, mix_gain))
    branch_x = low_back(low(dense(normed, lru_in_weight)))
    branch_pre = low_back(dense(normed, gelu_in_weight))
    branch_y = jax.nn.gelu(branch_pre)
    positions = tokens.shape[0]
    taps = conv_weight.shape[1]
    extended = jnp.concatenate([jnp.zeros((taps - 1, branch_x.shape[1]), jnp.float32), branch_x], axis=0)
    conv_out = low(convolve(extended, conv_weight, conv_bias, positions))
    gate_pre = low_back(block_product(conv_out, recurrence_weight))
    input_pre = low_back(block_product(conv_out, input_gate_weight))
    factor, driving = coefficients(gate_pre, input_pre, conv_out, recurrence_bias, input_gate_bias, decay_param)
    products, states = lax.associative_scan(linear_pair, (factor, driving), axis=0)
    states_low = low_back(low(states))
    product = low(states_low * branch_y)
    middle = tokens + low_back(dense(product, out_weight))
    normed2 = low(rms_scale(middle, mlp_gain))
    gate_val = low_back(dense(normed2, gate_weight))
    up_val = low_back(dense(normed2, up_weight))
    hidden = low(jax.nn.gelu(gate_val) * up_val)
    return middle + dense(hidden, down_weight)

def reference(tokens, cotangent, mix_gain, lru_in_weight, gelu_in_weight, out_weight, conv_weight, conv_bias, recurrence_weight, recurrence_bias, input_gate_weight, input_gate_bias, decay_param, mlp_gain, gate_weight, up_weight, down_weight):
    params = tuple((member.astype(jnp.float32) for member in (mix_gain, lru_in_weight, gelu_in_weight, out_weight, conv_weight, conv_bias, recurrence_weight, recurrence_bias, input_gate_weight, input_gate_bias, decay_param, mlp_gain, gate_weight, up_weight, down_weight)))

    def one_sequence(totals, pair):
        seq_tokens, seq_grad = pair
        output, pullback = jax.vjp(forward, seq_tokens.astype(jnp.float32), params)
        input_grad, param_grads = pullback(seq_grad.astype(jnp.float32))
        totals = jax.tree.map(lambda first, second: first + second, totals, param_grads)
        return (totals, (output.astype(jnp.bfloat16), input_grad.astype(jnp.bfloat16)))
    zeros = tuple((jnp.zeros_like(member) for member in params))
    totals, outputs = lax.scan(one_sequence, zeros, (tokens, cotangent))
    return (outputs[0], outputs[1], totals[0], totals[1], totals[2], totals[3], totals[4], totals[5], totals[6], totals[7], totals[8], totals[9], totals[10], totals[11], totals[12], totals[13], totals[14])
```

```python
import functools

import jax
import jax.numpy as jnp
from jax import lax
from jax.experimental import pallas as pl
from jax.experimental.pallas import tpu as pltpu
from jax.sharding import PartitionSpec as P

EPSILON = 1e-06
RATE_SCALE = 8.0
CHUNK = 128
LOW = jnp.bfloat16
WIDE = jnp.float32


def rms_scale(values, gain):
    scale = lax.rsqrt(jnp.mean(values * values, axis=-1, keepdims=True) + EPSILON)
    return values * scale * gain


def dot(left, right):
    return jnp.dot(left, right, preferred_element_type=WIDE)


def outer_sum(left, right):
    return lax.dot_general(left, right, (((0,), (0,)), ((), ())), preferred_element_type=WIDE)


def times_transpose(left, right):
    return lax.dot_general(left, right, (((1,), (1,)), ((), ())), preferred_element_type=WIDE)


def one_minus_exp(value):
    series = jnp.full_like(value, 1.0 / 40320.0)
    for bottom in (5040.0, 720.0, 120.0, 24.0, 6.0, 2.0, 1.0):
        series = 1.0 / bottom - value * series
    return jnp.where(value < 0.4, value * series, 1.0 - jnp.exp(-value))


def sigmoid(value):
    return 0.5 * jnp.tanh(0.5 * value) + 0.5


def lane_tiles(channels):
    return -(-channels // 128)


def put(tiles, rows, value):
    channels = value.shape[1]
    for n in range(lane_tiles(channels)):
        size = min(128, channels - n * 128)
        tiles[n, rows, 0:size] = value[:, n * 128 : n * 128 + size]


def get(tiles, rows, channels):
    return jnp.concatenate(
        [
            tiles[n, rows, 0 : min(128, channels - n * 128)]
            for n in range(lane_tiles(channels))
        ],
        axis=1,
    )


def scan_segments(step, count, tiles):
    def body(i, carried):
        return tuple(step(i, n, *carried[n]) for n in range(tiles))

    start = (jnp.zeros((8, 128), WIDE), jnp.ones((8, 128), WIDE))
    ends = lax.fori_loop(0, count, body, (start,) * tiles, unroll=4)
    return [jnp.concatenate([end[which] for end in ends], axis=1) for which in (0, 1)]


def mixer_forward_kernel(
    x_ref, wr_ref, wi_ref, par_ref,
    conv_ref, r_ref, i_ref, f_ref, m_ref, st_ref,
    ext, factors, drive, prod,
):
    positions, channels = x_ref.shape
    segment = positions // 8
    chunks = positions // CHUNK
    ext[0:8, :] = jnp.zeros((8, channels), WIDE)
    st_ref[0:8, :] = jnp.zeros((8, channels), WIDE)

    @pl.loop(0, chunks)
    def _(c):
        base = pl.multiple_of(c * CHUNK, CHUNK)
        ext[pl.ds(base + 8, CHUNK), :] = x_ref[pl.ds(base, CHUNK), :].astype(WIDE)

    @pl.loop(0, chunks)
    def _(c):
        base = pl.multiple_of(c * CHUNK, CHUNK)
        rows = pl.ds(base, CHUNK)
        block = ext[pl.ds(base, CHUNK + 8), :]
        conv = jnp.broadcast_to(par_ref[4:5, :], (CHUNK, channels))
        for k in range(4):
            conv = conv + par_ref[k : k + 1, :] * block[8 - k : 8 - k + CHUNK]
        conv_low = conv.astype(LOW)
        conv_ref[rows, :] = conv_low
        r = jax.nn.sigmoid(dot(conv_low, wr_ref[...]) + par_ref[5:6, :])
        gate = jax.nn.sigmoid(dot(conv_low, wi_ref[...]) + par_ref[6:7, :])
        log_decay = r * par_ref[7:8, :]
        m = jnp.sqrt(one_minus_exp(-2.0 * log_decay))
        r_ref[rows, :] = r
        i_ref[rows, :] = gate
        factor = jnp.exp(log_decay)
        f_ref[rows, :] = factor
        m_ref[rows, :] = m
        put(factors, rows, factor)
        put(drive, rows, m * gate * conv_low.astype(WIDE))

    def step(i, n, state, product):
        rows = pl.ds(i, 8, stride=segment)
        factor = factors[n, rows, :]
        state = factor * state + drive[n, rows, :]
        product = factor * product
        drive[n, rows, :] = state
        prod[n, rows, :] = product
        return state, product

    state, product = scan_segments(step, segment, lane_tiles(channels))
    state, product = state[:, :channels], product[:, :channels]
    carry = jnp.zeros((1, channels), WIDE)
    for k in range(8):
        for part in range(segment // CHUNK):
            base = k * segment + part * CHUNK
            rows = slice(base, base + CHUNK)
            st_ref[base + 8 : base + 8 + CHUNK, :] = (
                get(drive, rows, channels) + get(prod, rows, channels) * carry
            )
        carry = state[k : k + 1] + product[k : k + 1] * carry


def mixer_backward_kernel(
    ds_ref, x_ref, conv_ref, r_ref, i_ref, f_ref, m_ref, st_ref, wr_ref, wi_ref, par_ref,
    xg_ref, wrg_ref, wig_ref, sums_ref,
    ext, factors, adj, prod, cg, carries, wr_sum, wi_sum,
):
    positions, channels = x_ref.shape
    segment = positions // 8
    chunks = positions // CHUNK
    ext[0:8, :] = jnp.zeros((8, channels), WIDE)
    cg[pl.ds(positions, 8), :] = jnp.zeros((8, channels), WIDE)
    wr_sum[...] = jnp.zeros_like(wr_sum)
    wi_sum[...] = jnp.zeros_like(wi_sum)

    @pl.loop(0, chunks)
    def _(c):
        base = pl.multiple_of(c * CHUNK, CHUNK)
        ext[pl.ds(base + 8, CHUNK), :] = x_ref[pl.ds(base, CHUNK), :].astype(WIDE)
        put(adj, pl.ds(base, CHUNK), ds_ref[pl.ds(base, CHUNK), :].astype(WIDE))
        put(factors, pl.ds(base, CHUNK), f_ref[pl.ds(base, CHUNK), :])

    def step(j, n, flow, product):
        rows = pl.ds(segment - 1 - j, 8, stride=segment)
        factor = factors[n, rows, :]
        adjoint = adj[n, rows, :] + flow
        adj[n, rows, :] = adjoint
        prod[n, rows, :] = product
        return factor * adjoint, factor * product

    flow, product = scan_segments(step, segment, lane_tiles(channels))
    flow, product = flow[:, :channels], product[:, :channels]
    carry = jnp.zeros((1, channels), WIDE)
    for k in range(7, -1, -1):
        carries[k : k + 1, :] = carry
        carry = flow[k : k + 1] + product[k : k + 1] * carry

    def grads(c, sums):
        base = pl.multiple_of(c * CHUNK, CHUNK)
        rows = pl.ds(base, CHUNK)
        adjoint = get(adj, rows, channels) + get(prod, rows, channels) * carries[pl.ds(base // segment, 1), :]
        before = st_ref[pl.ds(base, CHUNK + 8), :][7 : 7 + CHUNK]
        conv_low = conv_ref[rows, :]
        conv = conv_low.astype(WIDE)
        r = r_ref[rows, :]
        gate = i_ref[rows, :]
        factor = f_ref[rows, :]
        m = m_ref[rows, :]
        driven = adjoint * gate
        by_log = adjoint * before * factor - driven * conv * factor * factor / m
        by_r = by_log * par_ref[7:8, :] * r * (1.0 - r)
        by_i = adjoint * m * conv * gate * (1.0 - gate)
        by_r_low = by_r.astype(LOW)
        by_i_low = by_i.astype(LOW)
        conv_grad = (
            driven * m
            + times_transpose(by_r_low, wr_ref[...])
            + times_transpose(by_i_low, wi_ref[...])
        )
        cg[rows, :] = conv_grad
        wr_sum[...] += outer_sum(conv_low, by_r_low)
        wi_sum[...] += outer_sum(conv_low, by_i_low)
        block = ext[pl.ds(base, CHUNK + 8), :]
        rows_of = [conv_grad * block[8 - k : 8 - k + CHUNK] for k in range(4)]
        rows_of += [conv_grad, by_r, by_i, by_log * r]
        return tuple(
            total + jnp.sum(member, axis=0, keepdims=True) for total, member in zip(sums, rows_of)
        )

    zero = jnp.zeros((1, channels), WIDE)
    sums = lax.fori_loop(0, chunks, grads, (zero,) * 8)
    for k in range(8):
        sums_ref[k : k + 1, :] = sums[k]
    size = wrg_ref.shape[1]
    for n in range(channels // size):
        block = slice(n * size, (n + 1) * size)
        wrg_ref[block, :] = wr_sum[block, block]
        wig_ref[block, :] = wi_sum[block, block]

    @pl.loop(0, chunks)
    def _(c):
        base = pl.multiple_of(c * CHUNK, CHUNK)
        block = cg[pl.ds(base, CHUNK + 8), :]
        total = jnp.zeros((CHUNK, channels), WIDE)
        for k in range(4):
            total = total + par_ref[k : k + 1, :] * block[k : k + CHUNK]
        xg_ref[pl.ds(base, CHUNK), :] = total.astype(LOW)


def mixer_forward(x, wr, wi, par):
    positions, channels = x.shape
    wide = jax.ShapeDtypeStruct((positions, channels), WIDE)
    return pl.pallas_call(
        mixer_forward_kernel,
        out_shape=(
            jax.ShapeDtypeStruct((positions, channels), LOW), wide, wide, wide, wide,
            jax.ShapeDtypeStruct((positions + 8, channels), WIDE),
        ),
        scratch_shapes=[pltpu.VMEM((positions + 8, channels), WIDE)]
        + [pltpu.VMEM((lane_tiles(channels), positions, 128), WIDE)] * 3,
        compiler_params=pltpu.CompilerParams(vmem_limit_bytes=48 * 2**20),
        name="mixer_forward",
    )(x, wr, wi, par)


def mixer_backward(ds, x, saved, wr, wi, par, size):
    positions, channels = x.shape
    square = jax.ShapeDtypeStruct((channels, size), WIDE)
    return pl.pallas_call(
        mixer_backward_kernel,
        out_shape=(
            jax.ShapeDtypeStruct((positions, channels), LOW), square, square,
            jax.ShapeDtypeStruct((8, channels), WIDE),
        ),
        scratch_shapes=[pltpu.VMEM((positions + 8, channels), WIDE)]
        + [pltpu.VMEM((lane_tiles(channels), positions, 128), WIDE)] * 3
        + [pltpu.VMEM((positions + 8, channels), WIDE), pltpu.VMEM((8, channels), WIDE)]
        + [pltpu.VMEM((channels, channels), WIDE)] * 2,
        compiler_params=pltpu.CompilerParams(vmem_limit_bytes=48 * 2**20),
        name="mixer_backward",
    )(ds, x, *saved, wr, wi, par)


def gather_columns(weights):
    shards = lax.axis_size("seq")
    rows = weights[0].shape[0]
    widths = [member.shape[1] // shards for member in weights]
    stacked = jnp.concatenate(
        [member.reshape(rows, shards, width) for member, width in zip(weights, widths)], axis=2
    )
    mine = lax.all_to_all(stacked.transpose(1, 0, 2), "seq", split_axis=0, concat_axis=0)
    whole = lax.all_gather(mine, "fsdp", axis=1)
    return whole.reshape(-1, sum(widths))


def scatter_columns(grad, widths, rows):
    shards, groups = lax.axis_size("seq"), lax.axis_size("fsdp")
    parts = grad.astype(LOW).reshape(shards, groups, rows, sum(widths)).transpose(1, 0, 2, 3)
    mine = lax.psum_scatter(parts, "fsdp", scatter_dimension=0, tiled=False)
    swapped = lax.all_to_all(mine, "seq", split_axis=0, concat_axis=0).astype(WIDE)
    outs, first = [], 0
    for width in widths:
        outs.append(swapped[:, :, first : first + width].transpose(1, 0, 2).reshape(rows, -1))
        first += width
    return outs


def block_diagonal(weight, blocks):
    size = weight.shape[1]
    shaped = weight.reshape(blocks, size, size)
    full = jnp.zeros((blocks, size, blocks, size), weight.dtype)
    for n in range(blocks):
        full = full.at[n, :, n, :].set(shaped[n])
    return full.reshape(blocks * size, blocks * size)


def local(
    tokens, cotangent, mix_gain, lru_in_weight, gelu_in_weight, out_weight, conv_weight, conv_bias,
    recurrence_weight, recurrence_bias, input_gate_weight, input_gate_bias, decay_param, mlp_gain,
    gate_weight, up_weight, down_weight,
):
    positions, width = tokens.shape[1:]
    rows = lru_in_weight.shape[0]
    shards = lax.axis_size("seq")
    channels = lru_in_weight.shape[1] // shards
    hidden_width = gate_weight.shape[1] // shards
    size = recurrence_weight.shape[1]

    gains = lax.all_gather(
        jnp.stack([mix_gain, mlp_gain], axis=1), ("seq", "fsdp"), axis=0, tiled=True
    ).astype(WIDE)
    mix_scale, mlp_scale = gains[:, 0], gains[:, 1]
    in_whole = gather_columns([lru_in_weight, gelu_in_weight])
    lru_params = lax.all_gather(
        jnp.concatenate(
            [
                recurrence_weight, input_gate_weight, conv_weight, conv_bias[:, None],
                recurrence_bias[:, None], input_gate_bias[:, None], decay_param[:, None],
            ],
            axis=1,
        ),
        "fsdp", axis=0, tiled=True,
    )
    out_whole = lax.all_gather(out_weight, "fsdp", axis=0, tiled=True)
    glu_whole = gather_columns([gate_weight, up_weight])
    down_whole = lax.all_gather(down_weight, "fsdp", axis=0, tiled=True)

    wr = block_diagonal(lru_params[:, :size], channels // size)
    wi = block_diagonal(lru_params[:, size : 2 * size], channels // size)
    vectors = lru_params[:, 2 * size :].astype(WIDE).T
    decay = vectors[7]
    par = jnp.concatenate([vectors[:7], -RATE_SCALE * jax.nn.softplus(-decay)[None]], axis=0)

    resid_in = tokens.reshape(positions, width).astype(WIDE)
    grad_low = cotangent.reshape(positions, width)
    normed_low = rms_scale(resid_in, mix_scale).astype(LOW)
    normed_all = lax.all_gather(normed_low, "seq", axis=0, tiled=True)
    grad_all = lax.all_gather(grad_low, "seq", axis=0, tiled=True)
    branch_x = dot(normed_all, in_whole[:, :channels]).astype(LOW)
    branch_pre = dot(normed_all, in_whole[:, channels:])
    branch_y = jax.nn.gelu(branch_pre)

    saved = mixer_forward(branch_x, wr, wi, par)
    states_f = saved[5][8:].astype(LOW).astype(WIDE)
    product = (states_f * branch_y).astype(LOW)
    mixed = lax.psum_scatter(
        dot(product, out_whole).astype(LOW), "seq", scatter_dimension=0, tiled=True
    )
    middle = resid_in + mixed.astype(WIDE)
    normed2_low = rms_scale(middle, mlp_scale).astype(LOW)
    normed2_all = lax.all_gather(normed2_low, "seq", axis=0, tiled=True)
    gate_whole, up_whole = glu_whole[:, :hidden_width], glu_whole[:, hidden_width:]
    gate_val = dot(normed2_all, gate_whole)
    up_val = dot(normed2_all, up_whole)
    hidden = (jax.nn.gelu(gate_val) * up_val).astype(LOW)
    fed = lax.psum_scatter(
        dot(hidden, down_whole).astype(LOW), "seq", scatter_dimension=0, tiled=True
    )
    result = middle + fed.astype(WIDE)

    hidden_grad = times_transpose(grad_all, down_whole)
    unused, pull_glu = jax.vjp(lambda first, second: jax.nn.gelu(first) * second, gate_val, up_val)
    gate_grad, up_grad = pull_glu(hidden_grad)
    gate_low, up_low = gate_grad.astype(LOW), up_grad.astype(LOW)
    normed2_grad = lax.psum_scatter(
        (times_transpose(gate_low, gate_whole) + times_transpose(up_low, up_whole)).astype(LOW),
        "seq", scatter_dimension=0, tiled=True,
    ).astype(WIDE)
    unused, pull_norm2 = jax.vjp(rms_scale, middle, mlp_scale)
    middle_part, mlp_gain_grad = pull_norm2(normed2_grad)
    middle_grad = grad_low.astype(WIDE) + middle_part
    mixed_all = lax.all_gather(middle_grad.astype(LOW), "seq", axis=0, tiled=True)

    product_grad = times_transpose(mixed_all, out_whole)
    states_grad = (product_grad * branch_y).astype(LOW)
    unused, pull_gelu = jax.vjp(jax.nn.gelu, branch_pre)
    (pre_grad,) = pull_gelu(product_grad * states_f)
    pre_low = pre_grad.astype(LOW)
    x_low, wr_grad, wi_grad, sums = mixer_backward(states_grad, branch_x, saved, wr, wi, par, size)

    normed_grad = lax.psum_scatter(
        (
            times_transpose(x_low, in_whole[:, :channels])
            + times_transpose(pre_low, in_whole[:, channels:])
        ).astype(LOW),
        "seq", scatter_dimension=0, tiled=True,
    ).astype(WIDE)
    unused, pull_norm = jax.vjp(rms_scale, resid_in, mix_scale)
    input_part, mix_gain_grad = pull_norm(normed_grad)
    input_grad = middle_grad + input_part

    down_grad = lax.psum_scatter(
        outer_sum(hidden, grad_all).astype(LOW), "fsdp", scatter_dimension=0, tiled=True
    ).astype(WIDE)
    glu_grad = jnp.concatenate(
        [outer_sum(normed2_all, gate_low), outer_sum(normed2_all, up_low)], axis=1
    )
    gate_w_grad, up_w_grad = scatter_columns(glu_grad, [hidden_width] * 2, rows)
    out_grad = lax.psum_scatter(
        outer_sum(product, mixed_all).astype(LOW), "fsdp", scatter_dimension=0, tiled=True
    ).astype(WIDE)
    in_grad = jnp.concatenate(
        [outer_sum(normed_all, x_low), outer_sum(normed_all, pre_low)], axis=1
    )
    lru_in_grad, gelu_in_grad = scatter_columns(in_grad, [channels] * 2, rows)
    small = jnp.concatenate(
        [
            wr_grad, wi_grad, sums[:7].T,
            (sums[7] * RATE_SCALE * jax.nn.sigmoid(-decay))[:, None],
        ],
        axis=1,
    )
    small = lax.psum_scatter(
        small.reshape(lax.axis_size("fsdp"), -1, small.shape[1]),
        "fsdp", scatter_dimension=0, tiled=False,
    )
    gain_parts = jnp.stack([mix_gain_grad, mlp_gain_grad]).reshape(2, -1, rows).transpose(1, 0, 2)
    gain_grads = lax.psum_scatter(
        gain_parts, ("seq", "fsdp"), scatter_dimension=0, tiled=False
    )
    first = 2 * size
    return (
        result.astype(LOW).reshape(tokens.shape),
        input_grad.astype(LOW).reshape(tokens.shape),
        gain_grads[0],
        lru_in_grad,
        gelu_in_grad,
        out_grad,
        small[:, first : first + 4],
        small[:, first + 4],
        small[:, :size],
        small[:, first + 5],
        small[:, size : 2 * size],
        small[:, first + 6],
        small[:, first + 7],
        gain_grads[1],
        gate_w_grad,
        up_w_grad,
        down_grad,
    )


def solution(mesh):
    tokens = P("fsdp", "seq", None)
    vector = P(("seq", "fsdp"))
    matrix = P(("seq", "fsdp"), None)
    ranks = (1, 2, 2, 2, 2, 1, 2, 1, 2, 1, 1, 1, 2, 2, 2)
    specs = (tokens, tokens) + tuple(vector if rank == 1 else matrix for rank in ranks)
    return jax.shard_map(local, mesh=mesh, in_specs=specs, out_specs=specs, check_vma=False)
```

```python
import functools

import jax
import jax.numpy as jnp
from jax import lax
from jax.experimental import pallas as pl
from jax.experimental.pallas import tpu as pltpu
from jax.sharding import PartitionSpec as P

EPSILON = 1e-06
RATE_SCALE = 8.0
CHUNK = 128
LOW = jnp.bfloat16
WIDE = jnp.float32


def rms_scale(values, gain):
    scale = lax.rsqrt(jnp.mean(values * values, axis=-1, keepdims=True) + EPSILON)
    return values * scale * gain


def dot(left, right):
    return jnp.dot(left, right, preferred_element_type=WIDE)


def outer_sum(left, right):
    return lax.dot_general(left, right, (((0,), (0,)), ((), ())), preferred_element_type=WIDE)


def times_transpose(left, right):
    return lax.dot_general(left, right, (((1,), (1,)), ((), ())), preferred_element_type=WIDE)


def one_minus_exp(value):
    series = jnp.full_like(value, 1.0 / 40320.0)
    for bottom in (5040.0, 720.0, 120.0, 24.0, 6.0, 2.0, 1.0):
        series = 1.0 / bottom - value * series
    return jnp.where(value < 0.4, value * series, 1.0 - jnp.exp(-value))


def sigmoid(value):
    return 0.5 * jnp.tanh(0.5 * value) + 0.5


def lane_tiles(channels):
    return -(-channels // 128)


def put(tiles, rows, value):
    channels = value.shape[1]
    for n in range(lane_tiles(channels)):
        size = min(128, channels - n * 128)
        tiles[n, rows, 0:size] = value[:, n * 128 : n * 128 + size]


def get(tiles, rows, channels):
    return jnp.concatenate(
        [
            tiles[n, rows, 0 : min(128, channels - n * 128)]
            for n in range(lane_tiles(channels))
        ],
        axis=1,
    )


def scan_segments(step, count, tiles):
    def body(i, carried):
        return tuple(step(i, n, *carried[n]) for n in range(tiles))

    start = (jnp.zeros((8, 128), WIDE), jnp.ones((8, 128), WIDE))
    ends = lax.fori_loop(0, count, body, (start,) * tiles, unroll=4)
    return [jnp.concatenate([end[which] for end in ends], axis=1) for which in (0, 1)]


MESH = pl.DeviceIdType.MESH
VMEM_BYTES = 58 * 2**20
ANY = pl.BlockSpec(memory_space=pl.ANY)
HELD = pl.BlockSpec(memory_space=pltpu.VMEM)
ROOT = 0.7978845608028654
CUBE = 0.044715


def dma(*shape):
    return pltpu.SemaphoreType.DMA(shape)


def remote(src, dst, send, recv, axis, index):
    return pltpu.make_async_remote_copy(
        src_ref=src, dst_ref=dst, send_sem=send, recv_sem=recv,
        device_id={axis: index}, device_id_type=MESH,
    )


def gelu(value):
    return 0.5 * value * (1.0 + jnp.tanh(ROOT * (value + CUBE * value * value * value)))


def gelu_and_slope(value):
    square = value * value
    bent = jnp.tanh(ROOT * (value + CUBE * square * value))
    half = 0.5 * (1.0 + bent)
    slope = half + 0.5 * value * (1.0 - bent * bent) * (ROOT * (1.0 + 3.0 * CUBE * square))
    return value * half, slope


class Place:
    def __init__(self, shards, groups):
        self.shards, self.groups, self.line = shards, groups, shards // 2
        self.s, self.f = lax.axis_index("seq"), lax.axis_index("fsdp")
        self.z, self.c = self.s // 2, lax.rem(self.s, 2)
        self.sibling = 2 * self.z + 1 - self.c

    def enter(self, seq=True, fsdp=True):
        barrier = pltpu.get_barrier_semaphore()
        met = 0
        for axis, mine, count, wanted in (
            ("seq", self.s, self.shards, seq), ("fsdp", self.f, self.groups, fsdp),
        ):
            for d in range(1, count if wanted else 1):
                pl.semaphore_signal(
                    barrier, inc=1, device_id={axis: lax.rem(mine + d, count)}, device_id_type=MESH
                )
                met += 1
        pl.semaphore_wait(barrier, met)


class Spread:
    def __init__(self, at, src, dst, send, recv, axis="fsdp"):
        self.at, self.src, self.dst, self.send, self.recv, self.axis = at, src, dst, send, recv, axis
        self.mine, self.count = (at.f, at.groups) if axis == "fsdp" else (at.s, at.shards)

    def copy(self, d):
        peer = lax.rem(self.mine + d, self.count)
        return remote(
            self.src(peer), self.dst(self.mine), self.send.at[d], self.recv.at[d], self.axis, peer
        )

    def start(self):
        for d in range(1, self.count):
            self.copy(d).start()

    def source(self, d):
        return lax.rem(self.mine + self.count - d, self.count)

    def arrive(self, d):
        origin = self.source(d)
        remote(
            self.src(origin), self.dst(origin), self.send.at[d], self.recv.at[d], self.axis, origin
        ).wait_recv()

    def sent(self):
        for d in range(1, self.count):
            self.copy(d).wait_send()

    def finish(self):
        for d in range(1, self.count):
            self.arrive(d)
        self.sent()


class LineGather:
    def __init__(self, at, src, buf, send, recv, pieces):
        self.at, self.src, self.buf, self.send, self.recv, self.pieces = at, src, buf, send, recv, pieces
        self.rows = buf.shape[1] // pieces

    def copy(self, slot, piece, kind, first=False):
        at = self.at
        rows = pl.ds(piece * self.rows, self.rows)
        there = self.buf.at[slot, rows]
        peer = (at.sibling, at.s + 2, at.s - 2)[kind]
        return remote(
            self.src.at[rows] if first else there, there,
            self.send.at[slot, piece, kind], self.recv.at[slot, piece], "seq", peer,
        )

    def start(self):
        at = self.at
        for piece in range(self.pieces):
            @pl.when(at.z + 1 < at.line)
            def _():
                self.copy(at.s, piece, 1, True).start()

            @pl.when(at.z > 0)
            def _():
                self.copy(at.s, piece, 2, True).start()

            self.copy(at.s, piece, 0, True).start()

    def arrive(self, chip):
        at = self.at
        slot = 2 * chip + at.c
        for piece in range(self.pieces):
            self.copy(slot, piece, 0).wait_recv()

            @pl.when((chip < at.z) & (at.z + 1 < at.line))
            def _():
                self.copy(slot, piece, 1).start()

            @pl.when((chip > at.z) & (at.z > 0))
            def _():
                self.copy(slot, piece, 2).start()

            self.copy(slot, piece, 0).start()

    def settle(self, chip):
        for piece in range(self.pieces):
            self.copy(2 * chip + 1 - self.at.c, piece, 0).wait_recv()

    def distances(self, body):
        at = self.at
        self.settle(at.z)
        body(at.z)

        @pl.loop(1, at.line)
        def _(d):
            @pl.when(at.z - d >= 0)
            def _():
                self.arrive(at.z - d)

            @pl.when(at.z + d < at.line)
            def _():
                self.arrive(at.z + d)

            @pl.loop(0, 2)
            def _(side):
                chip = at.z - d + 2 * d * side

                @pl.when((chip >= 0) & (chip < at.line))
                def _():
                    self.settle(chip)
                    body(chip)

    def sent(self):
        at = self.at
        for chip in range(at.line):
            slot = 2 * chip + at.c
            for piece in range(self.pieces):
                self.copy(slot, piece, 0).wait_send()

                @pl.when((chip <= at.z) & (at.z + 1 < at.line))
                def _():
                    self.copy(slot, piece, 1).wait_send()

                @pl.when((chip >= at.z) & (at.z > 0))
                def _():
                    self.copy(slot, piece, 2).wait_send()


class LineScatter:
    def __init__(self, at, own, other, heard, out, into, sems, pieces):
        self.at, self.own, self.other, self.heard, self.out, self.into = at, own, other, heard, out, into
        self.sib_send, self.sib_recv, self.send, self.recv = sems
        self.pieces = pieces
        self.rows = own.shape[1] // pieces

    @staticmethod
    def scratch(line, rows, width, pieces):
        low = pltpu.VMEM((line, rows, width), LOW)
        return [
            pltpu.VMEM((line, rows, width), WIDE), low, low, low,
            pltpu.VMEM((line + 1, rows, width), LOW),
            dma(line), dma(line), dma(line, pieces), dma(line + 1, pieces),
        ]

    def across(self, chip):
        return remote(
            self.other.at[chip], self.heard.at[chip], self.sib_send.at[chip],
            self.sib_recv.at[chip], "seq", self.at.sibling,
        )

    def along(self, chip, piece, up):
        at = self.at
        rows = pl.ds(pl.multiple_of(piece * self.rows, self.rows), self.rows)
        there = chip if up else jnp.where(chip == at.z - 1, at.line, chip)
        return remote(
            self.out.at[chip, rows], self.into.at[there, rows], self.send.at[chip, piece],
            self.recv.at[there, piece], "seq", at.s + 2 if up else at.s - 2,
        )

    def landed(self, index, piece):
        rows = pl.ds(pl.multiple_of(piece * self.rows, self.rows), self.rows)
        there = self.into.at[index, rows]
        remote(
            there, there, self.recv.at[index, piece], self.recv.at[index, piece], "seq", self.at.sibling
        ).wait_recv()

    def add(self, chip, piece, extras, store):
        @pl.loop(0, self.rows // 16)
        def _(block):
            rows = pl.ds(pl.multiple_of(piece * self.rows + block * 16, 16), 16)
            total = self.own[chip, rows, :] + self.heard[chip, rows, :].astype(WIDE)
            for known, index in extras:
                total = total + jnp.where(known, self.into[index, rows, :].astype(WIDE), 0.0)
            store(rows, total)

    def step(self, k):
        at = self.at
        for up in (True, False):
            chip = at.line - 1 - k if up else k
            passes = at.z > 0 if up else at.z + 1 < at.line

            @pl.when(chip > at.z if up else chip < at.z)
            def _():
                self.across(chip).wait_recv()

                @pl.loop(0, self.pieces)
                def _(piece):
                    @pl.when(passes)
                    def _():
                        self.landed(chip, piece)

                    def store(rows, total):
                        self.out[chip, rows, :] = total.astype(LOW)

                    self.add(chip, piece, [(passes, chip)], store)
                    self.along(chip, piece, up).start()

    def steps(self, first=0):
        @pl.loop(first, self.at.line - 1)
        def _(k):
            self.step(k)

    def finish(self, store):
        at = self.at
        below, above = at.z > 0, at.z + 1 < at.line
        self.across(at.z).wait_recv()

        @pl.loop(0, self.pieces)
        def _(piece):
            @pl.when(below)
            def _():
                self.landed(at.z, piece)

            @pl.when(above)
            def _():
                self.landed(at.line, piece)

            self.add(at.z, piece, [(below, at.z), (above, at.line)], store)

    def sent(self):
        at = self.at
        for chip in range(at.line):
            self.across(chip).wait_send()

            @pl.loop(0, self.pieces)
            def _(piece):
                @pl.when(chip > at.z)
                def _():
                    self.along(chip, piece, True).wait_send()

                @pl.when(chip < at.z)
                def _():
                    self.along(chip, piece, False).wait_send()


def normalise(source, gain, store, rows):
    @pl.loop(0, rows // 16)
    def _(block):
        here = pl.ds(pl.multiple_of(block * 16, 16), 16)
        values = source(here)
        scale = lax.rsqrt(jnp.mean(values * values, axis=-1, keepdims=True) + EPSILON)
        store(here, (values * scale * gain).astype(LOW))


def mixer_rows(positions):
    return [pl.ds(pl.multiple_of(n, CHUNK), CHUNK) for n in range(0, positions, CHUNK)]


def mix_in_kernel(
    tokens, in_shard, glu_shard, out_shard, down_shard, small, vecs, gain_shard,
    normed, in_whole, x_ref, pre_ref, conv_ref, r_ref, i_ref, f_ref, m_ref, st_ref,
    product_ref, par_ref, wr_ref, wi_ref, gains, glu_mine, out_whole, down_whole,
    held, small_all, vecs_all, gain_all, ext, factors, drive, prod,
    local_sems, tok_send, tok_recv, in_sems, in_xy_send, in_xy_recv, glu_sems, xy_sems, gain_sems,
):
    groups, shards = in_whole.shape[1], in_whole.shape[0]
    at = Place(shards, groups)
    s, f = at.s, at.f
    positions, channels = x_ref.shape
    width = tokens.shape[1]
    rows = in_shard.shape[1]
    segment = positions // 8
    chunks = positions // CHUNK

    keep = [
        (tokens, held.at[s]), (in_shard.at[s], in_whole.at[s, f]), (glu_shard.at[s], glu_mine.at[s]),
        (out_shard, out_whole.at[f]), (down_shard, down_whole.at[f]), (small, small_all.at[f]),
        (vecs, vecs_all.at[f]), (gain_shard, gain_all.at[s, f]),
    ]
    keep = [pltpu.make_async_copy(a, b, local_sems.at[n]) for n, (a, b) in enumerate(keep)]
    for copy in keep:
        copy.start()
    at.enter()

    def over_fsdp(src, dst, n):
        return Spread(at, lambda peer: src, lambda origin: dst.at[origin], xy_sems.at[n, 0], xy_sems.at[n, 1])

    gain_xy = Spread(
        at, lambda peer: gain_shard, lambda origin: gain_all.at[s, origin],
        xy_sems.at[0, 0], xy_sems.at[0, 1],
    )
    small_xy = over_fsdp(small, small_all, 1)
    vecs_xy = over_fsdp(vecs, vecs_all, 2)
    out_xy = over_fsdp(out_shard, out_whole, 3)
    down_xy = over_fsdp(down_shard, down_whole, 4)
    in_z = Spread(
        at, lambda peer: in_shard.at[peer], lambda origin: in_whole.at[origin, f],
        in_sems.at[0], in_sems.at[1], "seq",
    )
    glu_z = Spread(
        at, lambda peer: glu_shard.at[peer], lambda origin: glu_mine.at[origin],
        glu_sems.at[0], glu_sems.at[1], "seq",
    )
    gain_z = Spread(
        at, lambda peer: gain_all.at[s], lambda origin: gain_all.at[origin],
        gain_sems.at[0], gain_sems.at[1], "seq",
    )

    def in_xy(index):
        return Spread(
            at, lambda peer: in_whole.at[index, f], lambda origin: in_whole.at[index, origin],
            in_xy_send.at[index], in_xy_recv.at[index],
        )

    gather = LineGather(at, tokens, held, tok_send, tok_recv, tok_send.shape[1])
    gain_xy.start()
    in_z.start()
    keep[1].wait()
    in_xy(s).start()
    gather.start()
    vecs_xy.start()
    small_xy.start()
    keep[7].wait()
    gain_xy.finish()
    gain_z.start()
    for d in range(1, shards):
        in_z.arrive(d)
        in_xy(in_z.source(d)).start()
    out_xy.start()
    gain_z.finish()
    for origin in range(shards):
        for other in range(groups):
            first = (origin * groups + other) * rows
            gains[:, first : first + rows] = gain_all[origin, other]
    keep[0].wait()

    def take(chip):
        for core in range(2):
            slot = 2 * chip + core

            def store(here, value):
                normed[slot, here, :] = value

            normalise(
                lambda here: held[slot, here, :].astype(WIDE), gains[0:1, :], store, tokens.shape[0]
            )

    gather.distances(take)
    glu_z.start()
    keep[6].wait()
    vecs_xy.finish()
    keep[5].wait()
    small_xy.finish()
    size = small.shape[1] // 2
    local = small.shape[0]
    wr_ref[...] = jnp.zeros_like(wr_ref)
    wi_ref[...] = jnp.zeros_like(wi_ref)
    flat = small_all[...].reshape(channels, 2 * size)
    for n in range(channels // size):
        block = slice(n * size, (n + 1) * size)
        wr_ref[block, block] = flat[block, :size]
        wi_ref[block, block] = flat[block, size:]
    for other in range(groups):
        par_ref[:, other * local : (other + 1) * local] = vecs_all[other]
    ext[0:8, :] = jnp.zeros((8, channels), WIDE)
    st_ref[0:8, :] = jnp.zeros((8, channels), WIDE)
    for index in range(shards):
        for d in range(1, groups):
            in_xy(index).arrive(d)
    down_xy.start()

    @pl.loop(0, at.line)
    def _(chip):
        pair = normed[pl.ds(2 * chip, 2), :, :].reshape(2 * tokens.shape[0], width)
        both = dot(pair, in_whole[...].reshape(width, 2 * channels))
        base = pl.multiple_of(chip * 2 * tokens.shape[0], CHUNK)
        here = pl.ds(base, 2 * tokens.shape[0])
        x_low = both[:, :channels].astype(LOW)
        x_ref[here, :] = x_low
        ext[pl.ds(base + 8, 2 * tokens.shape[0]), :] = x_low.astype(WIDE)
        pre_ref[here, :] = both[:, channels:]

    @pl.loop(0, chunks)
    def _(n):
        base = pl.multiple_of(n * CHUNK, CHUNK)
        here = pl.ds(base, CHUNK)
        block = ext[pl.ds(base, CHUNK + 8), :]
        conv = jnp.broadcast_to(par_ref[4:5, :], (CHUNK, channels))
        for k in range(4):
            conv = conv + par_ref[k : k + 1, :] * block[8 - k : 8 - k + CHUNK]
        conv_low = conv.astype(LOW)
        conv_ref[here, :] = conv_low
        r = jax.nn.sigmoid(dot(conv_low, wr_ref[...]) + par_ref[5:6, :])
        gate = jax.nn.sigmoid(dot(conv_low, wi_ref[...]) + par_ref[6:7, :])
        log_decay = r * par_ref[7:8, :]
        m = jnp.sqrt(one_minus_exp(-2.0 * log_decay))
        factor = jnp.exp(log_decay)
        r_ref[here, :] = r
        i_ref[here, :] = gate
        f_ref[here, :] = factor
        m_ref[here, :] = m
        put(factors, here, factor)
        put(drive, here, m * gate * conv_low.astype(WIDE))

    def step(i, n, state, product):
        here = pl.ds(i, 8, stride=segment)
        factor = factors[n, here, :]
        state = factor * state + drive[n, here, :]
        product = factor * product
        drive[n, here, :] = state
        prod[n, here, :] = product
        return state, product

    state, product = scan_segments(step, segment, lane_tiles(channels))
    state, product = state[:, :channels], product[:, :channels]
    carry = jnp.zeros((1, channels), WIDE)
    for k in range(8):
        for part in range(segment // CHUNK):
            base = k * segment + part * CHUNK
            here = slice(base, base + CHUNK)
            states = get(drive, here, channels) + get(prod, here, channels) * carry
            st_ref[base + 8 : base + 8 + CHUNK, :] = states
            product_ref[here, :] = (
                states.astype(LOW).astype(WIDE) * gelu(pre_ref[here, :])
            ).astype(LOW)
        carry = state[k : k + 1] + product[k : k + 1] * carry

    glu_z.finish()
    out_xy.finish()
    down_xy.finish()
    gather.sent()
    in_z.sent()
    for index in range(shards):
        in_xy(index).sent()
    for n in (2, 3, 4):
        keep[n].wait()


def mix_in(tokens, in_shard, glu_shard, out_shard, down_shard, small, vecs, gain_shard, groups):
    shards, rows, both = in_shard.shape
    block, width = tokens.shape
    positions, channels = shards * block, both // 2
    local = small.shape[0]
    pieces = 2
    wide = jax.ShapeDtypeStruct((positions, channels), WIDE)
    low = jax.ShapeDtypeStruct((positions, channels), LOW)
    square = jax.ShapeDtypeStruct((channels, channels), LOW)
    held = [
        jax.ShapeDtypeStruct((shards, block, width), LOW),
        jax.ShapeDtypeStruct((shards, groups, rows, both), LOW),
        low, wide, low, wide, wide, wide, wide,
        jax.ShapeDtypeStruct((positions + 8, channels), WIDE),
        low, jax.ShapeDtypeStruct((8, channels), WIDE), square, square,
        jax.ShapeDtypeStruct((8, width), WIDE),
    ]
    far = [
        jax.ShapeDtypeStruct((shards, rows, glu_shard.shape[2]), LOW),
        jax.ShapeDtypeStruct((groups,) + out_shard.shape, LOW),
        jax.ShapeDtypeStruct((groups,) + down_shard.shape, LOW),
    ]
    return pl.pallas_call(
        mix_in_kernel,
        out_shape=held + far,
        in_specs=[HELD] + [ANY] * 7,
        out_specs=[HELD] * len(held) + [ANY] * len(far),
        scratch_shapes=[
            pltpu.VMEM((shards, block, width), LOW),
            pltpu.VMEM((groups,) + small.shape, LOW),
            pltpu.VMEM((groups,) + vecs.shape, WIDE),
            pltpu.VMEM((shards, groups) + gain_shard.shape, WIDE),
            pltpu.VMEM((positions + 8, channels), WIDE),
        ]
        + [pltpu.VMEM((lane_tiles(channels), positions, 128), WIDE)] * 3
        + [
            dma(8), dma(shards, pieces, 3), dma(shards, pieces), dma(2, shards), dma(shards, groups),
            dma(shards, groups), dma(2, shards), dma(5, 2, groups), dma(2, shards),
        ],
        compiler_params=pltpu.CompilerParams(
            collective_id=1, has_side_effects=True, vmem_limit_bytes=VMEM_BYTES
        ),
        name="mix_in",
    )(tokens, in_shard, glu_shard, out_shard, down_shard, small, vecs, gain_shard)


def mixer_forward_kernel(
    x_ref, wr_ref, wi_ref, par_ref,
    conv_ref, r_ref, i_ref, f_ref, m_ref, st_ref,
    ext, factors, drive, prod,
):
    positions, channels = x_ref.shape
    segment = positions // 8
    chunks = positions // CHUNK
    ext[0:8, :] = jnp.zeros((8, channels), WIDE)
    st_ref[0:8, :] = jnp.zeros((8, channels), WIDE)

    @pl.loop(0, chunks)
    def _(c):
        base = pl.multiple_of(c * CHUNK, CHUNK)
        ext[pl.ds(base + 8, CHUNK), :] = x_ref[pl.ds(base, CHUNK), :].astype(WIDE)

    @pl.loop(0, chunks)
    def _(c):
        base = pl.multiple_of(c * CHUNK, CHUNK)
        rows = pl.ds(base, CHUNK)
        block = ext[pl.ds(base, CHUNK + 8), :]
        conv = jnp.broadcast_to(par_ref[4:5, :], (CHUNK, channels))
        for k in range(4):
            conv = conv + par_ref[k : k + 1, :] * block[8 - k : 8 - k + CHUNK]
        conv_low = conv.astype(LOW)
        conv_ref[rows, :] = conv_low
        r = jax.nn.sigmoid(dot(conv_low, wr_ref[...]) + par_ref[5:6, :])
        gate = jax.nn.sigmoid(dot(conv_low, wi_ref[...]) + par_ref[6:7, :])
        log_decay = r * par_ref[7:8, :]
        m = jnp.sqrt(one_minus_exp(-2.0 * log_decay))
        r_ref[rows, :] = r
        i_ref[rows, :] = gate
        factor = jnp.exp(log_decay)
        f_ref[rows, :] = factor
        m_ref[rows, :] = m
        put(factors, rows, factor)
        put(drive, rows, m * gate * conv_low.astype(WIDE))

    def step(i, n, state, product):
        rows = pl.ds(i, 8, stride=segment)
        factor = factors[n, rows, :]
        state = factor * state + drive[n, rows, :]
        product = factor * product
        drive[n, rows, :] = state
        prod[n, rows, :] = product
        return state, product

    state, product = scan_segments(step, segment, lane_tiles(channels))
    state, product = state[:, :channels], product[:, :channels]
    carry = jnp.zeros((1, channels), WIDE)
    for k in range(8):
        for part in range(segment // CHUNK):
            base = k * segment + part * CHUNK
            rows = slice(base, base + CHUNK)
            st_ref[base + 8 : base + 8 + CHUNK, :] = (
                get(drive, rows, channels) + get(prod, rows, channels) * carry
            )
        carry = state[k : k + 1] + product[k : k + 1] * carry


def mixer_backward_kernel(
    ds_ref, x_ref, conv_ref, r_ref, i_ref, f_ref, m_ref, st_ref, wr_ref, wi_ref, par_ref,
    xg_ref, wrg_ref, wig_ref, sums_ref,
    ext, factors, adj, prod, cg, carries, wr_sum, wi_sum,
):
    positions, channels = x_ref.shape
    segment = positions // 8
    chunks = positions // CHUNK
    ext[0:8, :] = jnp.zeros((8, channels), WIDE)
    cg[pl.ds(positions, 8), :] = jnp.zeros((8, channels), WIDE)
    wr_sum[...] = jnp.zeros_like(wr_sum)
    wi_sum[...] = jnp.zeros_like(wi_sum)

    @pl.loop(0, chunks)
    def _(c):
        base = pl.multiple_of(c * CHUNK, CHUNK)
        ext[pl.ds(base + 8, CHUNK), :] = x_ref[pl.ds(base, CHUNK), :].astype(WIDE)
        put(adj, pl.ds(base, CHUNK), ds_ref[pl.ds(base, CHUNK), :].astype(WIDE))
        put(factors, pl.ds(base, CHUNK), f_ref[pl.ds(base, CHUNK), :])

    def step(j, n, flow, product):
        rows = pl.ds(segment - 1 - j, 8, stride=segment)
        factor = factors[n, rows, :]
        adjoint = adj[n, rows, :] + flow
        adj[n, rows, :] = adjoint
        prod[n, rows, :] = product
        return factor * adjoint, factor * product

    flow, product = scan_segments(step, segment, lane_tiles(channels))
    flow, product = flow[:, :channels], product[:, :channels]
    carry = jnp.zeros((1, channels), WIDE)
    for k in range(7, -1, -1):
        carries[k : k + 1, :] = carry
        carry = flow[k : k + 1] + product[k : k + 1] * carry

    def grads(c, sums):
        base = pl.multiple_of(c * CHUNK, CHUNK)
        rows = pl.ds(base, CHUNK)
        adjoint = get(adj, rows, channels) + get(prod, rows, channels) * carries[pl.ds(base // segment, 1), :]
        before = st_ref[pl.ds(base, CHUNK + 8), :][7 : 7 + CHUNK]
        conv_low = conv_ref[rows, :]
        conv = conv_low.astype(WIDE)
        r = r_ref[rows, :]
        gate = i_ref[rows, :]
        factor = f_ref[rows, :]
        m = m_ref[rows, :]
        driven = adjoint * gate
        by_log = adjoint * before * factor - driven * conv * factor * factor / m
        by_r = by_log * par_ref[7:8, :] * r * (1.0 - r)
        by_i = adjoint * m * conv * gate * (1.0 - gate)
        by_r_low = by_r.astype(LOW)
        by_i_low = by_i.astype(LOW)
        conv_grad = (
            driven * m
            + times_transpose(by_r_low, wr_ref[...])
            + times_transpose(by_i_low, wi_ref[...])
        )
        cg[rows, :] = conv_grad
        wr_sum[...] += outer_sum(conv_low, by_r_low)
        wi_sum[...] += outer_sum(conv_low, by_i_low)
        block = ext[pl.ds(base, CHUNK + 8), :]
        rows_of = [conv_grad * block[8 - k : 8 - k + CHUNK] for k in range(4)]
        rows_of += [conv_grad, by_r, by_i, by_log * r]
        return tuple(
            total + jnp.sum(member, axis=0, keepdims=True) for total, member in zip(sums, rows_of)
        )

    zero = jnp.zeros((1, channels), WIDE)
    sums = lax.fori_loop(0, chunks, grads, (zero,) * 8)
    for k in range(8):
        sums_ref[k : k + 1, :] = sums[k]
    size = wrg_ref.shape[1]
    for n in range(channels // size):
        block = slice(n * size, (n + 1) * size)
        wrg_ref[block, :] = wr_sum[block, block]
        wig_ref[block, :] = wi_sum[block, block]

    @pl.loop(0, chunks)
    def _(c):
        base = pl.multiple_of(c * CHUNK, CHUNK)
        block = cg[pl.ds(base, CHUNK + 8), :]
        total = jnp.zeros((CHUNK, channels), WIDE)
        for k in range(4):
            total = total + par_ref[k : k + 1, :] * block[k : k + CHUNK]
        xg_ref[pl.ds(base, CHUNK), :] = total.astype(LOW)


def mixer_forward(x, wr, wi, par):
    positions, channels = x.shape
    wide = jax.ShapeDtypeStruct((positions, channels), WIDE)
    return pl.pallas_call(
        mixer_forward_kernel,
        out_shape=(
            jax.ShapeDtypeStruct((positions, channels), LOW), wide, wide, wide, wide,
            jax.ShapeDtypeStruct((positions + 8, channels), WIDE),
        ),
        scratch_shapes=[pltpu.VMEM((positions + 8, channels), WIDE)]
        + [pltpu.VMEM((lane_tiles(channels), positions, 128), WIDE)] * 3,
        compiler_params=pltpu.CompilerParams(vmem_limit_bytes=48 * 2**20),
        name="mixer_forward",
    )(x, wr, wi, par)


def mixer_backward(ds, x, saved, wr, wi, par, size):
    positions, channels = x.shape
    square = jax.ShapeDtypeStruct((channels, size), WIDE)
    return pl.pallas_call(
        mixer_backward_kernel,
        out_shape=(
            jax.ShapeDtypeStruct((positions, channels), LOW), square, square,
            jax.ShapeDtypeStruct((8, channels), WIDE),
        ),
        scratch_shapes=[pltpu.VMEM((positions + 8, channels), WIDE)]
        + [pltpu.VMEM((lane_tiles(channels), positions, 128), WIDE)] * 3
        + [pltpu.VMEM((positions + 8, channels), WIDE), pltpu.VMEM((8, channels), WIDE)]
        + [pltpu.VMEM((channels, channels), WIDE)] * 2,
        compiler_params=pltpu.CompilerParams(vmem_limit_bytes=48 * 2**20),
        name="mixer_backward",
    )(ds, x, *saved, wr, wi, par)


def gather_columns(weights):
    shards = lax.axis_size("seq")
    rows = weights[0].shape[0]
    widths = [member.shape[1] // shards for member in weights]
    stacked = jnp.concatenate(
        [member.reshape(rows, shards, width) for member, width in zip(weights, widths)], axis=2
    )
    mine = lax.all_to_all(stacked.transpose(1, 0, 2), "seq", split_axis=0, concat_axis=0)
    whole = lax.all_gather(mine, "fsdp", axis=1)
    return whole.reshape(-1, sum(widths))


def scatter_columns(grad, widths, rows):
    shards, groups = lax.axis_size("seq"), lax.axis_size("fsdp")
    parts = grad.astype(LOW).reshape(shards, groups, rows, sum(widths)).transpose(1, 0, 2, 3)
    mine = lax.psum_scatter(parts, "fsdp", scatter_dimension=0, tiled=False)
    swapped = lax.all_to_all(mine, "seq", split_axis=0, concat_axis=0).astype(WIDE)
    outs, first = [], 0
    for width in widths:
        outs.append(swapped[:, :, first : first + width].transpose(1, 0, 2).reshape(rows, -1))
        first += width
    return outs


def block_diagonal(weight, blocks):
    size = weight.shape[1]
    shaped = weight.reshape(blocks, size, size)
    full = jnp.zeros((blocks, size, blocks, size), weight.dtype)
    for n in range(blocks):
        full = full.at[n, :, n, :].set(shaped[n])
    return full.reshape(blocks * size, blocks * size)


def general(
    tokens, cotangent, mix_gain, lru_in_weight, gelu_in_weight, out_weight, conv_weight, conv_bias,
    recurrence_weight, recurrence_bias, input_gate_weight, input_gate_bias, decay_param, mlp_gain,
    gate_weight, up_weight, down_weight,
):
    positions, width = tokens.shape[1:]
    rows = lru_in_weight.shape[0]
    shards = lax.axis_size("seq")
    channels = lru_in_weight.shape[1] // shards
    hidden_width = gate_weight.shape[1] // shards
    size = recurrence_weight.shape[1]

    gains = lax.all_gather(
        jnp.stack([mix_gain, mlp_gain], axis=1), ("seq", "fsdp"), axis=0, tiled=True
    ).astype(WIDE)
    mix_scale, mlp_scale = gains[:, 0], gains[:, 1]
    in_whole = gather_columns([lru_in_weight, gelu_in_weight])
    lru_params = lax.all_gather(
        jnp.concatenate(
            [
                recurrence_weight, input_gate_weight, conv_weight, conv_bias[:, None],
                recurrence_bias[:, None], input_gate_bias[:, None], decay_param[:, None],
            ],
            axis=1,
        ),
        "fsdp", axis=0, tiled=True,
    )
    out_whole = lax.all_gather(out_weight, "fsdp", axis=0, tiled=True)
    glu_whole = gather_columns([gate_weight, up_weight])
    down_whole = lax.all_gather(down_weight, "fsdp", axis=0, tiled=True)

    wr = block_diagonal(lru_params[:, :size], channels // size)
    wi = block_diagonal(lru_params[:, size : 2 * size], channels // size)
    vectors = lru_params[:, 2 * size :].astype(WIDE).T
    decay = vectors[7]
    par = jnp.concatenate([vectors[:7], -RATE_SCALE * jax.nn.softplus(-decay)[None]], axis=0)

    resid_in = tokens.reshape(positions, width).astype(WIDE)
    grad_low = cotangent.reshape(positions, width)
    normed_low = rms_scale(resid_in, mix_scale).astype(LOW)
    normed_all = lax.all_gather(normed_low, "seq", axis=0, tiled=True)
    grad_all = lax.all_gather(grad_low, "seq", axis=0, tiled=True)
    branch_x = dot(normed_all, in_whole[:, :channels]).astype(LOW)
    branch_pre = dot(normed_all, in_whole[:, channels:])
    branch_y = jax.nn.gelu(branch_pre)

    saved = mixer_forward(branch_x, wr, wi, par)
    states_f = saved[5][8:].astype(LOW).astype(WIDE)
    product = (states_f * branch_y).astype(LOW)
    mixed = lax.psum_scatter(
        dot(product, out_whole).astype(LOW), "seq", scatter_dimension=0, tiled=True
    )
    middle = resid_in + mixed.astype(WIDE)
    normed2_low = rms_scale(middle, mlp_scale).astype(LOW)
    normed2_all = lax.all_gather(normed2_low, "seq", axis=0, tiled=True)
    gate_whole, up_whole = glu_whole[:, :hidden_width], glu_whole[:, hidden_width:]
    gate_val = dot(normed2_all, gate_whole)
    up_val = dot(normed2_all, up_whole)
    hidden = (jax.nn.gelu(gate_val) * up_val).astype(LOW)
    fed = lax.psum_scatter(
        dot(hidden, down_whole).astype(LOW), "seq", scatter_dimension=0, tiled=True
    )
    result = middle + fed.astype(WIDE)

    hidden_grad = times_transpose(grad_all, down_whole)
    unused, pull_glu = jax.vjp(lambda first, second: jax.nn.gelu(first) * second, gate_val, up_val)
    gate_grad, up_grad = pull_glu(hidden_grad)
    gate_low, up_low = gate_grad.astype(LOW), up_grad.astype(LOW)
    normed2_grad = lax.psum_scatter(
        (times_transpose(gate_low, gate_whole) + times_transpose(up_low, up_whole)).astype(LOW),
        "seq", scatter_dimension=0, tiled=True,
    ).astype(WIDE)
    unused, pull_norm2 = jax.vjp(rms_scale, middle, mlp_scale)
    middle_part, mlp_gain_grad = pull_norm2(normed2_grad)
    middle_grad = grad_low.astype(WIDE) + middle_part
    mixed_all = lax.all_gather(middle_grad.astype(LOW), "seq", axis=0, tiled=True)

    product_grad = times_transpose(mixed_all, out_whole)
    states_grad = (product_grad * branch_y).astype(LOW)
    unused, pull_gelu = jax.vjp(jax.nn.gelu, branch_pre)
    (pre_grad,) = pull_gelu(product_grad * states_f)
    pre_low = pre_grad.astype(LOW)
    x_low, wr_grad, wi_grad, sums = mixer_backward(states_grad, branch_x, saved, wr, wi, par, size)

    normed_grad = lax.psum_scatter(
        (
            times_transpose(x_low, in_whole[:, :channels])
            + times_transpose(pre_low, in_whole[:, channels:])
        ).astype(LOW),
        "seq", scatter_dimension=0, tiled=True,
    ).astype(WIDE)
    unused, pull_norm = jax.vjp(rms_scale, resid_in, mix_scale)
    input_part, mix_gain_grad = pull_norm(normed_grad)
    input_grad = middle_grad + input_part

    down_grad = lax.psum_scatter(
        outer_sum(hidden, grad_all).astype(LOW), "fsdp", scatter_dimension=0, tiled=True
    ).astype(WIDE)
    glu_grad = jnp.concatenate(
        [outer_sum(normed2_all, gate_low), outer_sum(normed2_all, up_low)], axis=1
    )
    gate_w_grad, up_w_grad = scatter_columns(glu_grad, [hidden_width] * 2, rows)
    out_grad = lax.psum_scatter(
        outer_sum(product, mixed_all).astype(LOW), "fsdp", scatter_dimension=0, tiled=True
    ).astype(WIDE)
    in_grad = jnp.concatenate(
        [outer_sum(normed_all, x_low), outer_sum(normed_all, pre_low)], axis=1
    )
    lru_in_grad, gelu_in_grad = scatter_columns(in_grad, [channels] * 2, rows)
    small = jnp.concatenate(
        [
            wr_grad, wi_grad, sums[:7].T,
            (sums[7] * RATE_SCALE * jax.nn.sigmoid(-decay))[:, None],
        ],
        axis=1,
    )
    small = lax.psum_scatter(
        small.reshape(lax.axis_size("fsdp"), -1, small.shape[1]),
        "fsdp", scatter_dimension=0, tiled=False,
    )
    gain_parts = jnp.stack([mix_gain_grad, mlp_gain_grad]).reshape(2, -1, rows).transpose(1, 0, 2)
    gain_grads = lax.psum_scatter(
        gain_parts, ("seq", "fsdp"), scatter_dimension=0, tiled=False
    )
    first = 2 * size
    return (
        result.astype(LOW).reshape(tokens.shape),
        input_grad.astype(LOW).reshape(tokens.shape),
        gain_grads[0],
        lru_in_grad,
        gelu_in_grad,
        out_grad,
        small[:, first : first + 4],
        small[:, first + 4],
        small[:, :size],
        small[:, first + 5],
        small[:, size : 2 * size],
        small[:, first + 6],
        small[:, first + 7],
        gain_grads[1],
        gate_w_grad,
        up_w_grad,
        down_grad,
    )


def aligned(
    tokens, cotangent, mix_gain, lru_in_weight, gelu_in_weight, out_weight, conv_weight, conv_bias,
    recurrence_weight, recurrence_bias, input_gate_weight, input_gate_bias, decay_param, mlp_gain,
    gate_weight, up_weight, down_weight,
):
    positions, width = tokens.shape[1:]
    rows = lru_in_weight.shape[0]
    shards = lax.axis_size("seq")
    channels = lru_in_weight.shape[1] // shards
    hidden_width = gate_weight.shape[1] // shards
    size = recurrence_weight.shape[1]

    groups = lax.axis_size("fsdp")
    resid_in = tokens.reshape(positions, width).astype(WIDE)
    grad_low = cotangent.reshape(positions, width)

    def by_column(first, second):
        parts = [member.reshape(rows, shards, -1) for member in (first, second)]
        return jnp.concatenate(parts, axis=2).transpose(1, 0, 2)

    own_decay = decay_param.astype(WIDE)
    vecs = jnp.concatenate(
        [
            conv_weight.astype(WIDE).T,
            jnp.stack([conv_bias, recurrence_bias, input_gate_bias]).astype(WIDE),
            -RATE_SCALE * jax.nn.softplus(-own_decay)[None],
        ],
        axis=0,
    )
    gain_shard = jnp.pad(jnp.stack([mix_gain, mlp_gain]).astype(WIDE), ((0, 6), (0, 0)))
    (
        normed_all, in_whole, branch_x, branch_pre, *saved, product, par, wr, wi, gains,
        glu_mine, out_whole, down_whole,
    ) = mix_in(
        tokens.reshape(positions, width), by_column(lru_in_weight, gelu_in_weight),
        by_column(gate_weight, up_weight), out_weight, down_weight,
        jnp.concatenate([recurrence_weight, input_gate_weight], axis=1), vecs, gain_shard, groups,
    )
    normed_all = normed_all.reshape(-1, width)
    in_whole = in_whole.reshape(width, -1)
    out_whole = out_whole.reshape(-1, width)
    down_whole = down_whole.reshape(-1, width)
    mix_scale, mlp_scale = gains[0], gains[1]
    glu_whole = lax.all_gather(glu_mine, "fsdp", axis=1).reshape(width, -1)
    grad_all = lax.all_gather(grad_low, "seq", axis=0, tiled=True)
    branch_y = jax.nn.gelu(branch_pre)
    states_f = saved[5][8:].astype(LOW).astype(WIDE)
    mixed = lax.psum_scatter(
        dot(product, out_whole).astype(LOW), "seq", scatter_dimension=0, tiled=True
    )
    middle = resid_in + mixed.astype(WIDE)
    normed2_low = rms_scale(middle, mlp_scale).astype(LOW)
    normed2_all = lax.all_gather(normed2_low, "seq", axis=0, tiled=True)
    gate_whole, up_whole = glu_whole[:, :hidden_width], glu_whole[:, hidden_width:]
    gate_val = dot(normed2_all, gate_whole)
    up_val = dot(normed2_all, up_whole)
    hidden = (jax.nn.gelu(gate_val) * up_val).astype(LOW)
    fed = lax.psum_scatter(
        dot(hidden, down_whole).astype(LOW), "seq", scatter_dimension=0, tiled=True
    )
    result = middle + fed.astype(WIDE)

    hidden_grad = times_transpose(grad_all, down_whole)
    unused, pull_glu = jax.vjp(lambda first, second: jax.nn.gelu(first) * second, gate_val, up_val)
    gate_grad, up_grad = pull_glu(hidden_grad)
    gate_low, up_low = gate_grad.astype(LOW), up_grad.astype(LOW)
    normed2_grad = lax.psum_scatter(
        (times_transpose(gate_low, gate_whole) + times_transpose(up_low, up_whole)).astype(LOW),
        "seq", scatter_dimension=0, tiled=True,
    ).astype(WIDE)
    unused, pull_norm2 = jax.vjp(rms_scale, middle, mlp_scale)
    middle_part, mlp_gain_grad = pull_norm2(normed2_grad)
    middle_grad = grad_low.astype(WIDE) + middle_part
    mixed_all = lax.all_gather(middle_grad.astype(LOW), "seq", axis=0, tiled=True)

    product_grad = times_transpose(mixed_all, out_whole)
    states_grad = (product_grad * branch_y).astype(LOW)
    unused, pull_gelu = jax.vjp(jax.nn.gelu, branch_pre)
    (pre_grad,) = pull_gelu(product_grad * states_f)
    pre_low = pre_grad.astype(LOW)
    x_low, wr_grad, wi_grad, sums = mixer_backward(states_grad, branch_x, saved, wr, wi, par, size)

    normed_grad = lax.psum_scatter(
        (
            times_transpose(x_low, in_whole[:, :channels])
            + times_transpose(pre_low, in_whole[:, channels:])
        ).astype(LOW),
        "seq", scatter_dimension=0, tiled=True,
    ).astype(WIDE)
    unused, pull_norm = jax.vjp(rms_scale, resid_in, mix_scale)
    input_part, mix_gain_grad = pull_norm(normed_grad)
    input_grad = middle_grad + input_part

    down_grad = lax.psum_scatter(
        outer_sum(hidden, grad_all).astype(LOW), "fsdp", scatter_dimension=0, tiled=True
    ).astype(WIDE)
    glu_grad = jnp.concatenate(
        [outer_sum(normed2_all, gate_low), outer_sum(normed2_all, up_low)], axis=1
    )
    gate_w_grad, up_w_grad = scatter_columns(glu_grad, [hidden_width] * 2, rows)
    out_grad = lax.psum_scatter(
        outer_sum(product, mixed_all).astype(LOW), "fsdp", scatter_dimension=0, tiled=True
    ).astype(WIDE)
    in_grad = jnp.concatenate(
        [outer_sum(normed_all, x_low), outer_sum(normed_all, pre_low)], axis=1
    )
    lru_in_grad, gelu_in_grad = scatter_columns(in_grad, [channels] * 2, rows)
    small = jnp.concatenate(
        [
            wr_grad, wi_grad, sums[:7].T,
            (sums[7] * RATE_SCALE)[:, None],
        ],
        axis=1,
    )
    small = lax.psum_scatter(
        small.reshape(lax.axis_size("fsdp"), -1, small.shape[1]),
        "fsdp", scatter_dimension=0, tiled=False,
    )
    gain_parts = jnp.stack([mix_gain_grad, mlp_gain_grad]).reshape(2, -1, rows).transpose(1, 0, 2)
    gain_grads = lax.psum_scatter(
        gain_parts, ("seq", "fsdp"), scatter_dimension=0, tiled=False
    )
    first = 2 * size
    return (
        result.astype(LOW).reshape(tokens.shape),
        input_grad.astype(LOW).reshape(tokens.shape),
        gain_grads[0],
        lru_in_grad,
        gelu_in_grad,
        out_grad,
        small[:, first : first + 4],
        small[:, first + 4],
        small[:, :size],
        small[:, first + 5],
        small[:, size : 2 * size],
        small[:, first + 6],
        small[:, first + 7] * jax.nn.sigmoid(-own_decay),
        gain_grads[1],
        gate_w_grad,
        up_w_grad,
        down_grad,
    )


def solution(mesh):
    shards, groups = mesh.shape["seq"], mesh.shape["fsdp"]

    def local(*arrays):
        rows, small_rows = arrays[3].shape[0], arrays[5].shape[0]
        simple = shards % 2 == 0 and rows % 16 == 0 and small_rows % 16 == 0
        simple = simple and arrays[0].shape[1] * shards % (8 * CHUNK) == 0
        return (aligned if simple else general)(*arrays)

    tokens = P("fsdp", "seq", None)
    vector = P(("seq", "fsdp"))
    matrix = P(("seq", "fsdp"), None)
    ranks = (1, 2, 2, 2, 2, 1, 2, 1, 2, 1, 1, 1, 2, 2, 2)
    specs = (tokens, tokens) + tuple(vector if rank == 1 else matrix for rank in ranks)
    return jax.shard_map(local, mesh=mesh, in_specs=specs, out_specs=specs, check_vma=False)
```

```python
import functools

import jax
import jax.numpy as jnp
from jax import lax
from jax.experimental import pallas as pl
from jax.experimental.pallas import tpu as pltpu
from jax.sharding import PartitionSpec as P

EPSILON = 1e-06
RATE_SCALE = 8.0
CHUNK = 128
LOW = jnp.bfloat16
WIDE = jnp.float32


def rms_scale(values, gain):
    scale = lax.rsqrt(jnp.mean(values * values, axis=-1, keepdims=True) + EPSILON)
    return values * scale * gain


def dot(left, right):
    return jnp.dot(left, right, preferred_element_type=WIDE)


def outer_sum(left, right):
    return lax.dot_general(left, right, (((0,), (0,)), ((), ())), preferred_element_type=WIDE)


def times_transpose(left, right):
    return lax.dot_general(left, right, (((1,), (1,)), ((), ())), preferred_element_type=WIDE)


def one_minus_exp(value):
    series = jnp.full_like(value, 1.0 / 40320.0)
    for bottom in (5040.0, 720.0, 120.0, 24.0, 6.0, 2.0, 1.0):
        series = 1.0 / bottom - value * series
    return jnp.where(value < 0.4, value * series, 1.0 - jnp.exp(-value))


def sigmoid(value):
    return 0.5 * jnp.tanh(0.5 * value) + 0.5


def lane_tiles(channels):
    return -(-channels // 128)


def put(tiles, rows, value):
    channels = value.shape[1]
    for n in range(lane_tiles(channels)):
        size = min(128, channels - n * 128)
        tiles[n, rows, 0:size] = value[:, n * 128 : n * 128 + size]


def get(tiles, rows, channels):
    return jnp.concatenate(
        [
            tiles[n, rows, 0 : min(128, channels - n * 128)]
            for n in range(lane_tiles(channels))
        ],
        axis=1,
    )


def scan_segments(step, count, tiles):
    def body(i, carried):
        return tuple(step(i, n, *carried[n]) for n in range(tiles))

    start = (jnp.zeros((8, 128), WIDE), jnp.ones((8, 128), WIDE))
    ends = lax.fori_loop(0, count, body, (start,) * tiles, unroll=4)
    return [jnp.concatenate([end[which] for end in ends], axis=1) for which in (0, 1)]


MESH = pl.DeviceIdType.MESH
VMEM_BYTES = 58 * 2**20
ANY = pl.BlockSpec(memory_space=pl.ANY)
HELD = pl.BlockSpec(memory_space=pltpu.VMEM)
ROOT = 0.7978845608028654
CUBE = 0.044715


def dma(*shape):
    return pltpu.SemaphoreType.DMA(shape)


def remote(src, dst, send, recv, axis, index):
    return pltpu.make_async_remote_copy(
        src_ref=src, dst_ref=dst, send_sem=send, recv_sem=recv,
        device_id={axis: index}, device_id_type=MESH,
    )


def gelu(value):
    return 0.5 * value * (1.0 + jnp.tanh(ROOT * (value + CUBE * value * value * value)))


def gelu_and_slope(value):
    square = value * value
    bent = jnp.tanh(ROOT * (value + CUBE * square * value))
    half = 0.5 * (1.0 + bent)
    slope = half + 0.5 * value * (1.0 - bent * bent) * (ROOT * (1.0 + 3.0 * CUBE * square))
    return value * half, slope


class Place:
    def __init__(self, shards, groups):
        self.shards, self.groups, self.line = shards, groups, shards // 2
        self.s, self.f = lax.axis_index("seq"), lax.axis_index("fsdp")
        self.z, self.c = self.s // 2, lax.rem(self.s, 2)
        self.sibling = 2 * self.z + 1 - self.c

    def enter(self, seq=True, fsdp=True):
        barrier = pltpu.get_barrier_semaphore()
        met = 0
        for axis, mine, count, wanted in (
            ("seq", self.s, self.shards, seq), ("fsdp", self.f, self.groups, fsdp),
        ):
            for d in range(1, count if wanted else 1):
                pl.semaphore_signal(
                    barrier, inc=1, device_id={axis: lax.rem(mine + d, count)}, device_id_type=MESH
                )
                met += 1
        pl.semaphore_wait(barrier, met)


class Spread:
    def __init__(self, at, src, dst, send, recv, axis="fsdp"):
        self.at, self.src, self.dst, self.send, self.recv, self.axis = at, src, dst, send, recv, axis
        self.mine, self.count = (at.f, at.groups) if axis == "fsdp" else (at.s, at.shards)

    def copy(self, d):
        peer = lax.rem(self.mine + d, self.count)
        return remote(
            self.src(peer), self.dst(self.mine), self.send.at[d], self.recv.at[d], self.axis, peer
        )

    def start(self):
        for d in range(1, self.count):
            self.copy(d).start()

    def source(self, d):
        return lax.rem(self.mine + self.count - d, self.count)

    def arrive(self, d):
        origin = self.source(d)
        remote(
            self.src(origin), self.dst(origin), self.send.at[d], self.recv.at[d], self.axis, origin
        ).wait_recv()

    def sent(self):
        for d in range(1, self.count):
            self.copy(d).wait_send()

    def finish(self):
        for d in range(1, self.count):
            self.arrive(d)
        self.sent()


class LineGather:
    def __init__(self, at, src, buf, send, recv, pieces):
        self.at, self.src, self.buf, self.send, self.recv, self.pieces = at, src, buf, send, recv, pieces
        self.rows = buf.shape[1] // pieces

    def copy(self, slot, piece, kind, first=False):
        at = self.at
        rows = pl.ds(piece * self.rows, self.rows)
        there = self.buf.at[slot, rows]
        peer = (at.sibling, at.s + 2, at.s - 2)[kind]
        return remote(
            self.src.at[rows] if first else there, there,
            self.send.at[slot, piece, kind], self.recv.at[slot, piece], "seq", peer,
        )

    def start(self):
        at = self.at
        for piece in range(self.pieces):
            @pl.when(at.z + 1 < at.line)
            def _():
                self.copy(at.s, piece, 1, True).start()

            @pl.when(at.z > 0)
            def _():
                self.copy(at.s, piece, 2, True).start()

            self.copy(at.s, piece, 0, True).start()

    def arrive(self, chip):
        at = self.at
        slot = 2 * chip + at.c
        for piece in range(self.pieces):
            self.copy(slot, piece, 0).wait_recv()

            @pl.when((chip < at.z) & (at.z + 1 < at.line))
            def _():
                self.copy(slot, piece, 1).start()

            @pl.when((chip > at.z) & (at.z > 0))
            def _():
                self.copy(slot, piece, 2).start()

            self.copy(slot, piece, 0).start()

    def settle(self, chip):
        for piece in range(self.pieces):
            self.copy(2 * chip + 1 - self.at.c, piece, 0).wait_recv()

    def distances(self, body):
        at = self.at
        self.settle(at.z)
        body(at.z)

        @pl.loop(1, at.line)
        def _(d):
            @pl.when(at.z - d >= 0)
            def _():
                self.arrive(at.z - d)

            @pl.when(at.z + d < at.line)
            def _():
                self.arrive(at.z + d)

            @pl.loop(0, 2)
            def _(side):
                chip = at.z - d + 2 * d * side

                @pl.when((chip >= 0) & (chip < at.line))
                def _():
                    self.settle(chip)
                    body(chip)

    def sent(self):
        at = self.at
        for chip in range(at.line):
            slot = 2 * chip + at.c
            for piece in range(self.pieces):
                self.copy(slot, piece, 0).wait_send()

                @pl.when((chip <= at.z) & (at.z + 1 < at.line))
                def _():
                    self.copy(slot, piece, 1).wait_send()

                @pl.when((chip >= at.z) & (at.z > 0))
                def _():
                    self.copy(slot, piece, 2).wait_send()


class LineScatter:
    def __init__(self, at, own, other, heard, out, into, sems, pieces):
        self.at, self.own, self.other, self.heard, self.out, self.into = at, own, other, heard, out, into
        self.sib_send, self.sib_recv, self.send, self.recv = sems
        self.pieces = pieces
        self.rows = own.shape[1] // pieces

    @staticmethod
    def scratch(line, rows, width, pieces):
        low = pltpu.VMEM((line, rows, width), LOW)
        return [
            pltpu.VMEM((line, rows, width), WIDE), low, low, low,
            pltpu.VMEM((line + 1, rows, width), LOW),
            dma(line), dma(line), dma(line, pieces), dma(line + 1, pieces),
        ]

    def across(self, chip):
        return remote(
            self.other.at[chip], self.heard.at[chip], self.sib_send.at[chip],
            self.sib_recv.at[chip], "seq", self.at.sibling,
        )

    def along(self, chip, piece, up):
        at = self.at
        rows = pl.ds(pl.multiple_of(piece * self.rows, self.rows), self.rows)
        there = chip if up else jnp.where(chip == at.z - 1, at.line, chip)
        return remote(
            self.out.at[chip, rows], self.into.at[there, rows], self.send.at[chip, piece],
            self.recv.at[there, piece], "seq", at.s + 2 if up else at.s - 2,
        )

    def landed(self, index, piece):
        rows = pl.ds(pl.multiple_of(piece * self.rows, self.rows), self.rows)
        there = self.into.at[index, rows]
        remote(
            there, there, self.recv.at[index, piece], self.recv.at[index, piece], "seq", self.at.sibling
        ).wait_recv()

    def add(self, chip, piece, extras, store):
        @pl.loop(0, self.rows // 16)
        def _(block):
            rows = pl.ds(pl.multiple_of(piece * self.rows + block * 16, 16), 16)
            total = self.own[chip, rows, :].astype(WIDE) + self.heard[chip, rows, :].astype(WIDE)
            for known, index in extras:
                total = total + jnp.where(known, self.into[index, rows, :].astype(WIDE), 0.0)
            store(rows, total)

    def step(self, k):
        at = self.at
        for up in (True, False):
            chip = at.line - 1 - k if up else k
            passes = at.z > 0 if up else at.z + 1 < at.line

            @pl.when(chip > at.z if up else chip < at.z)
            def _():
                self.across(chip).wait_recv()

                @pl.loop(0, self.pieces)
                def _(piece):
                    @pl.when(passes)
                    def _():
                        self.landed(chip, piece)

                    def store(rows, total):
                        self.out[chip, rows, :] = total.astype(LOW)

                    self.add(chip, piece, [(passes, chip)], store)
                    self.along(chip, piece, up).start()

    def steps(self, first=0):
        @pl.loop(first, self.at.line - 1)
        def _(k):
            self.step(k)

    def finish(self, store):
        at = self.at
        below, above = at.z > 0, at.z + 1 < at.line
        self.across(at.z).wait_recv()

        @pl.loop(0, self.pieces)
        def _(piece):
            @pl.when(below)
            def _():
                self.landed(at.z, piece)

            @pl.when(above)
            def _():
                self.landed(at.line, piece)

            self.add(at.z, piece, [(below, at.z), (above, at.line)], store)

    def sent(self):
        at = self.at
        for chip in range(at.line):
            self.across(chip).wait_send()

            @pl.loop(0, self.pieces)
            def _(piece):
                @pl.when(chip > at.z)
                def _():
                    self.along(chip, piece, True).wait_send()

                @pl.when(chip < at.z)
                def _():
                    self.along(chip, piece, False).wait_send()


def normalise(source, gain, store, rows):
    @pl.loop(0, rows // 16)
    def _(block):
        here = pl.ds(pl.multiple_of(block * 16, 16), 16)
        values = source(here)
        scale = lax.rsqrt(jnp.mean(values * values, axis=-1, keepdims=True) + EPSILON)
        store(here, (values * scale * gain).astype(LOW))


def mixer_rows(positions):
    return [pl.ds(pl.multiple_of(n, CHUNK), CHUNK) for n in range(0, positions, CHUNK)]


def mix_in_kernel(
    tokens, in_shard, glu_shard, out_shard, down_shard, small, vecs, gain_shard,
    normed, in_whole, ext, pre_ref, conv_ref, r_ref, i_ref, st_ref,
    product_ref, par_ref, wr_ref, wi_ref, gains, glu_mine, out_whole, down_whole,
    held, small_all, vecs_all, gain_all, factors, drive, prod,
    local_sems, tok_send, tok_recv, in_sems, in_xy_send, in_xy_recv, glu_sems, xy_sems, gain_sems,
):
    groups, shards = in_whole.shape[1], in_whole.shape[0]
    at = Place(shards, groups)
    s, f = at.s, at.f
    positions, channels = pre_ref.shape
    width = tokens.shape[1]
    rows = in_shard.shape[1]
    segment = positions // 8
    chunks = positions // CHUNK

    keep = [
        (tokens, held.at[s]), (in_shard.at[s], in_whole.at[s, f]), (glu_shard.at[s], glu_mine.at[s]),
        (out_shard, out_whole.at[f]), (down_shard, down_whole.at[f]), (small, small_all.at[f]),
        (vecs, vecs_all.at[f]), (gain_shard, gain_all.at[s, f]),
    ]
    keep = [pltpu.make_async_copy(a, b, local_sems.at[n]) for n, (a, b) in enumerate(keep)]
    for copy in keep:
        copy.start()
    at.enter()

    def over_fsdp(src, dst, n):
        return Spread(at, lambda peer: src, lambda origin: dst.at[origin], xy_sems.at[n, 0], xy_sems.at[n, 1])

    gain_xy = Spread(
        at, lambda peer: gain_shard, lambda origin: gain_all.at[s, origin],
        xy_sems.at[0, 0], xy_sems.at[0, 1],
    )
    small_xy = over_fsdp(small, small_all, 1)
    vecs_xy = over_fsdp(vecs, vecs_all, 2)
    out_xy = over_fsdp(out_shard, out_whole, 3)
    down_xy = over_fsdp(down_shard, down_whole, 4)
    in_z = Spread(
        at, lambda peer: in_shard.at[peer], lambda origin: in_whole.at[origin, f],
        in_sems.at[0], in_sems.at[1], "seq",
    )
    glu_z = Spread(
        at, lambda peer: glu_shard.at[peer], lambda origin: glu_mine.at[origin],
        glu_sems.at[0], glu_sems.at[1], "seq",
    )
    gain_z = Spread(
        at, lambda peer: gain_all.at[s], lambda origin: gain_all.at[origin],
        gain_sems.at[0], gain_sems.at[1], "seq",
    )

    def in_xy(index):
        return Spread(
            at, lambda peer: in_whole.at[index, f], lambda origin: in_whole.at[index, origin],
            in_xy_send.at[index], in_xy_recv.at[index],
        )

    gather = LineGather(at, tokens, held, tok_send, tok_recv, tok_send.shape[1])
    gain_xy.start()
    in_z.start()
    keep[1].wait()
    in_xy(s).start()
    gather.start()
    vecs_xy.start()
    small_xy.start()
    keep[7].wait()
    gain_xy.finish()
    gain_z.start()
    for d in range(1, shards):
        in_z.arrive(d)
        in_xy(in_z.source(d)).start()
    out_xy.start()
    gain_z.finish()
    for origin in range(shards):
        for other in range(groups):
            first = (origin * groups + other) * rows
            gains[:, first : first + rows] = gain_all[origin, other]
    keep[0].wait()

    def take(chip):
        for core in range(2):
            slot = 2 * chip + core

            def store(here, value):
                normed[slot, here, :] = value

            normalise(
                lambda here: held[slot, here, :].astype(WIDE), gains[0:1, :], store, tokens.shape[0]
            )

    gather.distances(take)
    glu_z.start()
    keep[6].wait()
    vecs_xy.finish()
    keep[5].wait()
    small_xy.finish()
    size = small.shape[1] // 2
    local = small.shape[0]
    wr_ref[...] = jnp.zeros_like(wr_ref)
    wi_ref[...] = jnp.zeros_like(wi_ref)
    flat = small_all[...].reshape(channels, 2 * size)
    for n in range(channels // size):
        block = slice(n * size, (n + 1) * size)
        wr_ref[block, block] = flat[block, :size]
        wi_ref[block, block] = flat[block, size:]
    for other in range(groups):
        par_ref[:, other * local : (other + 1) * local] = vecs_all[other]
    ext[0:8, :] = jnp.zeros((8, channels), WIDE)
    st_ref[0:8, :] = jnp.zeros((8, channels), WIDE)
    for index in range(shards):
        for d in range(1, groups):
            in_xy(index).arrive(d)
    down_xy.start()

    @pl.loop(0, at.line)
    def _(chip):
        pair = normed[pl.ds(2 * chip, 2), :, :].reshape(2 * tokens.shape[0], width)
        both = dot(pair, in_whole[...].reshape(width, 2 * channels))
        base = pl.multiple_of(chip * 2 * tokens.shape[0], CHUNK)
        here = pl.ds(base, 2 * tokens.shape[0])
        ext[pl.ds(base + 8, 2 * tokens.shape[0]), :] = both[:, :channels].astype(LOW).astype(WIDE)
        pre_ref[here, :] = both[:, channels:]

    @pl.loop(0, chunks)
    def _(n):
        base = pl.multiple_of(n * CHUNK, CHUNK)
        here = pl.ds(base, CHUNK)
        block = ext[pl.ds(base, CHUNK + 8), :]
        conv = jnp.broadcast_to(par_ref[4:5, :], (CHUNK, channels))
        for k in range(4):
            conv = conv + par_ref[k : k + 1, :] * block[8 - k : 8 - k + CHUNK]
        conv_low = conv.astype(LOW)
        conv_ref[here, :] = conv_low
        r = jax.nn.sigmoid(dot(conv_low, wr_ref[...]) + par_ref[5:6, :])
        gate = jax.nn.sigmoid(dot(conv_low, wi_ref[...]) + par_ref[6:7, :])
        log_decay = r * par_ref[7:8, :]
        m = jnp.sqrt(one_minus_exp(-2.0 * log_decay))
        factor = jnp.exp(log_decay)
        r_ref[here, :] = r
        i_ref[here, :] = gate
        put(factors, here, factor)
        put(drive, here, m * gate * conv_low.astype(WIDE))

    def step(i, n, state, product):
        here = pl.ds(i, 8, stride=segment)
        factor = factors[n, here, :]
        state = factor * state + drive[n, here, :]
        product = factor * product
        drive[n, here, :] = state
        prod[n, here, :] = product
        return state, product

    state, product = scan_segments(step, segment, lane_tiles(channels))
    state, product = state[:, :channels], product[:, :channels]
    carry = jnp.zeros((1, channels), WIDE)
    for k in range(8):
        for part in range(segment // CHUNK):
            base = k * segment + part * CHUNK
            here = slice(base, base + CHUNK)
            states = get(drive, here, channels) + get(prod, here, channels) * carry
            st_ref[base + 8 : base + 8 + CHUNK, :] = states
            product_ref[here, :] = (
                states.astype(LOW).astype(WIDE) * gelu(pre_ref[here, :])
            ).astype(LOW)
        carry = state[k : k + 1] + product[k : k + 1] * carry

    glu_z.finish()
    out_xy.finish()
    down_xy.finish()
    gather.sent()
    in_z.sent()
    for index in range(shards):
        in_xy(index).sent()
    for n in (2, 3, 4):
        keep[n].wait()


def mix_in(tokens, in_shard, glu_shard, out_shard, down_shard, small, vecs, gain_shard, groups):
    shards, rows, both = in_shard.shape
    block, width = tokens.shape
    positions, channels = shards * block, both // 2
    local = small.shape[0]
    pieces = 2
    wide = jax.ShapeDtypeStruct((positions, channels), WIDE)
    low = jax.ShapeDtypeStruct((positions, channels), LOW)
    longer = jax.ShapeDtypeStruct((positions + 8, channels), WIDE)
    square = jax.ShapeDtypeStruct((channels, channels), LOW)
    held = [
        jax.ShapeDtypeStruct((shards, block, width), LOW),
        jax.ShapeDtypeStruct((shards, groups, rows, both), LOW),
        longer, wide, low, wide, wide, longer,
        low, jax.ShapeDtypeStruct((8, channels), WIDE), square, square,
        jax.ShapeDtypeStruct((8, width), WIDE),
    ]
    far = [
        jax.ShapeDtypeStruct((shards, rows, glu_shard.shape[2]), LOW),
        jax.ShapeDtypeStruct((groups,) + out_shard.shape, LOW),
        jax.ShapeDtypeStruct((groups,) + down_shard.shape, LOW),
    ]
    return pl.pallas_call(
        mix_in_kernel,
        out_shape=held + far,
        in_specs=[HELD] + [ANY] * 7,
        out_specs=[HELD] * len(held) + [ANY] * len(far),
        scratch_shapes=[
            pltpu.VMEM((shards, block, width), LOW),
            pltpu.VMEM((groups,) + small.shape, LOW),
            pltpu.VMEM((groups,) + vecs.shape, WIDE),
            pltpu.VMEM((shards, groups) + gain_shard.shape, WIDE),
        ]
        + [pltpu.VMEM((lane_tiles(channels), positions, 128), WIDE)] * 3
        + [
            dma(8), dma(shards, pieces, 3), dma(shards, pieces), dma(2, shards), dma(shards, groups),
            dma(shards, groups), dma(2, shards), dma(5, 2, groups), dma(2, shards),
        ],
        compiler_params=pltpu.CompilerParams(
            collective_id=1, has_side_effects=True, vmem_limit_bytes=VMEM_BYTES
        ),
        name="mix_in",
    )(tokens, in_shard, glu_shard, out_shard, down_shard, small, vecs, gain_shard)


def feed_kernel(
    product, out_whole, glu_mine, down_in, cotangent, tokens, gains,
    middle, middle_grad, mixed_low, gain_sums, fed_own, fed_other, glu_grad, down_grad,
    held, cots, glu, down, both, hidden, wide_pair, hidden_pair, tile, normed2, staged, down_staged,
    own, other, heard, out, into, sib_send, sib_recv, line_send, line_recv,
    local_sems, glu_send, glu_recv, two_send, two_recv, cot_send, cot_recv, stage_sems,
):
    shards, groups = glu.shape[0], glu.shape[1]
    at = Place(shards, groups)
    s, f = at.s, at.f
    block, width = tokens.shape
    units = down.shape[0]
    pair = 2 * block

    keep = [(glu_mine, glu.at[:, f]), (down_in, down), (cotangent, cots.at[s])]
    keep = [pltpu.make_async_copy(a, b, local_sems.at[n]) for n, (a, b) in enumerate(keep)]
    for copy in keep:
        copy.start()
    at.enter()
    def glu_xy(index):
        return Spread(
            at, lambda peer: glu_mine.at[index], lambda origin: glu.at[index, origin],
            glu_send.at[index], glu_recv.at[index],
        )

    cot_z = LineGather(at, cotangent, cots, cot_send, cot_recv, cot_send.shape[1])
    two_z = LineGather(at, normed2, held, two_send, two_recv, two_send.shape[1])
    sums = LineScatter(
        at, own, other, heard, out, into, (sib_send, sib_recv, line_send, line_recv), line_send.shape[1]
    )
    for index in range(shards):
        glu_xy(index).start()
    cot_z.start()

    def split(chip, columns, value, mine, theirs):
        tile[...] = value.reshape(2, block, value.shape[1])
        mine[chip, :, columns] = tile[at.c].astype(mine.dtype)
        theirs[chip, :, columns] = tile[1 - at.c].astype(theirs.dtype)

    def columns_of(j):
        return pl.ds(pl.multiple_of(j * 256, 256), 256)

    def pair_rows(chip):
        return pl.ds(pl.multiple_of(chip * pair, pair), pair)

    def project(chip):
        @pl.loop(0, width // 256)
        def _(j):
            value = dot(product[pair_rows(chip), :], out_whole[:, columns_of(j)])
            split(chip, columns_of(j), value, own, other)

        sums.across(chip).start()

    for k in range(at.line // 2):
        project(at.line - 1 - k)
        project(k)
        sums.step(k)
    sums.steps(at.line // 2)

    def to_middle(here, total):
        values = total + tokens[here, :].astype(WIDE)
        middle[here, :] = values
        scale = lax.rsqrt(jnp.mean(values * values, axis=-1, keepdims=True) + EPSILON)
        normed2[here, :] = (values * scale * gains[1:2, :]).astype(LOW)

    sums.finish(to_middle)
    two_z.start()
    own_copy = pltpu.make_async_copy(normed2, held.at[s], local_sems.at[3])
    own_copy.start()
    keep[0].wait()
    keep[1].wait()
    keep[2].wait()
    sums.sent()
    own_copy.wait()
    for index in range(shards):
        glu_xy(index).finish()

    def feed(chip):
        here = pair_rows(chip)
        rows = held[pl.ds(2 * chip, 2), :, :].reshape(pair, width)
        grads = cots[pl.ds(2 * chip, 2), :, :].reshape(pair, width)

        @pl.loop(0, 2 * units // 256)
        def _(j):
            wide_pair[:, columns_of(j)] = dot(
                rows, glu[:, :, :, columns_of(j)].reshape(width, 256)
            )

        @pl.loop(0, units // 256)
        def _(j):
            hidden_pair[:, columns_of(j)] = times_transpose(grads, down[columns_of(j), :])

        @pl.loop(0, pair // 16)
        def _(n):
            part = pl.ds(pl.multiple_of(n * 16, 16), 16)
            there = pl.ds(pl.multiple_of(chip * pair + n * 16, 16), 16)
            opened, slope = gelu_and_slope(wide_pair[part, :units])
            up = wide_pair[part, units:]
            grad = hidden_pair[part, :]
            hidden[there, :] = (opened * up).astype(LOW)
            both[there, :units] = (grad * up * slope).astype(LOW)
            both[there, units:] = (grad * opened).astype(LOW)

        @pl.loop(0, shards)
        def _(j):
            value = times_transpose(both[here, :], glu[j].reshape(width // shards, 2 * units))
            split(chip, columns_of(j), value, own, other)

        sums.across(chip).start()

        @pl.loop(0, width // 256)
        def _(j):
            split(chip, columns_of(j), dot(hidden[here, :], down[:, columns_of(j)]), fed_own, fed_other)

    two_z.settle(at.z)
    cot_z.settle(at.z)
    feed(at.z)

    @pl.loop(1, at.line)
    def _(d):
        for gather in (two_z, cot_z):
            @pl.when(at.z - d >= 0)
            def _():
                gather.arrive(at.z - d)

            @pl.when(at.z + d < at.line)
            def _():
                gather.arrive(at.z + d)

        @pl.loop(0, 2)
        def _(side):
            chip = at.z - d + 2 * d * side

            @pl.when((chip >= 0) & (chip < at.line))
            def _():
                two_z.settle(chip)
                cot_z.settle(chip)
                feed(chip)

    def glu_out(j):
        return pltpu.make_async_copy(
            staged.at[lax.rem(j, 2)], glu_grad.at[:, j], stage_sems.at[lax.rem(j, 2)]
        )

    def glu_sums(first, last):
        @pl.loop(first, last)
        def _(j):
            @pl.when(j >= 2)
            def _():
                glu_out(j - 2).wait()

            rows = held[:, :, columns_of(j)].reshape(shards * block, 256)
            staged[lax.rem(j, 2)] = outer_sum(rows, both[...]).astype(LOW).reshape(staged.shape[1:])
            glu_out(j).start()

    def down_out(j):
        return pltpu.make_async_copy(
            down_staged.at[lax.rem(j, 2)], down_grad.at[columns_of(j)], stage_sems.at[2 + lax.rem(j, 2)]
        )

    def down_sums():
        @pl.loop(0, units // 256)
        def _(j):
            @pl.when(j >= 2)
            def _():
                down_out(j - 2).wait()

            grads = cots[...].reshape(shards * block, width)
            down_staged[lax.rem(j, 2)] = outer_sum(hidden[:, columns_of(j)], grads).astype(LOW)
            down_out(j).start()

    sums.step(0)
    down_sums()
    for k in range(1, at.line - 1):
        sums.step(k)
        glu_sums((k - 1) * shards // (at.line - 1), k * shards // (at.line - 1))
    glu_sums((at.line - 2) * shards // (at.line - 1), shards)
    gain_sums[...] = jnp.zeros_like(gain_sums)

    def back(here, grad):
        values = middle[here, :]
        scale = lax.rsqrt(jnp.mean(values * values, axis=-1, keepdims=True) + EPSILON)
        scaled = grad * gains[1:2, :]
        along = jnp.mean(scaled * values, axis=-1, keepdims=True)
        total = cotangent[here, :].astype(WIDE) + scale * scaled - values * (scale * scale * scale * along)
        middle_grad[here, :] = total
        mixed_low[here, :] = total.astype(LOW)
        gain_sums[0:1, :] += jnp.sum(grad * values * scale, axis=0, keepdims=True)

    sums.finish(back)
    for j in range(shards - 2, shards):
        glu_out(j).wait()
    for j in range(max(units // 256 - 2, 0), units // 256):
        down_out(j).wait()
    sums.sent()
    two_z.sent()
    cot_z.sent()


def feed(product, out_whole, glu_mine, down_whole, cotangent, tokens, gains, groups):
    shards, rows, both = glu_mine.shape
    block, width = tokens.shape
    units = both // 2
    line, pieces, thirds = shards // 2, 2, 4
    own = jax.ShapeDtypeStruct((block, width), WIDE)
    low = jax.ShapeDtypeStruct((line, block, width), LOW)
    outs = [
        own, own, jax.ShapeDtypeStruct((block, width), LOW), jax.ShapeDtypeStruct((8, width), WIDE),
        low, low,
        jax.ShapeDtypeStruct((groups, shards, rows, both), LOW),
        jax.ShapeDtypeStruct((units, width), LOW),
    ]
    gathered = pltpu.VMEM((shards, block, width), LOW)
    return pl.pallas_call(
        feed_kernel,
        out_shape=outs,
        in_specs=[HELD, HELD, ANY, ANY, HELD, HELD, HELD],
        out_specs=[HELD] * 6 + [ANY] * 2,
        scratch_shapes=[
            gathered, gathered,
            pltpu.VMEM((shards, groups, rows, both), LOW),
            pltpu.VMEM((units, width), LOW),
            pltpu.VMEM((shards * block, both), LOW),
            pltpu.VMEM((shards * block, units), LOW),
            pltpu.VMEM((2 * block, both), WIDE),
            pltpu.VMEM((2 * block, units), WIDE),
            pltpu.VMEM((2, block, 256), WIDE),
            pltpu.VMEM((block, width), LOW),
            pltpu.VMEM((2, groups, rows, both), LOW),
            pltpu.VMEM((2, 256, width), LOW),
        ]
        + LineScatter.scratch(line, block, width, thirds)
        + [
            dma(4), dma(shards, groups), dma(shards, groups), dma(shards, pieces, 3), dma(shards, pieces),
            dma(shards, pieces, 3), dma(shards, pieces), dma(4),
        ],
        compiler_params=pltpu.CompilerParams(
            collective_id=2, has_side_effects=True, vmem_limit_bytes=VMEM_BYTES
        ),
        name="feed",
    )(product, out_whole, glu_mine, down_whole, cotangent, tokens, gains)


def back_kernel(
    mixed, fed_own, fed_other, middle, middle_grad, tokens, gains, par_ref, wr_ref, wi_ref,
    out_far, in_far, normed_far, product_far, ext_far, pre_far, conv_far, r_far, i_far, st_far,
    glu_grad, down_grad,
    result, tokens_grad, gain_sums, wr_grad, wi_grad, sums_ref, out_grad, in_grad, glu_heard, down_heard,
    held, in_whole, out_whole, product, ext, pre, conv_ref, r_ref, i_ref, st_ref,
    both, pair_grad, tile, staged, factors, adj, prod, cg, carries, wr_sum, wi_sum,
    fed_heard, fed_out, fed_into, fed_sib_send, fed_sib_recv, fed_send, fed_recv,
    own, other, heard, out, into, sib_send, sib_recv, line_send, line_recv,
    local_sems, held_send, held_recv, glu_sems, down_sems, stage_sems,
):
    shards, groups = in_whole.shape[0], in_whole.shape[1]
    at = Place(shards, groups)
    s, f = at.s, at.f
    block, width = tokens.shape
    positions, channels = product.shape
    pair = 2 * block
    segment = positions // 8
    chunks = positions // CHUNK

    keep = [
        (mixed, held.at[s]), (out_far, out_whole), (pre_far, pre), (st_far, st_ref),
        (product_far, product), (r_far, r_ref), (i_far, i_ref), (conv_far, conv_ref),
        (ext_far, ext), (in_far, in_whole), (glu_grad.at[f], glu_heard.at[f]),
        (down_grad.at[f], down_heard.at[f]), (normed_far, held),
    ]
    keep = [pltpu.make_async_copy(a, b, local_sems.at[n]) for n, (a, b) in enumerate(keep)]
    for copy in keep[:-1]:
        copy.start()
    at.enter()
    glu_xy = Spread(
        at, lambda peer: glu_grad.at[peer], lambda origin: glu_heard.at[origin],
        glu_sems.at[0], glu_sems.at[1],
    )
    down_xy = Spread(
        at, lambda peer: down_grad.at[peer], lambda origin: down_heard.at[origin],
        down_sems.at[0], down_sems.at[1],
    )
    mixed_z = LineGather(at, mixed, held, held_send, held_recv, held_send.shape[1])
    fed = LineScatter(
        at, fed_own, fed_other, fed_heard, fed_out, fed_into,
        (fed_sib_send, fed_sib_recv, fed_send, fed_recv), fed_send.shape[1],
    )
    sums = LineScatter(
        at, own, other, heard, out, into, (sib_send, sib_recv, line_send, line_recv), line_send.shape[1]
    )
    mixed_z.start()
    down_xy.start()
    glu_xy.start()
    for k in range(at.line // 2):
        fed.across(at.line - 1 - k).start()
        fed.across(k).start()

    def columns_of(j):
        return pl.ds(pl.multiple_of(j * 256, 256), 256)

    for n in (1, 2, 3):
        keep[n].wait()
    keep[0].wait()

    def mixed_back(chip):
        rows = held[pl.ds(2 * chip, 2), :, :].reshape(pair, width)
        pair_grad[...] = times_transpose(rows, out_whole[...])

        @pl.loop(0, pair // 64)
        def _(n):
            grad = pair_grad[pl.ds(pl.multiple_of(n * 64, 64), 64), :]
            base = pl.multiple_of(chip * pair + n * 64, 64)
            here = pl.ds(base, 64)
            opened, slope = gelu_and_slope(pre[here, :])
            states = st_ref[pl.ds(base + 8, 64), :].astype(LOW).astype(WIDE)
            put(adj, here, (grad * opened).astype(LOW).astype(WIDE))
            both[here, channels:] = (grad * states * slope).astype(LOW)

    mixed_z.distances(mixed_back)
    fed.step(0)
    keep[5].wait()

    @pl.loop(0, chunks)
    def _(n):
        here = pl.ds(pl.multiple_of(n * CHUNK, CHUNK), CHUNK)
        put(factors, here, jnp.exp(r_ref[here, :] * par_ref[7:8, :]))

    def step(j, n, flow, product):
        here = pl.ds(segment - 1 - j, 8, stride=segment)
        factor = factors[n, here, :]
        adjoint = adj[n, here, :] + flow
        adj[n, here, :] = adjoint
        prod[n, here, :] = product
        return factor * adjoint, factor * product

    flow, through = scan_segments(step, segment, lane_tiles(channels))
    flow, through = flow[:, :channels], through[:, :channels]
    carry = jnp.zeros((1, channels), WIDE)
    for k in range(7, -1, -1):
        carries[k : k + 1, :] = carry
        carry = flow[k : k + 1] + through[k : k + 1] * carry
    fed.step(1)
    for n in (6, 7, 8):
        keep[n].wait()
    cg[pl.ds(positions, 8), :] = jnp.zeros((8, channels), WIDE)
    wr_sum[...] = jnp.zeros_like(wr_sum)
    wi_sum[...] = jnp.zeros_like(wi_sum)

    def grads(c, sums):
        base = pl.multiple_of(c * CHUNK, CHUNK)
        rows = pl.ds(base, CHUNK)
        adjoint = get(adj, rows, channels) + get(prod, rows, channels) * carries[pl.ds(base // segment, 1), :]
        before = st_ref[pl.ds(base, CHUNK + 8), :][7 : 7 + CHUNK]
        conv_low = conv_ref[rows, :]
        conv = conv_low.astype(WIDE)
        r = r_ref[rows, :]
        gate = i_ref[rows, :]
        factor = get(factors, rows, channels)
        m = jnp.sqrt(one_minus_exp(-2.0 * (r * par_ref[7:8, :])))
        driven = adjoint * gate
        by_log = adjoint * before * factor - driven * conv * factor * factor / m
        by_r = by_log * par_ref[7:8, :] * r * (1.0 - r)
        by_i = adjoint * m * conv * gate * (1.0 - gate)
        by_r_low = by_r.astype(LOW)
        by_i_low = by_i.astype(LOW)
        conv_grad = (
            driven * m
            + times_transpose(by_r_low, wr_ref[...])
            + times_transpose(by_i_low, wi_ref[...])
        )
        cg[rows, :] = conv_grad
        wr_sum[...] += outer_sum(conv_low, by_r_low)
        wi_sum[...] += outer_sum(conv_low, by_i_low)
        near = ext[pl.ds(base, CHUNK + 8), :]
        rows_of = [conv_grad * near[8 - k : 8 - k + CHUNK] for k in range(4)]
        rows_of += [conv_grad, by_r, by_i, by_log * r]
        return tuple(
            total + jnp.sum(member, axis=0, keepdims=True) for total, member in zip(sums, rows_of)
        )

    zero = jnp.zeros((1, channels), WIDE)
    totals = lax.fori_loop(0, chunks, grads, (zero,) * 8)
    for k in range(8):
        sums_ref[k : k + 1, :] = totals[k]
    size = wr_grad.shape[1]
    for n in range(channels // size):
        part = slice(n * size, (n + 1) * size)
        wr_grad[part, :] = wr_sum[part, part]
        wi_grad[part, :] = wi_sum[part, part]

    @pl.loop(0, chunks)
    def _(c):
        base = pl.multiple_of(c * CHUNK, CHUNK)
        near = cg[pl.ds(base, CHUNK + 8), :]
        total = jnp.zeros((CHUNK, channels), WIDE)
        for k in range(4):
            total = total + par_ref[k : k + 1, :] * near[k : k + CHUNK]
        both[pl.ds(base, CHUNK), :channels] = total.astype(LOW)

    fed.steps(2)
    keep[9].wait()

    def project(chip):
        rows = both[pl.ds(pl.multiple_of(chip * pair, pair), pair), :]

        @pl.loop(0, shards)
        def _(j):
            value = times_transpose(rows, in_whole[j].reshape(width // shards, 2 * channels))
            tile[...] = value.reshape(2, block, value.shape[1])
            own[chip, :, columns_of(j)] = tile[at.c]
            other[chip, :, columns_of(j)] = tile[1 - at.c].astype(LOW)

        sums.across(chip).start()

    for k in range(at.line // 2):
        project(at.line - 1 - k)
        project(k)
        sums.step(k)
    keep[4].wait()

    @pl.loop(0, width // 256)
    def _(j):
        columns = columns_of(j)
        grads = held[:, :, columns].reshape(positions, 256)
        out_grad[:, columns] = outer_sum(product[...], grads).astype(LOW)

    mixed_z.sent()
    keep[12].start()

    def store_result(here, total):
        result[here, :] = (middle[here, :] + total).astype(LOW)

    fed.finish(store_result)
    sums.steps(at.line // 2)
    keep[12].wait()

    def in_out(j):
        return pltpu.make_async_copy(
            staged.at[lax.rem(j, 2)], in_grad.at[:, j], stage_sems.at[lax.rem(j, 2)]
        )

    @pl.loop(0, shards)
    def _(j):
        @pl.when(j >= 2)
        def _():
            in_out(j - 2).wait()

        rows = held[:, :, columns_of(j)].reshape(positions, 256)
        staged[lax.rem(j, 2)] = outer_sum(rows, both[...]).astype(LOW).reshape(staged.shape[1:])
        in_out(j).start()

    gain_sums[...] = jnp.zeros_like(gain_sums)

    def back(here, grad):
        values = tokens[here, :].astype(WIDE)
        scale = lax.rsqrt(jnp.mean(values * values, axis=-1, keepdims=True) + EPSILON)
        scaled = grad * gains[0:1, :]
        along = jnp.mean(scaled * values, axis=-1, keepdims=True)
        total = middle_grad[here, :] + scale * scaled - values * (scale * scale * scale * along)
        tokens_grad[here, :] = total.astype(LOW)
        gain_sums[0:1, :] += jnp.sum(grad * values * scale, axis=0, keepdims=True)

    sums.finish(back)
    for j in range(shards - 2, shards):
        in_out(j).wait()
    fed.sent()
    sums.sent()
    keep[10].wait()
    keep[11].wait()
    down_xy.finish()
    glu_xy.finish()


def back(
    mixed, fed_own, fed_other, middle, middle_grad, tokens, gains, par, wr, wi,
    out_whole, in_whole, normed, product, ext, pre, conv, r, i, st, glu_grad, down_grad, size,
):
    shards, groups, rows, both = in_whole.shape
    block, width = tokens.shape
    positions, channels = product.shape
    line, pieces, thirds = shards // 2, 2, 4
    low = pltpu.VMEM((line, block, width), LOW)
    short = jax.ShapeDtypeStruct((block, width), LOW)
    square = jax.ShapeDtypeStruct((channels, size), WIDE)
    outs = [
        short, short, jax.ShapeDtypeStruct((8, width), WIDE), square, square,
        jax.ShapeDtypeStruct((8, channels), WIDE),
        jax.ShapeDtypeStruct((channels, width), LOW),
        jax.ShapeDtypeStruct((groups, shards, rows, both), LOW),
        jax.ShapeDtypeStruct(glu_grad.shape, LOW),
        jax.ShapeDtypeStruct(down_grad.shape, LOW),
    ]
    far = [out_whole, in_whole, normed, product, ext, pre, conv, r, i, st]
    near = [in_whole, out_whole, product, ext, pre, conv, r, i, st]
    return pl.pallas_call(
        back_kernel,
        out_shape=outs,
        in_specs=[HELD, HELD, ANY] + [HELD] * 7 + [ANY] * (len(far) + 2),
        out_specs=[HELD] * 7 + [ANY] * 3,
        scratch_shapes=[pltpu.VMEM((shards, block, width), LOW)]
        + [pltpu.VMEM(member.shape, member.dtype) for member in near]
        + [
            pltpu.VMEM((positions, 2 * channels), LOW),
            pltpu.VMEM((2 * block, channels), WIDE),
            pltpu.VMEM((2, block, 256), WIDE),
            pltpu.VMEM((2, groups, rows, both), LOW),
        ]
        + [pltpu.VMEM((lane_tiles(channels), positions, 128), WIDE)] * 3
        + [pltpu.VMEM((positions + 8, channels), WIDE), pltpu.VMEM((8, channels), WIDE)]
        + [pltpu.VMEM((channels, channels), WIDE)] * 2
        + LineScatter.scratch(line, block, width, thirds)[2:]
        + LineScatter.scratch(line, block, width, thirds)
        + [
            dma(13), dma(shards, pieces, 3), dma(shards, pieces), dma(2, groups), dma(2, groups), dma(2),
        ],
        compiler_params=pltpu.CompilerParams(
            collective_id=3, has_side_effects=True, vmem_limit_bytes=VMEM_BYTES
        ),
        name="back",
    )(
        mixed, fed_own, fed_other, middle, middle_grad, tokens, gains, par, wr, wi, *far,
        glu_grad, down_grad,
    )


def tail_kernel(
    glu_far, in_grad, out_grad, small, gain_parts,
    glu_out, in_out, out_heard, small_heard, gain_out,
    glu_heard, glu_sum, in_heard, in_sum, gain_heard, gain_sum,
    local_sems, in_xy_sems, out_sems, small_sems, gain_xy_sems, glu_sems, in_sems, gain_sems,
):
    groups, shards = glu_far.shape[0], glu_far.shape[1]
    at = Place(shards, groups)
    s, f = at.s, at.f
    keep = [
        (glu_far, glu_heard), (in_grad.at[f], in_heard.at[f]), (out_grad.at[f], out_heard.at[f]),
        (small.at[f], small_heard.at[f]), (gain_parts.at[f], gain_heard.at[f]),
    ]
    keep = [pltpu.make_async_copy(a, b, local_sems.at[n]) for n, (a, b) in enumerate(keep)]
    for copy in keep:
        copy.start()
    at.enter()

    def over_fsdp(src, dst, sems):
        return Spread(
            at, lambda peer: src.at[peer], lambda origin: dst.at[origin], sems.at[0], sems.at[1]
        )

    def over_seq(src, dst, sems):
        return Spread(
            at, lambda peer: src.at[peer], lambda origin: dst.at[origin], sems.at[0], sems.at[1], "seq"
        )

    gain_xy = over_fsdp(gain_parts, gain_heard, gain_xy_sems)
    in_xy = over_fsdp(in_grad, in_heard, in_xy_sems)
    small_xy = over_fsdp(small, small_heard, small_sems)
    out_xy = over_fsdp(out_grad, out_heard, out_sems)
    glu_z = over_seq(glu_sum, glu_out, glu_sems)
    in_z = over_seq(in_sum, in_out, in_sems)
    gain_z = over_seq(gain_sum, gain_out, gain_sems)
    for spread in (gain_xy, in_xy, small_xy, out_xy):
        spread.start()

    def add(parts, total, peer):
        @pl.loop(0, total.shape[1] // 16)
        def _(n):
            here = pl.ds(pl.multiple_of(n * 16, 16), 16)
            value = parts[0, peer, here, :].astype(WIDE)
            for origin in range(1, groups):
                value = value + parts[origin, peer, here, :].astype(WIDE)
            total[peer, here, :] = value.astype(total.dtype)

    def swap(parts, total, spread, into, sem):
        @pl.loop(1, shards)
        def _(d):
            peer = lax.rem(s + d, shards)
            add(parts, total, peer)
            spread.copy(d).start()

        add(parts, total, s)
        mine = pltpu.make_async_copy(total.at[s], into.at[s], sem)
        mine.start()
        return mine

    keep[0].wait()
    glu_own = swap(glu_heard, glu_sum, glu_z, glu_out, local_sems.at[5])
    gain_xy.finish()
    keep[4].wait()
    total = gain_heard[0]
    for origin in range(1, groups):
        total = total + gain_heard[origin]
    gain_sum[...] = total
    gain_z.start()
    gain_own = pltpu.make_async_copy(gain_sum.at[s], gain_out.at[s], local_sems.at[6])
    gain_own.start()
    in_xy.finish()
    keep[1].wait()
    in_own = swap(in_heard, in_sum, in_z, in_out, local_sems.at[7])
    for spread in (gain_z, small_xy, out_xy, glu_z, in_z):
        spread.finish()
    for copy in (keep[2], keep[3], glu_own, gain_own, in_own):
        copy.wait()


def tail(glu_heard, in_grad, out_grad, small, gain_parts):
    groups, shards, rows, both = glu_heard.shape
    wide = in_grad.shape[3]
    outs = [
        jax.ShapeDtypeStruct((shards, rows, both), LOW),
        jax.ShapeDtypeStruct((shards, rows, wide), LOW),
        jax.ShapeDtypeStruct(out_grad.shape, LOW),
        jax.ShapeDtypeStruct(small.shape, WIDE),
        jax.ShapeDtypeStruct(gain_parts.shape[1:], WIDE),
    ]
    return pl.pallas_call(
        tail_kernel,
        out_shape=outs,
        in_specs=[ANY] * 5,
        out_specs=[ANY] * 5,
        scratch_shapes=[
            pltpu.VMEM(glu_heard.shape, LOW),
            pltpu.VMEM((shards, rows, both), LOW),
            pltpu.VMEM(in_grad.shape, LOW),
            pltpu.VMEM((shards, rows, wide), LOW),
            pltpu.VMEM(gain_parts.shape, WIDE),
            pltpu.VMEM(gain_parts.shape[1:], WIDE),
            dma(8), dma(2, groups), dma(2, groups), dma(2, groups), dma(2, groups),
            dma(2, shards), dma(2, shards), dma(2, shards),
        ],
        compiler_params=pltpu.CompilerParams(
            collective_id=4, has_side_effects=True, vmem_limit_bytes=VMEM_BYTES
        ),
        name="tail",
    )(glu_heard, in_grad, out_grad, small, gain_parts)


def mixer_forward_kernel(
    x_ref, wr_ref, wi_ref, par_ref,
    conv_ref, r_ref, i_ref, f_ref, m_ref, st_ref,
    ext, factors, drive, prod,
):
    positions, channels = x_ref.shape
    segment = positions // 8
    chunks = positions // CHUNK
    ext[0:8, :] = jnp.zeros((8, channels), WIDE)
    st_ref[0:8, :] = jnp.zeros((8, channels), WIDE)

    @pl.loop(0, chunks)
    def _(c):
        base = pl.multiple_of(c * CHUNK, CHUNK)
        ext[pl.ds(base + 8, CHUNK), :] = x_ref[pl.ds(base, CHUNK), :].astype(WIDE)

    @pl.loop(0, chunks)
    def _(c):
        base = pl.multiple_of(c * CHUNK, CHUNK)
        rows = pl.ds(base, CHUNK)
        block = ext[pl.ds(base, CHUNK + 8), :]
        conv = jnp.broadcast_to(par_ref[4:5, :], (CHUNK, channels))
        for k in range(4):
            conv = conv + par_ref[k : k + 1, :] * block[8 - k : 8 - k + CHUNK]
        conv_low = conv.astype(LOW)
        conv_ref[rows, :] = conv_low
        r = jax.nn.sigmoid(dot(conv_low, wr_ref[...]) + par_ref[5:6, :])
        gate = jax.nn.sigmoid(dot(conv_low, wi_ref[...]) + par_ref[6:7, :])
        log_decay = r * par_ref[7:8, :]
        m = jnp.sqrt(one_minus_exp(-2.0 * log_decay))
        r_ref[rows, :] = r
        i_ref[rows, :] = gate
        factor = jnp.exp(log_decay)
        f_ref[rows, :] = factor
        m_ref[rows, :] = m
        put(factors, rows, factor)
        put(drive, rows, m * gate * conv_low.astype(WIDE))

    def step(i, n, state, product):
        rows = pl.ds(i, 8, stride=segment)
        factor = factors[n, rows, :]
        state = factor * state + drive[n, rows, :]
        product = factor * product
        drive[n, rows, :] = state
        prod[n, rows, :] = product
        return state, product

    state, product = scan_segments(step, segment, lane_tiles(channels))
    state, product = state[:, :channels], product[:, :channels]
    carry = jnp.zeros((1, channels), WIDE)
    for k in range(8):
        for part in range(segment // CHUNK):
            base = k * segment + part * CHUNK
            rows = slice(base, base + CHUNK)
            st_ref[base + 8 : base + 8 + CHUNK, :] = (
                get(drive, rows, channels) + get(prod, rows, channels) * carry
            )
        carry = state[k : k + 1] + product[k : k + 1] * carry


def mixer_backward_kernel(
    ds_ref, x_ref, conv_ref, r_ref, i_ref, f_ref, m_ref, st_ref, wr_ref, wi_ref, par_ref,
    xg_ref, wrg_ref, wig_ref, sums_ref,
    ext, factors, adj, prod, cg, carries, wr_sum, wi_sum,
):
    positions, channels = x_ref.shape
    segment = positions // 8
    chunks = positions // CHUNK
    ext[0:8, :] = jnp.zeros((8, channels), WIDE)
    cg[pl.ds(positions, 8), :] = jnp.zeros((8, channels), WIDE)
    wr_sum[...] = jnp.zeros_like(wr_sum)
    wi_sum[...] = jnp.zeros_like(wi_sum)

    @pl.loop(0, chunks)
    def _(c):
        base = pl.multiple_of(c * CHUNK, CHUNK)
        ext[pl.ds(base + 8, CHUNK), :] = x_ref[pl.ds(base, CHUNK), :].astype(WIDE)
        put(adj, pl.ds(base, CHUNK), ds_ref[pl.ds(base, CHUNK), :].astype(WIDE))
        put(factors, pl.ds(base, CHUNK), f_ref[pl.ds(base, CHUNK), :])

    def step(j, n, flow, product):
        rows = pl.ds(segment - 1 - j, 8, stride=segment)
        factor = factors[n, rows, :]
        adjoint = adj[n, rows, :] + flow
        adj[n, rows, :] = adjoint
        prod[n, rows, :] = product
        return factor * adjoint, factor * product

    flow, product = scan_segments(step, segment, lane_tiles(channels))
    flow, product = flow[:, :channels], product[:, :channels]
    carry = jnp.zeros((1, channels), WIDE)
    for k in range(7, -1, -1):
        carries[k : k + 1, :] = carry
        carry = flow[k : k + 1] + product[k : k + 1] * carry

    def grads(c, sums):
        base = pl.multiple_of(c * CHUNK, CHUNK)
        rows = pl.ds(base, CHUNK)
        adjoint = get(adj, rows, channels) + get(prod, rows, channels) * carries[pl.ds(base // segment, 1), :]
        before = st_ref[pl.ds(base, CHUNK + 8), :][7 : 7 + CHUNK]
        conv_low = conv_ref[rows, :]
        conv = conv_low.astype(WIDE)
        r = r_ref[rows, :]
        gate = i_ref[rows, :]
        factor = f_ref[rows, :]
        m = m_ref[rows, :]
        driven = adjoint * gate
        by_log = adjoint * before * factor - driven * conv * factor * factor / m
        by_r = by_log * par_ref[7:8, :] * r * (1.0 - r)
        by_i = adjoint * m * conv * gate * (1.0 - gate)
        by_r_low = by_r.astype(LOW)
        by_i_low = by_i.astype(LOW)
        conv_grad = (
            driven * m
            + times_transpose(by_r_low, wr_ref[...])
            + times_transpose(by_i_low, wi_ref[...])
        )
        cg[rows, :] = conv_grad
        wr_sum[...] += outer_sum(conv_low, by_r_low)
        wi_sum[...] += outer_sum(conv_low, by_i_low)
        block = ext[pl.ds(base, CHUNK + 8), :]
        rows_of = [conv_grad * block[8 - k : 8 - k + CHUNK] for k in range(4)]
        rows_of += [conv_grad, by_r, by_i, by_log * r]
        return tuple(
            total + jnp.sum(member, axis=0, keepdims=True) for total, member in zip(sums, rows_of)
        )

    zero = jnp.zeros((1, channels), WIDE)
    sums = lax.fori_loop(0, chunks, grads, (zero,) * 8)
    for k in range(8):
        sums_ref[k : k + 1, :] = sums[k]
    size = wrg_ref.shape[1]
    for n in range(channels // size):
        block = slice(n * size, (n + 1) * size)
        wrg_ref[block, :] = wr_sum[block, block]
        wig_ref[block, :] = wi_sum[block, block]

    @pl.loop(0, chunks)
    def _(c):
        base = pl.multiple_of(c * CHUNK, CHUNK)
        block = cg[pl.ds(base, CHUNK + 8), :]
        total = jnp.zeros((CHUNK, channels), WIDE)
        for k in range(4):
            total = total + par_ref[k : k + 1, :] * block[k : k + CHUNK]
        xg_ref[pl.ds(base, CHUNK), :] = total.astype(LOW)


def mixer_forward(x, wr, wi, par):
    positions, channels = x.shape
    wide = jax.ShapeDtypeStruct((positions, channels), WIDE)
    return pl.pallas_call(
        mixer_forward_kernel,
        out_shape=(
            jax.ShapeDtypeStruct((positions, channels), LOW), wide, wide, wide, wide,
            jax.ShapeDtypeStruct((positions + 8, channels), WIDE),
        ),
        scratch_shapes=[pltpu.VMEM((positions + 8, channels), WIDE)]
        + [pltpu.VMEM((lane_tiles(channels), positions, 128), WIDE)] * 3,
        compiler_params=pltpu.CompilerParams(vmem_limit_bytes=48 * 2**20),
        name="mixer_forward",
    )(x, wr, wi, par)


def mixer_backward(ds, x, saved, wr, wi, par, size):
    positions, channels = x.shape
    square = jax.ShapeDtypeStruct((channels, size), WIDE)
    return pl.pallas_call(
        mixer_backward_kernel,
        out_shape=(
            jax.ShapeDtypeStruct((positions, channels), LOW), square, square,
            jax.ShapeDtypeStruct((8, channels), WIDE),
        ),
        scratch_shapes=[pltpu.VMEM((positions + 8, channels), WIDE)]
        + [pltpu.VMEM((lane_tiles(channels), positions, 128), WIDE)] * 3
        + [pltpu.VMEM((positions + 8, channels), WIDE), pltpu.VMEM((8, channels), WIDE)]
        + [pltpu.VMEM((channels, channels), WIDE)] * 2,
        compiler_params=pltpu.CompilerParams(vmem_limit_bytes=48 * 2**20),
        name="mixer_backward",
    )(ds, x, *saved, wr, wi, par)


def gather_columns(weights):
    shards = lax.axis_size("seq")
    rows = weights[0].shape[0]
    widths = [member.shape[1] // shards for member in weights]
    stacked = jnp.concatenate(
        [member.reshape(rows, shards, width) for member, width in zip(weights, widths)], axis=2
    )
    mine = lax.all_to_all(stacked.transpose(1, 0, 2), "seq", split_axis=0, concat_axis=0)
    whole = lax.all_gather(mine, "fsdp", axis=1)
    return whole.reshape(-1, sum(widths))


def scatter_columns(grad, widths, rows):
    shards, groups = lax.axis_size("seq"), lax.axis_size("fsdp")
    parts = grad.astype(LOW).reshape(shards, groups, rows, sum(widths)).transpose(1, 0, 2, 3)
    mine = lax.psum_scatter(parts, "fsdp", scatter_dimension=0, tiled=False)
    swapped = lax.all_to_all(mine, "seq", split_axis=0, concat_axis=0).astype(WIDE)
    outs, first = [], 0
    for width in widths:
        outs.append(swapped[:, :, first : first + width].transpose(1, 0, 2).reshape(rows, -1))
        first += width
    return outs


def block_diagonal(weight, blocks):
    size = weight.shape[1]
    shaped = weight.reshape(blocks, size, size)
    full = jnp.zeros((blocks, size, blocks, size), weight.dtype)
    for n in range(blocks):
        full = full.at[n, :, n, :].set(shaped[n])
    return full.reshape(blocks * size, blocks * size)


def general(
    tokens, cotangent, mix_gain, lru_in_weight, gelu_in_weight, out_weight, conv_weight, conv_bias,
    recurrence_weight, recurrence_bias, input_gate_weight, input_gate_bias, decay_param, mlp_gain,
    gate_weight, up_weight, down_weight,
):
    positions, width = tokens.shape[1:]
    rows = lru_in_weight.shape[0]
    shards = lax.axis_size("seq")
    channels = lru_in_weight.shape[1] // shards
    hidden_width = gate_weight.shape[1] // shards
    size = recurrence_weight.shape[1]

    gains = lax.all_gather(
        jnp.stack([mix_gain, mlp_gain], axis=1), ("seq", "fsdp"), axis=0, tiled=True
    ).astype(WIDE)
    mix_scale, mlp_scale = gains[:, 0], gains[:, 1]
    in_whole = gather_columns([lru_in_weight, gelu_in_weight])
    lru_params = lax.all_gather(
        jnp.concatenate(
            [
                recurrence_weight, input_gate_weight, conv_weight, conv_bias[:, None],
                recurrence_bias[:, None], input_gate_bias[:, None], decay_param[:, None],
            ],
            axis=1,
        ),
        "fsdp", axis=0, tiled=True,
    )
    out_whole = lax.all_gather(out_weight, "fsdp", axis=0, tiled=True)
    glu_whole = gather_columns([gate_weight, up_weight])
    down_whole = lax.all_gather(down_weight, "fsdp", axis=0, tiled=True)

    wr = block_diagonal(lru_params[:, :size], channels // size)
    wi = block_diagonal(lru_params[:, size : 2 * size], channels // size)
    vectors = lru_params[:, 2 * size :].astype(WIDE).T
    decay = vectors[7]
    par = jnp.concatenate([vectors[:7], -RATE_SCALE * jax.nn.softplus(-decay)[None]], axis=0)

    resid_in = tokens.reshape(positions, width).astype(WIDE)
    grad_low = cotangent.reshape(positions, width)
    normed_low = rms_scale(resid_in, mix_scale).astype(LOW)
    normed_all = lax.all_gather(normed_low, "seq", axis=0, tiled=True)
    grad_all = lax.all_gather(grad_low, "seq", axis=0, tiled=True)
    branch_x = dot(normed_all, in_whole[:, :channels]).astype(LOW)
    branch_pre = dot(normed_all, in_whole[:, channels:])
    branch_y = jax.nn.gelu(branch_pre)

    saved = mixer_forward(branch_x, wr, wi, par)
    states_f = saved[5][8:].astype(LOW).astype(WIDE)
    product = (states_f * branch_y).astype(LOW)
    mixed = lax.psum_scatter(
        dot(product, out_whole).astype(LOW), "seq", scatter_dimension=0, tiled=True
    )
    middle = resid_in + mixed.astype(WIDE)
    normed2_low = rms_scale(middle, mlp_scale).astype(LOW)
    normed2_all = lax.all_gather(normed2_low, "seq", axis=0, tiled=True)
    gate_whole, up_whole = glu_whole[:, :hidden_width], glu_whole[:, hidden_width:]
    gate_val = dot(normed2_all, gate_whole)
    up_val = dot(normed2_all, up_whole)
    hidden = (jax.nn.gelu(gate_val) * up_val).astype(LOW)
    fed = lax.psum_scatter(
        dot(hidden, down_whole).astype(LOW), "seq", scatter_dimension=0, tiled=True
    )
    result = middle + fed.astype(WIDE)

    hidden_grad = times_transpose(grad_all, down_whole)
    unused, pull_glu = jax.vjp(lambda first, second: jax.nn.gelu(first) * second, gate_val, up_val)
    gate_grad, up_grad = pull_glu(hidden_grad)
    gate_low, up_low = gate_grad.astype(LOW), up_grad.astype(LOW)
    normed2_grad = lax.psum_scatter(
        (times_transpose(gate_low, gate_whole) + times_transpose(up_low, up_whole)).astype(LOW),
        "seq", scatter_dimension=0, tiled=True,
    ).astype(WIDE)
    unused, pull_norm2 = jax.vjp(rms_scale, middle, mlp_scale)
    middle_part, mlp_gain_grad = pull_norm2(normed2_grad)
    middle_grad = grad_low.astype(WIDE) + middle_part
    mixed_all = lax.all_gather(middle_grad.astype(LOW), "seq", axis=0, tiled=True)

    product_grad = times_transpose(mixed_all, out_whole)
    states_grad = (product_grad * branch_y).astype(LOW)
    unused, pull_gelu = jax.vjp(jax.nn.gelu, branch_pre)
    (pre_grad,) = pull_gelu(product_grad * states_f)
    pre_low = pre_grad.astype(LOW)
    x_low, wr_grad, wi_grad, sums = mixer_backward(states_grad, branch_x, saved, wr, wi, par, size)

    normed_grad = lax.psum_scatter(
        (
            times_transpose(x_low, in_whole[:, :channels])
            + times_transpose(pre_low, in_whole[:, channels:])
        ).astype(LOW),
        "seq", scatter_dimension=0, tiled=True,
    ).astype(WIDE)
    unused, pull_norm = jax.vjp(rms_scale, resid_in, mix_scale)
    input_part, mix_gain_grad = pull_norm(normed_grad)
    input_grad = middle_grad + input_part

    down_grad = lax.psum_scatter(
        outer_sum(hidden, grad_all).astype(LOW), "fsdp", scatter_dimension=0, tiled=True
    ).astype(WIDE)
    glu_grad = jnp.concatenate(
        [outer_sum(normed2_all, gate_low), outer_sum(normed2_all, up_low)], axis=1
    )
    gate_w_grad, up_w_grad = scatter_columns(glu_grad, [hidden_width] * 2, rows)
    out_grad = lax.psum_scatter(
        outer_sum(product, mixed_all).astype(LOW), "fsdp", scatter_dimension=0, tiled=True
    ).astype(WIDE)
    in_grad = jnp.concatenate(
        [outer_sum(normed_all, x_low), outer_sum(normed_all, pre_low)], axis=1
    )
    lru_in_grad, gelu_in_grad = scatter_columns(in_grad, [channels] * 2, rows)
    small = jnp.concatenate(
        [
            wr_grad, wi_grad, sums[:7].T,
            (sums[7] * RATE_SCALE * jax.nn.sigmoid(-decay))[:, None],
        ],
        axis=1,
    )
    small = lax.psum_scatter(
        small.reshape(lax.axis_size("fsdp"), -1, small.shape[1]),
        "fsdp", scatter_dimension=0, tiled=False,
    )
    gain_parts = jnp.stack([mix_gain_grad, mlp_gain_grad]).reshape(2, -1, rows).transpose(1, 0, 2)
    gain_grads = lax.psum_scatter(
        gain_parts, ("seq", "fsdp"), scatter_dimension=0, tiled=False
    )
    first = 2 * size
    return (
        result.astype(LOW).reshape(tokens.shape),
        input_grad.astype(LOW).reshape(tokens.shape),
        gain_grads[0],
        lru_in_grad,
        gelu_in_grad,
        out_grad,
        small[:, first : first + 4],
        small[:, first + 4],
        small[:, :size],
        small[:, first + 5],
        small[:, size : 2 * size],
        small[:, first + 6],
        small[:, first + 7],
        gain_grads[1],
        gate_w_grad,
        up_w_grad,
        down_grad,
    )


def aligned(
    tokens, cotangent, mix_gain, lru_in_weight, gelu_in_weight, out_weight, conv_weight, conv_bias,
    recurrence_weight, recurrence_bias, input_gate_weight, input_gate_bias, decay_param, mlp_gain,
    gate_weight, up_weight, down_weight,
):
    positions, width = tokens.shape[1:]
    rows = lru_in_weight.shape[0]
    shards = lax.axis_size("seq")
    channels = lru_in_weight.shape[1] // shards
    hidden_width = gate_weight.shape[1] // shards
    size = recurrence_weight.shape[1]

    groups = lax.axis_size("fsdp")
    resid_in = tokens.reshape(positions, width).astype(WIDE)
    grad_low = cotangent.reshape(positions, width)

    def by_column(first, second):
        parts = [member.reshape(rows, shards, -1) for member in (first, second)]
        return jnp.concatenate(parts, axis=2).transpose(1, 0, 2)

    own_decay = decay_param.astype(WIDE)
    vecs = jnp.concatenate(
        [
            conv_weight.astype(WIDE).T,
            jnp.stack([conv_bias, recurrence_bias, input_gate_bias]).astype(WIDE),
            -RATE_SCALE * jax.nn.softplus(-own_decay)[None],
        ],
        axis=0,
    )
    gain_shard = jnp.pad(jnp.stack([mix_gain, mlp_gain]).astype(WIDE), ((0, 6), (0, 0)))
    tokens_low = tokens.reshape(positions, width)
    (
        normed, in_whole, ext, branch_pre, conv_low, recur_gate, input_gate, states, product, par, wr, wi,
        gains, glu_mine, out_whole, down_whole,
    ) = mix_in(
        tokens_low, by_column(lru_in_weight, gelu_in_weight), by_column(gate_weight, up_weight),
        out_weight, down_weight, jnp.concatenate([recurrence_weight, input_gate_weight], axis=1),
        vecs, gain_shard, groups,
    )
    out_whole = out_whole.reshape(-1, width)
    middle, middle_grad, mixed_low, mlp_sums, fed_own, fed_other, glu_grad, down_grad = feed(
        product, out_whole, glu_mine, down_whole.reshape(-1, width), grad_low, tokens_low, gains, groups
    )
    (
        result, tokens_grad, mix_sums, wr_grad, wi_grad, sums, out_grad, in_grad, glu_heard, down_heard,
    ) = back(
        mixed_low, fed_own, fed_other, middle, middle_grad, tokens_low, gains, par, wr, wi,
        out_whole, in_whole, normed, product, ext, branch_pre, conv_low, recur_gate, input_gate, states,
        glu_grad, down_grad.reshape(groups, -1, width), size,
    )
    small_rows = recurrence_weight.shape[0]
    vector_parts = sums.reshape(8, groups, small_rows).transpose(1, 0, 2)
    small = jnp.concatenate(
        [
            jnp.concatenate([wr_grad, wi_grad], axis=1).reshape(groups, small_rows, 2 * size),
            jnp.pad(vector_parts, ((0, 0), (0, 0), (0, 2 * size - small_rows))),
        ],
        axis=1,
    )
    gain_parts = jnp.stack([mix_sums[0], mlp_sums[0]]).reshape(2, shards, groups, rows)
    gain_parts = jnp.pad(gain_parts.transpose(2, 1, 0, 3), ((0, 0), (0, 0), (0, 6), (0, 0)))
    glu_out, in_out, out_heard, small_heard, gain_out = tail(
        glu_heard, in_grad, out_grad.reshape(groups, -1, width), small, gain_parts
    )

    def rows_of(parts, first, size):
        return parts[:, :, first : first + size].astype(WIDE).transpose(1, 0, 2).reshape(rows, -1)

    small = jnp.sum(small_heard, axis=0)
    vector_sums = small[small_rows:, :small_rows]
    gain_grads = jnp.sum(gain_out, axis=0)
    return (
        result.reshape(tokens.shape),
        tokens_grad.reshape(tokens.shape),
        gain_grads[0],
        rows_of(in_out, 0, channels),
        rows_of(in_out, channels, channels),
        jnp.sum(out_heard.astype(WIDE), axis=0),
        vector_sums[:4].T,
        vector_sums[4],
        small[:small_rows, :size],
        vector_sums[5],
        small[:small_rows, size : 2 * size],
        vector_sums[6],
        vector_sums[7] * RATE_SCALE * jax.nn.sigmoid(-own_decay),
        gain_grads[1],
        rows_of(glu_out, 0, hidden_width),
        rows_of(glu_out, hidden_width, hidden_width),
        jnp.sum(down_heard.astype(WIDE), axis=0),
    )


def solution(mesh):
    shards, groups = mesh.shape["seq"], mesh.shape["fsdp"]

    def local(*arrays):
        rows, small_rows = arrays[3].shape[0], arrays[5].shape[0]
        simple = shards % 2 == 0 and rows % 16 == 0 and small_rows % 16 == 0
        simple = simple and arrays[0].shape[1] * shards % (8 * CHUNK) == 0
        return (aligned if simple else general)(*arrays)

    tokens = P("fsdp", "seq", None)
    vector = P(("seq", "fsdp"))
    matrix = P(("seq", "fsdp"), None)
    ranks = (1, 2, 2, 2, 2, 1, 2, 1, 2, 1, 1, 1, 2, 2, 2)
    specs = (tokens, tokens) + tuple(vector if rank == 1 else matrix for rank in ranks)
    return jax.shard_map(local, mesh=mesh, in_specs=specs, out_specs=specs, check_vma=False)
```

```python
import functools

import jax
import jax.numpy as jnp
from jax import lax
from jax.experimental import pallas as pl
from jax.experimental.pallas import tpu as pltpu
from jax.sharding import PartitionSpec as P

EPSILON = 1e-06
RATE_SCALE = 8.0
CHUNK = 128
LOW = jnp.bfloat16
WIDE = jnp.float32


def rms_scale(values, gain):
    scale = lax.rsqrt(jnp.mean(values * values, axis=-1, keepdims=True) + EPSILON)
    return values * scale * gain


def dot(left, right):
    return jnp.dot(left, right, preferred_element_type=WIDE)


def outer_sum(left, right):
    return lax.dot_general(left, right, (((0,), (0,)), ((), ())), preferred_element_type=WIDE)


def times_transpose(left, right):
    return lax.dot_general(left, right, (((1,), (1,)), ((), ())), preferred_element_type=WIDE)


def one_minus_exp(value):
    series = jnp.full_like(value, 1.0 / 40320.0)
    for bottom in (5040.0, 720.0, 120.0, 24.0, 6.0, 2.0, 1.0):
        series = 1.0 / bottom - value * series
    return jnp.where(value < 0.4, value * series, 1.0 - jnp.exp(-value))


def sigmoid(value):
    return 0.5 * jnp.tanh(0.5 * value) + 0.5


def lane_tiles(channels):
    return -(-channels // 128)


def put(tiles, rows, value):
    channels = value.shape[1]
    for n in range(lane_tiles(channels)):
        size = min(128, channels - n * 128)
        tiles[n, rows, 0:size] = value[:, n * 128 : n * 128 + size]


def get(tiles, rows, channels):
    return jnp.concatenate(
        [
            tiles[n, rows, 0 : min(128, channels - n * 128)]
            for n in range(lane_tiles(channels))
        ],
        axis=1,
    )


def scan_segments(step, count, tiles):
    def body(i, carried):
        return tuple(step(i, n, *carried[n]) for n in range(tiles))

    start = (jnp.zeros((8, 128), WIDE), jnp.ones((8, 128), WIDE))
    ends = lax.fori_loop(0, count, body, (start,) * tiles, unroll=4)
    return [jnp.concatenate([end[which] for end in ends], axis=1) for which in (0, 1)]


MESH = pl.DeviceIdType.MESH
VMEM_BYTES = 61 * 2**20
ANY = pl.BlockSpec(memory_space=pl.ANY)
HELD = pl.BlockSpec(memory_space=pltpu.VMEM)
ROOT = 0.7978845608028654
CUBE = 0.044715


def dma(*shape):
    return pltpu.SemaphoreType.DMA(shape)


def remote(src, dst, send, recv, axis, index):
    return pltpu.make_async_remote_copy(
        src_ref=src, dst_ref=dst, send_sem=send, recv_sem=recv,
        device_id={axis: index}, device_id_type=MESH,
    )


def gelu(value):
    return 0.5 * value * (1.0 + jnp.tanh(ROOT * (value + CUBE * value * value * value)))


def gelu_and_slope(value):
    square = value * value
    bent = jnp.tanh(ROOT * (value + CUBE * square * value))
    half = 0.5 * (1.0 + bent)
    slope = half + 0.5 * value * (1.0 - bent * bent) * (ROOT * (1.0 + 3.0 * CUBE * square))
    return value * half, slope


class Place:
    def __init__(self, shards, groups):
        self.shards, self.groups, self.line = shards, groups, shards // 2
        self.s, self.f = lax.axis_index("seq"), lax.axis_index("fsdp")
        self.z, self.c = self.s // 2, lax.rem(self.s, 2)
        self.sibling = 2 * self.z + 1 - self.c

    def nearest(self, n):
        chip = 0
        for z in range(self.line):
            for place, other in enumerate(sorted(range(self.line), key=lambda y: abs(y - z))):
                chip = jnp.where((self.z == z) & (n == place), other, chip)
        return chip

    def enter(self, seq=True, fsdp=True):
        barrier = pltpu.get_barrier_semaphore()
        met = 0
        for axis, mine, count, wanted in (
            ("seq", self.s, self.shards, seq), ("fsdp", self.f, self.groups, fsdp),
        ):
            for d in range(1, count if wanted else 1):
                pl.semaphore_signal(
                    barrier, inc=1, device_id={axis: lax.rem(mine + d, count)}, device_id_type=MESH
                )
                met += 1
        pl.semaphore_wait(barrier, met)


class Spread:
    def __init__(self, at, src, dst, send, recv, axis="fsdp"):
        self.at, self.src, self.dst, self.send, self.recv, self.axis = at, src, dst, send, recv, axis
        self.mine, self.count = (at.f, at.groups) if axis == "fsdp" else (at.s, at.shards)

    def copy(self, d):
        peer = lax.rem(self.mine + d, self.count)
        return remote(
            self.src(peer), self.dst(self.mine), self.send.at[d], self.recv.at[d], self.axis, peer
        )

    def start(self):
        for d in range(1, self.count):
            self.copy(d).start()

    def source(self, d):
        return lax.rem(self.mine + self.count - d, self.count)

    def arrive(self, d):
        origin = self.source(d)
        remote(
            self.src(origin), self.dst(origin), self.send.at[d], self.recv.at[d], self.axis, origin
        ).wait_recv()

    def sent(self):
        for d in range(1, self.count):
            self.copy(d).wait_send()

    def finish(self):
        for d in range(1, self.count):
            self.arrive(d)
        self.sent()


class LineGather:
    def __init__(self, at, src, buf, send, recv, pieces):
        self.at, self.src, self.buf, self.send, self.recv, self.pieces = at, src, buf, send, recv, pieces
        self.rows = buf.shape[1] // pieces

    def copy(self, slot, piece, kind, first=False):
        at = self.at
        rows = pl.ds(piece * self.rows, self.rows)
        there = self.buf.at[slot, rows]
        peer = (at.sibling, at.s + 2, at.s - 2)[kind]
        return remote(
            self.src.at[rows] if first else there, there,
            self.send.at[slot, piece, kind], self.recv.at[slot, piece], "seq", peer,
        )

    def start(self):
        at = self.at
        for piece in range(self.pieces):
            @pl.when(at.z + 1 < at.line)
            def _():
                self.copy(at.s, piece, 1, True).start()

            @pl.when(at.z > 0)
            def _():
                self.copy(at.s, piece, 2, True).start()

            self.copy(at.s, piece, 0, True).start()

    def arrive(self, chip, piece):
        at = self.at
        slot = 2 * chip + at.c
        self.copy(slot, piece, 0).wait_recv()

        @pl.when((chip < at.z) & (at.z + 1 < at.line))
        def _():
            self.copy(slot, piece, 1).start()

        @pl.when((chip > at.z) & (at.z > 0))
        def _():
            self.copy(slot, piece, 2).start()

        self.copy(slot, piece, 0).start()

    def settle(self, chip):
        for piece in range(self.pieces):
            self.copy(2 * chip + 1 - self.at.c, piece, 0).wait_recv()

    def pass_on(self, d):
        at = self.at
        for piece in range(self.pieces):
            for chip, known in ((at.z - d, at.z - d >= 0), (at.z + d, at.z + d < at.line)):
                @pl.when(known)
                def _():
                    self.arrive(chip, piece)

    def distances(self, body, beside=None):
        at = self.at

        @pl.loop(0, at.line)
        def _(n):
            @pl.when(n > 0)
            def _():
                self.pass_on(n)
                if beside is not None:
                    beside(n)

            chip = at.nearest(n)
            self.settle(chip)
            body(chip)

    def sent(self):
        at = self.at
        for chip in range(at.line):
            slot = 2 * chip + at.c
            for piece in range(self.pieces):
                self.copy(slot, piece, 0).wait_send()

                @pl.when((chip <= at.z) & (at.z + 1 < at.line))
                def _():
                    self.copy(slot, piece, 1).wait_send()

                @pl.when((chip >= at.z) & (at.z > 0))
                def _():
                    self.copy(slot, piece, 2).wait_send()


class LineScatter:
    def __init__(self, at, own, other, heard, into, sems, pieces):
        self.at, self.own, self.other, self.heard, self.into = at, own, other, heard, into
        self.sib_send, self.sib_recv, self.send, self.recv = sems
        self.pieces = pieces
        self.rows = own.shape[1] // pieces

    @staticmethod
    def scratch(line, rows, width, pieces):
        low = pltpu.VMEM((line, rows, width), LOW)
        return [
            pltpu.VMEM((line, rows, width), WIDE), low, low, low,
            dma(line), dma(line), dma(line, pieces), dma(line, pieces),
        ]

    def across(self, chip):
        return remote(
            self.other.at[chip], self.heard.at[chip], self.sib_send.at[chip],
            self.sib_recv.at[chip], "seq", self.at.sibling,
        )

    def whole_way(self, chip, start):
        if self.at.line < 4:
            return False
        return jnp.abs(chip - start) == self.at.line - 1

    def joined(self, chip):
        at = self.at
        if at.line < 4:
            return False
        return ((at.z == 1) & (chip == at.line - 1)) | ((at.z == at.line - 2) & (chip == 0))

    def along(self, chip, piece):
        at = self.at
        rows = pl.ds(pl.multiple_of(piece * self.rows, self.rows), self.rows)
        target, slot = chip, at.z
        if at.line >= 4:
            stop = jnp.where(chip > at.z, at.z + 1, at.z - 1)
            target = jnp.where(self.whole_way(chip, at.z), stop, chip)
            slot = jnp.where(self.whole_way(chip, at.z), stop, at.z)
        return remote(
            self.other.at[chip, rows], self.into.at[slot, rows], self.send.at[chip, piece],
            self.recv.at[slot, piece], "seq", 2 * target + at.c,
        )

    def landed(self, slot, piece):
        rows = pl.ds(pl.multiple_of(piece * self.rows, self.rows), self.rows)
        there = self.into.at[slot, rows]
        remote(
            there, there, self.recv.at[slot, piece], self.recv.at[slot, piece], "seq", self.at.sibling
        ).wait_recv()

    def add(self, chip, piece, extras, store):
        @pl.loop(0, self.rows // 16)
        def _(block):
            rows = pl.ds(pl.multiple_of(piece * self.rows + block * 16, 16), 16)
            total = self.own[chip, rows, :].astype(WIDE) + self.heard[chip, rows, :].astype(WIDE)
            for known, slot in extras:
                here = self.into[slot, rows, :].astype(WIDE)
                total = total + (here if known is True else jnp.where(known, here, 0.0))
            store(rows, total)

    def store_out(self, chip):
        def store(rows, total):
            self.other[chip, rows, :] = total.astype(LOW)

        return store

    def push(self, chip):
        at = self.at
        goes = chip != at.z
        if at.line >= 4:
            goes = goes & jnp.logical_not(self.joined(chip))

        @pl.when(goes)
        def _():
            self.across(chip).wait()

            @pl.loop(0, self.pieces)
            def _(piece):
                self.add(chip, piece, [], self.store_out(chip))
                self.along(chip, piece).start()

    def join(self):
        at = self.at
        if at.line < 4:
            return

        @pl.when((at.z == 1) | (at.z == at.line - 2))
        def _():
            chip = jnp.where(at.z == 1, at.line - 1, 0)
            self.across(chip).wait()

            @pl.loop(0, self.pieces)
            def _(piece):
                self.landed(at.z, piece)
                self.add(chip, piece, [(True, at.z)], self.store_out(chip))
                self.along(chip, piece).start()

    def finish(self, store):
        at = self.at
        self.across(at.z).wait_recv()

        def known(chip):
            heard = chip != at.z
            return heard & jnp.logical_not(self.whole_way(chip, at.z)) if at.line >= 4 else heard

        @pl.loop(0, self.pieces)
        def _(piece):
            for chip in range(at.line):
                @pl.when(known(chip))
                def _():
                    self.landed(chip, piece)

            self.add(at.z, piece, [(known(chip), chip) for chip in range(at.line)], store)

    def sent(self):
        at = self.at
        self.across(at.z).wait_send()
        for chip in range(at.line):
            @pl.when(chip != at.z)
            def _():
                @pl.loop(0, self.pieces)
                def _(piece):
                    self.along(chip, piece).wait_send()


def normalise(source, gain, store, rows):
    @pl.loop(0, rows // 16)
    def _(block):
        here = pl.ds(pl.multiple_of(block * 16, 16), 16)
        values = source(here)
        scale = lax.rsqrt(jnp.mean(values * values, axis=-1, keepdims=True) + EPSILON)
        store(here, (values * scale * gain).astype(LOW))


def mixer_rows(positions):
    return [pl.ds(pl.multiple_of(n, CHUNK), CHUNK) for n in range(0, positions, CHUNK)]


def mix_in_kernel(
    tokens, in_shard, glu_shard, out_shard, down_shard, small, vecs, gain_shard,
    normed, in_whole, ext, pre_ref, conv_ref, r_ref, i_ref, st_ref,
    product_ref, par_ref, wr_ref, wi_ref, gains, glu_mine, out_whole, down_whole,
    held, small_all, vecs_all, gain_all, factors, drive, prod,
    local_sems, tok_send, tok_recv, in_sems, in_xy_send, in_xy_recv, glu_sems, xy_sems, gain_sems,
):
    groups, shards = in_whole.shape[1], in_whole.shape[0]
    at = Place(shards, groups)
    s, f = at.s, at.f
    positions, channels = pre_ref.shape
    width = tokens.shape[1]
    rows = in_shard.shape[1]
    segment = positions // 8
    chunks = positions // CHUNK

    keep = [
        (tokens, held.at[s]), (in_shard.at[s], in_whole.at[s, f]), (glu_shard.at[s], glu_mine.at[s]),
        (out_shard, out_whole.at[f]), (down_shard, down_whole.at[f]), (small, small_all.at[f]),
        (vecs, vecs_all.at[f]), (gain_shard, gain_all.at[s, f]),
    ]
    keep = [pltpu.make_async_copy(a, b, local_sems.at[n]) for n, (a, b) in enumerate(keep)]
    for copy in keep:
        copy.start()
    at.enter()

    def over_fsdp(src, dst, n):
        return Spread(at, lambda peer: src, lambda origin: dst.at[origin], xy_sems.at[n, 0], xy_sems.at[n, 1])

    gain_xy = Spread(
        at, lambda peer: gain_shard, lambda origin: gain_all.at[s, origin],
        xy_sems.at[0, 0], xy_sems.at[0, 1],
    )
    small_xy = over_fsdp(small, small_all, 1)
    vecs_xy = over_fsdp(vecs, vecs_all, 2)
    out_xy = over_fsdp(out_shard, out_whole, 3)
    down_xy = over_fsdp(down_shard, down_whole, 4)
    in_z = Spread(
        at, lambda peer: in_shard.at[peer], lambda origin: in_whole.at[origin, f],
        in_sems.at[0], in_sems.at[1], "seq",
    )
    glu_z = Spread(
        at, lambda peer: glu_shard.at[peer], lambda origin: glu_mine.at[origin],
        glu_sems.at[0], glu_sems.at[1], "seq",
    )
    gain_z = Spread(
        at, lambda peer: gain_all.at[s], lambda origin: gain_all.at[origin],
        gain_sems.at[0], gain_sems.at[1], "seq",
    )

    def in_xy(index):
        return Spread(
            at, lambda peer: in_whole.at[index, f], lambda origin: in_whole.at[index, origin],
            in_xy_send.at[index], in_xy_recv.at[index],
        )

    gather = LineGather(at, tokens, held, tok_send, tok_recv, tok_send.shape[1])
    gain_xy.start()
    in_z.start()
    keep[1].wait()
    in_xy(s).start()
    gather.start()
    vecs_xy.start()
    small_xy.start()
    keep[7].wait()
    gain_xy.finish()
    gain_z.start()
    for d in range(1, shards):
        in_z.arrive(d)
        in_xy(in_z.source(d)).start()
    out_xy.start()
    glu_z.start()
    down_xy.start()
    gain_z.finish()
    for origin in range(shards):
        for other in range(groups):
            first = (origin * groups + other) * rows
            gains[:, first : first + rows] = gain_all[origin, other]
    keep[0].wait()

    def take(chip):
        for core in range(2):
            slot = 2 * chip + core

            def store(here, value):
                normed[slot, here, :] = value

            normalise(
                lambda here: held[slot, here, :].astype(WIDE), gains[0:1, :], store, tokens.shape[0]
            )

    gather.distances(take)
    keep[6].wait()
    vecs_xy.finish()
    keep[5].wait()
    small_xy.finish()
    size = small.shape[1] // 2
    local = small.shape[0]
    wr_ref[...] = jnp.zeros_like(wr_ref)
    wi_ref[...] = jnp.zeros_like(wi_ref)
    flat = small_all[...].reshape(channels, 2 * size)
    for n in range(channels // size):
        block = slice(n * size, (n + 1) * size)
        wr_ref[block, block] = flat[block, :size]
        wi_ref[block, block] = flat[block, size:]
    for other in range(groups):
        par_ref[:, other * local : (other + 1) * local] = vecs_all[other]
    ext[0:8, :] = jnp.zeros((8, channels), WIDE)
    st_ref[0:8, :] = jnp.zeros((8, channels), WIDE)
    for index in range(shards):
        for d in range(1, groups):
            in_xy(index).arrive(d)
    @pl.loop(0, at.line)
    def _(chip):
        pair = normed[pl.ds(2 * chip, 2), :, :].reshape(2 * tokens.shape[0], width)
        both = dot(pair, in_whole[...].reshape(width, 2 * channels))
        base = pl.multiple_of(chip * 2 * tokens.shape[0], CHUNK)
        here = pl.ds(base, 2 * tokens.shape[0])
        ext[pl.ds(base + 8, 2 * tokens.shape[0]), :] = both[:, :channels].astype(LOW).astype(WIDE)
        pre_ref[here, :] = both[:, channels:]

    @pl.loop(0, chunks)
    def _(n):
        base = pl.multiple_of(n * CHUNK, CHUNK)
        here = pl.ds(base, CHUNK)
        block = ext[pl.ds(base, CHUNK + 8), :]
        conv = jnp.broadcast_to(par_ref[4:5, :], (CHUNK, channels))
        for k in range(4):
            conv = conv + par_ref[k : k + 1, :] * block[8 - k : 8 - k + CHUNK]
        conv_low = conv.astype(LOW)
        conv_ref[here, :] = conv_low
        r = jax.nn.sigmoid(dot(conv_low, wr_ref[...]) + par_ref[5:6, :])
        gate = jax.nn.sigmoid(dot(conv_low, wi_ref[...]) + par_ref[6:7, :])
        log_decay = r * par_ref[7:8, :]
        m = jnp.sqrt(one_minus_exp(-2.0 * log_decay))
        factor = jnp.exp(log_decay)
        r_ref[here, :] = r
        i_ref[here, :] = gate
        put(factors, here, factor)
        put(drive, here, m * gate * conv_low.astype(WIDE))

    def step(i, n, state, product):
        here = pl.ds(i, 8, stride=segment)
        factor = factors[n, here, :]
        state = factor * state + drive[n, here, :]
        product = factor * product
        drive[n, here, :] = state
        prod[n, here, :] = product
        return state, product

    state, product = scan_segments(step, segment, lane_tiles(channels))
    state, product = state[:, :channels], product[:, :channels]
    carry = jnp.zeros((1, channels), WIDE)
    for k in range(8):
        for part in range(segment // CHUNK):
            base = k * segment + part * CHUNK
            here = slice(base, base + CHUNK)
            states = get(drive, here, channels) + get(prod, here, channels) * carry
            st_ref[base + 8 : base + 8 + CHUNK, :] = states
            product_ref[here, :] = (
                states.astype(LOW).astype(WIDE) * gelu(pre_ref[here, :])
            ).astype(LOW)
        carry = state[k : k + 1] + product[k : k + 1] * carry

    glu_z.finish()
    out_xy.finish()
    down_xy.finish()
    gather.sent()
    in_z.sent()
    for index in range(shards):
        in_xy(index).sent()
    for n in (2, 3, 4):
        keep[n].wait()


def mix_in(tokens, in_shard, glu_shard, out_shard, down_shard, small, vecs, gain_shard, groups):
    shards, rows, both = in_shard.shape
    block, width = tokens.shape
    positions, channels = shards * block, both // 2
    local = small.shape[0]
    pieces = 2
    wide = jax.ShapeDtypeStruct((positions, channels), WIDE)
    low = jax.ShapeDtypeStruct((positions, channels), LOW)
    longer = jax.ShapeDtypeStruct((positions + 8, channels), WIDE)
    square = jax.ShapeDtypeStruct((channels, channels), LOW)
    held = [
        jax.ShapeDtypeStruct((shards, block, width), LOW),
        jax.ShapeDtypeStruct((shards, groups, rows, both), LOW),
        longer, wide, low, wide, wide, longer,
        low, jax.ShapeDtypeStruct((8, channels), WIDE), square, square,
        jax.ShapeDtypeStruct((8, width), WIDE),
    ]
    far = [
        jax.ShapeDtypeStruct((shards, rows, glu_shard.shape[2]), LOW),
        jax.ShapeDtypeStruct((groups,) + out_shard.shape, LOW),
        jax.ShapeDtypeStruct((groups,) + down_shard.shape, LOW),
    ]
    return pl.pallas_call(
        mix_in_kernel,
        out_shape=held + far,
        in_specs=[HELD] * 5 + [ANY] * 3,
        out_specs=[HELD] * len(held) + [ANY] * len(far),
        scratch_shapes=[
            pltpu.VMEM((shards, block, width), LOW),
            pltpu.VMEM((groups,) + small.shape, LOW),
            pltpu.VMEM((groups,) + vecs.shape, WIDE),
            pltpu.VMEM((shards, groups) + gain_shard.shape, WIDE),
        ]
        + [pltpu.VMEM((lane_tiles(channels), positions, 128), WIDE)] * 3
        + [
            dma(8), dma(shards, pieces, 3), dma(shards, pieces), dma(2, shards), dma(shards, groups),
            dma(shards, groups), dma(2, shards), dma(5, 2, groups), dma(2, shards),
        ],
        compiler_params=pltpu.CompilerParams(
            collective_id=1, has_side_effects=True, vmem_limit_bytes=VMEM_BYTES
        ),
        name="mix_in",
    )(tokens, in_shard, glu_shard, out_shard, down_shard, small, vecs, gain_shard)


def feed_kernel(
    product, out_whole, glu_mine, down_in, cotangent, tokens, gains,
    middle, middle_grad, mixed_low, gain_sums, fed_own, fed_other, glu_grad, down_grad,
    held, cots, glu, down, both, hidden, wide_pair, hidden_pair, normed2, staged, down_staged,
    own, other, heard, into, sib_send, sib_recv, line_send, line_recv,
    local_sems, glu_send, glu_recv, two_send, two_recv, cot_send, cot_recv, stage_sems,
):
    shards, groups = glu.shape[0], glu.shape[1]
    at = Place(shards, groups)
    s, f = at.s, at.f
    block, width = tokens.shape
    units = down.shape[0]
    pair = 2 * block

    keep = [(glu_mine, glu.at[:, f]), (down_in, down), (cotangent, cots.at[s])]
    keep = [pltpu.make_async_copy(a, b, local_sems.at[n]) for n, (a, b) in enumerate(keep)]
    for copy in keep:
        copy.start()
    at.enter()
    def glu_xy(index):
        return Spread(
            at, lambda peer: glu_mine.at[index], lambda origin: glu.at[index, origin],
            glu_send.at[index], glu_recv.at[index],
        )

    cot_z = LineGather(at, cotangent, cots, cot_send, cot_recv, cot_send.shape[1])
    two_z = LineGather(at, normed2, held, two_send, two_recv, two_send.shape[1])
    sums = LineScatter(
        at, own, other, heard, into, (sib_send, sib_recv, line_send, line_recv), line_send.shape[1]
    )
    for index in range(shards):
        glu_xy(index).start()
    cot_z.start()

    def split(chip, columns, value, mine, theirs):
        first = at.c == 0
        mine[chip, :, columns] = jnp.where(first, value[:block], value[block:]).astype(mine.dtype)
        theirs[chip, :, columns] = jnp.where(first, value[block:], value[:block]).astype(theirs.dtype)

    def columns_of(j):
        return pl.ds(pl.multiple_of(j * 256, 256), 256)

    def pair_rows(chip):
        return pl.ds(pl.multiple_of(chip * pair, pair), pair)

    def project(chip):
        @pl.loop(0, width // 256)
        def _(j):
            value = dot(product[pair_rows(chip), :], out_whole[:, columns_of(j)])
            split(chip, columns_of(j), value, own, other)

        sums.across(chip).start()

    for k in range(at.line // 2):
        project(at.line - 1 - k)
        project(k)
        sums.push(at.line - 1 - k)
        sums.push(k)
    cot_z.pass_on(1)
    sums.join()
    for d in range(2, at.line):
        cot_z.pass_on(d)

    def to_middle(here, total):
        values = total + tokens[here, :].astype(WIDE)
        middle[here, :] = values
        scale = lax.rsqrt(jnp.mean(values * values, axis=-1, keepdims=True) + EPSILON)
        normed2[here, :] = (values * scale * gains[1:2, :]).astype(LOW)

    sums.finish(to_middle)
    two_z.start()
    own_copy = pltpu.make_async_copy(normed2, held.at[s], local_sems.at[3])
    own_copy.start()
    keep[0].wait()
    keep[1].wait()
    keep[2].wait()
    sums.sent()
    own_copy.wait()
    for index in range(shards):
        glu_xy(index).finish()

    def feed(chip):
        here = pair_rows(chip)
        rows = held[pl.ds(2 * chip, 2), :, :].reshape(pair, width)
        grads = cots[pl.ds(2 * chip, 2), :, :].reshape(pair, width)

        @pl.loop(0, 2 * units // 256)
        def _(j):
            wide_pair[:, columns_of(j)] = dot(
                rows, glu[:, :, :, columns_of(j)].reshape(width, 256)
            )

        @pl.loop(0, units // 256)
        def _(j):
            hidden_pair[:, columns_of(j)] = times_transpose(grads, down[columns_of(j), :])

        @pl.loop(0, pair // 16)
        def _(n):
            part = pl.ds(pl.multiple_of(n * 16, 16), 16)
            there = pl.ds(pl.multiple_of(chip * pair + n * 16, 16), 16)
            opened, slope = gelu_and_slope(wide_pair[part, :units])
            up = wide_pair[part, units:]
            grad = hidden_pair[part, :]
            hidden[there, :] = (opened * up).astype(LOW)
            both[there, :units] = (grad * up * slope).astype(LOW)
            both[there, units:] = (grad * opened).astype(LOW)

        @pl.loop(0, shards)
        def _(j):
            value = times_transpose(both[here, :], glu[j].reshape(width // shards, 2 * units))
            split(chip, columns_of(j), value, own, other)

        sums.across(chip).start()

        @pl.loop(0, width // 256)
        def _(j):
            split(chip, columns_of(j), dot(hidden[here, :], down[:, columns_of(j)]), fed_own, fed_other)

    for chip in range(at.line):
        cot_z.settle(chip)
    two_z.distances(feed)

    def glu_out(j):
        return pltpu.make_async_copy(
            staged.at[lax.rem(j, 2)], glu_grad.at[:, j], stage_sems.at[lax.rem(j, 2)]
        )

    def glu_sums(first, last):
        @pl.loop(first, last)
        def _(j):
            @pl.when(j >= 2)
            def _():
                glu_out(j - 2).wait()

            rows = held[:, :, columns_of(j)].reshape(shards * block, 256)
            staged[lax.rem(j, 2)] = outer_sum(rows, both[...]).astype(LOW).reshape(staged.shape[1:])
            glu_out(j).start()

    def down_out(j):
        return pltpu.make_async_copy(
            down_staged.at[lax.rem(j, 2)], down_grad.at[columns_of(j)], stage_sems.at[2 + lax.rem(j, 2)]
        )

    def down_sums():
        @pl.loop(0, units // 256)
        def _(j):
            @pl.when(j >= 2)
            def _():
                down_out(j - 2).wait()

            grads = cots[...].reshape(shards * block, width)
            down_staged[lax.rem(j, 2)] = outer_sum(hidden[:, columns_of(j)], grads).astype(LOW)
            down_out(j).start()

    for n in range(at.line - 1, 0, -1):
        sums.push(at.nearest(n))
    down_sums()
    sums.join()
    glu_sums(0, shards)
    gain_sums[...] = jnp.zeros_like(gain_sums)

    def back(here, grad):
        values = middle[here, :]
        scale = lax.rsqrt(jnp.mean(values * values, axis=-1, keepdims=True) + EPSILON)
        scaled = grad * gains[1:2, :]
        along = jnp.mean(scaled * values, axis=-1, keepdims=True)
        total = cotangent[here, :].astype(WIDE) + scale * scaled - values * (scale * scale * scale * along)
        middle_grad[here, :] = total
        mixed_low[here, :] = total.astype(LOW)
        gain_sums[0:1, :] += jnp.sum(grad * values * scale, axis=0, keepdims=True)

    sums.finish(back)
    for j in range(shards - 2, shards):
        glu_out(j).wait()
    for j in range(max(units // 256 - 2, 0), units // 256):
        down_out(j).wait()
    sums.sent()
    two_z.sent()
    cot_z.sent()


def feed(product, out_whole, glu_mine, down_whole, cotangent, tokens, gains, groups):
    shards, rows, both = glu_mine.shape
    block, width = tokens.shape
    units = both // 2
    line, pieces, thirds = shards // 2, 2, 2
    own = jax.ShapeDtypeStruct((block, width), WIDE)
    low = jax.ShapeDtypeStruct((line, block, width), LOW)
    outs = [
        own, own, jax.ShapeDtypeStruct((block, width), LOW), jax.ShapeDtypeStruct((8, width), WIDE),
        low, low,
        jax.ShapeDtypeStruct((groups, shards, rows, both), LOW),
        jax.ShapeDtypeStruct((units, width), LOW),
    ]
    gathered = pltpu.VMEM((shards, block, width), LOW)
    return pl.pallas_call(
        feed_kernel,
        out_shape=outs,
        in_specs=[HELD, HELD, ANY, ANY, HELD, HELD, HELD],
        out_specs=[HELD] * 6 + [ANY] * 2,
        scratch_shapes=[
            gathered, gathered,
            pltpu.VMEM((shards, groups, rows, both), LOW),
            pltpu.VMEM((units, width), LOW),
            pltpu.VMEM((shards * block, both), LOW),
            pltpu.VMEM((shards * block, units), LOW),
            pltpu.VMEM((2 * block, both), WIDE),
            pltpu.VMEM((2 * block, units), WIDE),
            pltpu.VMEM((block, width), LOW),
            pltpu.VMEM((2, groups, rows, both), LOW),
            pltpu.VMEM((2, 256, width), LOW),
        ]
        + LineScatter.scratch(line, block, width, thirds)
        + [
            dma(4), dma(shards, groups), dma(shards, groups), dma(shards, pieces, 3), dma(shards, pieces),
            dma(shards, pieces, 3), dma(shards, pieces), dma(4),
        ],
        compiler_params=pltpu.CompilerParams(
            collective_id=2, has_side_effects=True, vmem_limit_bytes=VMEM_BYTES
        ),
        name="feed",
    )(product, out_whole, glu_mine, down_whole, cotangent, tokens, gains)


def back_kernel(
    mixed, fed_own, fed_far, middle, middle_grad, tokens, gains, par_ref, wr_ref, wi_ref,
    out_far, in_far, normed_far, product_far, ext_far, pre_far, conv_far, r_far, i_far, st_far,
    glu_grad, down_grad, mlp_parts,
    result, tokens_grad, glu_out, in_out, out_heard, small_heard, gain_out, glu_heard, down_heard, in_grad,
    held, in_whole, out_whole, product, ext, pre, conv_ref, r_ref, i_ref, st_ref,
    both, pair_grad, staged, factors, adj, prod, cg, carries, wr_sum, wi_sum,
    out_sum, out_grad, small, gain_row, gain_parts, gain_heard, gain_sum, glu_parts, glu_sum, in_heard, in_sum,
    fed_other, fed_heard, fed_into, fed_sib_send, fed_sib_recv, fed_send, fed_recv,
    own, other, heard, into, sib_send, sib_recv, line_send, line_recv,
    local_sems, held_send, held_recv, glu_xy_sems, down_sems, stage_sems, in_xy_sems, out_sems,
    small_sems, gain_xy_sems, glu_sems, in_sems, gain_sems,
):
    shards, groups = in_whole.shape[0], in_whole.shape[1]
    at = Place(shards, groups)
    s, f = at.s, at.f
    block, width = tokens.shape
    positions, channels = product.shape
    rows = in_whole.shape[2]
    pair = 2 * block
    segment = positions // 8
    chunks = positions // CHUNK

    keep = [
        (mixed, held.at[s]), (out_far, out_whole), (pre_far, pre), (st_far, st_ref),
        (product_far, product), (r_far, r_ref), (i_far, i_ref), (conv_far, conv_ref),
        (ext_far, ext), (in_far, in_whole), (fed_far, fed_other), (normed_far, held),
    ]
    keep = [pltpu.make_async_copy(a, b, local_sems.at[n]) for n, (a, b) in enumerate(keep)]
    for copy in keep[:-1]:
        copy.start()
    at.enter()

    def over_fsdp(src, dst, sems):
        return Spread(
            at, lambda peer: src.at[peer], lambda origin: dst.at[origin], sems.at[0], sems.at[1]
        )

    def over_seq(src, dst, sems):
        return Spread(
            at, lambda peer: src.at[peer], lambda origin: dst.at[origin], sems.at[0], sems.at[1], "seq"
        )

    glu_xy = over_fsdp(glu_grad, glu_heard, glu_xy_sems)
    down_xy = over_fsdp(down_grad, down_heard, down_sems)
    in_xy = over_fsdp(in_grad, in_heard, in_xy_sems)
    out_xy = over_fsdp(out_grad, out_heard, out_sems)
    small_xy = over_fsdp(small, small_heard, small_sems)
    gain_xy = over_fsdp(gain_parts, gain_heard, gain_xy_sems)
    glu_z = over_seq(glu_sum, glu_out, glu_sems)
    in_z = over_seq(in_sum, in_out, in_sems)
    gain_z = over_seq(gain_sum, gain_out, gain_sems)
    mixed_z = LineGather(at, mixed, held, held_send, held_recv, held_send.shape[1])
    fed = LineScatter(
        at, fed_own, fed_other, fed_heard, fed_into,
        (fed_sib_send, fed_sib_recv, fed_send, fed_recv), fed_send.shape[1],
    )
    sums = LineScatter(
        at, own, other, heard, into, (sib_send, sib_recv, line_send, line_recv), line_send.shape[1]
    )
    mixed_z.start()
    glu_xy.start()
    out_sum[...] = jnp.zeros_like(out_sum)
    keep[10].wait()
    for k in range(at.line // 2):
        fed.across(at.line - 1 - k).start()
        fed.across(k).start()

    def columns_of(j):
        return pl.ds(pl.multiple_of(j * 256, 256), 256)

    for n in (0, 1, 2, 3, 4):
        keep[n].wait()

    def mixed_back(chip):
        rows = held[pl.ds(2 * chip, 2), :, :].reshape(pair, width)
        pair_grad[...] = times_transpose(rows, out_whole[...])

        @pl.loop(0, pair // 64)
        def _(n):
            grad = pair_grad[pl.ds(pl.multiple_of(n * 64, 64), 64), :]
            base = pl.multiple_of(chip * pair + n * 64, 64)
            here = pl.ds(base, 64)
            opened, slope = gelu_and_slope(pre[here, :])
            states = st_ref[pl.ds(base + 8, 64), :].astype(LOW).astype(WIDE)
            put(adj, here, (grad * opened).astype(LOW).astype(WIDE))
            both[here, channels:] = (grad * states * slope).astype(LOW)

        there = pl.ds(pl.multiple_of(chip * pair, pair), pair)

        @pl.loop(0, width // 256)
        def _(j):
            part = held[pl.ds(2 * chip, 2), :, columns_of(j)].reshape(pair, 256)
            out_sum[:, columns_of(j)] += outer_sum(product[there, :], part)

    for n in range(at.line - 1, 0, -1):
        fed.push(at.nearest(n))

    def fed_beside(n):
        @pl.when(n == 1)
        def _():
            fed.join()

    mixed_z.distances(mixed_back, fed_beside)
    keep[5].wait()

    @pl.loop(0, chunks)
    def _(n):
        here = pl.ds(pl.multiple_of(n * CHUNK, CHUNK), CHUNK)
        put(factors, here, jnp.exp(r_ref[here, :] * par_ref[7:8, :]))

    def step(j, n, flow, product):
        here = pl.ds(segment - 1 - j, 8, stride=segment)
        factor = factors[n, here, :]
        adjoint = adj[n, here, :] + flow
        adj[n, here, :] = adjoint
        prod[n, here, :] = product
        return factor * adjoint, factor * product

    flow, through = scan_segments(step, segment, lane_tiles(channels))
    flow, through = flow[:, :channels], through[:, :channels]
    carry = jnp.zeros((1, channels), WIDE)
    for k in range(7, -1, -1):
        carries[k : k + 1, :] = carry
        carry = flow[k : k + 1] + through[k : k + 1] * carry
    for n in (6, 7, 8):
        keep[n].wait()
    cg[pl.ds(positions, 8), :] = jnp.zeros((8, channels), WIDE)
    wr_sum[...] = jnp.zeros_like(wr_sum)
    wi_sum[...] = jnp.zeros_like(wi_sum)

    def grads(c, sums):
        base = pl.multiple_of(c * CHUNK, CHUNK)
        rows = pl.ds(base, CHUNK)
        adjoint = get(adj, rows, channels) + get(prod, rows, channels) * carries[pl.ds(base // segment, 1), :]
        before = st_ref[pl.ds(base, CHUNK + 8), :][7 : 7 + CHUNK]
        conv_low = conv_ref[rows, :]
        conv = conv_low.astype(WIDE)
        r = r_ref[rows, :]
        gate = i_ref[rows, :]
        factor = get(factors, rows, channels)
        m = jnp.sqrt(one_minus_exp(-2.0 * (r * par_ref[7:8, :])))
        driven = adjoint * gate
        by_log = adjoint * before * factor - driven * conv * factor * factor / m
        by_r = by_log * par_ref[7:8, :] * r * (1.0 - r)
        by_i = adjoint * m * conv * gate * (1.0 - gate)
        by_r_low = by_r.astype(LOW)
        by_i_low = by_i.astype(LOW)
        conv_grad = (
            driven * m
            + times_transpose(by_r_low, wr_ref[...])
            + times_transpose(by_i_low, wi_ref[...])
        )
        cg[rows, :] = conv_grad
        wr_sum[...] += outer_sum(conv_low, by_r_low)
        wi_sum[...] += outer_sum(conv_low, by_i_low)
        near = ext[pl.ds(base, CHUNK + 8), :]
        rows_of = [conv_grad * near[8 - k : 8 - k + CHUNK] for k in range(4)]
        rows_of += [conv_grad, by_r, by_i, by_log * r]
        return tuple(
            total + jnp.sum(member, axis=0, keepdims=True) for total, member in zip(sums, rows_of)
        )

    zero = jnp.zeros((1, channels), WIDE)
    totals = lax.fori_loop(0, chunks, grads, (zero,) * 8)
    @pl.loop(0, chunks)
    def _(c):
        base = pl.multiple_of(c * CHUNK, CHUNK)
        near = cg[pl.ds(base, CHUNK + 8), :]
        total = jnp.zeros((CHUNK, channels), WIDE)
        for k in range(4):
            total = total + par_ref[k : k + 1, :] * near[k : k + CHUNK]
        both[pl.ds(base, CHUNK), :channels] = total.astype(LOW)

    keep[9].wait()

    def project(chip):
        rows = both[pl.ds(pl.multiple_of(chip * pair, pair), pair), :]

        @pl.loop(0, shards)
        def _(j):
            value = times_transpose(rows, in_whole[j].reshape(width // shards, 2 * channels))
            first = at.c == 0
            own[chip, :, columns_of(j)] = jnp.where(first, value[:block], value[block:]).astype(LOW)
            other[chip, :, columns_of(j)] = jnp.where(first, value[block:], value[:block]).astype(LOW)

        sums.across(chip).start()

    for k in range(at.line // 2):
        project(at.line - 1 - k)
        project(k)
        sums.push(at.line - 1 - k)
        sums.push(k)
    mixed_z.sent()
    keep[11].start()
    local = small.shape[1] - 8
    size = small.shape[2] // 2
    for n in range(channels // size):
        part = slice(n * size, (n + 1) * size)
        wr_sum[part, :size] = wr_sum[part, part]
        wi_sum[part, :size] = wi_sum[part, part]
    for group in range(groups):
        part = slice(group * local, (group + 1) * local)
        small[group, :local, :size] = wr_sum[part, :size]
        small[group, :local, size:] = wi_sum[part, :size]
        for k in range(8):
            small[group, local + k : local + k + 1, :local] = totals[k][:, part]
    small_xy.start()
    keep[11].wait()

    def in_done(j):
        return pltpu.make_async_copy(
            staged.at[lax.rem(j, 2)], in_grad.at[:, j], stage_sems.at[lax.rem(j, 2)]
        )

    @pl.loop(0, shards)
    def _(j):
        @pl.when(j >= 2)
        def _():
            in_done(j - 2).wait()

        part = held[:, :, columns_of(j)].reshape(positions, 256)
        staged[lax.rem(j, 2)] = outer_sum(part, both[...]).astype(LOW).reshape(staged.shape[1:])
        in_done(j).start()

    for j in range(shards - 2, shards):
        in_done(j).wait()
    in_xy.start()
    in_own = pltpu.make_async_copy(in_grad.at[f], in_heard.at[f], local_sems.at[12])
    in_own.start()
    sums.join()
    glu_xy.finish()
    down_xy.start()

    def glu_load(d, origin):
        peer = lax.rem(s + d, shards)
        half = lax.rem(d, 2)
        return pltpu.make_async_copy(
            glu_heard.at[origin, peer], glu_parts.at[half, origin], glu_sems.at[2 + half, origin]
        )

    def glu_load_own(d):
        peer = lax.rem(s + d, shards)
        half = lax.rem(d, 2)
        return pltpu.make_async_copy(
            glu_grad.at[f, peer], glu_parts.at[half, f], glu_sems.at[2 + half, f]
        )

    def glu_loads(d):
        glu_load_own(d).start()
        for hop in range(1, groups):
            glu_load(d, lax.rem(f + hop, groups)).start()

    def add(parts, total, peer):
        @pl.loop(0, total.shape[1] // 16)
        def _(n):
            here = pl.ds(pl.multiple_of(n * 16, 16), 16)
            value = parts[0, here, :].astype(WIDE)
            for origin in range(1, groups):
                value = value + parts[origin, here, :].astype(WIDE)
            total[peer, here, :] = value.astype(total.dtype)

    glu_loads(1)

    @pl.loop(1, shards + 1)
    def _(d):
        @pl.when(d < shards)
        def _():
            glu_loads(d + 1)

        for origin in range(groups):
            glu_load(d, origin).wait()
        add(glu_parts.at[lax.rem(d, 2)], glu_sum, lax.rem(s + d, shards))

        @pl.when(d < shards)
        def _():
            glu_z.copy(d).start()

    glu_own = pltpu.make_async_copy(glu_sum.at[s], glu_out.at[s], local_sems.at[13])
    glu_own.start()
    out_grad[...] = out_sum[...].astype(LOW).reshape(out_grad.shape)
    out_xy.start()
    gain_row[...] = jnp.zeros_like(gain_row)

    def store_result(here, total):
        result[here, :] = (middle[here, :] + total).astype(LOW)

    fed.finish(store_result)

    def back(here, grad):
        values = tokens[here, :].astype(WIDE)
        scale = lax.rsqrt(jnp.mean(values * values, axis=-1, keepdims=True) + EPSILON)
        scaled = grad * gains[0:1, :]
        along = jnp.mean(scaled * values, axis=-1, keepdims=True)
        total = middle_grad[here, :] + scale * scaled - values * (scale * scale * scale * along)
        tokens_grad[here, :] = total.astype(LOW)
        gain_row[0:1, :] += jnp.sum(grad * values * scale, axis=0, keepdims=True)

    sums.finish(back)
    for group in range(groups):
        for shard in range(shards):
            first = (shard * groups + group) * rows
            gain_parts[group, shard, 0:1, :] = gain_row[0:1, first : first + rows]
            gain_parts[group, shard, 1:2, :] = mlp_parts[0:1, first : first + rows]
    gain_xy.start()
    in_own.wait()
    in_xy.finish()

    @pl.loop(1, shards + 1)
    def _(d):
        peer = lax.rem(s + d, shards)
        add(in_heard.at[:, peer], in_sum, peer)

        @pl.when(d < shards)
        def _():
            in_z.copy(d).start()

    last = [
        pltpu.make_async_copy(in_sum.at[s], in_out.at[s], local_sems.at[14]),
        pltpu.make_async_copy(out_grad.at[f], out_heard.at[f], local_sems.at[15]),
        pltpu.make_async_copy(small.at[f], small_heard.at[f], local_sems.at[16]),
    ]
    for copy in last:
        copy.start()
    gain_xy.finish()
    total = gain_parts[f]
    for d in range(1, groups):
        total = total + gain_heard[lax.rem(f + d, groups)]
    gain_sum[...] = total
    gain_z.start()
    gain_own = pltpu.make_async_copy(gain_sum.at[s], gain_out.at[s], local_sems.at[17])
    gain_own.start()
    fed.sent()
    sums.sent()
    for spread in (down_xy, small_xy, out_xy, glu_z, gain_z, in_z):
        spread.finish()
    for copy in (glu_own, gain_own, *last):
        copy.wait()


def back(
    mixed, fed_own, fed_other, middle, middle_grad, tokens, gains, par, wr, wi,
    out_whole, in_whole, normed, product, ext, pre, conv, r, i, st, glu_grad, down_grad, mlp_sums, size,
):
    shards, groups, rows, both = in_whole.shape
    block, width = tokens.shape
    positions, channels = product.shape
    line, pieces, halves = shards // 2, 2, 2
    local = channels // groups
    low = pltpu.VMEM((line, block, width), LOW)
    short = jax.ShapeDtypeStruct((block, width), LOW)
    glu_shape = glu_grad.shape[1:]
    in_shape = (groups, shards, rows, both)
    outs = [
        short, short, jax.ShapeDtypeStruct(glu_shape, LOW), jax.ShapeDtypeStruct(in_shape[1:], LOW),
        jax.ShapeDtypeStruct((groups, local, width), LOW),
        jax.ShapeDtypeStruct((groups, local + 8, 2 * size), WIDE),
        jax.ShapeDtypeStruct((shards, 8, rows), WIDE),
        jax.ShapeDtypeStruct(glu_grad.shape, LOW), jax.ShapeDtypeStruct(down_grad.shape, LOW),
        jax.ShapeDtypeStruct(in_shape, LOW),
    ]
    far = [out_whole, in_whole, normed, product, ext, pre, conv, r, i, st]
    near = [in_whole, out_whole, product, ext, pre, conv, r, i, st]
    return pl.pallas_call(
        back_kernel,
        out_shape=outs,
        in_specs=[HELD, HELD, ANY] + [HELD] * 7 + [ANY] * (len(far) + 2) + [HELD],
        out_specs=[HELD] * 2 + [ANY] * 8,
        scratch_shapes=[pltpu.VMEM((shards, block, width), LOW)]
        + [pltpu.VMEM(member.shape, member.dtype) for member in near]
        + [
            pltpu.VMEM((positions, 2 * channels), LOW),
            pltpu.VMEM((2 * block, channels), WIDE),
            pltpu.VMEM((2, groups, rows, both), LOW),
        ]
        + [pltpu.VMEM((lane_tiles(channels), positions, 128), WIDE)] * 3
        + [pltpu.VMEM((positions + 8, channels), WIDE), pltpu.VMEM((8, channels), WIDE)]
        + [pltpu.VMEM((channels, channels), WIDE)] * 2
        + [
            pltpu.VMEM((channels, width), WIDE),
            pltpu.VMEM((groups, local, width), LOW),
            pltpu.VMEM((groups, local + 8, 2 * size), WIDE),
            pltpu.VMEM((8, width), WIDE),
            pltpu.VMEM((groups, shards, 8, rows), WIDE),
            pltpu.VMEM((groups, shards, 8, rows), WIDE),
            pltpu.VMEM((shards, 8, rows), WIDE),
            pltpu.VMEM((2, groups) + glu_shape[1:], LOW),
            pltpu.VMEM(glu_shape, LOW),
            pltpu.VMEM(in_shape, LOW),
            pltpu.VMEM(in_shape[1:], LOW),
        ]
        + LineScatter.scratch(line, block, width, halves)[1:]
        + [low]
        + LineScatter.scratch(line, block, width, halves)[1:]
        + [
            dma(18), dma(shards, pieces, 3), dma(shards, pieces), dma(2, groups), dma(2, groups), dma(2),
            dma(2, groups), dma(2, groups), dma(2, groups), dma(2, groups),
            dma(4, shards), dma(2, shards), dma(2, shards),
        ],
        compiler_params=pltpu.CompilerParams(
            collective_id=3, has_side_effects=True, vmem_limit_bytes=VMEM_BYTES
        ),
        name="back",
    )(
        mixed, fed_own, fed_other, middle, middle_grad, tokens, gains, par, wr, wi, *far,
        glu_grad, down_grad, mlp_sums,
    )


def mixer_forward_kernel(
    x_ref, wr_ref, wi_ref, par_ref,
    conv_ref, r_ref, i_ref, f_ref, m_ref, st_ref,
    ext, factors, drive, prod,
):
    positions, channels = x_ref.shape
    segment = positions // 8
    chunks = positions // CHUNK
    ext[0:8, :] = jnp.zeros((8, channels), WIDE)
    st_ref[0:8, :] = jnp.zeros((8, channels), WIDE)

    @pl.loop(0, chunks)
    def _(c):
        base = pl.multiple_of(c * CHUNK, CHUNK)
        ext[pl.ds(base + 8, CHUNK), :] = x_ref[pl.ds(base, CHUNK), :].astype(WIDE)

    @pl.loop(0, chunks)
    def _(c):
        base = pl.multiple_of(c * CHUNK, CHUNK)
        rows = pl.ds(base, CHUNK)
        block = ext[pl.ds(base, CHUNK + 8), :]
        conv = jnp.broadcast_to(par_ref[4:5, :], (CHUNK, channels))
        for k in range(4):
            conv = conv + par_ref[k : k + 1, :] * block[8 - k : 8 - k + CHUNK]
        conv_low = conv.astype(LOW)
        conv_ref[rows, :] = conv_low
        r = jax.nn.sigmoid(dot(conv_low, wr_ref[...]) + par_ref[5:6, :])
        gate = jax.nn.sigmoid(dot(conv_low, wi_ref[...]) + par_ref[6:7, :])
        log_decay = r * par_ref[7:8, :]
        m = jnp.sqrt(one_minus_exp(-2.0 * log_decay))
        r_ref[rows, :] = r
        i_ref[rows, :] = gate
        factor = jnp.exp(log_decay)
        f_ref[rows, :] = factor
        m_ref[rows, :] = m
        put(factors, rows, factor)
        put(drive, rows, m * gate * conv_low.astype(WIDE))

    def step(i, n, state, product):
        rows = pl.ds(i, 8, stride=segment)
        factor = factors[n, rows, :]
        state = factor * state + drive[n, rows, :]
        product = factor * product
        drive[n, rows, :] = state
        prod[n, rows, :] = product
        return state, product

    state, product = scan_segments(step, segment, lane_tiles(channels))
    state, product = state[:, :channels], product[:, :channels]
    carry = jnp.zeros((1, channels), WIDE)
    for k in range(8):
        for part in range(segment // CHUNK):
            base = k * segment + part * CHUNK
            rows = slice(base, base + CHUNK)
            st_ref[base + 8 : base + 8 + CHUNK, :] = (
                get(drive, rows, channels) + get(prod, rows, channels) * carry
            )
        carry = state[k : k + 1] + product[k : k + 1] * carry


def mixer_backward_kernel(
    ds_ref, x_ref, conv_ref, r_ref, i_ref, f_ref, m_ref, st_ref, wr_ref, wi_ref, par_ref,
    xg_ref, wrg_ref, wig_ref, sums_ref,
    ext, factors, adj, prod, cg, carries, wr_sum, wi_sum,
):
    positions, channels = x_ref.shape
    segment = positions // 8
    chunks = positions // CHUNK
    ext[0:8, :] = jnp.zeros((8, channels), WIDE)
    cg[pl.ds(positions, 8), :] = jnp.zeros((8, channels), WIDE)
    wr_sum[...] = jnp.zeros_like(wr_sum)
    wi_sum[...] = jnp.zeros_like(wi_sum)

    @pl.loop(0, chunks)
    def _(c):
        base = pl.multiple_of(c * CHUNK, CHUNK)
        ext[pl.ds(base + 8, CHUNK), :] = x_ref[pl.ds(base, CHUNK), :].astype(WIDE)
        put(adj, pl.ds(base, CHUNK), ds_ref[pl.ds(base, CHUNK), :].astype(WIDE))
        put(factors, pl.ds(base, CHUNK), f_ref[pl.ds(base, CHUNK), :])

    def step(j, n, flow, product):
        rows = pl.ds(segment - 1 - j, 8, stride=segment)
        factor = factors[n, rows, :]
        adjoint = adj[n, rows, :] + flow
        adj[n, rows, :] = adjoint
        prod[n, rows, :] = product
        return factor * adjoint, factor * product

    flow, product = scan_segments(step, segment, lane_tiles(channels))
    flow, product = flow[:, :channels], product[:, :channels]
    carry = jnp.zeros((1, channels), WIDE)
    for k in range(7, -1, -1):
        carries[k : k + 1, :] = carry
        carry = flow[k : k + 1] + product[k : k + 1] * carry

    def grads(c, sums):
        base = pl.multiple_of(c * CHUNK, CHUNK)
        rows = pl.ds(base, CHUNK)
        adjoint = get(adj, rows, channels) + get(prod, rows, channels) * carries[pl.ds(base // segment, 1), :]
        before = st_ref[pl.ds(base, CHUNK + 8), :][7 : 7 + CHUNK]
        conv_low = conv_ref[rows, :]
        conv = conv_low.astype(WIDE)
        r = r_ref[rows, :]
        gate = i_ref[rows, :]
        factor = f_ref[rows, :]
        m = m_ref[rows, :]
        driven = adjoint * gate
        by_log = adjoint * before * factor - driven * conv * factor * factor / m
        by_r = by_log * par_ref[7:8, :] * r * (1.0 - r)
        by_i = adjoint * m * conv * gate * (1.0 - gate)
        by_r_low = by_r.astype(LOW)
        by_i_low = by_i.astype(LOW)
        conv_grad = (
            driven * m
            + times_transpose(by_r_low, wr_ref[...])
            + times_transpose(by_i_low, wi_ref[...])
        )
        cg[rows, :] = conv_grad
        wr_sum[...] += outer_sum(conv_low, by_r_low)
        wi_sum[...] += outer_sum(conv_low, by_i_low)
        block = ext[pl.ds(base, CHUNK + 8), :]
        rows_of = [conv_grad * block[8 - k : 8 - k + CHUNK] for k in range(4)]
        rows_of += [conv_grad, by_r, by_i, by_log * r]
        return tuple(
            total + jnp.sum(member, axis=0, keepdims=True) for total, member in zip(sums, rows_of)
        )

    zero = jnp.zeros((1, channels), WIDE)
    sums = lax.fori_loop(0, chunks, grads, (zero,) * 8)
    for k in range(8):
        sums_ref[k : k + 1, :] = sums[k]
    size = wrg_ref.shape[1]
    for n in range(channels // size):
        block = slice(n * size, (n + 1) * size)
        wrg_ref[block, :] = wr_sum[block, block]
        wig_ref[block, :] = wi_sum[block, block]

    @pl.loop(0, chunks)
    def _(c):
        base = pl.multiple_of(c * CHUNK, CHUNK)
        block = cg[pl.ds(base, CHUNK + 8), :]
        total = jnp.zeros((CHUNK, channels), WIDE)
        for k in range(4):
            total = total + par_ref[k : k + 1, :] * block[k : k + CHUNK]
        xg_ref[pl.ds(base, CHUNK), :] = total.astype(LOW)


def mixer_forward(x, wr, wi, par):
    positions, channels = x.shape
    wide = jax.ShapeDtypeStruct((positions, channels), WIDE)
    return pl.pallas_call(
        mixer_forward_kernel,
        out_shape=(
            jax.ShapeDtypeStruct((positions, channels), LOW), wide, wide, wide, wide,
            jax.ShapeDtypeStruct((positions + 8, channels), WIDE),
        ),
        scratch_shapes=[pltpu.VMEM((positions + 8, channels), WIDE)]
        + [pltpu.VMEM((lane_tiles(channels), positions, 128), WIDE)] * 3,
        compiler_params=pltpu.CompilerParams(vmem_limit_bytes=48 * 2**20),
        name="mixer_forward",
    )(x, wr, wi, par)


def mixer_backward(ds, x, saved, wr, wi, par, size):
    positions, channels = x.shape
    square = jax.ShapeDtypeStruct((channels, size), WIDE)
    return pl.pallas_call(
        mixer_backward_kernel,
        out_shape=(
            jax.ShapeDtypeStruct((positions, channels), LOW), square, square,
            jax.ShapeDtypeStruct((8, channels), WIDE),
        ),
        scratch_shapes=[pltpu.VMEM((positions + 8, channels), WIDE)]
        + [pltpu.VMEM((lane_tiles(channels), positions, 128), WIDE)] * 3
        + [pltpu.VMEM((positions + 8, channels), WIDE), pltpu.VMEM((8, channels), WIDE)]
        + [pltpu.VMEM((channels, channels), WIDE)] * 2,
        compiler_params=pltpu.CompilerParams(vmem_limit_bytes=48 * 2**20),
        name="mixer_backward",
    )(ds, x, *saved, wr, wi, par)


def gather_columns(weights):
    shards = lax.axis_size("seq")
    rows = weights[0].shape[0]
    widths = [member.shape[1] // shards for member in weights]
    stacked = jnp.concatenate(
        [member.reshape(rows, shards, width) for member, width in zip(weights, widths)], axis=2
    )
    mine = lax.all_to_all(stacked.transpose(1, 0, 2), "seq", split_axis=0, concat_axis=0)
    whole = lax.all_gather(mine, "fsdp", axis=1)
    return whole.reshape(-1, sum(widths))


def scatter_columns(grad, widths, rows):
    shards, groups = lax.axis_size("seq"), lax.axis_size("fsdp")
    parts = grad.astype(LOW).reshape(shards, groups, rows, sum(widths)).transpose(1, 0, 2, 3)
    mine = lax.psum_scatter(parts, "fsdp", scatter_dimension=0, tiled=False)
    swapped = lax.all_to_all(mine, "seq", split_axis=0, concat_axis=0).astype(WIDE)
    outs, first = [], 0
    for width in widths:
        outs.append(swapped[:, :, first : first + width].transpose(1, 0, 2).reshape(rows, -1))
        first += width
    return outs


def block_diagonal(weight, blocks):
    size = weight.shape[1]
    shaped = weight.reshape(blocks, size, size)
    full = jnp.zeros((blocks, size, blocks, size), weight.dtype)
    for n in range(blocks):
        full = full.at[n, :, n, :].set(shaped[n])
    return full.reshape(blocks * size, blocks * size)


def general(
    tokens, cotangent, mix_gain, lru_in_weight, gelu_in_weight, out_weight, conv_weight, conv_bias,
    recurrence_weight, recurrence_bias, input_gate_weight, input_gate_bias, decay_param, mlp_gain,
    gate_weight, up_weight, down_weight,
):
    positions, width = tokens.shape[1:]
    rows = lru_in_weight.shape[0]
    shards = lax.axis_size("seq")
    channels = lru_in_weight.shape[1] // shards
    hidden_width = gate_weight.shape[1] // shards
    size = recurrence_weight.shape[1]

    gains = lax.all_gather(
        jnp.stack([mix_gain, mlp_gain], axis=1), ("seq", "fsdp"), axis=0, tiled=True
    ).astype(WIDE)
    mix_scale, mlp_scale = gains[:, 0], gains[:, 1]
    in_whole = gather_columns([lru_in_weight, gelu_in_weight])
    lru_params = lax.all_gather(
        jnp.concatenate(
            [
                recurrence_weight, input_gate_weight, conv_weight, conv_bias[:, None],
                recurrence_bias[:, None], input_gate_bias[:, None], decay_param[:, None],
            ],
            axis=1,
        ),
        "fsdp", axis=0, tiled=True,
    )
    out_whole = lax.all_gather(out_weight, "fsdp", axis=0, tiled=True)
    glu_whole = gather_columns([gate_weight, up_weight])
    down_whole = lax.all_gather(down_weight, "fsdp", axis=0, tiled=True)

    wr = block_diagonal(lru_params[:, :size], channels // size)
    wi = block_diagonal(lru_params[:, size : 2 * size], channels // size)
    vectors = lru_params[:, 2 * size :].astype(WIDE).T
    decay = vectors[7]
    par = jnp.concatenate([vectors[:7], -RATE_SCALE * jax.nn.softplus(-decay)[None]], axis=0)

    resid_in = tokens.reshape(positions, width).astype(WIDE)
    grad_low = cotangent.reshape(positions, width)
    normed_low = rms_scale(resid_in, mix_scale).astype(LOW)
    normed_all = lax.all_gather(normed_low, "seq", axis=0, tiled=True)
    grad_all = lax.all_gather(grad_low, "seq", axis=0, tiled=True)
    branch_x = dot(normed_all, in_whole[:, :channels]).astype(LOW)
    branch_pre = dot(normed_all, in_whole[:, channels:])
    branch_y = jax.nn.gelu(branch_pre)

    saved = mixer_forward(branch_x, wr, wi, par)
    states_f = saved[5][8:].astype(LOW).astype(WIDE)
    product = (states_f * branch_y).astype(LOW)
    mixed = lax.psum_scatter(
        dot(product, out_whole).astype(LOW), "seq", scatter_dimension=0, tiled=True
    )
    middle = resid_in + mixed.astype(WIDE)
    normed2_low = rms_scale(middle, mlp_scale).astype(LOW)
    normed2_all = lax.all_gather(normed2_low, "seq", axis=0, tiled=True)
    gate_whole, up_whole = glu_whole[:, :hidden_width], glu_whole[:, hidden_width:]
    gate_val = dot(normed2_all, gate_whole)
    up_val = dot(normed2_all, up_whole)
    hidden = (jax.nn.gelu(gate_val) * up_val).astype(LOW)
    fed = lax.psum_scatter(
        dot(hidden, down_whole).astype(LOW), "seq", scatter_dimension=0, tiled=True
    )
    result = middle + fed.astype(WIDE)

    hidden_grad = times_transpose(grad_all, down_whole)
    unused, pull_glu = jax.vjp(lambda first, second: jax.nn.gelu(first) * second, gate_val, up_val)
    gate_grad, up_grad = pull_glu(hidden_grad)
    gate_low, up_low = gate_grad.astype(LOW), up_grad.astype(LOW)
    normed2_grad = lax.psum_scatter(
        (times_transpose(gate_low, gate_whole) + times_transpose(up_low, up_whole)).astype(LOW),
        "seq", scatter_dimension=0, tiled=True,
    ).astype(WIDE)
    unused, pull_norm2 = jax.vjp(rms_scale, middle, mlp_scale)
    middle_part, mlp_gain_grad = pull_norm2(normed2_grad)
    middle_grad = grad_low.astype(WIDE) + middle_part
    mixed_all = lax.all_gather(middle_grad.astype(LOW), "seq", axis=0, tiled=True)

    product_grad = times_transpose(mixed_all, out_whole)
    states_grad = (product_grad * branch_y).astype(LOW)
    unused, pull_gelu = jax.vjp(jax.nn.gelu, branch_pre)
    (pre_grad,) = pull_gelu(product_grad * states_f)
    pre_low = pre_grad.astype(LOW)
    x_low, wr_grad, wi_grad, sums = mixer_backward(states_grad, branch_x, saved, wr, wi, par, size)

    normed_grad = lax.psum_scatter(
        (
            times_transpose(x_low, in_whole[:, :channels])
            + times_transpose(pre_low, in_whole[:, channels:])
        ).astype(LOW),
        "seq", scatter_dimension=0, tiled=True,
    ).astype(WIDE)
    unused, pull_norm = jax.vjp(rms_scale, resid_in, mix_scale)
    input_part, mix_gain_grad = pull_norm(normed_grad)
    input_grad = middle_grad + input_part

    down_grad = lax.psum_scatter(
        outer_sum(hidden, grad_all).astype(LOW), "fsdp", scatter_dimension=0, tiled=True
    ).astype(WIDE)
    glu_grad = jnp.concatenate(
        [outer_sum(normed2_all, gate_low), outer_sum(normed2_all, up_low)], axis=1
    )
    gate_w_grad, up_w_grad = scatter_columns(glu_grad, [hidden_width] * 2, rows)
    out_grad = lax.psum_scatter(
        outer_sum(product, mixed_all).astype(LOW), "fsdp", scatter_dimension=0, tiled=True
    ).astype(WIDE)
    in_grad = jnp.concatenate(
        [outer_sum(normed_all, x_low), outer_sum(normed_all, pre_low)], axis=1
    )
    lru_in_grad, gelu_in_grad = scatter_columns(in_grad, [channels] * 2, rows)
    small = jnp.concatenate(
        [
            wr_grad, wi_grad, sums[:7].T,
            (sums[7] * RATE_SCALE * jax.nn.sigmoid(-decay))[:, None],
        ],
        axis=1,
    )
    small = lax.psum_scatter(
        small.reshape(lax.axis_size("fsdp"), -1, small.shape[1]),
        "fsdp", scatter_dimension=0, tiled=False,
    )
    gain_parts = jnp.stack([mix_gain_grad, mlp_gain_grad]).reshape(2, -1, rows).transpose(1, 0, 2)
    gain_grads = lax.psum_scatter(
        gain_parts, ("seq", "fsdp"), scatter_dimension=0, tiled=False
    )
    first = 2 * size
    return (
        result.astype(LOW).reshape(tokens.shape),
        input_grad.astype(LOW).reshape(tokens.shape),
        gain_grads[0],
        lru_in_grad,
        gelu_in_grad,
        out_grad,
        small[:, first : first + 4],
        small[:, first + 4],
        small[:, :size],
        small[:, first + 5],
        small[:, size : 2 * size],
        small[:, first + 6],
        small[:, first + 7],
        gain_grads[1],
        gate_w_grad,
        up_w_grad,
        down_grad,
    )


def aligned(
    tokens, cotangent, mix_gain, lru_in_weight, gelu_in_weight, out_weight, conv_weight, conv_bias,
    recurrence_weight, recurrence_bias, input_gate_weight, input_gate_bias, decay_param, mlp_gain,
    gate_weight, up_weight, down_weight,
):
    positions, width = tokens.shape[1:]
    rows = lru_in_weight.shape[0]
    shards = lax.axis_size("seq")
    channels = lru_in_weight.shape[1] // shards
    hidden_width = gate_weight.shape[1] // shards
    size = recurrence_weight.shape[1]

    groups = lax.axis_size("fsdp")
    resid_in = tokens.reshape(positions, width).astype(WIDE)
    grad_low = cotangent.reshape(positions, width)

    def by_column(first, second):
        parts = [member.reshape(rows, shards, -1) for member in (first, second)]
        return jnp.concatenate(parts, axis=2).transpose(1, 0, 2)

    own_decay = decay_param.astype(WIDE)
    vecs = jnp.concatenate(
        [
            conv_weight.astype(WIDE).T,
            jnp.stack([conv_bias, recurrence_bias, input_gate_bias]).astype(WIDE),
            -RATE_SCALE * jax.nn.softplus(-own_decay)[None],
        ],
        axis=0,
    )
    gain_shard = jnp.pad(jnp.stack([mix_gain, mlp_gain]).astype(WIDE), ((0, 6), (0, 0)))
    tokens_low = tokens.reshape(positions, width)
    (
        normed, in_whole, ext, branch_pre, conv_low, recur_gate, input_gate, states, product, par, wr, wi,
        gains, glu_mine, out_whole, down_whole,
    ) = mix_in(
        tokens_low, by_column(lru_in_weight, gelu_in_weight), by_column(gate_weight, up_weight),
        out_weight, down_weight, jnp.concatenate([recurrence_weight, input_gate_weight], axis=1),
        vecs, gain_shard, groups,
    )
    out_whole = out_whole.reshape(-1, width)
    middle, middle_grad, mixed_low, mlp_sums, fed_own, fed_other, glu_grad, down_grad = feed(
        product, out_whole, glu_mine, down_whole.reshape(-1, width), grad_low, tokens_low, gains, groups
    )
    down_grad = down_grad.reshape(groups, -1, width)
    (
        result, tokens_grad, glu_out, in_out, out_heard, small_heard, gain_out, unused, down_heard, unused,
    ) = back(
        mixed_low, fed_own, fed_other, middle, middle_grad, tokens_low, gains, par, wr, wi,
        out_whole, in_whole, normed, product, ext, branch_pre, conv_low, recur_gate, input_gate, states,
        glu_grad, down_grad, mlp_sums, size,
    )
    small_rows = recurrence_weight.shape[0]
    mine = jnp.arange(groups)[:, None, None] == lax.axis_index("fsdp")
    down_heard = jnp.where(mine, down_grad, down_heard)

    def rows_of(parts, first, size):
        return parts[:, :, first : first + size].astype(WIDE).transpose(1, 0, 2).reshape(rows, -1)

    small = jnp.sum(small_heard, axis=0)
    vector_sums = small[small_rows:, :small_rows]
    gain_grads = jnp.sum(gain_out, axis=0)
    return (
        result.reshape(tokens.shape),
        tokens_grad.reshape(tokens.shape),
        gain_grads[0],
        rows_of(in_out, 0, channels),
        rows_of(in_out, channels, channels),
        jnp.sum(out_heard.astype(WIDE), axis=0),
        vector_sums[:4].T,
        vector_sums[4],
        small[:small_rows, :size],
        vector_sums[5],
        small[:small_rows, size : 2 * size],
        vector_sums[6],
        vector_sums[7] * RATE_SCALE * jax.nn.sigmoid(-own_decay),
        gain_grads[1],
        rows_of(glu_out, 0, hidden_width),
        rows_of(glu_out, hidden_width, hidden_width),
        jnp.sum(down_heard.astype(WIDE), axis=0),
    )


def solution(mesh):
    shards, groups = mesh.shape["seq"], mesh.shape["fsdp"]

    def local(*arrays):
        rows, small_rows = arrays[3].shape[0], arrays[5].shape[0]
        simple = shards % 2 == 0 and rows % 16 == 0 and small_rows % 16 == 0
        simple = simple and arrays[0].shape[1] * shards % (8 * CHUNK) == 0
        return (aligned if simple else general)(*arrays)

    tokens = P("fsdp", "seq", None)
    vector = P(("seq", "fsdp"))
    matrix = P(("seq", "fsdp"), None)
    ranks = (1, 2, 2, 2, 2, 1, 2, 1, 2, 1, 1, 1, 2, 2, 2)
    specs = (tokens, tokens) + tuple(vector if rank == 1 else matrix for rank in ranks)
    return jax.shard_map(local, mesh=mesh, in_specs=specs, out_specs=specs, check_vma=False)
```

```python
import functools

import jax
import jax.numpy as jnp
from jax import lax
from jax.experimental import pallas as pl
from jax.experimental.pallas import tpu as pltpu
from jax.sharding import PartitionSpec as P

EPSILON = 1e-06
RATE_SCALE = 8.0
CHUNK = 128
LOW = jnp.bfloat16
WIDE = jnp.float32


def rms_scale(values, gain):
    scale = lax.rsqrt(jnp.mean(values * values, axis=-1, keepdims=True) + EPSILON)
    return values * scale * gain


def dot(left, right):
    return jnp.dot(left, right, preferred_element_type=WIDE)


def outer_sum(left, right):
    return lax.dot_general(left, right, (((0,), (0,)), ((), ())), preferred_element_type=WIDE)


def times_transpose(left, right):
    return lax.dot_general(left, right, (((1,), (1,)), ((), ())), preferred_element_type=WIDE)


def one_minus_exp(value):
    series = jnp.full_like(value, 1.0 / 40320.0)
    for bottom in (5040.0, 720.0, 120.0, 24.0, 6.0, 2.0, 1.0):
        series = 1.0 / bottom - value * series
    return jnp.where(value < 0.4, value * series, 1.0 - jnp.exp(-value))


def sigmoid(value):
    return 0.5 * jnp.tanh(0.5 * value) + 0.5


def lane_tiles(channels):
    return -(-channels // 128)


def put(tiles, rows, value):
    channels = value.shape[1]
    for n in range(lane_tiles(channels)):
        size = min(128, channels - n * 128)
        tiles[n, rows, 0:size] = value[:, n * 128 : n * 128 + size]


def get(tiles, rows, channels):
    return jnp.concatenate(
        [
            tiles[n, rows, 0 : min(128, channels - n * 128)]
            for n in range(lane_tiles(channels))
        ],
        axis=1,
    )


def scan_segments(step, count, tiles):
    def body(i, carried):
        return tuple(step(i, n, *carried[n]) for n in range(tiles))

    start = (jnp.zeros((8, 128), WIDE), jnp.ones((8, 128), WIDE))
    ends = lax.fori_loop(0, count, body, (start,) * tiles, unroll=4)
    return [jnp.concatenate([end[which] for end in ends], axis=1) for which in (0, 1)]


MESH = pl.DeviceIdType.MESH
VMEM_BYTES = 61 * 2**20
ANY = pl.BlockSpec(memory_space=pl.ANY)
HELD = pl.BlockSpec(memory_space=pltpu.VMEM)
ROOT = 0.7978845608028654
CUBE = 0.044715


def dma(*shape):
    return pltpu.SemaphoreType.DMA(shape)


def remote(src, dst, send, recv, axis, index):
    return pltpu.make_async_remote_copy(
        src_ref=src, dst_ref=dst, send_sem=send, recv_sem=recv,
        device_id={axis: index}, device_id_type=MESH,
    )


def gelu(value):
    return 0.5 * value * (1.0 + jnp.tanh(ROOT * (value + CUBE * value * value * value)))


def gelu_and_slope(value):
    square = value * value
    bent = jnp.tanh(ROOT * (value + CUBE * square * value))
    half = 0.5 * (1.0 + bent)
    slope = half + 0.5 * value * (1.0 - bent * bent) * (ROOT * (1.0 + 3.0 * CUBE * square))
    return value * half, slope


class Place:
    def __init__(self, shards, groups):
        self.shards, self.groups, self.line = shards, groups, shards // 2
        self.s, self.f = lax.axis_index("seq"), lax.axis_index("fsdp")
        self.z, self.c = self.s // 2, lax.rem(self.s, 2)
        self.sibling = 2 * self.z + 1 - self.c

    def nearest(self, n):
        chip = 0
        for z in range(self.line):
            for place, other in enumerate(sorted(range(self.line), key=lambda y: abs(y - z))):
                chip = jnp.where((self.z == z) & (n == place), other, chip)
        return chip

    def enter(self, seq=True, fsdp=True):
        barrier = pltpu.get_barrier_semaphore()
        met = 0
        for axis, mine, count, wanted in (
            ("seq", self.s, self.shards, seq), ("fsdp", self.f, self.groups, fsdp),
        ):
            for d in range(1, count if wanted else 1):
                pl.semaphore_signal(
                    barrier, inc=1, device_id={axis: lax.rem(mine + d, count)}, device_id_type=MESH
                )
                met += 1
        pl.semaphore_wait(barrier, met)


class Spread:
    def __init__(self, at, src, dst, send, recv, axis="fsdp"):
        self.at, self.src, self.dst, self.send, self.recv, self.axis = at, src, dst, send, recv, axis
        self.mine, self.count = (at.f, at.groups) if axis == "fsdp" else (at.s, at.shards)

    def copy(self, d):
        peer = lax.rem(self.mine + d, self.count)
        return remote(
            self.src(peer), self.dst(self.mine), self.send.at[d], self.recv.at[d], self.axis, peer
        )

    def start(self):
        for d in range(1, self.count):
            self.copy(d).start()

    def source(self, d):
        return lax.rem(self.mine + self.count - d, self.count)

    def arrive(self, d):
        origin = self.source(d)
        remote(
            self.src(origin), self.dst(origin), self.send.at[d], self.recv.at[d], self.axis, origin
        ).wait_recv()

    def sent(self):
        for d in range(1, self.count):
            self.copy(d).wait_send()

    def finish(self):
        for d in range(1, self.count):
            self.arrive(d)
        self.sent()


class LineGather:
    def __init__(self, at, src, buf, send, recv, pieces):
        self.at, self.src, self.buf, self.send, self.recv, self.pieces = at, src, buf, send, recv, pieces
        self.rows = buf.shape[1] // pieces

    def copy(self, slot, piece, kind, first=False):
        at = self.at
        rows = pl.ds(piece * self.rows, self.rows)
        there = self.buf.at[slot, rows]
        peer = (at.sibling, at.s + 2, at.s - 2)[kind]
        return remote(
            self.src.at[rows] if first else there, there,
            self.send.at[slot, piece, kind], self.recv.at[slot, piece], "seq", peer,
        )

    def start(self):
        at = self.at
        for piece in range(self.pieces):
            @pl.when(at.z + 1 < at.line)
            def _():
                self.copy(at.s, piece, 1, True).start()

            @pl.when(at.z > 0)
            def _():
                self.copy(at.s, piece, 2, True).start()

            self.copy(at.s, piece, 0, True).start()

    def arrive(self, chip, piece):
        at = self.at
        slot = 2 * chip + at.c
        self.copy(slot, piece, 0).wait_recv()

        @pl.when((chip < at.z) & (at.z + 1 < at.line))
        def _():
            self.copy(slot, piece, 1).start()

        @pl.when((chip > at.z) & (at.z > 0))
        def _():
            self.copy(slot, piece, 2).start()

        self.copy(slot, piece, 0).start()

    def settle(self, chip):
        for piece in range(self.pieces):
            self.copy(2 * chip + 1 - self.at.c, piece, 0).wait_recv()

    def pass_on(self, d):
        at = self.at
        for piece in range(self.pieces):
            for chip, known in ((at.z - d, at.z - d >= 0), (at.z + d, at.z + d < at.line)):
                @pl.when(known)
                def _():
                    self.arrive(chip, piece)

    def distances(self, body, beside=None):
        at = self.at

        @pl.loop(0, at.line)
        def _(n):
            @pl.when(n > 0)
            def _():
                self.pass_on(n)
                if beside is not None:
                    beside(n)

            chip = at.nearest(n)
            self.settle(chip)
            body(chip)

    def sent(self):
        at = self.at
        for chip in range(at.line):
            slot = 2 * chip + at.c
            for piece in range(self.pieces):
                self.copy(slot, piece, 0).wait_send()

                @pl.when((chip <= at.z) & (at.z + 1 < at.line))
                def _():
                    self.copy(slot, piece, 1).wait_send()

                @pl.when((chip >= at.z) & (at.z > 0))
                def _():
                    self.copy(slot, piece, 2).wait_send()


class LineScatter:
    def __init__(self, at, own, other, heard, into, sems, pieces):
        self.at, self.own, self.other, self.heard, self.into = at, own, other, heard, into
        self.sib_send, self.sib_recv, self.send, self.recv = sems
        self.pieces = pieces
        self.rows = own.shape[1] // pieces

    @staticmethod
    def scratch(line, rows, width, pieces):
        low = pltpu.VMEM((line, rows, width), LOW)
        return [
            pltpu.VMEM((line, rows, width), WIDE), low, low, low,
            dma(line), dma(line), dma(line, pieces), dma(line, pieces),
        ]

    def across(self, chip):
        return remote(
            self.other.at[chip], self.heard.at[chip], self.sib_send.at[chip],
            self.sib_recv.at[chip], "seq", self.at.sibling,
        )

    def whole_way(self, chip, start):
        if self.at.line < 4:
            return False
        return jnp.abs(chip - start) == self.at.line - 1

    def joined(self, chip):
        at = self.at
        if at.line < 4:
            return False
        return ((at.z == 1) & (chip == at.line - 1)) | ((at.z == at.line - 2) & (chip == 0))

    def along(self, chip, piece):
        at = self.at
        rows = pl.ds(pl.multiple_of(piece * self.rows, self.rows), self.rows)
        target, slot = chip, at.z
        if at.line >= 4:
            stop = jnp.where(chip > at.z, at.z + 1, at.z - 1)
            target = jnp.where(self.whole_way(chip, at.z), stop, chip)
            slot = jnp.where(self.whole_way(chip, at.z), stop, at.z)
        return remote(
            self.other.at[chip, rows], self.into.at[slot, rows], self.send.at[chip, piece],
            self.recv.at[slot, piece], "seq", 2 * target + at.c,
        )

    def landed(self, slot, piece):
        rows = pl.ds(pl.multiple_of(piece * self.rows, self.rows), self.rows)
        there = self.into.at[slot, rows]
        remote(
            there, there, self.recv.at[slot, piece], self.recv.at[slot, piece], "seq", self.at.sibling
        ).wait_recv()

    def add(self, chip, piece, extras, store):
        @pl.loop(0, self.rows // 16)
        def _(block):
            rows = pl.ds(pl.multiple_of(piece * self.rows + block * 16, 16), 16)
            total = self.own[chip, rows, :].astype(WIDE) + self.heard[chip, rows, :].astype(WIDE)
            for known, slot in extras:
                here = self.into[slot, rows, :].astype(WIDE)
                total = total + (here if known is True else jnp.where(known, here, 0.0))
            store(rows, total)

    def store_out(self, chip):
        def store(rows, total):
            self.other[chip, rows, :] = total.astype(LOW)

        return store

    def goes(self, chip):
        goes = chip != self.at.z
        return goes & jnp.logical_not(self.joined(chip)) if self.at.line >= 4 else goes

    def prepare(self, chip):
        @pl.when(self.goes(chip))
        def _():
            self.across(chip).wait()

            @pl.loop(0, self.pieces)
            def _(piece):
                self.add(chip, piece, [], self.store_out(chip))

    def launch(self, chip):
        @pl.when(self.goes(chip))
        def _():
            @pl.loop(0, self.pieces)
            def _(piece):
                self.along(chip, piece).start()

    def push(self, chip):
        @pl.when(self.goes(chip))
        def _():
            self.across(chip).wait()

            @pl.loop(0, self.pieces)
            def _(piece):
                self.add(chip, piece, [], self.store_out(chip))
                self.along(chip, piece).start()

    def join(self):
        at = self.at
        if at.line < 4:
            return

        @pl.when((at.z == 1) | (at.z == at.line - 2))
        def _():
            chip = jnp.where(at.z == 1, at.line - 1, 0)
            self.across(chip).wait()

            @pl.loop(0, self.pieces)
            def _(piece):
                self.landed(at.z, piece)
                self.add(chip, piece, [(True, at.z)], self.store_out(chip))
                self.along(chip, piece).start()

    def finish(self, store):
        at = self.at
        self.across(at.z).wait_recv()

        def known(chip):
            heard = chip != at.z
            return heard & jnp.logical_not(self.whole_way(chip, at.z)) if at.line >= 4 else heard

        @pl.loop(0, self.pieces)
        def _(piece):
            for chip in range(at.line):
                @pl.when(known(chip))
                def _():
                    self.landed(chip, piece)

            self.add(at.z, piece, [(known(chip), chip) for chip in range(at.line)], store)

    def sent(self):
        at = self.at
        self.across(at.z).wait_send()
        for chip in range(at.line):
            @pl.when(chip != at.z)
            def _():
                @pl.loop(0, self.pieces)
                def _(piece):
                    self.along(chip, piece).wait_send()


def normalise(source, gain, store, rows):
    @pl.loop(0, rows // 16)
    def _(block):
        here = pl.ds(pl.multiple_of(block * 16, 16), 16)
        values = source(here)
        scale = lax.rsqrt(jnp.mean(values * values, axis=-1, keepdims=True) + EPSILON)
        store(here, (values * scale * gain).astype(LOW))


def mixer_rows(positions):
    return [pl.ds(pl.multiple_of(n, CHUNK), CHUNK) for n in range(0, positions, CHUNK)]


def mix_in_kernel(
    tokens, in_shard, glu_shard, out_shard, down_shard, small, vecs, gain_shard,
    normed_far, in_far, ext_far, pre_far, conv_far, r_far, i_far, st_far,
    product_far, par_ref, wr_ref, wi_ref, gains, glu_mine, out_whole, down_whole,
    normed, in_whole, ext, pre_ref, conv_ref, r_ref, i_ref, st_ref, product_ref,
    held, small_all, vecs_all, gain_all, factors, drive, prod,
    local_sems, tok_send, tok_recv, in_sems, in_xy_send, in_xy_recv, glu_sems, xy_sems, gain_sems, leave_sems,
):
    groups, shards = in_whole.shape[1], in_whole.shape[0]
    at = Place(shards, groups)
    s, f = at.s, at.f
    positions, channels = pre_ref.shape
    width = tokens.shape[1]
    rows = in_shard.shape[1]
    segment = positions // 8
    chunks = positions // CHUNK

    leaving = [
        (normed, normed_far), (in_whole, in_far), (ext, ext_far), (pre_ref, pre_far), (conv_ref, conv_far),
        (r_ref, r_far), (i_ref, i_far), (st_ref, st_far), (product_ref, product_far),
    ]
    leaving = [pltpu.make_async_copy(a, b, leave_sems.at[n]) for n, (a, b) in enumerate(leaving)]
    keep = [
        (tokens, held.at[s]), (in_shard.at[s], in_whole.at[s, f]), (glu_shard.at[s], glu_mine.at[s]),
        (out_shard, out_whole.at[f]), (down_shard, down_whole.at[f]), (small, small_all.at[f]),
        (vecs, vecs_all.at[f]), (gain_shard, gain_all.at[s, f]),
    ]
    keep = [pltpu.make_async_copy(a, b, local_sems.at[n]) for n, (a, b) in enumerate(keep)]
    for copy in keep:
        copy.start()
    at.enter()

    def over_fsdp(src, dst, n):
        return Spread(at, lambda peer: src, lambda origin: dst.at[origin], xy_sems.at[n, 0], xy_sems.at[n, 1])

    gain_xy = Spread(
        at, lambda peer: gain_shard, lambda origin: gain_all.at[s, origin],
        xy_sems.at[0, 0], xy_sems.at[0, 1],
    )
    small_xy = over_fsdp(small, small_all, 1)
    vecs_xy = over_fsdp(vecs, vecs_all, 2)
    out_xy = over_fsdp(out_shard, out_whole, 3)
    down_xy = over_fsdp(down_shard, down_whole, 4)
    in_z = Spread(
        at, lambda peer: in_shard.at[peer], lambda origin: in_whole.at[origin, f],
        in_sems.at[0], in_sems.at[1], "seq",
    )
    glu_z = Spread(
        at, lambda peer: glu_shard.at[peer], lambda origin: glu_mine.at[origin],
        glu_sems.at[0], glu_sems.at[1], "seq",
    )
    gain_z = Spread(
        at, lambda peer: gain_all.at[s], lambda origin: gain_all.at[origin],
        gain_sems.at[0], gain_sems.at[1], "seq",
    )

    def in_xy(index):
        return Spread(
            at, lambda peer: in_whole.at[index, f], lambda origin: in_whole.at[index, origin],
            in_xy_send.at[index], in_xy_recv.at[index],
        )

    gather = LineGather(at, tokens, held, tok_send, tok_recv, tok_send.shape[1])
    gain_xy.start()
    in_z.start()
    keep[1].wait()
    in_xy(s).start()
    gather.start()
    vecs_xy.start()
    small_xy.start()
    keep[7].wait()
    gain_xy.finish()
    gain_z.start()
    for d in range(1, shards):
        in_z.arrive(d)
        in_xy(in_z.source(d)).start()
    out_xy.start()
    glu_z.start()
    down_xy.start()
    gain_z.finish()
    for origin in range(shards):
        for other in range(groups):
            first = (origin * groups + other) * rows
            gains[:, first : first + rows] = gain_all[origin, other]
    keep[0].wait()

    def take(chip):
        for core in range(2):
            slot = 2 * chip + core

            def store(here, value):
                normed[slot, here, :] = value

            normalise(
                lambda here: held[slot, here, :].astype(WIDE), gains[0:1, :], store, tokens.shape[0]
            )

    gather.distances(take)
    leaving[0].start()
    keep[6].wait()
    vecs_xy.finish()
    keep[5].wait()
    small_xy.finish()
    size = small.shape[1] // 2
    local = small.shape[0]
    wr_ref[...] = jnp.zeros_like(wr_ref)
    wi_ref[...] = jnp.zeros_like(wi_ref)
    flat = small_all[...].reshape(channels, 2 * size)
    for n in range(channels // size):
        block = slice(n * size, (n + 1) * size)
        wr_ref[block, block] = flat[block, :size]
        wi_ref[block, block] = flat[block, size:]
    for other in range(groups):
        par_ref[:, other * local : (other + 1) * local] = vecs_all[other]
    ext[0:8, :] = jnp.zeros((8, channels), WIDE)
    st_ref[0:8, :] = jnp.zeros((8, channels), WIDE)
    for index in range(shards):
        for d in range(1, groups):
            in_xy(index).arrive(d)
    leaving[1].start()
    @pl.loop(0, at.line)
    def _(chip):
        pair = normed[pl.ds(2 * chip, 2), :, :].reshape(2 * tokens.shape[0], width)
        both = dot(pair, in_whole[...].reshape(width, 2 * channels))
        base = pl.multiple_of(chip * 2 * tokens.shape[0], CHUNK)
        here = pl.ds(base, 2 * tokens.shape[0])
        ext[pl.ds(base + 8, 2 * tokens.shape[0]), :] = both[:, :channels].astype(LOW).astype(WIDE)
        pre_ref[here, :] = both[:, channels:]

    @pl.loop(0, chunks)
    def _(n):
        base = pl.multiple_of(n * CHUNK, CHUNK)
        here = pl.ds(base, CHUNK)
        block = ext[pl.ds(base, CHUNK + 8), :]
        conv = jnp.broadcast_to(par_ref[4:5, :], (CHUNK, channels))
        for k in range(4):
            conv = conv + par_ref[k : k + 1, :] * block[8 - k : 8 - k + CHUNK]
        conv_low = conv.astype(LOW)
        conv_ref[here, :] = conv_low
        r = jax.nn.sigmoid(dot(conv_low, wr_ref[...]) + par_ref[5:6, :])
        gate = jax.nn.sigmoid(dot(conv_low, wi_ref[...]) + par_ref[6:7, :])
        log_decay = r * par_ref[7:8, :]
        m = jnp.sqrt(one_minus_exp(-2.0 * log_decay))
        factor = jnp.exp(log_decay)
        r_ref[here, :] = r
        i_ref[here, :] = gate
        put(factors, here, factor)
        put(drive, here, m * gate * conv_low.astype(WIDE))

    for n in range(2, 7):
        leaving[n].start()

    def step(i, n, state, product):
        here = pl.ds(i, 8, stride=segment)
        factor = factors[n, here, :]
        state = factor * state + drive[n, here, :]
        product = factor * product
        drive[n, here, :] = state
        prod[n, here, :] = product
        return state, product

    state, product = scan_segments(step, segment, lane_tiles(channels))
    state, product = state[:, :channels], product[:, :channels]
    carry = jnp.zeros((1, channels), WIDE)
    for k in range(8):
        for part in range(segment // CHUNK):
            base = k * segment + part * CHUNK
            here = slice(base, base + CHUNK)
            states = get(drive, here, channels) + get(prod, here, channels) * carry
            st_ref[base + 8 : base + 8 + CHUNK, :] = states
            product_ref[here, :] = (
                states.astype(LOW).astype(WIDE) * gelu(pre_ref[here, :])
            ).astype(LOW)
        carry = state[k : k + 1] + product[k : k + 1] * carry

    leaving[7].start()
    leaving[8].start()
    glu_z.finish()
    out_xy.finish()
    down_xy.finish()
    gather.sent()
    in_z.sent()
    for index in range(shards):
        in_xy(index).sent()
    for n in (2, 3, 4):
        keep[n].wait()
    for copy in leaving:
        copy.wait()


def mix_in(tokens, in_shard, glu_shard, out_shard, down_shard, small, vecs, gain_shard, groups):
    shards, rows, both = in_shard.shape
    block, width = tokens.shape
    positions, channels = shards * block, both // 2
    local = small.shape[0]
    pieces = 2
    wide = jax.ShapeDtypeStruct((positions, channels), WIDE)
    low = jax.ShapeDtypeStruct((positions, channels), LOW)
    longer = jax.ShapeDtypeStruct((positions + 8, channels), WIDE)
    square = jax.ShapeDtypeStruct((channels, channels), LOW)
    saved = [
        jax.ShapeDtypeStruct((shards, block, width), LOW),
        jax.ShapeDtypeStruct((shards, groups, rows, both), LOW),
        longer, wide, low, wide, wide, longer,
        low,
    ]
    held = [
        jax.ShapeDtypeStruct((8, channels), WIDE), square, square, jax.ShapeDtypeStruct((8, width), WIDE),
    ]
    far = [
        jax.ShapeDtypeStruct((shards, rows, glu_shard.shape[2]), LOW),
        jax.ShapeDtypeStruct((groups,) + out_shard.shape, LOW),
        jax.ShapeDtypeStruct((groups,) + down_shard.shape, LOW),
    ]
    return pl.pallas_call(
        mix_in_kernel,
        out_shape=saved + held + far,
        in_specs=[HELD] * 5 + [ANY] * 3,
        out_specs=[ANY] * len(saved) + [HELD] * len(held) + [ANY] * len(far),
        scratch_shapes=[pltpu.VMEM(member.shape, member.dtype) for member in saved]
        + [
            pltpu.VMEM((shards, block, width), LOW),
            pltpu.VMEM((groups,) + small.shape, LOW),
            pltpu.VMEM((groups,) + vecs.shape, WIDE),
            pltpu.VMEM((shards, groups) + gain_shard.shape, WIDE),
        ]
        + [pltpu.VMEM((lane_tiles(channels), positions, 128), WIDE)] * 3
        + [
            dma(8), dma(shards, pieces, 3), dma(shards, pieces), dma(2, shards), dma(shards, groups),
            dma(shards, groups), dma(2, shards), dma(5, 2, groups), dma(2, shards), dma(9),
        ],
        compiler_params=pltpu.CompilerParams(
            collective_id=1, has_side_effects=True, vmem_limit_bytes=VMEM_BYTES
        ),
        name="mix_in",
    )(tokens, in_shard, glu_shard, out_shard, down_shard, small, vecs, gain_shard)


def feed_kernel(
    product_far, out_far, glu_mine, down_in, cotangent, tokens, gains,
    middle, middle_grad, mixed_low, gain_sums, fed_own_far, fed_other_far, glu_grad, down_grad,
    product, out_whole, fed_own, fed_other, held, cots, glu, down, both, hidden, wide_pair, hidden_pair, normed2, staged, down_staged,
    own, other, heard, into, sib_send, sib_recv, line_send, line_recv,
    local_sems, glu_send, glu_recv, two_send, two_recv, cot_send, cot_recv, stage_sems,
):
    shards, groups = glu.shape[0], glu.shape[1]
    at = Place(shards, groups)
    s, f = at.s, at.f
    block, width = tokens.shape
    units = down.shape[0]
    pair = 2 * block

    keep = [(glu_mine, glu.at[:, f]), (down_in, down), (cotangent, cots.at[s])]
    keep += [(product_far, product), (out_far, out_whole)]
    keep = [pltpu.make_async_copy(a, b, local_sems.at[n]) for n, (a, b) in enumerate(keep)]
    for copy in keep:
        copy.start()
    at.enter()
    def glu_xy(index):
        return Spread(
            at, lambda peer: glu_mine.at[index], lambda origin: glu.at[index, origin],
            glu_send.at[index], glu_recv.at[index],
        )

    cot_z = LineGather(at, cotangent, cots, cot_send, cot_recv, cot_send.shape[1])
    two_z = LineGather(at, normed2, held, two_send, two_recv, two_send.shape[1])
    sums = LineScatter(
        at, own, other, heard, into, (sib_send, sib_recv, line_send, line_recv), line_send.shape[1]
    )
    for index in range(shards):
        glu_xy(index).start()
    cot_z.start()

    def split(chip, columns, value, mine, theirs):
        first = at.c == 0
        mine[chip, :, columns] = jnp.where(first, value[:block], value[block:]).astype(mine.dtype)
        theirs[chip, :, columns] = jnp.where(first, value[block:], value[:block]).astype(theirs.dtype)

    def columns_of(j):
        return pl.ds(pl.multiple_of(j * 256, 256), 256)

    def pair_rows(chip):
        return pl.ds(pl.multiple_of(chip * pair, pair), pair)

    keep[3].wait()
    keep[4].wait()

    def project(chip):
        @pl.loop(0, width // 256)
        def _(j):
            value = dot(product[pair_rows(chip), :], out_whole[:, columns_of(j)])
            split(chip, columns_of(j), value, own, other)

        sums.across(chip).start()

    for k in range(at.line // 2):
        project(at.line - 1 - k)
        project(k)
        sums.push(at.line - 1 - k)
        sums.push(k)
    sums.join()
    cot_z.pass_on(1)

    def to_middle(here, total):
        values = total + tokens[here, :].astype(WIDE)
        middle[here, :] = values
        scale = lax.rsqrt(jnp.mean(values * values, axis=-1, keepdims=True) + EPSILON)
        normed2[here, :] = (values * scale * gains[1:2, :]).astype(LOW)

    sums.finish(to_middle)
    two_z.start()
    own_copy = pltpu.make_async_copy(normed2, held.at[s], local_sems.at[5])
    own_copy.start()
    keep[0].wait()
    keep[1].wait()
    keep[2].wait()
    sums.sent()
    own_copy.wait()
    for d in range(2, at.line):
        cot_z.pass_on(d)
    for index in range(shards):
        glu_xy(index).finish()

    def open_up(chip):
        rows = held[pl.ds(2 * chip, 2), :, :].reshape(pair, width)
        grads = cots[pl.ds(2 * chip, 2), :, :].reshape(pair, width)

        @pl.loop(0, 2 * units // 256)
        def _(j):
            wide_pair[:, columns_of(j)] = dot(
                rows, glu[:, :, :, columns_of(j)].reshape(width, 256)
            )

        @pl.loop(0, units // 256)
        def _(j):
            hidden_pair[:, columns_of(j)] = times_transpose(grads, down[columns_of(j), :])

        @pl.loop(0, pair // 16)
        def _(n):
            part = pl.ds(pl.multiple_of(n * 16, 16), 16)
            there = pl.ds(pl.multiple_of(chip * pair + n * 16, 16), 16)
            opened, slope = gelu_and_slope(wide_pair[part, :units])
            up = wide_pair[part, units:]
            grad = hidden_pair[part, :]
            hidden[there, :] = (opened * up).astype(LOW)
            both[there, :units] = (grad * up * slope).astype(LOW)
            both[there, units:] = (grad * opened).astype(LOW)

    def to_normed2(chip):
        @pl.loop(0, shards)
        def _(j):
            value = times_transpose(
                both[pair_rows(chip), :], glu[j].reshape(width // shards, 2 * units)
            )
            split(chip, columns_of(j), value, own, other)

        sums.across(chip).start()

    def to_fed(chip):
        @pl.loop(0, width // 256)
        def _(j):
            value = dot(hidden[pair_rows(chip), :], down[:, columns_of(j)])
            split(chip, columns_of(j), value, fed_own, fed_other)

    cot_z.settle(at.z)
    two_z.settle(at.z)

    @pl.loop(1, at.line + 1)
    def _(n):
        chip = at.nearest(lax.rem(n, at.line))

        @pl.when(n < at.line)
        def _():
            two_z.pass_on(n)
            two_z.settle(chip)
            cot_z.settle(chip)

        open_up(chip)

        @pl.when(n > 1)
        def _():
            sums.push(at.nearest(n - 1))

        to_normed2(chip)

    sums.join()

    def glu_out(j):
        return pltpu.make_async_copy(
            staged.at[lax.rem(j, 2)], glu_grad.at[:, j], stage_sems.at[lax.rem(j, 2)]
        )

    def glu_sums(first, last):
        @pl.loop(first, last)
        def _(j):
            @pl.when(j >= 2)
            def _():
                glu_out(j - 2).wait()

            rows = held[:, :, columns_of(j)].reshape(shards * block, 256)
            staged[lax.rem(j, 2)] = outer_sum(rows, both[...]).astype(LOW).reshape(staged.shape[1:])
            glu_out(j).start()

    def down_out(j):
        return pltpu.make_async_copy(
            down_staged.at[lax.rem(j, 2)], down_grad.at[columns_of(j)], stage_sems.at[2 + lax.rem(j, 2)]
        )

    def down_sums():
        @pl.loop(0, units // 256)
        def _(j):
            @pl.when(j >= 2)
            def _():
                down_out(j - 2).wait()

            grads = cots[...].reshape(shards * block, width)
            down_staged[lax.rem(j, 2)] = outer_sum(hidden[:, columns_of(j)], grads).astype(LOW)
            down_out(j).start()

    down_sums()

    @pl.loop(0, at.line)
    def _(chip):
        to_fed(chip)

    fed_leave = [
        pltpu.make_async_copy(fed_own, fed_own_far, local_sems.at[6]),
        pltpu.make_async_copy(fed_other, fed_other_far, local_sems.at[7]),
    ]
    for copy in fed_leave:
        copy.start()

    gain_sums[...] = jnp.zeros_like(gain_sums)

    def back(here, grad):
        values = middle[here, :]
        scale = lax.rsqrt(jnp.mean(values * values, axis=-1, keepdims=True) + EPSILON)
        scaled = grad * gains[1:2, :]
        along = jnp.mean(scaled * values, axis=-1, keepdims=True)
        total = cots[at.s, here, :].astype(WIDE) + scale * scaled - values * (scale * scale * scale * along)
        middle_grad[here, :] = total
        mixed_low[here, :] = total.astype(LOW)
        gain_sums[0:1, :] += jnp.sum(grad * values * scale, axis=0, keepdims=True)

    sums.finish(back)
    glu_sums(0, shards)
    for j in range(shards - 2, shards):
        glu_out(j).wait()
    for j in range(max(units // 256 - 2, 0), units // 256):
        down_out(j).wait()
    for copy in fed_leave:
        copy.wait()
    sums.sent()
    two_z.sent()
    cot_z.sent()


def feed(product, out_whole, glu_mine, down_whole, cotangent, tokens, gains, groups):
    shards, rows, both = glu_mine.shape
    block, width = tokens.shape
    units = both // 2
    line, pieces, thirds = shards // 2, 2, 2
    own = jax.ShapeDtypeStruct((block, width), WIDE)
    low = jax.ShapeDtypeStruct((line, block, width), LOW)
    outs = [
        own, own, jax.ShapeDtypeStruct((block, width), LOW), jax.ShapeDtypeStruct((8, width), WIDE),
        low, low,
        jax.ShapeDtypeStruct((groups, shards, rows, both), LOW),
        jax.ShapeDtypeStruct((units, width), LOW),
    ]
    gathered = pltpu.VMEM((shards, block, width), LOW)
    return pl.pallas_call(
        feed_kernel,
        out_shape=outs,
        in_specs=[ANY] * 5 + [HELD] * 2,
        out_specs=[HELD] * 4 + [ANY] * 4,
        scratch_shapes=[
            pltpu.VMEM(product.shape, LOW), pltpu.VMEM(out_whole.shape, LOW),
            pltpu.VMEM(low.shape, LOW), pltpu.VMEM(low.shape, LOW), gathered, gathered,
            pltpu.VMEM((shards, groups, rows, both), LOW),
            pltpu.VMEM((units, width), LOW),
            pltpu.VMEM((shards * block, both), LOW),
            pltpu.VMEM((shards * block, units), LOW),
            pltpu.VMEM((2 * block, both), WIDE),
            pltpu.VMEM((2 * block, units), WIDE),
            pltpu.VMEM((block, width), LOW),
            pltpu.VMEM((2, groups, rows, both), LOW),
            pltpu.VMEM((2, 256, width), LOW),
        ]
        + LineScatter.scratch(line, block, width, thirds)
        + [
            dma(8), dma(shards, groups), dma(shards, groups), dma(shards, pieces, 3), dma(shards, pieces),
            dma(shards, pieces, 3), dma(shards, pieces), dma(4),
        ],
        compiler_params=pltpu.CompilerParams(
            collective_id=2, has_side_effects=True, vmem_limit_bytes=VMEM_BYTES
        ),
        name="feed",
    )(product, out_whole, glu_mine, down_whole, cotangent, tokens, gains)


def back_kernel(
    mixed, fed_own_far, fed_far, middle_far, middle_grad_far, tokens_far, gains, par_ref, wr_ref, wi_ref,
    out_far, in_far, normed_far, product_far, ext_far, pre_far, conv_far, r_far, i_far, st_far,
    glu_grad, down_grad, mlp_parts,
    result, tokens_grad, glu_out, in_out, out_heard, small_heard, gain_out, glu_heard, in_grad, down_heard,
    fed_own, middle, middle_grad, tokens, held, in_whole, out_whole, product, ext, pre, conv_ref, r_ref, i_ref, st_ref,
    both, pair_grad, staged, factors, adj, prod, cg, carries, wr_sum, wi_sum,
    out_sum, out_grad, small, gain_row, gain_parts, gain_heard, gain_sum, glu_parts, glu_sum, in_heard, in_sum,
    fed_other, fed_heard, fed_into, fed_sib_send, fed_sib_recv, fed_send, fed_recv,
    own, other, heard, into, sib_send, sib_recv, line_send, line_recv,
    local_sems, held_send, held_recv, glu_xy_sems, down_sems, stage_sems, in_xy_sems, out_sems,
    small_sems, gain_xy_sems, glu_sems, in_sems, gain_sems,
):
    shards, groups = in_whole.shape[0], in_whole.shape[1]
    at = Place(shards, groups)
    s, f = at.s, at.f
    block, width = tokens.shape
    positions, channels = product.shape
    rows = in_whole.shape[2]
    pair = 2 * block
    segment = positions // 8
    chunks = positions // CHUNK

    keep = [
        (mixed, held.at[s]), (out_far, out_whole), (pre_far, pre), (st_far, st_ref),
        (product_far, product), (r_far, r_ref), (i_far, i_ref), (conv_far, conv_ref),
        (ext_far, ext), (in_far, in_whole), (fed_far, fed_other), (normed_far, held), (fed_own_far, fed_own),
        (middle_far, middle), (middle_grad_far, middle_grad), (tokens_far, tokens),
    ]
    keep = [pltpu.make_async_copy(a, b, local_sems.at[n]) for n, (a, b) in enumerate(keep)]
    for copy in keep[:11] + keep[12:]:
        copy.start()
    at.enter()

    def over_fsdp(src, dst, sems):
        return Spread(
            at, lambda peer: src.at[peer], lambda origin: dst.at[origin], sems.at[0], sems.at[1]
        )

    def over_seq(src, dst, sems):
        return Spread(
            at, lambda peer: src.at[peer], lambda origin: dst.at[origin], sems.at[0], sems.at[1], "seq"
        )

    glu_xy = over_fsdp(glu_grad, glu_heard, glu_xy_sems)
    in_xy = over_fsdp(in_grad, in_heard, in_xy_sems)
    out_xy = over_fsdp(out_grad, out_heard, out_sems)
    down_xy = over_fsdp(down_grad, down_heard, down_sems)
    small_xy = over_fsdp(small, small_heard, small_sems)
    gain_xy = over_fsdp(gain_parts, gain_heard, gain_xy_sems)
    glu_z = over_seq(glu_sum, glu_out, glu_sems)
    in_z = over_seq(in_sum, in_out, in_sems)
    gain_z = over_seq(gain_sum, gain_out, gain_sems)
    mixed_z = LineGather(at, mixed, held, held_send, held_recv, held_send.shape[1])
    fed = LineScatter(
        at, fed_own, fed_other, fed_heard, fed_into,
        (fed_sib_send, fed_sib_recv, fed_send, fed_recv), fed_send.shape[1],
    )
    sums = LineScatter(
        at, own, other, heard, into, (sib_send, sib_recv, line_send, line_recv), line_send.shape[1]
    )
    mixed_z.start()
    glu_xy.start()
    out_sum[...] = jnp.zeros_like(out_sum)
    keep[10].wait()
    keep[12].wait()
    for k in range(at.line // 2):
        fed.across(at.line - 1 - k).start()
        fed.across(k).start()

    def columns_of(j):
        return pl.ds(pl.multiple_of(j * 256, 256), 256)

    for n in (0, 1, 2, 3, 4):
        keep[n].wait()

    def mixed_back(chip):
        rows = held[pl.ds(2 * chip, 2), :, :].reshape(pair, width)
        pair_grad[...] = times_transpose(rows, out_whole[...])

        @pl.loop(0, pair // 64)
        def _(n):
            grad = pair_grad[pl.ds(pl.multiple_of(n * 64, 64), 64), :]
            base = pl.multiple_of(chip * pair + n * 64, 64)
            here = pl.ds(base, 64)
            opened, slope = gelu_and_slope(pre[here, :])
            states = st_ref[pl.ds(base + 8, 64), :].astype(LOW).astype(WIDE)
            put(adj, here, (grad * opened).astype(LOW).astype(WIDE))
            both[here, channels:] = (grad * states * slope).astype(LOW)

        there = pl.ds(pl.multiple_of(chip * pair, pair), pair)

        @pl.loop(0, width // 256)
        def _(j):
            part = held[pl.ds(2 * chip, 2), :, columns_of(j)].reshape(pair, 256)
            out_sum[:, columns_of(j)] += outer_sum(product[there, :], part)

    for n in range(at.line - 1, 0, -1):
        fed.prepare(at.nearest(n))

    mixed_z.distances(mixed_back)
    for n in range(at.line - 1, 0, -1):
        fed.launch(at.nearest(n))
    keep[5].wait()

    @pl.loop(0, chunks)
    def _(n):
        here = pl.ds(pl.multiple_of(n * CHUNK, CHUNK), CHUNK)
        put(factors, here, jnp.exp(r_ref[here, :] * par_ref[7:8, :]))

    def step(j, n, flow, product):
        here = pl.ds(segment - 1 - j, 8, stride=segment)
        factor = factors[n, here, :]
        adjoint = adj[n, here, :] + flow
        adj[n, here, :] = adjoint
        prod[n, here, :] = product
        return factor * adjoint, factor * product

    flow, through = scan_segments(step, segment, lane_tiles(channels))
    flow, through = flow[:, :channels], through[:, :channels]
    carry = jnp.zeros((1, channels), WIDE)
    for k in range(7, -1, -1):
        carries[k : k + 1, :] = carry
        carry = flow[k : k + 1] + through[k : k + 1] * carry
    for n in (6, 7, 8):
        keep[n].wait()
    cg[pl.ds(positions, 8), :] = jnp.zeros((8, channels), WIDE)
    wr_sum[...] = jnp.zeros_like(wr_sum)
    wi_sum[...] = jnp.zeros_like(wi_sum)

    def grads(c, sums):
        base = pl.multiple_of(c * CHUNK, CHUNK)
        rows = pl.ds(base, CHUNK)
        adjoint = get(adj, rows, channels) + get(prod, rows, channels) * carries[pl.ds(base // segment, 1), :]
        before = st_ref[pl.ds(base, CHUNK + 8), :][7 : 7 + CHUNK]
        conv_low = conv_ref[rows, :]
        conv = conv_low.astype(WIDE)
        r = r_ref[rows, :]
        gate = i_ref[rows, :]
        factor = get(factors, rows, channels)
        m = jnp.sqrt(one_minus_exp(-2.0 * (r * par_ref[7:8, :])))
        driven = adjoint * gate
        by_log = adjoint * before * factor - driven * conv * factor * factor / m
        by_r = by_log * par_ref[7:8, :] * r * (1.0 - r)
        by_i = adjoint * m * conv * gate * (1.0 - gate)
        by_r_low = by_r.astype(LOW)
        by_i_low = by_i.astype(LOW)
        conv_grad = (
            driven * m
            + times_transpose(by_r_low, wr_ref[...])
            + times_transpose(by_i_low, wi_ref[...])
        )
        cg[rows, :] = conv_grad
        wr_sum[...] += outer_sum(conv_low, by_r_low)
        wi_sum[...] += outer_sum(conv_low, by_i_low)
        near = ext[pl.ds(base, CHUNK + 8), :]
        rows_of = [conv_grad * near[8 - k : 8 - k + CHUNK] for k in range(4)]
        rows_of += [conv_grad, by_r, by_i, by_log * r]
        return tuple(
            total + jnp.sum(member, axis=0, keepdims=True) for total, member in zip(sums, rows_of)
        )

    zero = jnp.zeros((1, channels), WIDE)
    totals = lax.fori_loop(0, chunks, grads, (zero,) * 8)
    @pl.loop(0, chunks)
    def _(c):
        base = pl.multiple_of(c * CHUNK, CHUNK)
        near = cg[pl.ds(base, CHUNK + 8), :]
        total = jnp.zeros((CHUNK, channels), WIDE)
        for k in range(4):
            total = total + par_ref[k : k + 1, :] * near[k : k + CHUNK]
        both[pl.ds(base, CHUNK), :channels] = total.astype(LOW)

    fed.join()
    keep[9].wait()

    def project(chip):
        rows = both[pl.ds(pl.multiple_of(chip * pair, pair), pair), :]

        @pl.loop(0, shards)
        def _(j):
            value = times_transpose(rows, in_whole[j].reshape(width // shards, 2 * channels))
            first = at.c == 0
            own[chip, :, columns_of(j)] = jnp.where(first, value[:block], value[block:]).astype(LOW)
            other[chip, :, columns_of(j)] = jnp.where(first, value[block:], value[:block]).astype(LOW)

        sums.across(chip).start()

    for k in range(at.line // 2):
        project(at.line - 1 - k)
        project(k)
        sums.push(at.line - 1 - k)
        sums.push(k)
    mixed_z.sent()
    keep[11].start()
    local = small.shape[1] - 8
    size = small.shape[2] // 2
    for n in range(channels // size):
        part = slice(n * size, (n + 1) * size)
        wr_sum[part, :size] = wr_sum[part, part]
        wi_sum[part, :size] = wi_sum[part, part]
    for group in range(groups):
        part = slice(group * local, (group + 1) * local)
        small[group, :local, :size] = wr_sum[part, :size]
        small[group, :local, size:] = wi_sum[part, :size]
        for k in range(8):
            small[group, local + k : local + k + 1, :local] = totals[k][:, part]
    small_xy.start()
    keep[11].wait()

    def in_done(j):
        return pltpu.make_async_copy(
            staged.at[lax.rem(j, 2)], in_grad.at[:, j], stage_sems.at[lax.rem(j, 2)]
        )

    @pl.loop(0, shards)
    def _(j):
        @pl.when(j >= 2)
        def _():
            in_done(j - 2).wait()

        part = held[:, :, columns_of(j)].reshape(positions, 256)
        staged[lax.rem(j, 2)] = outer_sum(part, both[...]).astype(LOW).reshape(staged.shape[1:])
        in_done(j).start()

    for j in range(shards - 2, shards):
        in_done(j).wait()
    in_xy.start()
    in_own = pltpu.make_async_copy(in_grad.at[f], in_heard.at[f], local_sems.at[16])
    in_own.start()
    sums.join()
    glu_xy.finish()

    def glu_load(d, origin):
        peer = lax.rem(s + d, shards)
        half = lax.rem(d, 2)
        return pltpu.make_async_copy(
            glu_heard.at[origin, peer], glu_parts.at[half, origin], glu_sems.at[2 + half, origin]
        )

    def glu_load_own(d):
        peer = lax.rem(s + d, shards)
        half = lax.rem(d, 2)
        return pltpu.make_async_copy(
            glu_grad.at[f, peer], glu_parts.at[half, f], glu_sems.at[2 + half, f]
        )

    def glu_loads(d):
        glu_load_own(d).start()
        for hop in range(1, groups):
            glu_load(d, lax.rem(f + hop, groups)).start()

    def add(parts, total, peer):
        @pl.loop(0, total.shape[1] // 16)
        def _(n):
            here = pl.ds(pl.multiple_of(n * 16, 16), 16)
            value = parts[0, here, :].astype(WIDE)
            for origin in range(1, groups):
                value = value + parts[origin, here, :].astype(WIDE)
            total[peer, here, :] = value.astype(total.dtype)

    glu_loads(1)

    @pl.loop(1, shards + 1)
    def _(d):
        @pl.when(d < shards)
        def _():
            glu_loads(d + 1)

        for origin in range(groups):
            glu_load(d, origin).wait()
        add(glu_parts.at[lax.rem(d, 2)], glu_sum, lax.rem(s + d, shards))

        @pl.when(d < shards)
        def _():
            glu_z.copy(d).start()

    glu_own = pltpu.make_async_copy(glu_sum.at[s], glu_out.at[s], local_sems.at[17])
    glu_own.start()
    out_grad[...] = out_sum[...].astype(LOW).reshape(out_grad.shape)
    out_xy.start()
    gain_row[...] = jnp.zeros_like(gain_row)

    for n in (13, 14, 15):
        keep[n].wait()

    def store_result(here, total):
        result[here, :] = (middle[here, :] + total).astype(LOW)

    fed.finish(store_result)

    def back(here, grad):
        values = tokens[here, :].astype(WIDE)
        scale = lax.rsqrt(jnp.mean(values * values, axis=-1, keepdims=True) + EPSILON)
        scaled = grad * gains[0:1, :]
        along = jnp.mean(scaled * values, axis=-1, keepdims=True)
        total = middle_grad[here, :] + scale * scaled - values * (scale * scale * scale * along)
        tokens_grad[here, :] = total.astype(LOW)
        gain_row[0:1, :] += jnp.sum(grad * values * scale, axis=0, keepdims=True)

    sums.finish(back)
    for group in range(groups):
        for shard in range(shards):
            first = (shard * groups + group) * rows
            gain_parts[group, shard, 0:1, :] = gain_row[0:1, first : first + rows]
            gain_parts[group, shard, 1:2, :] = mlp_parts[0:1, first : first + rows]
    gain_xy.start()
    in_own.wait()
    in_xy.finish()
    down_xy.start()

    @pl.loop(1, shards + 1)
    def _(d):
        peer = lax.rem(s + d, shards)
        add(in_heard.at[:, peer], in_sum, peer)

        @pl.when(d < shards)
        def _():
            in_z.copy(d).start()

    last = [
        pltpu.make_async_copy(in_sum.at[s], in_out.at[s], local_sems.at[18]),
        pltpu.make_async_copy(out_grad.at[f], out_heard.at[f], local_sems.at[19]),
        pltpu.make_async_copy(small.at[f], small_heard.at[f], local_sems.at[20]),
    ]
    for copy in last:
        copy.start()
    gain_xy.finish()
    total = gain_parts[f]
    for d in range(1, groups):
        total = total + gain_heard[lax.rem(f + d, groups)]
    gain_sum[...] = total
    gain_z.start()
    gain_own = pltpu.make_async_copy(gain_sum.at[s], gain_out.at[s], local_sems.at[21])
    gain_own.start()
    fed.sent()
    sums.sent()
    for spread in (small_xy, out_xy, down_xy, glu_z, gain_z, in_z):
        spread.finish()
    for copy in (glu_own, gain_own, *last):
        copy.wait()


def back(
    mixed, fed_own, fed_other, middle, middle_grad, tokens, gains, par, wr, wi,
    out_whole, in_whole, normed, product, ext, pre, conv, r, i, st, glu_grad, down_grad, mlp_sums, size,
):
    shards, groups, rows, both = in_whole.shape
    block, width = tokens.shape
    positions, channels = product.shape
    line, pieces, halves = shards // 2, 2, 2
    local = channels // groups
    low = pltpu.VMEM((line, block, width), LOW)
    short = jax.ShapeDtypeStruct((block, width), LOW)
    glu_shape = glu_grad.shape[1:]
    in_shape = (groups, shards, rows, both)
    outs = [
        short, short, jax.ShapeDtypeStruct(glu_shape, LOW), jax.ShapeDtypeStruct(in_shape[1:], LOW),
        jax.ShapeDtypeStruct((groups, local, width), LOW),
        jax.ShapeDtypeStruct((groups, local + 8, 2 * size), WIDE),
        jax.ShapeDtypeStruct((shards, 8, rows), WIDE),
        jax.ShapeDtypeStruct(glu_grad.shape, LOW), jax.ShapeDtypeStruct(in_shape, LOW),
        jax.ShapeDtypeStruct(down_grad.shape, LOW),
    ]
    late = [fed_own, middle, middle_grad, tokens]
    far = [out_whole, in_whole, normed, product, ext, pre, conv, r, i, st]
    near = [in_whole, out_whole, product, ext, pre, conv, r, i, st]
    return pl.pallas_call(
        back_kernel,
        out_shape=outs,
        in_specs=[ANY] * 6 + [HELD] * 4 + [ANY] * (len(far) + 2) + [HELD],
        out_specs=[HELD] * 2 + [ANY] * 8,
        scratch_shapes=[pltpu.VMEM(member.shape, member.dtype) for member in late]
        + [pltpu.VMEM((shards, block, width), LOW)]
        + [pltpu.VMEM(member.shape, member.dtype) for member in near]
        + [
            pltpu.VMEM((positions, 2 * channels), LOW),
            pltpu.VMEM((2 * block, channels), WIDE),
            pltpu.VMEM((2, groups, rows, both), LOW),
        ]
        + [pltpu.VMEM((lane_tiles(channels), positions, 128), WIDE)] * 3
        + [pltpu.VMEM((positions + 8, channels), WIDE), pltpu.VMEM((8, channels), WIDE)]
        + [pltpu.VMEM((channels, channels), WIDE)] * 2
        + [
            pltpu.VMEM((channels, width), WIDE),
            pltpu.VMEM((groups, local, width), LOW),
            pltpu.VMEM((groups, local + 8, 2 * size), WIDE),
            pltpu.VMEM((8, width), WIDE),
            pltpu.VMEM((groups, shards, 8, rows), WIDE),
            pltpu.VMEM((groups, shards, 8, rows), WIDE),
            pltpu.VMEM((shards, 8, rows), WIDE),
            pltpu.VMEM((2, groups) + glu_shape[1:], LOW),
            pltpu.VMEM(glu_shape, LOW),
            pltpu.VMEM(in_shape, LOW),
            pltpu.VMEM(in_shape[1:], LOW),
        ]
        + LineScatter.scratch(line, block, width, halves)[1:]
        + [low]
        + LineScatter.scratch(line, block, width, halves)[1:]
        + [
            dma(22), dma(shards, pieces, 3), dma(shards, pieces), dma(2, groups), dma(2, groups), dma(2),
            dma(2, groups), dma(2, groups), dma(2, groups), dma(2, groups),
            dma(4, shards), dma(2, shards), dma(2, shards),
        ],
        compiler_params=pltpu.CompilerParams(
            collective_id=3, has_side_effects=True, vmem_limit_bytes=VMEM_BYTES
        ),
        name="back",
    )(
        mixed, fed_own, fed_other, middle, middle_grad, tokens, gains, par, wr, wi, *far,
        glu_grad, down_grad, mlp_sums,
    )


def mixer_forward_kernel(
    x_ref, wr_ref, wi_ref, par_ref,
    conv_ref, r_ref, i_ref, f_ref, m_ref, st_ref,
    ext, factors, drive, prod,
):
    positions, channels = x_ref.shape
    segment = positions // 8
    chunks = positions // CHUNK
    ext[0:8, :] = jnp.zeros((8, channels), WIDE)
    st_ref[0:8, :] = jnp.zeros((8, channels), WIDE)

    @pl.loop(0, chunks)
    def _(c):
        base = pl.multiple_of(c * CHUNK, CHUNK)
        ext[pl.ds(base + 8, CHUNK), :] = x_ref[pl.ds(base, CHUNK), :].astype(WIDE)

    @pl.loop(0, chunks)
    def _(c):
        base = pl.multiple_of(c * CHUNK, CHUNK)
        rows = pl.ds(base, CHUNK)
        block = ext[pl.ds(base, CHUNK + 8), :]
        conv = jnp.broadcast_to(par_ref[4:5, :], (CHUNK, channels))
        for k in range(4):
            conv = conv + par_ref[k : k + 1, :] * block[8 - k : 8 - k + CHUNK]
        conv_low = conv.astype(LOW)
        conv_ref[rows, :] = conv_low
        r = jax.nn.sigmoid(dot(conv_low, wr_ref[...]) + par_ref[5:6, :])
        gate = jax.nn.sigmoid(dot(conv_low, wi_ref[...]) + par_ref[6:7, :])
        log_decay = r * par_ref[7:8, :]
        m = jnp.sqrt(one_minus_exp(-2.0 * log_decay))
        r_ref[rows, :] = r
        i_ref[rows, :] = gate
        factor = jnp.exp(log_decay)
        f_ref[rows, :] = factor
        m_ref[rows, :] = m
        put(factors, rows, factor)
        put(drive, rows, m * gate * conv_low.astype(WIDE))

    def step(i, n, state, product):
        rows = pl.ds(i, 8, stride=segment)
        factor = factors[n, rows, :]
        state = factor * state + drive[n, rows, :]
        product = factor * product
        drive[n, rows, :] = state
        prod[n, rows, :] = product
        return state, product

    state, product = scan_segments(step, segment, lane_tiles(channels))
    state, product = state[:, :channels], product[:, :channels]
    carry = jnp.zeros((1, channels), WIDE)
    for k in range(8):
        for part in range(segment // CHUNK):
            base = k * segment + part * CHUNK
            rows = slice(base, base + CHUNK)
            st_ref[base + 8 : base + 8 + CHUNK, :] = (
                get(drive, rows, channels) + get(prod, rows, channels) * carry
            )
        carry = state[k : k + 1] + product[k : k + 1] * carry


def mixer_backward_kernel(
    ds_ref, x_ref, conv_ref, r_ref, i_ref, f_ref, m_ref, st_ref, wr_ref, wi_ref, par_ref,
    xg_ref, wrg_ref, wig_ref, sums_ref,
    ext, factors, adj, prod, cg, carries, wr_sum, wi_sum,
):
    positions, channels = x_ref.shape
    segment = positions // 8
    chunks = positions // CHUNK
    ext[0:8, :] = jnp.zeros((8, channels), WIDE)
    cg[pl.ds(positions, 8), :] = jnp.zeros((8, channels), WIDE)
    wr_sum[...] = jnp.zeros_like(wr_sum)
    wi_sum[...] = jnp.zeros_like(wi_sum)

    @pl.loop(0, chunks)
    def _(c):
        base = pl.multiple_of(c * CHUNK, CHUNK)
        ext[pl.ds(base + 8, CHUNK), :] = x_ref[pl.ds(base, CHUNK), :].astype(WIDE)
        put(adj, pl.ds(base, CHUNK), ds_ref[pl.ds(base, CHUNK), :].astype(WIDE))
        put(factors, pl.ds(base, CHUNK), f_ref[pl.ds(base, CHUNK), :])

    def step(j, n, flow, product):
        rows = pl.ds(segment - 1 - j, 8, stride=segment)
        factor = factors[n, rows, :]
        adjoint = adj[n, rows, :] + flow
        adj[n, rows, :] = adjoint
        prod[n, rows, :] = product
        return factor * adjoint, factor * product

    flow, product = scan_segments(step, segment, lane_tiles(channels))
    flow, product = flow[:, :channels], product[:, :channels]
    carry = jnp.zeros((1, channels), WIDE)
    for k in range(7, -1, -1):
        carries[k : k + 1, :] = carry
        carry = flow[k : k + 1] + product[k : k + 1] * carry

    def grads(c, sums):
        base = pl.multiple_of(c * CHUNK, CHUNK)
        rows = pl.ds(base, CHUNK)
        adjoint = get(adj, rows, channels) + get(prod, rows, channels) * carries[pl.ds(base // segment, 1), :]
        before = st_ref[pl.ds(base, CHUNK + 8), :][7 : 7 + CHUNK]
        conv_low = conv_ref[rows, :]
        conv = conv_low.astype(WIDE)
        r = r_ref[rows, :]
        gate = i_ref[rows, :]
        factor = f_ref[rows, :]
        m = m_ref[rows, :]
        driven = adjoint * gate
        by_log = adjoint * before * factor - driven * conv * factor * factor / m
        by_r = by_log * par_ref[7:8, :] * r * (1.0 - r)
        by_i = adjoint * m * conv * gate * (1.0 - gate)
        by_r_low = by_r.astype(LOW)
        by_i_low = by_i.astype(LOW)
        conv_grad = (
            driven * m
            + times_transpose(by_r_low, wr_ref[...])
            + times_transpose(by_i_low, wi_ref[...])
        )
        cg[rows, :] = conv_grad
        wr_sum[...] += outer_sum(conv_low, by_r_low)
        wi_sum[...] += outer_sum(conv_low, by_i_low)
        block = ext[pl.ds(base, CHUNK + 8), :]
        rows_of = [conv_grad * block[8 - k : 8 - k + CHUNK] for k in range(4)]
        rows_of += [conv_grad, by_r, by_i, by_log * r]
        return tuple(
            total + jnp.sum(member, axis=0, keepdims=True) for total, member in zip(sums, rows_of)
        )

    zero = jnp.zeros((1, channels), WIDE)
    sums = lax.fori_loop(0, chunks, grads, (zero,) * 8)
    for k in range(8):
        sums_ref[k : k + 1, :] = sums[k]
    size = wrg_ref.shape[1]
    for n in range(channels // size):
        block = slice(n * size, (n + 1) * size)
        wrg_ref[block, :] = wr_sum[block, block]
        wig_ref[block, :] = wi_sum[block, block]

    @pl.loop(0, chunks)
    def _(c):
        base = pl.multiple_of(c * CHUNK, CHUNK)
        block = cg[pl.ds(base, CHUNK + 8), :]
        total = jnp.zeros((CHUNK, channels), WIDE)
        for k in range(4):
            total = total + par_ref[k : k + 1, :] * block[k : k + CHUNK]
        xg_ref[pl.ds(base, CHUNK), :] = total.astype(LOW)


def mixer_forward(x, wr, wi, par):
    positions, channels = x.shape
    wide = jax.ShapeDtypeStruct((positions, channels), WIDE)
    return pl.pallas_call(
        mixer_forward_kernel,
        out_shape=(
            jax.ShapeDtypeStruct((positions, channels), LOW), wide, wide, wide, wide,
            jax.ShapeDtypeStruct((positions + 8, channels), WIDE),
        ),
        scratch_shapes=[pltpu.VMEM((positions + 8, channels), WIDE)]
        + [pltpu.VMEM((lane_tiles(channels), positions, 128), WIDE)] * 3,
        compiler_params=pltpu.CompilerParams(vmem_limit_bytes=48 * 2**20),
        name="mixer_forward",
    )(x, wr, wi, par)


def mixer_backward(ds, x, saved, wr, wi, par, size):
    positions, channels = x.shape
    square = jax.ShapeDtypeStruct((channels, size), WIDE)
    return pl.pallas_call(
        mixer_backward_kernel,
        out_shape=(
            jax.ShapeDtypeStruct((positions, channels), LOW), square, square,
            jax.ShapeDtypeStruct((8, channels), WIDE),
        ),
        scratch_shapes=[pltpu.VMEM((positions + 8, channels), WIDE)]
        + [pltpu.VMEM((lane_tiles(channels), positions, 128), WIDE)] * 3
        + [pltpu.VMEM((positions + 8, channels), WIDE), pltpu.VMEM((8, channels), WIDE)]
        + [pltpu.VMEM((channels, channels), WIDE)] * 2,
        compiler_params=pltpu.CompilerParams(vmem_limit_bytes=48 * 2**20),
        name="mixer_backward",
    )(ds, x, *saved, wr, wi, par)


def gather_columns(weights):
    shards = lax.axis_size("seq")
    rows = weights[0].shape[0]
    widths = [member.shape[1] // shards for member in weights]
    stacked = jnp.concatenate(
        [member.reshape(rows, shards, width) for member, width in zip(weights, widths)], axis=2
    )
    mine = lax.all_to_all(stacked.transpose(1, 0, 2), "seq", split_axis=0, concat_axis=0)
    whole = lax.all_gather(mine, "fsdp", axis=1)
    return whole.reshape(-1, sum(widths))


def scatter_columns(grad, widths, rows):
    shards, groups = lax.axis_size("seq"), lax.axis_size("fsdp")
    parts = grad.astype(LOW).reshape(shards, groups, rows, sum(widths)).transpose(1, 0, 2, 3)
    mine = lax.psum_scatter(parts, "fsdp", scatter_dimension=0, tiled=False)
    swapped = lax.all_to_all(mine, "seq", split_axis=0, concat_axis=0).astype(WIDE)
    outs, first = [], 0
    for width in widths:
        outs.append(swapped[:, :, first : first + width].transpose(1, 0, 2).reshape(rows, -1))
        first += width
    return outs


def block_diagonal(weight, blocks):
    size = weight.shape[1]
    shaped = weight.reshape(blocks, size, size)
    full = jnp.zeros((blocks, size, blocks, size), weight.dtype)
    for n in range(blocks):
        full = full.at[n, :, n, :].set(shaped[n])
    return full.reshape(blocks * size, blocks * size)


def general(
    tokens, cotangent, mix_gain, lru_in_weight, gelu_in_weight, out_weight, conv_weight, conv_bias,
    recurrence_weight, recurrence_bias, input_gate_weight, input_gate_bias, decay_param, mlp_gain,
    gate_weight, up_weight, down_weight,
):
    positions, width = tokens.shape[1:]
    rows = lru_in_weight.shape[0]
    shards = lax.axis_size("seq")
    channels = lru_in_weight.shape[1] // shards
    hidden_width = gate_weight.shape[1] // shards
    size = recurrence_weight.shape[1]

    gains = lax.all_gather(
        jnp.stack([mix_gain, mlp_gain], axis=1), ("seq", "fsdp"), axis=0, tiled=True
    ).astype(WIDE)
    mix_scale, mlp_scale = gains[:, 0], gains[:, 1]
    in_whole = gather_columns([lru_in_weight, gelu_in_weight])
    lru_params = lax.all_gather(
        jnp.concatenate(
            [
                recurrence_weight, input_gate_weight, conv_weight, conv_bias[:, None],
                recurrence_bias[:, None], input_gate_bias[:, None], decay_param[:, None],
            ],
            axis=1,
        ),
        "fsdp", axis=0, tiled=True,
    )
    out_whole = lax.all_gather(out_weight, "fsdp", axis=0, tiled=True)
    glu_whole = gather_columns([gate_weight, up_weight])
    down_whole = lax.all_gather(down_weight, "fsdp", axis=0, tiled=True)

    wr = block_diagonal(lru_params[:, :size], channels // size)
    wi = block_diagonal(lru_params[:, size : 2 * size], channels // size)
    vectors = lru_params[:, 2 * size :].astype(WIDE).T
    decay = vectors[7]
    par = jnp.concatenate([vectors[:7], -RATE_SCALE * jax.nn.softplus(-decay)[None]], axis=0)

    resid_in = tokens.reshape(positions, width).astype(WIDE)
    grad_low = cotangent.reshape(positions, width)
    normed_low = rms_scale(resid_in, mix_scale).astype(LOW)
    normed_all = lax.all_gather(normed_low, "seq", axis=0, tiled=True)
    grad_all = lax.all_gather(grad_low, "seq", axis=0, tiled=True)
    branch_x = dot(normed_all, in_whole[:, :channels]).astype(LOW)
    branch_pre = dot(normed_all, in_whole[:, channels:])
    branch_y = jax.nn.gelu(branch_pre)

    saved = mixer_forward(branch_x, wr, wi, par)
    states_f = saved[5][8:].astype(LOW).astype(WIDE)
    product = (states_f * branch_y).astype(LOW)
    mixed = lax.psum_scatter(
        dot(product, out_whole).astype(LOW), "seq", scatter_dimension=0, tiled=True
    )
    middle = resid_in + mixed.astype(WIDE)
    normed2_low = rms_scale(middle, mlp_scale).astype(LOW)
    normed2_all = lax.all_gather(normed2_low, "seq", axis=0, tiled=True)
    gate_whole, up_whole = glu_whole[:, :hidden_width], glu_whole[:, hidden_width:]
    gate_val = dot(normed2_all, gate_whole)
    up_val = dot(normed2_all, up_whole)
    hidden = (jax.nn.gelu(gate_val) * up_val).astype(LOW)
    fed = lax.psum_scatter(
        dot(hidden, down_whole).astype(LOW), "seq", scatter_dimension=0, tiled=True
    )
    result = middle + fed.astype(WIDE)

    hidden_grad = times_transpose(grad_all, down_whole)
    unused, pull_glu = jax.vjp(lambda first, second: jax.nn.gelu(first) * second, gate_val, up_val)
    gate_grad, up_grad = pull_glu(hidden_grad)
    gate_low, up_low = gate_grad.astype(LOW), up_grad.astype(LOW)
    normed2_grad = lax.psum_scatter(
        (times_transpose(gate_low, gate_whole) + times_transpose(up_low, up_whole)).astype(LOW),
        "seq", scatter_dimension=0, tiled=True,
    ).astype(WIDE)
    unused, pull_norm2 = jax.vjp(rms_scale, middle, mlp_scale)
    middle_part, mlp_gain_grad = pull_norm2(normed2_grad)
    middle_grad = grad_low.astype(WIDE) + middle_part
    mixed_all = lax.all_gather(middle_grad.astype(LOW), "seq", axis=0, tiled=True)

    product_grad = times_transpose(mixed_all, out_whole)
    states_grad = (product_grad * branch_y).astype(LOW)
    unused, pull_gelu = jax.vjp(jax.nn.gelu, branch_pre)
    (pre_grad,) = pull_gelu(product_grad * states_f)
    pre_low = pre_grad.astype(LOW)
    x_low, wr_grad, wi_grad, sums = mixer_backward(states_grad, branch_x, saved, wr, wi, par, size)

    normed_grad = lax.psum_scatter(
        (
            times_transpose(x_low, in_whole[:, :channels])
            + times_transpose(pre_low, in_whole[:, channels:])
        ).astype(LOW),
        "seq", scatter_dimension=0, tiled=True,
    ).astype(WIDE)
    unused, pull_norm = jax.vjp(rms_scale, resid_in, mix_scale)
    input_part, mix_gain_grad = pull_norm(normed_grad)
    input_grad = middle_grad + input_part

    down_grad = lax.psum_scatter(
        outer_sum(hidden, grad_all).astype(LOW), "fsdp", scatter_dimension=0, tiled=True
    ).astype(WIDE)
    glu_grad = jnp.concatenate(
        [outer_sum(normed2_all, gate_low), outer_sum(normed2_all, up_low)], axis=1
    )
    gate_w_grad, up_w_grad = scatter_columns(glu_grad, [hidden_width] * 2, rows)
    out_grad = lax.psum_scatter(
        outer_sum(product, mixed_all).astype(LOW), "fsdp", scatter_dimension=0, tiled=True
    ).astype(WIDE)
    in_grad = jnp.concatenate(
        [outer_sum(normed_all, x_low), outer_sum(normed_all, pre_low)], axis=1
    )
    lru_in_grad, gelu_in_grad = scatter_columns(in_grad, [channels] * 2, rows)
    small = jnp.concatenate(
        [
            wr_grad, wi_grad, sums[:7].T,
            (sums[7] * RATE_SCALE * jax.nn.sigmoid(-decay))[:, None],
        ],
        axis=1,
    )
    small = lax.psum_scatter(
        small.reshape(lax.axis_size("fsdp"), -1, small.shape[1]),
        "fsdp", scatter_dimension=0, tiled=False,
    )
    gain_parts = jnp.stack([mix_gain_grad, mlp_gain_grad]).reshape(2, -1, rows).transpose(1, 0, 2)
    gain_grads = lax.psum_scatter(
        gain_parts, ("seq", "fsdp"), scatter_dimension=0, tiled=False
    )
    first = 2 * size
    return (
        result.astype(LOW).reshape(tokens.shape),
        input_grad.astype(LOW).reshape(tokens.shape),
        gain_grads[0],
        lru_in_grad,
        gelu_in_grad,
        out_grad,
        small[:, first : first + 4],
        small[:, first + 4],
        small[:, :size],
        small[:, first + 5],
        small[:, size : 2 * size],
        small[:, first + 6],
        small[:, first + 7],
        gain_grads[1],
        gate_w_grad,
        up_w_grad,
        down_grad,
    )


def aligned(
    tokens, cotangent, mix_gain, lru_in_weight, gelu_in_weight, out_weight, conv_weight, conv_bias,
    recurrence_weight, recurrence_bias, input_gate_weight, input_gate_bias, decay_param, mlp_gain,
    gate_weight, up_weight, down_weight,
):
    positions, width = tokens.shape[1:]
    rows = lru_in_weight.shape[0]
    shards = lax.axis_size("seq")
    channels = lru_in_weight.shape[1] // shards
    hidden_width = gate_weight.shape[1] // shards
    size = recurrence_weight.shape[1]

    groups = lax.axis_size("fsdp")
    resid_in = tokens.reshape(positions, width).astype(WIDE)
    grad_low = cotangent.reshape(positions, width)

    def by_column(first, second):
        parts = [member.reshape(rows, shards, -1) for member in (first, second)]
        return jnp.concatenate(parts, axis=2).transpose(1, 0, 2)

    own_decay = decay_param.astype(WIDE)
    vecs = jnp.concatenate(
        [
            conv_weight.astype(WIDE).T,
            jnp.stack([conv_bias, recurrence_bias, input_gate_bias]).astype(WIDE),
            -RATE_SCALE * jax.nn.softplus(-own_decay)[None],
        ],
        axis=0,
    )
    gain_shard = jnp.pad(jnp.stack([mix_gain, mlp_gain]).astype(WIDE), ((0, 6), (0, 0)))
    tokens_low = tokens.reshape(positions, width)
    (
        normed, in_whole, ext, branch_pre, conv_low, recur_gate, input_gate, states, product, par, wr, wi,
        gains, glu_mine, out_whole, down_whole,
    ) = mix_in(
        tokens_low, by_column(lru_in_weight, gelu_in_weight), by_column(gate_weight, up_weight),
        out_weight, down_weight, jnp.concatenate([recurrence_weight, input_gate_weight], axis=1),
        vecs, gain_shard, groups,
    )
    out_whole = out_whole.reshape(-1, width)
    middle, middle_grad, mixed_low, mlp_sums, fed_own, fed_other, glu_grad, down_grad = feed(
        product, out_whole, glu_mine, down_whole.reshape(-1, width), grad_low, tokens_low, gains, groups
    )
    down_grad = down_grad.reshape(groups, -1, width)
    (
        result, tokens_grad, glu_out, in_out, out_heard, small_heard, gain_out, unused, unused, down_heard,
    ) = back(
        mixed_low, fed_own, fed_other, middle, middle_grad, tokens_low, gains, par, wr, wi,
        out_whole, in_whole, normed, product, ext, branch_pre, conv_low, recur_gate, input_gate, states,
        glu_grad, down_grad, mlp_sums, size,
    )
    small_rows = recurrence_weight.shape[0]
    mine = jnp.arange(groups)[:, None, None] == lax.axis_index("fsdp")
    down_heard = jnp.where(mine, down_grad, down_heard)

    def rows_of(parts, first, size):
        return parts[:, :, first : first + size].astype(WIDE).transpose(1, 0, 2).reshape(rows, -1)

    small = jnp.sum(small_heard, axis=0)
    vector_sums = small[small_rows:, :small_rows]
    gain_grads = jnp.sum(gain_out, axis=0)
    return (
        result.reshape(tokens.shape),
        tokens_grad.reshape(tokens.shape),
        gain_grads[0],
        rows_of(in_out, 0, channels),
        rows_of(in_out, channels, channels),
        jnp.sum(out_heard.astype(WIDE), axis=0),
        vector_sums[:4].T,
        vector_sums[4],
        small[:small_rows, :size],
        vector_sums[5],
        small[:small_rows, size : 2 * size],
        vector_sums[6],
        vector_sums[7] * RATE_SCALE * jax.nn.sigmoid(-own_decay),
        gain_grads[1],
        rows_of(glu_out, 0, hidden_width),
        rows_of(glu_out, hidden_width, hidden_width),
        jnp.sum(down_heard.astype(WIDE), axis=0),
    )


def solution(mesh):
    shards, groups = mesh.shape["seq"], mesh.shape["fsdp"]

    def local(*arrays):
        rows, small_rows = arrays[3].shape[0], arrays[5].shape[0]
        simple = shards % 2 == 0 and rows % 16 == 0 and small_rows % 16 == 0
        simple = simple and arrays[0].shape[1] * shards % (8 * CHUNK) == 0
        return (aligned if simple else general)(*arrays)

    tokens = P("fsdp", "seq", None)
    vector = P(("seq", "fsdp"))
    matrix = P(("seq", "fsdp"), None)
    ranks = (1, 2, 2, 2, 2, 1, 2, 1, 2, 1, 1, 1, 2, 2, 2)
    specs = (tokens, tokens) + tuple(vector if rank == 1 else matrix for rank in ranks)
    return jax.shard_map(local, mesh=mesh, in_specs=specs, out_specs=specs, check_vma=False)
```

```python
import functools

import jax
import jax.numpy as jnp
from jax import lax
from jax.experimental import pallas as pl
from jax.experimental.pallas import tpu as pltpu
from jax.sharding import PartitionSpec as P

EPSILON = 1e-06
RATE_SCALE = 8.0
CHUNK = 128
LOW = jnp.bfloat16
WIDE = jnp.float32


def rms_scale(values, gain):
    scale = lax.rsqrt(jnp.mean(values * values, axis=-1, keepdims=True) + EPSILON)
    return values * scale * gain


def dot(left, right):
    return jnp.dot(left, right, preferred_element_type=WIDE)


def outer_sum(left, right):
    return lax.dot_general(left, right, (((0,), (0,)), ((), ())), preferred_element_type=WIDE)


def times_transpose(left, right):
    return lax.dot_general(left, right, (((1,), (1,)), ((), ())), preferred_element_type=WIDE)


def one_minus_exp(value):
    series = jnp.full_like(value, 1.0 / 40320.0)
    for bottom in (5040.0, 720.0, 120.0, 24.0, 6.0, 2.0, 1.0):
        series = 1.0 / bottom - value * series
    return jnp.where(value < 0.4, value * series, 1.0 - jnp.exp(-value))


def sigmoid(value):
    return 0.5 * jnp.tanh(0.5 * value) + 0.5


def lane_tiles(channels):
    return -(-channels // 128)


def put(tiles, rows, value):
    channels = value.shape[1]
    for n in range(lane_tiles(channels)):
        size = min(128, channels - n * 128)
        tiles[n, rows, 0:size] = value[:, n * 128 : n * 128 + size]


def get(tiles, rows, channels):
    return jnp.concatenate(
        [
            tiles[n, rows, 0 : min(128, channels - n * 128)]
            for n in range(lane_tiles(channels))
        ],
        axis=1,
    )


def scan_segments(step, count, tiles):
    def body(i, carried):
        return tuple(step(i, n, *carried[n]) for n in range(tiles))

    start = (jnp.zeros((8, 128), WIDE), jnp.ones((8, 128), WIDE))
    ends = lax.fori_loop(0, count, body, (start,) * tiles, unroll=4)
    return [jnp.concatenate([end[which] for end in ends], axis=1) for which in (0, 1)]


MESH = pl.DeviceIdType.MESH
VMEM_BYTES = 61 * 2**20
ANY = pl.BlockSpec(memory_space=pl.ANY)
HELD = pl.BlockSpec(memory_space=pltpu.VMEM)
ROOT = 0.7978845608028654
CUBE = 0.044715


def dma(*shape):
    return pltpu.SemaphoreType.DMA(shape)


def remote(src, dst, send, recv, axis, index):
    return pltpu.make_async_remote_copy(
        src_ref=src, dst_ref=dst, send_sem=send, recv_sem=recv,
        device_id={axis: index}, device_id_type=MESH,
    )


def gelu(value):
    return 0.5 * value * (1.0 + jnp.tanh(ROOT * (value + CUBE * value * value * value)))


def gelu_and_slope(value):
    square = value * value
    bent = jnp.tanh(ROOT * (value + CUBE * square * value))
    half = 0.5 * (1.0 + bent)
    slope = half + 0.5 * value * (1.0 - bent * bent) * (ROOT * (1.0 + 3.0 * CUBE * square))
    return value * half, slope


class Place:
    def __init__(self, shards, groups):
        self.shards, self.groups, self.line = shards, groups, shards // 2
        self.s, self.f = lax.axis_index("seq"), lax.axis_index("fsdp")
        self.z, self.c = self.s // 2, lax.rem(self.s, 2)
        self.sibling = 2 * self.z + 1 - self.c

    def nearest(self, n):
        chip = 0
        for z in range(self.line):
            for place, other in enumerate(sorted(range(self.line), key=lambda y: abs(y - z))):
                chip = jnp.where((self.z == z) & (n == place), other, chip)
        return chip

    def enter(self, seq=True, fsdp=True):
        barrier = pltpu.get_barrier_semaphore()
        met = 0
        for axis, mine, count, wanted in (
            ("seq", self.s, self.shards, seq), ("fsdp", self.f, self.groups, fsdp),
        ):
            for d in range(1, count if wanted else 1):
                pl.semaphore_signal(
                    barrier, inc=1, device_id={axis: lax.rem(mine + d, count)}, device_id_type=MESH
                )
                met += 1
        pl.semaphore_wait(barrier, met)


class Spread:
    def __init__(self, at, src, dst, send, recv, axis="fsdp"):
        self.at, self.src, self.dst, self.send, self.recv, self.axis = at, src, dst, send, recv, axis
        self.mine, self.count = (at.f, at.groups) if axis == "fsdp" else (at.s, at.shards)

    def copy(self, d):
        peer = lax.rem(self.mine + d, self.count)
        return remote(
            self.src(peer), self.dst(self.mine), self.send.at[d], self.recv.at[d], self.axis, peer
        )

    def start(self):
        for d in range(1, self.count):
            self.copy(d).start()

    def source(self, d):
        return lax.rem(self.mine + self.count - d, self.count)

    def arrive(self, d):
        origin = self.source(d)
        remote(
            self.src(origin), self.dst(origin), self.send.at[d], self.recv.at[d], self.axis, origin
        ).wait_recv()

    def sent(self):
        for d in range(1, self.count):
            self.copy(d).wait_send()

    def finish(self):
        for d in range(1, self.count):
            self.arrive(d)
        self.sent()


class LineGather:
    def __init__(self, at, src, buf, send, recv, pieces):
        self.at, self.src, self.buf, self.send, self.recv, self.pieces = at, src, buf, send, recv, pieces
        self.rows = buf.shape[1] // pieces

    def copy(self, slot, piece, kind, first=False):
        at = self.at
        rows = pl.ds(piece * self.rows, self.rows)
        there = self.buf.at[slot, rows]
        peer = (at.sibling, at.s + 2, at.s - 2)[kind]
        return remote(
            self.src.at[rows] if first else there, there,
            self.send.at[slot, piece, kind], self.recv.at[slot, piece], "seq", peer,
        )

    def start(self, first=0, last=None):
        at = self.at
        for piece in range(first, self.pieces if last is None else last):
            @pl.when(at.z + 1 < at.line)
            def _():
                self.copy(at.s, piece, 1, True).start()

            @pl.when(at.z > 0)
            def _():
                self.copy(at.s, piece, 2, True).start()

            self.copy(at.s, piece, 0, True).start()

    def arrive(self, chip, piece):
        at = self.at
        slot = 2 * chip + at.c
        self.copy(slot, piece, 0).wait_recv()

        @pl.when((chip < at.z) & (at.z + 1 < at.line))
        def _():
            self.copy(slot, piece, 1).start()

        @pl.when((chip > at.z) & (at.z > 0))
        def _():
            self.copy(slot, piece, 2).start()

        self.copy(slot, piece, 0).start()

    def settle(self, chip):
        for piece in range(self.pieces):
            self.copy(2 * chip + 1 - self.at.c, piece, 0).wait_recv()

    def pass_on(self, d):
        at = self.at
        for piece in range(self.pieces):
            for chip, known in ((at.z - d, at.z - d >= 0), (at.z + d, at.z + d < at.line)):
                @pl.when(known)
                def _():
                    self.arrive(chip, piece)

    def distances(self, body, beside=None):
        at = self.at

        @pl.loop(0, at.line)
        def _(n):
            @pl.when(n > 0)
            def _():
                self.pass_on(n)
                if beside is not None:
                    beside(n)

            chip = at.nearest(n)
            self.settle(chip)
            body(chip)

    def sent(self):
        at = self.at
        for chip in range(at.line):
            slot = 2 * chip + at.c
            for piece in range(self.pieces):
                self.copy(slot, piece, 0).wait_send()

                @pl.when((chip <= at.z) & (at.z + 1 < at.line))
                def _():
                    self.copy(slot, piece, 1).wait_send()

                @pl.when((chip >= at.z) & (at.z > 0))
                def _():
                    self.copy(slot, piece, 2).wait_send()


class LineScatter:
    def __init__(self, at, parts, heard, into, sems, pieces):
        self.at, self.parts, self.heard, self.into = at, parts, heard, into
        self.sib_send, self.sib_recv, self.send, self.recv = sems
        self.pieces = pieces
        self.rows = parts.shape[2] // pieces

    @staticmethod
    def scratch(line, rows, width, pieces):
        low = pltpu.VMEM((line, rows, width), LOW)
        return [
            pltpu.VMEM((line, 2, rows, width), LOW), low, low,
            dma(line), dma(line), dma(line, pieces), dma(line, pieces),
        ]

    def across(self, chip):
        return remote(
            self.parts.at[chip, 1 - self.at.c], self.heard.at[chip], self.sib_send.at[chip],
            self.sib_recv.at[chip], "seq", self.at.sibling,
        )

    def whole_way(self, chip, start):
        if self.at.line < 4:
            return False
        return jnp.abs(chip - start) == self.at.line - 1

    def joined(self, chip):
        at = self.at
        if at.line < 4:
            return False
        return ((at.z == 1) & (chip == at.line - 1)) | ((at.z == at.line - 2) & (chip == 0))

    def along(self, chip, piece):
        at = self.at
        rows = pl.ds(pl.multiple_of(piece * self.rows, self.rows), self.rows)
        target, slot = chip, at.z
        if at.line >= 4:
            stop = jnp.where(chip > at.z, at.z + 1, at.z - 1)
            target = jnp.where(self.whole_way(chip, at.z), stop, chip)
            slot = jnp.where(self.whole_way(chip, at.z), stop, at.z)
        return remote(
            self.parts.at[chip, 1 - at.c, rows], self.into.at[slot, rows], self.send.at[chip, piece],
            self.recv.at[slot, piece], "seq", 2 * target + at.c,
        )

    def landed(self, slot, piece):
        rows = pl.ds(pl.multiple_of(piece * self.rows, self.rows), self.rows)
        there = self.into.at[slot, rows]
        remote(
            there, there, self.recv.at[slot, piece], self.recv.at[slot, piece], "seq", self.at.sibling
        ).wait_recv()

    def add(self, chip, piece, extras, store):
        @pl.loop(0, self.rows // 16)
        def _(block):
            rows = pl.ds(pl.multiple_of(piece * self.rows + block * 16, 16), 16)
            total = self.parts[chip, self.at.c, rows, :].astype(WIDE) + self.heard[chip, rows, :].astype(WIDE)
            for known, slot in extras:
                here = self.into[slot, rows, :].astype(WIDE)
                total = total + (here if known is True else jnp.where(known, here, 0.0))
            store(rows, total)

    def store_out(self, chip):
        def store(rows, total):
            self.parts[chip, 1 - self.at.c, rows, :] = total.astype(LOW)

        return store

    def goes(self, chip):
        goes = chip != self.at.z
        return goes & jnp.logical_not(self.joined(chip)) if self.at.line >= 4 else goes

    def push(self, chip, first=0, last=None):
        @pl.when(self.goes(chip))
        def _():
            if first == 0:
                self.across(chip).wait()

            @pl.loop(first, self.pieces if last is None else last)
            def _(piece):
                self.add(chip, piece, [], self.store_out(chip))
                self.along(chip, piece).start()

    def join(self, first=0, last=None):
        at = self.at
        if at.line < 4:
            return

        @pl.when((at.z == 1) | (at.z == at.line - 2))
        def _():
            chip = jnp.where(at.z == 1, at.line - 1, 0)
            if first == 0:
                self.across(chip).wait()

            @pl.loop(first, self.pieces if last is None else last)
            def _(piece):
                self.landed(at.z, piece)
                self.add(chip, piece, [(True, at.z)], self.store_out(chip))
                self.along(chip, piece).start()

    def finish(self, store, first=0, last=None):
        at = self.at
        if first == 0:
            self.across(at.z).wait_recv()

        def known(chip):
            heard = chip != at.z
            return heard & jnp.logical_not(self.whole_way(chip, at.z)) if at.line >= 4 else heard

        @pl.loop(first, self.pieces if last is None else last)
        def _(piece):
            for chip in range(at.line):
                @pl.when(known(chip))
                def _():
                    self.landed(chip, piece)

            self.add(at.z, piece, [(known(chip), chip) for chip in range(at.line)], store)

    def sent(self):
        at = self.at
        self.across(at.z).wait_send()
        for chip in range(at.line):
            @pl.when(chip != at.z)
            def _():
                @pl.loop(0, self.pieces)
                def _(piece):
                    self.along(chip, piece).wait_send()


def normalise(source, gain, store, rows):
    @pl.loop(0, rows // 16)
    def _(block):
        here = pl.ds(pl.multiple_of(block * 16, 16), 16)
        values = source(here)
        scale = lax.rsqrt(jnp.mean(values * values, axis=-1, keepdims=True) + EPSILON)
        store(here, (values * scale * gain).astype(LOW))


def mixer_rows(positions):
    return [pl.ds(pl.multiple_of(n, CHUNK), CHUNK) for n in range(0, positions, CHUNK)]


def mix_in_kernel(
    tokens, lru_rows, gelu_rows, gate_rows, up_rows, out_shard, down_shard, gate_block, input_block,
    vecs, gain_shard,
    normed_far, in_far, ext_far, pre_far, conv_far, r_far, i_far, st_far,
    product_far, par_ref, wr_ref, wi_ref, gains, glu_mine, out_whole, down_whole,
    normed, in_whole, ext, pre_ref, conv_ref, r_ref, i_ref, st_ref, product_ref,
    in_shard, glu_shard, small, held, small_all, vecs_all, gain_all, factors, drive, prod,
    local_sems, tok_send, tok_recv, in_sems, in_xy_send, in_xy_recv, glu_sems, xy_sems, gain_sems, leave_sems,
):
    groups, shards = in_whole.shape[1], in_whole.shape[0]
    at = Place(shards, groups)
    s, f = at.s, at.f
    positions, channels = pre_ref.shape
    width = tokens.shape[1]
    rows = in_shard.shape[1]
    segment = positions // 8
    chunks = positions // CHUNK

    units = gate_rows.shape[1] // shards
    for shard in range(shards):
        part = slice(shard * units, (shard + 1) * units)
        glu_shard[shard, :, :units] = gate_rows[:, part]
        glu_shard[shard, :, units:] = up_rows[:, part]
        part = slice(shard * channels, (shard + 1) * channels)
        in_shard[shard, :, :channels] = lru_rows[:, part]
        in_shard[shard, :, channels:] = gelu_rows[:, part]
    size = gate_block.shape[1]
    small[:, :size] = gate_block[...]
    small[:, size:] = input_block[...]
    leaving = [
        (normed, normed_far), (in_whole, in_far), (ext, ext_far), (pre_ref, pre_far), (conv_ref, conv_far),
        (r_ref, r_far), (i_ref, i_far), (st_ref, st_far), (product_ref, product_far),
    ]
    leaving = [pltpu.make_async_copy(a, b, leave_sems.at[n]) for n, (a, b) in enumerate(leaving)]
    keep = [
        (tokens, held.at[s]), (in_shard.at[s], in_whole.at[s, f]), (glu_shard.at[s], glu_mine.at[s]),
        (out_shard, out_whole.at[f]), (down_shard, down_whole.at[f]), (small, small_all.at[f]),
        (vecs, vecs_all.at[f]), (gain_shard, gain_all.at[s, f]),
    ]
    keep = [pltpu.make_async_copy(a, b, local_sems.at[n]) for n, (a, b) in enumerate(keep)]
    for copy in keep:
        copy.start()
    at.enter()

    def over_fsdp(src, dst, n):
        return Spread(at, lambda peer: src, lambda origin: dst.at[origin], xy_sems.at[n, 0], xy_sems.at[n, 1])

    gain_xy = Spread(
        at, lambda peer: gain_shard, lambda origin: gain_all.at[s, origin],
        xy_sems.at[0, 0], xy_sems.at[0, 1],
    )
    small_xy = over_fsdp(small, small_all, 1)
    vecs_xy = over_fsdp(vecs, vecs_all, 2)
    out_xy = over_fsdp(out_shard, out_whole, 3)
    down_xy = over_fsdp(down_shard, down_whole, 4)
    in_z = Spread(
        at, lambda peer: in_shard.at[peer], lambda origin: in_whole.at[origin, f],
        in_sems.at[0], in_sems.at[1], "seq",
    )
    glu_z = Spread(
        at, lambda peer: glu_shard.at[peer], lambda origin: glu_mine.at[origin],
        glu_sems.at[0], glu_sems.at[1], "seq",
    )
    gain_z = Spread(
        at, lambda peer: gain_all.at[s], lambda origin: gain_all.at[origin],
        gain_sems.at[0], gain_sems.at[1], "seq",
    )

    def in_xy(index):
        return Spread(
            at, lambda peer: in_whole.at[index, f], lambda origin: in_whole.at[index, origin],
            in_xy_send.at[index], in_xy_recv.at[index],
        )

    gather = LineGather(at, tokens, held, tok_send, tok_recv, tok_send.shape[1])
    gain_xy.start()
    in_z.start()
    keep[1].wait()
    in_xy(s).start()
    gather.start()
    vecs_xy.start()
    small_xy.start()
    keep[7].wait()
    gain_xy.finish()
    gain_z.start()
    for d in range(1, shards):
        in_z.arrive(d)
        in_xy(in_z.source(d)).start()
    out_xy.start()
    glu_z.start()
    down_xy.start()
    gain_z.finish()
    for origin in range(shards):
        for other in range(groups):
            first = (origin * groups + other) * rows
            gains[:, first : first + rows] = gain_all[origin, other]
    keep[0].wait()

    def take(chip):
        for core in range(2):
            slot = 2 * chip + core

            def store(here, value):
                normed[slot, here, :] = value

            normalise(
                lambda here: held[slot, here, :].astype(WIDE), gains[0:1, :], store, tokens.shape[0]
            )

    gather.distances(take)
    leaving[0].start()
    keep[6].wait()
    vecs_xy.finish()
    keep[5].wait()
    small_xy.finish()
    local = small.shape[0]
    wr_ref[...] = jnp.zeros_like(wr_ref)
    wi_ref[...] = jnp.zeros_like(wi_ref)
    flat = small_all[...].reshape(channels, 2 * size)
    for n in range(channels // size):
        block = slice(n * size, (n + 1) * size)
        wr_ref[block, block] = flat[block, :size]
        wi_ref[block, block] = flat[block, size:]
    for other in range(groups):
        par_ref[:, other * local : (other + 1) * local] = vecs_all[other]
    ext[0:8, :] = jnp.zeros((8, channels), WIDE)
    st_ref[0:8, :] = jnp.zeros((8, channels), WIDE)
    for index in range(shards):
        for d in range(1, groups):
            in_xy(index).arrive(d)
    leaving[1].start()
    @pl.loop(0, at.line)
    def _(chip):
        pair = normed[pl.ds(2 * chip, 2), :, :].reshape(2 * tokens.shape[0], width)
        both = dot(pair, in_whole[...].reshape(width, 2 * channels))
        base = pl.multiple_of(chip * 2 * tokens.shape[0], CHUNK)
        here = pl.ds(base, 2 * tokens.shape[0])
        ext[pl.ds(base + 8, 2 * tokens.shape[0]), :] = both[:, :channels].astype(LOW).astype(WIDE)
        pre_ref[here, :] = both[:, channels:]

    @pl.loop(0, chunks)
    def _(n):
        base = pl.multiple_of(n * CHUNK, CHUNK)
        here = pl.ds(base, CHUNK)
        block = ext[pl.ds(base, CHUNK + 8), :]
        conv = jnp.broadcast_to(par_ref[4:5, :], (CHUNK, channels))
        for k in range(4):
            conv = conv + par_ref[k : k + 1, :] * block[8 - k : 8 - k + CHUNK]
        conv_low = conv.astype(LOW)
        conv_ref[here, :] = conv_low
        r = jax.nn.sigmoid(dot(conv_low, wr_ref[...]) + par_ref[5:6, :])
        gate = jax.nn.sigmoid(dot(conv_low, wi_ref[...]) + par_ref[6:7, :])
        log_decay = r * par_ref[7:8, :]
        m = jnp.sqrt(one_minus_exp(-2.0 * log_decay))
        factor = jnp.exp(log_decay)
        r_ref[here, :] = r
        i_ref[here, :] = gate
        put(factors, here, factor)
        put(drive, here, m * gate * conv_low.astype(WIDE))

    for n in range(2, 7):
        leaving[n].start()

    def step(i, n, state, product):
        here = pl.ds(i, 8, stride=segment)
        factor = factors[n, here, :]
        state = factor * state + drive[n, here, :]
        product = factor * product
        drive[n, here, :] = state
        prod[n, here, :] = product
        return state, product

    state, product = scan_segments(step, segment, lane_tiles(channels))
    state, product = state[:, :channels], product[:, :channels]
    carry = jnp.zeros((1, channels), WIDE)
    for k in range(8):
        for part in range(segment // CHUNK):
            base = k * segment + part * CHUNK
            here = slice(base, base + CHUNK)
            states = get(drive, here, channels) + get(prod, here, channels) * carry
            st_ref[base + 8 : base + 8 + CHUNK, :] = states
            product_ref[here, :] = (
                states.astype(LOW).astype(WIDE) * gelu(pre_ref[here, :])
            ).astype(LOW)
        carry = state[k : k + 1] + product[k : k + 1] * carry

    leaving[7].start()
    leaving[8].start()
    glu_z.finish()
    out_xy.finish()
    down_xy.finish()
    gather.sent()
    in_z.sent()
    for index in range(shards):
        in_xy(index).sent()
    for n in (2, 3, 4):
        keep[n].wait()
    for copy in leaving:
        copy.wait()


def mix_in(
    tokens, lru_rows, gelu_rows, gate_rows, up_rows, out_shard, down_shard, gate_block, input_block,
    vecs, gain_shard, shards, groups,
):
    rows = lru_rows.shape[0]
    block, width = tokens.shape
    positions, channels = shards * block, lru_rows.shape[1] // shards
    both = 2 * channels
    in_shape = (shards, rows, both)
    glu_shape = (shards, rows, 2 * (gate_rows.shape[1] // shards))
    small_shape = (gate_block.shape[0], 2 * gate_block.shape[1])
    pieces = 2
    wide = jax.ShapeDtypeStruct((positions, channels), WIDE)
    low = jax.ShapeDtypeStruct((positions, channels), LOW)
    longer = jax.ShapeDtypeStruct((positions + 8, channels), WIDE)
    square = jax.ShapeDtypeStruct((channels, channels), LOW)
    saved = [
        jax.ShapeDtypeStruct((shards, block, width), LOW),
        jax.ShapeDtypeStruct((shards, groups, rows, both), LOW),
        longer, wide, low, wide, wide, longer,
        low,
    ]
    held = [
        jax.ShapeDtypeStruct((8, channels), WIDE), square, square, jax.ShapeDtypeStruct((8, width), WIDE),
    ]
    far = [
        jax.ShapeDtypeStruct(glu_shape, LOW),
        jax.ShapeDtypeStruct((groups,) + out_shard.shape, LOW),
        jax.ShapeDtypeStruct((groups,) + down_shard.shape, LOW),
    ]
    return pl.pallas_call(
        mix_in_kernel,
        out_shape=saved + held + far,
        in_specs=[HELD] * 9 + [ANY] * 2,
        out_specs=[ANY] * len(saved) + [HELD] * len(held) + [ANY] * len(far),
        scratch_shapes=[pltpu.VMEM(member.shape, member.dtype) for member in saved]
        + [
            pltpu.VMEM(in_shape, LOW), pltpu.VMEM(glu_shape, LOW), pltpu.VMEM(small_shape, LOW),
            pltpu.VMEM((shards, block, width), LOW),
            pltpu.VMEM((groups,) + small_shape, LOW),
            pltpu.VMEM((groups,) + vecs.shape, WIDE),
            pltpu.VMEM((shards, groups) + gain_shard.shape, WIDE),
        ]
        + [pltpu.VMEM((lane_tiles(channels), positions, 128), WIDE)] * 3
        + [
            dma(8), dma(shards, pieces, 3), dma(shards, pieces), dma(2, shards), dma(shards, groups),
            dma(shards, groups), dma(2, shards), dma(5, 2, groups), dma(2, shards), dma(9),
        ],
        compiler_params=pltpu.CompilerParams(
            collective_id=1, has_side_effects=True, vmem_limit_bytes=VMEM_BYTES
        ),
        name="mix_in",
    )(
        tokens, lru_rows, gelu_rows, gate_rows, up_rows, out_shard, down_shard, gate_block, input_block,
        vecs, gain_shard,
    )


def feed_kernel(
    product_far, out_far, glu_mine, down_in, cotangent, tokens, gains,
    middle, middle_grad, mixed_low, gain_sums, hidden_far, glu_grad, down_grad,
    product, out_whole, held, cots, glu, down, both, hidden, wide_pair, hidden_pair, normed2, staged, down_staged,
    parts, heard, into, sib_send, sib_recv, line_send, line_recv,
    local_sems, glu_send, glu_recv, two_send, two_recv, cot_send, cot_recv, stage_sems,
):
    shards, groups = glu.shape[0], glu.shape[1]
    at = Place(shards, groups)
    s, f = at.s, at.f
    block, width = tokens.shape
    units = down.shape[0]
    pair = 2 * block

    keep = [(glu_mine, glu.at[:, f]), (down_in, down), (cotangent, cots.at[s])]
    keep += [(product_far, product), (out_far, out_whole)]
    keep = [pltpu.make_async_copy(a, b, local_sems.at[n]) for n, (a, b) in enumerate(keep)]
    for copy in keep:
        copy.start()
    at.enter()
    def glu_xy(index):
        return Spread(
            at, lambda peer: glu_mine.at[index], lambda origin: glu.at[index, origin],
            glu_send.at[index], glu_recv.at[index],
        )

    cot_z = LineGather(at, cotangent, cots, cot_send, cot_recv, cot_send.shape[1])
    two_z = LineGather(at, normed2, held, two_send, two_recv, two_send.shape[1])
    sums = LineScatter(
        at, parts, heard, into, (sib_send, sib_recv, line_send, line_recv), line_send.shape[1]
    )
    for index in range(shards):
        glu_xy(index).start()
    cot_z.start()

    def split(chip, columns, value, parts):
        parts[chip, :, :, columns] = value.astype(LOW).reshape(2, block, value.shape[1])

    def columns_of(j):
        return pl.ds(pl.multiple_of(j * 256, 256), 256)

    def pair_rows(chip):
        return pl.ds(pl.multiple_of(chip * pair, pair), pair)

    keep[3].wait()
    keep[4].wait()

    def project(chip):
        @pl.loop(0, width // 256)
        def _(j):
            value = dot(product[pair_rows(chip), :], out_whole[:, columns_of(j)])
            split(chip, columns_of(j), value, parts)

        sums.across(chip).start()

    for k in range(at.line // 2):
        project(at.line - 1 - k)
        project(k)
        sums.push(at.line - 1 - k, 0, 1)
        sums.push(k, 0, 1)
    for k in range(at.line // 2):
        sums.push(at.line - 1 - k, 1)
        sums.push(k, 1)
    sums.join(0, 1)
    cot_z.pass_on(1)

    def to_middle(here, total):
        values = total + tokens[here, :].astype(WIDE)
        middle[here, :] = values
        scale = lax.rsqrt(jnp.mean(values * values, axis=-1, keepdims=True) + EPSILON)
        normed2[here, :] = (values * scale * gains[1:2, :]).astype(LOW)

    sums.finish(to_middle, 0, 1)
    two_z.start(0, 1)
    cot_z.pass_on(2)
    sums.join(1)
    sums.finish(to_middle, 1)
    two_z.start(1)
    own_copy = pltpu.make_async_copy(normed2, held.at[s], local_sems.at[5])
    own_copy.start()
    keep[0].wait()
    keep[1].wait()
    keep[2].wait()
    sums.sent()
    own_copy.wait()
    for d in range(3, at.line):
        cot_z.pass_on(d)
    for index in range(shards):
        glu_xy(index).finish()

    def open_up(chip):
        rows = held[pl.ds(2 * chip, 2), :, :].reshape(pair, width)
        grads = cots[pl.ds(2 * chip, 2), :, :].reshape(pair, width)

        @pl.loop(0, 2 * units // 256)
        def _(j):
            wide_pair[:, columns_of(j)] = dot(
                rows, glu[:, :, :, columns_of(j)].reshape(width, 256)
            )

        @pl.loop(0, units // 256)
        def _(j):
            hidden_pair[:, columns_of(j)] = times_transpose(grads, down[columns_of(j), :])

        @pl.loop(0, pair // 16)
        def _(n):
            part = pl.ds(pl.multiple_of(n * 16, 16), 16)
            there = pl.ds(pl.multiple_of(chip * pair + n * 16, 16), 16)
            opened, slope = gelu_and_slope(wide_pair[part, :units])
            up = wide_pair[part, units:]
            grad = hidden_pair[part, :]
            hidden[there, :] = (opened * up).astype(LOW)
            both[there, :units] = (grad * up * slope).astype(LOW)
            both[there, units:] = (grad * opened).astype(LOW)

    def to_normed2(chip):
        @pl.loop(0, shards)
        def _(j):
            value = times_transpose(
                both[pair_rows(chip), :], glu[j].reshape(width // shards, 2 * units)
            )
            split(chip, columns_of(j), value, parts)

        sums.across(chip).start()

    cot_z.settle(at.z)
    two_z.settle(at.z)

    @pl.loop(1, at.line + 1)
    def _(n):
        chip = at.nearest(lax.rem(n, at.line))

        @pl.when(n < at.line)
        def _():
            two_z.pass_on(n)
            two_z.settle(chip)
            cot_z.settle(chip)

        open_up(chip)

        @pl.when(n > 1)
        def _():
            sums.push(at.nearest(n - 1))

        to_normed2(chip)

    hidden_leave = pltpu.make_async_copy(hidden, hidden_far, local_sems.at[6])
    hidden_leave.start()
    sums.join()

    def glu_out(j):
        return pltpu.make_async_copy(
            staged.at[lax.rem(j, 2)], glu_grad.at[:, j], stage_sems.at[lax.rem(j, 2)]
        )

    def glu_sums(first, last):
        @pl.loop(first, last)
        def _(j):
            @pl.when(j >= 2)
            def _():
                glu_out(j - 2).wait()

            rows = held[:, :, columns_of(j)].reshape(shards * block, 256)
            staged[lax.rem(j, 2)] = outer_sum(rows, both[...]).astype(LOW).reshape(staged.shape[1:])
            glu_out(j).start()

    def down_out(j):
        return pltpu.make_async_copy(
            down_staged.at[lax.rem(j, 2)], down_grad.at[columns_of(j)], stage_sems.at[2 + lax.rem(j, 2)]
        )

    def down_sums():
        @pl.loop(0, units // 256)
        def _(j):
            @pl.when(j >= 2)
            def _():
                down_out(j - 2).wait()

            grads = cots[...].reshape(shards * block, width)
            down_staged[lax.rem(j, 2)] = outer_sum(hidden[:, columns_of(j)], grads).astype(LOW)
            down_out(j).start()

    down_sums()
    glu_sums(0, shards)
    gain_sums[...] = jnp.zeros_like(gain_sums)

    def back(here, grad):
        values = middle[here, :]
        scale = lax.rsqrt(jnp.mean(values * values, axis=-1, keepdims=True) + EPSILON)
        scaled = grad * gains[1:2, :]
        along = jnp.mean(scaled * values, axis=-1, keepdims=True)
        total = cots[at.s, here, :].astype(WIDE) + scale * scaled - values * (scale * scale * scale * along)
        middle_grad[here, :] = total
        mixed_low[here, :] = total.astype(LOW)
        gain_sums[0:1, :] += jnp.sum(grad * values * scale, axis=0, keepdims=True)

    sums.finish(back)
    for j in range(shards - 2, shards):
        glu_out(j).wait()
    for j in range(max(units // 256 - 2, 0), units // 256):
        down_out(j).wait()
    hidden_leave.wait()
    sums.sent()
    two_z.sent()
    cot_z.sent()


def feed(product, out_whole, glu_mine, down_whole, cotangent, tokens, gains, groups):
    shards, rows, both = glu_mine.shape
    block, width = tokens.shape
    units = both // 2
    line, pieces, thirds = shards // 2, 2, 2
    own = jax.ShapeDtypeStruct((block, width), WIDE)
    outs = [
        own, own, jax.ShapeDtypeStruct((block, width), LOW), jax.ShapeDtypeStruct((8, width), WIDE),
        jax.ShapeDtypeStruct((shards * block, units), LOW),
        jax.ShapeDtypeStruct((groups, shards, rows, both), LOW),
        jax.ShapeDtypeStruct((units, width), LOW),
    ]
    gathered = pltpu.VMEM((shards, block, width), LOW)
    return pl.pallas_call(
        feed_kernel,
        out_shape=outs,
        in_specs=[ANY] * 5 + [HELD] * 2,
        out_specs=[HELD] * 4 + [ANY] * 3,
        scratch_shapes=[
            pltpu.VMEM(product.shape, LOW), pltpu.VMEM(out_whole.shape, LOW),
            gathered, gathered,
            pltpu.VMEM((shards, groups, rows, both), LOW),
            pltpu.VMEM((units, width), LOW),
            pltpu.VMEM((shards * block, both), LOW),
            pltpu.VMEM((shards * block, units), LOW),
            pltpu.VMEM((2 * block, both), WIDE),
            pltpu.VMEM((2 * block, units), WIDE),
            pltpu.VMEM((block, width), LOW),
            pltpu.VMEM((2, groups, rows, both), LOW),
            pltpu.VMEM((2, 256, width), LOW),
        ]
        + LineScatter.scratch(line, block, width, thirds)
        + [
            dma(8), dma(shards, groups), dma(shards, groups), dma(shards, pieces, 3), dma(shards, pieces),
            dma(shards, pieces, 3), dma(shards, pieces), dma(4),
        ],
        compiler_params=pltpu.CompilerParams(
            collective_id=2, has_side_effects=True, vmem_limit_bytes=VMEM_BYTES
        ),
        name="feed",
    )(product, out_whole, glu_mine, down_whole, cotangent, tokens, gains)


def back_kernel(
    mixed, hidden_far, down_far, middle_far, middle_grad_far, tokens_far, gains, par_ref, wr_ref, wi_ref,
    out_far, in_far, normed_far, product_far, ext_far, pre_far, conv_far, r_far, i_far, st_far,
    glu_grad, down_grad, mlp_parts,
    result, tokens_grad, glu_out, in_out, out_heard, small_heard, gain_out, glu_heard, in_grad, down_heard,
    middle, middle_grad, tokens, held, in_whole, out_whole, product, ext, pre, conv_ref, r_ref, i_ref, st_ref,
    both, pair_grad, staged, adj, totals_ref, wr_sum, wi_sum,
    out_sum, out_grad, small, gain_row, gain_parts, gain_heard, gain_sum, glu_parts, glu_sum, in_heard, in_sum,
    fed_parts, fed_heard, fed_into, fed_sib_send, fed_sib_recv, fed_send, fed_recv,
    parts, heard, into, sib_send, sib_recv, line_send, line_recv,
    local_sems, held_send, held_recv, glu_xy_sems, down_sems, stage_sems, in_xy_sems, out_sems,
    small_sems, gain_xy_sems, glu_sems, in_sems, gain_sems,
):
    shards, groups = in_whole.shape[0], in_whole.shape[1]
    at = Place(shards, groups)
    s, f = at.s, at.f
    block, width = tokens.shape
    positions, channels = product.shape
    rows = in_whole.shape[2]
    pair = 2 * block
    segment = positions // 8
    chunks = positions // CHUNK

    keep = [
        (mixed, held.at[s]), (out_far, out_whole), (pre_far, pre), (st_far, st_ref),
        (product_far, product), (r_far, r_ref), (i_far, i_ref), (conv_far, conv_ref),
        (ext_far, ext), (in_far, in_whole), (mixed, held.at[s]), (normed_far, held),
        (middle_far, middle), (middle_grad_far, middle_grad), (tokens_far, tokens),
    ]
    keep = [pltpu.make_async_copy(a, b, local_sems.at[n]) for n, (a, b) in enumerate(keep)]
    for copy in keep[:10] + keep[12:]:
        copy.start()
    at.enter()

    def over_fsdp(src, dst, sems):
        return Spread(
            at, lambda peer: src.at[peer], lambda origin: dst.at[origin], sems.at[0], sems.at[1]
        )

    def over_seq(src, dst, sems):
        return Spread(
            at, lambda peer: src.at[peer], lambda origin: dst.at[origin], sems.at[0], sems.at[1], "seq"
        )

    glu_xy = over_fsdp(glu_grad, glu_heard, glu_xy_sems)
    in_xy = over_fsdp(in_grad, in_heard, in_xy_sems)
    out_xy = over_fsdp(out_grad, out_heard, out_sems)
    down_xy = over_fsdp(down_grad, down_heard, down_sems)
    small_xy = over_fsdp(small, small_heard, small_sems)
    gain_xy = over_fsdp(gain_parts, gain_heard, gain_xy_sems)
    glu_z = over_seq(glu_sum, glu_out, glu_sems)
    in_z = over_seq(in_sum, in_out, in_sems)
    gain_z = over_seq(gain_sum, gain_out, gain_sems)
    mixed_z = LineGather(at, mixed, held, held_send, held_recv, held_send.shape[1])
    fed = LineScatter(
        at, fed_parts, fed_heard, fed_into,
        (fed_sib_send, fed_sib_recv, fed_send, fed_recv), fed_send.shape[1],
    )
    sums = LineScatter(
        at, parts, heard, into, (sib_send, sib_recv, line_send, line_recv), line_send.shape[1]
    )
    mixed_z.start()
    glu_xy.start()
    out_sum[...] = jnp.zeros_like(out_sum)

    def columns_of(j):
        return pl.ds(pl.multiple_of(j * 256, 256), 256)

    def feed_out(hidden, down, sems):
        loads = [
            pltpu.make_async_copy(hidden_far, hidden, sems.at[0]),
            pltpu.make_async_copy(down_far, down, sems.at[1]),
        ]
        for load in loads:
            load.start()
        for load in loads:
            load.wait()

        def one(chip):
            @pl.loop(0, width // 256)
            def _(j):
                there = pl.ds(pl.multiple_of(chip * pair, pair), pair)
                value = dot(hidden[there, :], down[:, columns_of(j)])
                fed_parts[chip, :, :, columns_of(j)] = value.astype(LOW).reshape(2, block, 256)

            fed.across(chip).start()

        for k in range(at.line // 2):
            one(at.line - 1 - k)
            one(k)

    pl.run_scoped(
        feed_out, pltpu.VMEM(hidden_far.shape, LOW), pltpu.VMEM(down_far.shape, LOW), dma(2)
    )
    for n in (0, 1, 2, 3, 4):
        keep[n].wait()

    def mixed_back(chip):
        rows = held[pl.ds(2 * chip, 2), :, :].reshape(pair, width)
        pair_grad[...] = times_transpose(rows, out_whole[...])

        @pl.loop(0, pair // 64)
        def _(n):
            grad = pair_grad[pl.ds(pl.multiple_of(n * 64, 64), 64), :]
            base = pl.multiple_of(chip * pair + n * 64, 64)
            here = pl.ds(base, 64)
            opened, slope = gelu_and_slope(pre[here, :])
            states = st_ref[pl.ds(base + 8, 64), :].astype(LOW).astype(WIDE)
            put(adj, here, (grad * opened).astype(LOW).astype(WIDE))
            both[here, channels:] = (grad * states * slope).astype(LOW)

        there = pl.ds(pl.multiple_of(chip * pair, pair), pair)

        @pl.loop(0, width // 256)
        def _(j):
            part = held[pl.ds(2 * chip, 2), :, columns_of(j)].reshape(pair, 256)
            out_sum[:, columns_of(j)] += outer_sum(product[there, :], part)

    def fed_beside(n):
        @pl.when(n == 2)
        def _():
            @pl.loop(1, at.line)
            def _(far):
                fed.push(at.nearest(at.line - far))

    mixed_z.distances(mixed_back, fed_beside)
    def mix_back(factors, prod, cg, carries):
        keep[5].wait()

        @pl.loop(0, chunks)
        def _(n):
            here = pl.ds(pl.multiple_of(n * CHUNK, CHUNK), CHUNK)
            put(factors, here, jnp.exp(r_ref[here, :] * par_ref[7:8, :]))

        def step(j, n, flow, product):
            here = pl.ds(segment - 1 - j, 8, stride=segment)
            factor = factors[n, here, :]
            adjoint = adj[n, here, :] + flow
            adj[n, here, :] = adjoint
            prod[n, here, :] = product
            return factor * adjoint, factor * product

        flow, through = scan_segments(step, segment, lane_tiles(channels))
        flow, through = flow[:, :channels], through[:, :channels]
        carry = jnp.zeros((1, channels), WIDE)
        for k in range(7, -1, -1):
            carries[k : k + 1, :] = carry
            carry = flow[k : k + 1] + through[k : k + 1] * carry
        for n in (6, 7, 8):
            keep[n].wait()
        cg[pl.ds(positions, 8), :] = jnp.zeros((8, channels), WIDE)
        wr_sum[...] = jnp.zeros_like(wr_sum)
        wi_sum[...] = jnp.zeros_like(wi_sum)

        def grads(c, sums):
            base = pl.multiple_of(c * CHUNK, CHUNK)
            rows = pl.ds(base, CHUNK)
            adjoint = get(adj, rows, channels) + get(prod, rows, channels) * carries[pl.ds(base // segment, 1), :]
            before = st_ref[pl.ds(base, CHUNK + 8), :][7 : 7 + CHUNK]
            conv_low = conv_ref[rows, :]
            conv = conv_low.astype(WIDE)
            r = r_ref[rows, :]
            gate = i_ref[rows, :]
            factor = get(factors, rows, channels)
            m = jnp.sqrt(one_minus_exp(-2.0 * (r * par_ref[7:8, :])))
            driven = adjoint * gate
            by_log = adjoint * before * factor - driven * conv * factor * factor / m
            by_r = by_log * par_ref[7:8, :] * r * (1.0 - r)
            by_i = adjoint * m * conv * gate * (1.0 - gate)
            by_r_low = by_r.astype(LOW)
            by_i_low = by_i.astype(LOW)
            conv_grad = (
                driven * m
                + times_transpose(by_r_low, wr_ref[...])
                + times_transpose(by_i_low, wi_ref[...])
            )
            cg[rows, :] = conv_grad
            wr_sum[...] += outer_sum(conv_low, by_r_low)
            wi_sum[...] += outer_sum(conv_low, by_i_low)
            near = ext[pl.ds(base, CHUNK + 8), :]
            rows_of = [conv_grad * near[8 - k : 8 - k + CHUNK] for k in range(4)]
            rows_of += [conv_grad, by_r, by_i, by_log * r]
            return tuple(
                total + jnp.sum(member, axis=0, keepdims=True) for total, member in zip(sums, rows_of)
            )

        zero = jnp.zeros((1, channels), WIDE)
        totals = lax.fori_loop(0, chunks, grads, (zero,) * 8)
        for k in range(8):
            totals_ref[k : k + 1, :] = totals[k]
        @pl.loop(0, chunks)
        def _(c):
            base = pl.multiple_of(c * CHUNK, CHUNK)
            near = cg[pl.ds(base, CHUNK + 8), :]
            total = jnp.zeros((CHUNK, channels), WIDE)
            for k in range(4):
                total = total + par_ref[k : k + 1, :] * near[k : k + CHUNK]
            both[pl.ds(base, CHUNK), :channels] = total.astype(LOW)

    tiles = pltpu.VMEM((lane_tiles(channels), positions, 128), WIDE)
    pl.run_scoped(
        mix_back, tiles, tiles, pltpu.VMEM((positions + 8, channels), WIDE), pltpu.VMEM((8, channels), WIDE)
    )
    fed.join()
    keep[9].wait()

    def project(chip):
        rows = both[pl.ds(pl.multiple_of(chip * pair, pair), pair), :]

        @pl.loop(0, shards)
        def _(j):
            value = times_transpose(rows, in_whole[j].reshape(width // shards, 2 * channels))
            parts[chip, :, :, columns_of(j)] = value.astype(LOW).reshape(2, block, value.shape[1])

        sums.across(chip).start()

    for k in range(at.line // 2):
        project(at.line - 1 - k)
        project(k)
        sums.push(at.line - 1 - k)
        sums.push(k)
    mixed_z.sent()
    keep[11].start()
    local = small.shape[1] - 8
    size = small.shape[2] // 2
    for n in range(channels // size):
        part = slice(n * size, (n + 1) * size)
        wr_sum[part, :size] = wr_sum[part, part]
        wi_sum[part, :size] = wi_sum[part, part]
    for group in range(groups):
        part = slice(group * local, (group + 1) * local)
        small[group, :local, :size] = wr_sum[part, :size]
        small[group, :local, size:] = wi_sum[part, :size]
        for k in range(8):
            small[group, local + k : local + k + 1, :local] = totals_ref[k : k + 1, part]
    small_xy.start()
    keep[11].wait()

    def in_done(j):
        return pltpu.make_async_copy(
            staged.at[lax.rem(j, 2)], in_grad.at[:, j], stage_sems.at[lax.rem(j, 2)]
        )

    @pl.loop(0, shards)
    def _(j):
        @pl.when(j >= 2)
        def _():
            in_done(j - 2).wait()

        part = held[:, :, columns_of(j)].reshape(positions, 256)
        staged[lax.rem(j, 2)] = outer_sum(part, both[...]).astype(LOW).reshape(staged.shape[1:])
        in_done(j).start()

    for j in range(shards - 2, shards):
        in_done(j).wait()
    in_xy.start()
    in_own = pltpu.make_async_copy(in_grad.at[f], in_heard.at[f], local_sems.at[16])
    in_own.start()
    sums.join()
    glu_xy.finish()

    def glu_load(d, origin):
        peer = lax.rem(s + d, shards)
        half = lax.rem(d, 2)
        return pltpu.make_async_copy(
            glu_heard.at[origin, peer], glu_parts.at[half, origin], glu_sems.at[2 + half, origin]
        )

    def glu_load_own(d):
        peer = lax.rem(s + d, shards)
        half = lax.rem(d, 2)
        return pltpu.make_async_copy(
            glu_grad.at[f, peer], glu_parts.at[half, f], glu_sems.at[2 + half, f]
        )

    def glu_loads(d):
        glu_load_own(d).start()
        for hop in range(1, groups):
            glu_load(d, lax.rem(f + hop, groups)).start()

    def add(parts, total, peer):
        @pl.loop(0, total.shape[1] // 16)
        def _(n):
            here = pl.ds(pl.multiple_of(n * 16, 16), 16)
            value = parts[0, here, :].astype(WIDE)
            for origin in range(1, groups):
                value = value + parts[origin, here, :].astype(WIDE)
            total[peer, here, :] = value.astype(total.dtype)

    glu_loads(1)

    @pl.loop(1, shards + 1)
    def _(d):
        @pl.when(d < shards)
        def _():
            glu_loads(d + 1)

        for origin in range(groups):
            glu_load(d, origin).wait()
        add(glu_parts.at[lax.rem(d, 2)], glu_sum, lax.rem(s + d, shards))

        @pl.when(d < shards)
        def _():
            glu_z.copy(d).start()

    glu_own = pltpu.make_async_copy(glu_sum.at[s], glu_out.at[s], local_sems.at[17])
    glu_own.start()
    out_grad[...] = out_sum[...].astype(LOW).reshape(out_grad.shape)
    out_xy.start()
    gain_row[...] = jnp.zeros_like(gain_row)

    for n in (12, 13, 14):
        keep[n].wait()

    def store_result(here, total):
        result[here, :] = (middle[here, :] + total).astype(LOW)

    fed.finish(store_result)

    def back(here, grad):
        values = tokens[here, :].astype(WIDE)
        scale = lax.rsqrt(jnp.mean(values * values, axis=-1, keepdims=True) + EPSILON)
        scaled = grad * gains[0:1, :]
        along = jnp.mean(scaled * values, axis=-1, keepdims=True)
        total = middle_grad[here, :] + scale * scaled - values * (scale * scale * scale * along)
        tokens_grad[here, :] = total.astype(LOW)
        gain_row[0:1, :] += jnp.sum(grad * values * scale, axis=0, keepdims=True)

    sums.finish(back)
    for group in range(groups):
        for shard in range(shards):
            first = (shard * groups + group) * rows
            gain_parts[group, shard, 0:1, :] = gain_row[0:1, first : first + rows]
            gain_parts[group, shard, 1:2, :] = mlp_parts[0:1, first : first + rows]
    gain_xy.start()
    in_own.wait()
    in_xy.finish()
    down_xy.start()

    @pl.loop(1, shards + 1)
    def _(d):
        peer = lax.rem(s + d, shards)
        add(in_heard.at[:, peer], in_sum, peer)

        @pl.when(d < shards)
        def _():
            in_z.copy(d).start()

    last = [
        pltpu.make_async_copy(in_sum.at[s], in_out.at[s], local_sems.at[18]),
        pltpu.make_async_copy(out_grad.at[f], out_heard.at[f], local_sems.at[19]),
        pltpu.make_async_copy(small.at[f], small_heard.at[f], local_sems.at[20]),
    ]
    for copy in last:
        copy.start()
    gain_xy.finish()
    total = gain_parts[f]
    for d in range(1, groups):
        total = total + gain_heard[lax.rem(f + d, groups)]
    gain_sum[...] = total
    gain_z.start()
    gain_own = pltpu.make_async_copy(gain_sum.at[s], gain_out.at[s], local_sems.at[21])
    gain_own.start()
    fed.sent()
    sums.sent()
    for spread in (small_xy, out_xy, down_xy, glu_z, gain_z, in_z):
        spread.finish()
    for copy in (glu_own, gain_own, *last):
        copy.wait()


def back(
    mixed, hidden, down_whole, middle, middle_grad, tokens, gains, par, wr, wi,
    out_whole, in_whole, normed, product, ext, pre, conv, r, i, st, glu_grad, down_grad, mlp_sums, size,
):
    shards, groups, rows, both = in_whole.shape
    block, width = tokens.shape
    positions, channels = product.shape
    line, pieces, halves = shards // 2, 2, 2
    local = channels // groups
    short = jax.ShapeDtypeStruct((block, width), LOW)
    glu_shape = glu_grad.shape[1:]
    in_shape = (groups, shards, rows, both)
    outs = [
        short, short, jax.ShapeDtypeStruct(glu_shape, LOW), jax.ShapeDtypeStruct(in_shape[1:], LOW),
        jax.ShapeDtypeStruct((groups, local, width), LOW),
        jax.ShapeDtypeStruct((groups, local + 8, 2 * size), WIDE),
        jax.ShapeDtypeStruct((shards, 8, rows), WIDE),
        jax.ShapeDtypeStruct(glu_grad.shape, LOW), jax.ShapeDtypeStruct(in_shape, LOW),
        jax.ShapeDtypeStruct(down_grad.shape, LOW),
    ]
    late = [middle, middle_grad, tokens]
    far = [out_whole, in_whole, normed, product, ext, pre, conv, r, i, st]
    near = [in_whole, out_whole, product, ext, pre, conv, r, i, st]
    return pl.pallas_call(
        back_kernel,
        out_shape=outs,
        in_specs=[ANY] * 6 + [HELD] * 4 + [ANY] * (len(far) + 2) + [HELD],
        out_specs=[HELD] * 2 + [ANY] * 8,
        scratch_shapes=[pltpu.VMEM(member.shape, member.dtype) for member in late]
        + [pltpu.VMEM((shards, block, width), LOW)]
        + [pltpu.VMEM(member.shape, member.dtype) for member in near]
        + [
            pltpu.VMEM((positions, 2 * channels), LOW),
            pltpu.VMEM((2 * block, channels), WIDE),
            pltpu.VMEM((2, groups, rows, both), LOW),
        ]
        + [pltpu.VMEM((lane_tiles(channels), positions, 128), WIDE), pltpu.VMEM((8, channels), WIDE)]
        + [pltpu.VMEM((channels, channels), WIDE)] * 2
        + [
            pltpu.VMEM((channels, width), WIDE),
            pltpu.VMEM((groups, local, width), LOW),
            pltpu.VMEM((groups, local + 8, 2 * size), WIDE),
            pltpu.VMEM((8, width), WIDE),
            pltpu.VMEM((groups, shards, 8, rows), WIDE),
            pltpu.VMEM((groups, shards, 8, rows), WIDE),
            pltpu.VMEM((shards, 8, rows), WIDE),
            pltpu.VMEM((2, groups) + glu_shape[1:], LOW),
            pltpu.VMEM(glu_shape, LOW),
            pltpu.VMEM(in_shape, LOW),
            pltpu.VMEM(in_shape[1:], LOW),
        ]
        + LineScatter.scratch(line, block, width, halves) * 2
        + [
            dma(22), dma(shards, pieces, 3), dma(shards, pieces), dma(2, groups), dma(2, groups), dma(2),
            dma(2, groups), dma(2, groups), dma(2, groups), dma(2, groups),
            dma(4, shards), dma(2, shards), dma(2, shards),
        ],
        compiler_params=pltpu.CompilerParams(
            collective_id=3, has_side_effects=True, vmem_limit_bytes=VMEM_BYTES
        ),
        name="back",
    )(
        mixed, hidden, down_whole, middle, middle_grad, tokens, gains, par, wr, wi, *far,
        glu_grad, down_grad, mlp_sums,
    )


def settle_kernel(
    glu_far, ins_far, outs_far, down_heard, down_grad,
    gate_far, up_far, lru_far, gelu_far, out_far, down_far,
    glu, ins, outs, parts, gate_sum, up_sum, lru_sum, gelu_sum, out_sum, down_sum, sems, leave_sems,
):
    shards, rows, both = glu.shape
    groups = outs.shape[0]
    units, channels = both // 2, ins.shape[2] // 2
    f = lax.axis_index("fsdp")
    keep = [(glu_far, glu), (ins_far, ins), (outs_far, outs), (down_grad.at[f], parts.at[f])]
    for hop in range(1, groups):
        origin = lax.rem(f + hop, groups)
        keep.append((down_heard.at[origin], parts.at[origin]))
    keep = [pltpu.make_async_copy(a, b, sems.at[n]) for n, (a, b) in enumerate(keep)]
    for copy in keep:
        copy.start()
    leaving = [
        (gate_sum, gate_far), (up_sum, up_far), (lru_sum, lru_far), (gelu_sum, gelu_far),
        (out_sum, out_far), (down_sum, down_far),
    ]
    leaving = [pltpu.make_async_copy(a, b, leave_sems.at[n]) for n, (a, b) in enumerate(leaving)]
    keep[0].wait()
    for half, whole in enumerate((gate_sum, up_sum)):
        for shard in range(shards):
            part = slice(half * units, (half + 1) * units)
            whole[:, shard * units : (shard + 1) * units] = glu[shard, :, part].astype(WIDE)
        leaving[half].start()
    keep[1].wait()
    for half, whole in enumerate((lru_sum, gelu_sum)):
        for shard in range(shards):
            part = slice(half * channels, (half + 1) * channels)
            whole[:, shard * channels : (shard + 1) * channels] = ins[shard, :, part].astype(WIDE)
        leaving[2 + half].start()

    def add(terms, total):
        @pl.loop(0, total.shape[0] // 16)
        def _(n):
            here = pl.ds(pl.multiple_of(n * 16, 16), 16)
            value = terms[0, here, :].astype(WIDE)
            for origin in range(1, groups):
                value = value + terms[origin, here, :].astype(WIDE)
            total[here, :] = value

    keep[2].wait()
    add(outs, out_sum)
    leaving[4].start()
    for copy in keep[3:]:
        copy.wait()
    add(parts, down_sum)
    leaving[5].start()
    for copy in leaving:
        copy.wait()


def settle(glu, ins, outs, down_heard, down_grad):
    shards, rows, both = glu.shape
    groups, local, width = outs.shape
    units, channels = both // 2, ins.shape[2] // 2
    shapes = [(rows, shards * units)] * 2 + [(rows, shards * channels)] * 2
    shapes += [(local, width), down_grad.shape[1:]]
    return pl.pallas_call(
        settle_kernel,
        out_shape=[jax.ShapeDtypeStruct(shape, WIDE) for shape in shapes],
        in_specs=[ANY] * 5,
        out_specs=[ANY] * 6,
        scratch_shapes=[pltpu.VMEM(member.shape, LOW) for member in (glu, ins, outs, down_grad)]
        + [pltpu.VMEM(shape, WIDE) for shape in shapes]
        + [dma(groups + 3), dma(6)],
        compiler_params=pltpu.CompilerParams(vmem_limit_bytes=VMEM_BYTES),
        name="settle",
    )(glu, ins, outs, down_heard, down_grad)


def mixer_forward_kernel(
    x_ref, wr_ref, wi_ref, par_ref,
    conv_ref, r_ref, i_ref, f_ref, m_ref, st_ref,
    ext, factors, drive, prod,
):
    positions, channels = x_ref.shape
    segment = positions // 8
    chunks = positions // CHUNK
    ext[0:8, :] = jnp.zeros((8, channels), WIDE)
    st_ref[0:8, :] = jnp.zeros((8, channels), WIDE)

    @pl.loop(0, chunks)
    def _(c):
        base = pl.multiple_of(c * CHUNK, CHUNK)
        ext[pl.ds(base + 8, CHUNK), :] = x_ref[pl.ds(base, CHUNK), :].astype(WIDE)

    @pl.loop(0, chunks)
    def _(c):
        base = pl.multiple_of(c * CHUNK, CHUNK)
        rows = pl.ds(base, CHUNK)
        block = ext[pl.ds(base, CHUNK + 8), :]
        conv = jnp.broadcast_to(par_ref[4:5, :], (CHUNK, channels))
        for k in range(4):
            conv = conv + par_ref[k : k + 1, :] * block[8 - k : 8 - k + CHUNK]
        conv_low = conv.astype(LOW)
        conv_ref[rows, :] = conv_low
        r = jax.nn.sigmoid(dot(conv_low, wr_ref[...]) + par_ref[5:6, :])
        gate = jax.nn.sigmoid(dot(conv_low, wi_ref[...]) + par_ref[6:7, :])
        log_decay = r * par_ref[7:8, :]
        m = jnp.sqrt(one_minus_exp(-2.0 * log_decay))
        r_ref[rows, :] = r
        i_ref[rows, :] = gate
        factor = jnp.exp(log_decay)
        f_ref[rows, :] = factor
        m_ref[rows, :] = m
        put(factors, rows, factor)
        put(drive, rows, m * gate * conv_low.astype(WIDE))

    def step(i, n, state, product):
        rows = pl.ds(i, 8, stride=segment)
        factor = factors[n, rows, :]
        state = factor * state + drive[n, rows, :]
        product = factor * product
        drive[n, rows, :] = state
        prod[n, rows, :] = product
        return state, product

    state, product = scan_segments(step, segment, lane_tiles(channels))
    state, product = state[:, :channels], product[:, :channels]
    carry = jnp.zeros((1, channels), WIDE)
    for k in range(8):
        for part in range(segment // CHUNK):
            base = k * segment + part * CHUNK
            rows = slice(base, base + CHUNK)
            st_ref[base + 8 : base + 8 + CHUNK, :] = (
                get(drive, rows, channels) + get(prod, rows, channels) * carry
            )
        carry = state[k : k + 1] + product[k : k + 1] * carry


def mixer_backward_kernel(
    ds_ref, x_ref, conv_ref, r_ref, i_ref, f_ref, m_ref, st_ref, wr_ref, wi_ref, par_ref,
    xg_ref, wrg_ref, wig_ref, sums_ref,
    ext, factors, adj, prod, cg, carries, wr_sum, wi_sum,
):
    positions, channels = x_ref.shape
    segment = positions // 8
    chunks = positions // CHUNK
    ext[0:8, :] = jnp.zeros((8, channels), WIDE)
    cg[pl.ds(positions, 8), :] = jnp.zeros((8, channels), WIDE)
    wr_sum[...] = jnp.zeros_like(wr_sum)
    wi_sum[...] = jnp.zeros_like(wi_sum)

    @pl.loop(0, chunks)
    def _(c):
        base = pl.multiple_of(c * CHUNK, CHUNK)
        ext[pl.ds(base + 8, CHUNK), :] = x_ref[pl.ds(base, CHUNK), :].astype(WIDE)
        put(adj, pl.ds(base, CHUNK), ds_ref[pl.ds(base, CHUNK), :].astype(WIDE))
        put(factors, pl.ds(base, CHUNK), f_ref[pl.ds(base, CHUNK), :])

    def step(j, n, flow, product):
        rows = pl.ds(segment - 1 - j, 8, stride=segment)
        factor = factors[n, rows, :]
        adjoint = adj[n, rows, :] + flow
        adj[n, rows, :] = adjoint
        prod[n, rows, :] = product
        return factor * adjoint, factor * product

    flow, product = scan_segments(step, segment, lane_tiles(channels))
    flow, product = flow[:, :channels], product[:, :channels]
    carry = jnp.zeros((1, channels), WIDE)
    for k in range(7, -1, -1):
        carries[k : k + 1, :] = carry
        carry = flow[k : k + 1] + product[k : k + 1] * carry

    def grads(c, sums):
        base = pl.multiple_of(c * CHUNK, CHUNK)
        rows = pl.ds(base, CHUNK)
        adjoint = get(adj, rows, channels) + get(prod, rows, channels) * carries[pl.ds(base // segment, 1), :]
        before = st_ref[pl.ds(base, CHUNK + 8), :][7 : 7 + CHUNK]
        conv_low = conv_ref[rows, :]
        conv = conv_low.astype(WIDE)
        r = r_ref[rows, :]
        gate = i_ref[rows, :]
        factor = f_ref[rows, :]
        m = m_ref[rows, :]
        driven = adjoint * gate
        by_log = adjoint * before * factor - driven * conv * factor * factor / m
        by_r = by_log * par_ref[7:8, :] * r * (1.0 - r)
        by_i = adjoint * m * conv * gate * (1.0 - gate)
        by_r_low = by_r.astype(LOW)
        by_i_low = by_i.astype(LOW)
        conv_grad = (
            driven * m
            + times_transpose(by_r_low, wr_ref[...])
            + times_transpose(by_i_low, wi_ref[...])
        )
        cg[rows, :] = conv_grad
        wr_sum[...] += outer_sum(conv_low, by_r_low)
        wi_sum[...] += outer_sum(conv_low, by_i_low)
        block = ext[pl.ds(base, CHUNK + 8), :]
        rows_of = [conv_grad * block[8 - k : 8 - k + CHUNK] for k in range(4)]
        rows_of += [conv_grad, by_r, by_i, by_log * r]
        return tuple(
            total + jnp.sum(member, axis=0, keepdims=True) for total, member in zip(sums, rows_of)
        )

    zero = jnp.zeros((1, channels), WIDE)
    sums = lax.fori_loop(0, chunks, grads, (zero,) * 8)
    for k in range(8):
        sums_ref[k : k + 1, :] = sums[k]
    size = wrg_ref.shape[1]
    for n in range(channels // size):
        block = slice(n * size, (n + 1) * size)
        wrg_ref[block, :] = wr_sum[block, block]
        wig_ref[block, :] = wi_sum[block, block]

    @pl.loop(0, chunks)
    def _(c):
        base = pl.multiple_of(c * CHUNK, CHUNK)
        block = cg[pl.ds(base, CHUNK + 8), :]
        total = jnp.zeros((CHUNK, channels), WIDE)
        for k in range(4):
            total = total + par_ref[k : k + 1, :] * block[k : k + CHUNK]
        xg_ref[pl.ds(base, CHUNK), :] = total.astype(LOW)


def mixer_forward(x, wr, wi, par):
    positions, channels = x.shape
    wide = jax.ShapeDtypeStruct((positions, channels), WIDE)
    return pl.pallas_call(
        mixer_forward_kernel,
        out_shape=(
            jax.ShapeDtypeStruct((positions, channels), LOW), wide, wide, wide, wide,
            jax.ShapeDtypeStruct((positions + 8, channels), WIDE),
        ),
        scratch_shapes=[pltpu.VMEM((positions + 8, channels), WIDE)]
        + [pltpu.VMEM((lane_tiles(channels), positions, 128), WIDE)] * 3,
        compiler_params=pltpu.CompilerParams(vmem_limit_bytes=48 * 2**20),
        name="mixer_forward",
    )(x, wr, wi, par)


def mixer_backward(ds, x, saved, wr, wi, par, size):
    positions, channels = x.shape
    square = jax.ShapeDtypeStruct((channels, size), WIDE)
    return pl.pallas_call(
        mixer_backward_kernel,
        out_shape=(
            jax.ShapeDtypeStruct((positions, channels), LOW), square, square,
            jax.ShapeDtypeStruct((8, channels), WIDE),
        ),
        scratch_shapes=[pltpu.VMEM((positions + 8, channels), WIDE)]
        + [pltpu.VMEM((lane_tiles(channels), positions, 128), WIDE)] * 3
        + [pltpu.VMEM((positions + 8, channels), WIDE), pltpu.VMEM((8, channels), WIDE)]
        + [pltpu.VMEM((channels, channels), WIDE)] * 2,
        compiler_params=pltpu.CompilerParams(vmem_limit_bytes=48 * 2**20),
        name="mixer_backward",
    )(ds, x, *saved, wr, wi, par)


def gather_columns(weights):
    shards = lax.axis_size("seq")
    rows = weights[0].shape[0]
    widths = [member.shape[1] // shards for member in weights]
    stacked = jnp.concatenate(
        [member.reshape(rows, shards, width) for member, width in zip(weights, widths)], axis=2
    )
    mine = lax.all_to_all(stacked.transpose(1, 0, 2), "seq", split_axis=0, concat_axis=0)
    whole = lax.all_gather(mine, "fsdp", axis=1)
    return whole.reshape(-1, sum(widths))


def scatter_columns(grad, widths, rows):
    shards, groups = lax.axis_size("seq"), lax.axis_size("fsdp")
    parts = grad.astype(LOW).reshape(shards, groups, rows, sum(widths)).transpose(1, 0, 2, 3)
    mine = lax.psum_scatter(parts, "fsdp", scatter_dimension=0, tiled=False)
    swapped = lax.all_to_all(mine, "seq", split_axis=0, concat_axis=0).astype(WIDE)
    outs, first = [], 0
    for width in widths:
        outs.append(swapped[:, :, first : first + width].transpose(1, 0, 2).reshape(rows, -1))
        first += width
    return outs


def block_diagonal(weight, blocks):
    size = weight.shape[1]
    shaped = weight.reshape(blocks, size, size)
    full = jnp.zeros((blocks, size, blocks, size), weight.dtype)
    for n in range(blocks):
        full = full.at[n, :, n, :].set(shaped[n])
    return full.reshape(blocks * size, blocks * size)


def general(
    tokens, cotangent, mix_gain, lru_in_weight, gelu_in_weight, out_weight, conv_weight, conv_bias,
    recurrence_weight, recurrence_bias, input_gate_weight, input_gate_bias, decay_param, mlp_gain,
    gate_weight, up_weight, down_weight,
):
    positions, width = tokens.shape[1:]
    rows = lru_in_weight.shape[0]
    shards = lax.axis_size("seq")
    channels = lru_in_weight.shape[1] // shards
    hidden_width = gate_weight.shape[1] // shards
    size = recurrence_weight.shape[1]

    gains = lax.all_gather(
        jnp.stack([mix_gain, mlp_gain], axis=1), ("seq", "fsdp"), axis=0, tiled=True
    ).astype(WIDE)
    mix_scale, mlp_scale = gains[:, 0], gains[:, 1]
    in_whole = gather_columns([lru_in_weight, gelu_in_weight])
    lru_params = lax.all_gather(
        jnp.concatenate(
            [
                recurrence_weight, input_gate_weight, conv_weight, conv_bias[:, None],
                recurrence_bias[:, None], input_gate_bias[:, None], decay_param[:, None],
            ],
            axis=1,
        ),
        "fsdp", axis=0, tiled=True,
    )
    out_whole = lax.all_gather(out_weight, "fsdp", axis=0, tiled=True)
    glu_whole = gather_columns([gate_weight, up_weight])
    down_whole = lax.all_gather(down_weight, "fsdp", axis=0, tiled=True)

    wr = block_diagonal(lru_params[:, :size], channels // size)
    wi = block_diagonal(lru_params[:, size : 2 * size], channels // size)
    vectors = lru_params[:, 2 * size :].astype(WIDE).T
    decay = vectors[7]
    par = jnp.concatenate([vectors[:7], -RATE_SCALE * jax.nn.softplus(-decay)[None]], axis=0)

    resid_in = tokens.reshape(positions, width).astype(WIDE)
    grad_low = cotangent.reshape(positions, width)
    normed_low = rms_scale(resid_in, mix_scale).astype(LOW)
    normed_all = lax.all_gather(normed_low, "seq", axis=0, tiled=True)
    grad_all = lax.all_gather(grad_low, "seq", axis=0, tiled=True)
    branch_x = dot(normed_all, in_whole[:, :channels]).astype(LOW)
    branch_pre = dot(normed_all, in_whole[:, channels:])
    branch_y = jax.nn.gelu(branch_pre)

    saved = mixer_forward(branch_x, wr, wi, par)
    states_f = saved[5][8:].astype(LOW).astype(WIDE)
    product = (states_f * branch_y).astype(LOW)
    mixed = lax.psum_scatter(
        dot(product, out_whole).astype(LOW), "seq", scatter_dimension=0, tiled=True
    )
    middle = resid_in + mixed.astype(WIDE)
    normed2_low = rms_scale(middle, mlp_scale).astype(LOW)
    normed2_all = lax.all_gather(normed2_low, "seq", axis=0, tiled=True)
    gate_whole, up_whole = glu_whole[:, :hidden_width], glu_whole[:, hidden_width:]
    gate_val = dot(normed2_all, gate_whole)
    up_val = dot(normed2_all, up_whole)
    hidden = (jax.nn.gelu(gate_val) * up_val).astype(LOW)
    fed = lax.psum_scatter(
        dot(hidden, down_whole).astype(LOW), "seq", scatter_dimension=0, tiled=True
    )
    result = middle + fed.astype(WIDE)

    hidden_grad = times_transpose(grad_all, down_whole)
    unused, pull_glu = jax.vjp(lambda first, second: jax.nn.gelu(first) * second, gate_val, up_val)
    gate_grad, up_grad = pull_glu(hidden_grad)
    gate_low, up_low = gate_grad.astype(LOW), up_grad.astype(LOW)
    normed2_grad = lax.psum_scatter(
        (times_transpose(gate_low, gate_whole) + times_transpose(up_low, up_whole)).astype(LOW),
        "seq", scatter_dimension=0, tiled=True,
    ).astype(WIDE)
    unused, pull_norm2 = jax.vjp(rms_scale, middle, mlp_scale)
    middle_part, mlp_gain_grad = pull_norm2(normed2_grad)
    middle_grad = grad_low.astype(WIDE) + middle_part
    mixed_all = lax.all_gather(middle_grad.astype(LOW), "seq", axis=0, tiled=True)

    product_grad = times_transpose(mixed_all, out_whole)
    states_grad = (product_grad * branch_y).astype(LOW)
    unused, pull_gelu = jax.vjp(jax.nn.gelu, branch_pre)
    (pre_grad,) = pull_gelu(product_grad * states_f)
    pre_low = pre_grad.astype(LOW)
    x_low, wr_grad, wi_grad, sums = mixer_backward(states_grad, branch_x, saved, wr, wi, par, size)

    normed_grad = lax.psum_scatter(
        (
            times_transpose(x_low, in_whole[:, :channels])
            + times_transpose(pre_low, in_whole[:, channels:])
        ).astype(LOW),
        "seq", scatter_dimension=0, tiled=True,
    ).astype(WIDE)
    unused, pull_norm = jax.vjp(rms_scale, resid_in, mix_scale)
    input_part, mix_gain_grad = pull_norm(normed_grad)
    input_grad = middle_grad + input_part

    down_grad = lax.psum_scatter(
        outer_sum(hidden, grad_all).astype(LOW), "fsdp", scatter_dimension=0, tiled=True
    ).astype(WIDE)
    glu_grad = jnp.concatenate(
        [outer_sum(normed2_all, gate_low), outer_sum(normed2_all, up_low)], axis=1
    )
    gate_w_grad, up_w_grad = scatter_columns(glu_grad, [hidden_width] * 2, rows)
    out_grad = lax.psum_scatter(
        outer_sum(product, mixed_all).astype(LOW), "fsdp", scatter_dimension=0, tiled=True
    ).astype(WIDE)
    in_grad = jnp.concatenate(
        [outer_sum(normed_all, x_low), outer_sum(normed_all, pre_low)], axis=1
    )
    lru_in_grad, gelu_in_grad = scatter_columns(in_grad, [channels] * 2, rows)
    small = jnp.concatenate(
        [
            wr_grad, wi_grad, sums[:7].T,
            (sums[7] * RATE_SCALE * jax.nn.sigmoid(-decay))[:, None],
        ],
        axis=1,
    )
    small = lax.psum_scatter(
        small.reshape(lax.axis_size("fsdp"), -1, small.shape[1]),
        "fsdp", scatter_dimension=0, tiled=False,
    )
    gain_parts = jnp.stack([mix_gain_grad, mlp_gain_grad]).reshape(2, -1, rows).transpose(1, 0, 2)
    gain_grads = lax.psum_scatter(
        gain_parts, ("seq", "fsdp"), scatter_dimension=0, tiled=False
    )
    first = 2 * size
    return (
        result.astype(LOW).reshape(tokens.shape),
        input_grad.astype(LOW).reshape(tokens.shape),
        gain_grads[0],
        lru_in_grad,
        gelu_in_grad,
        out_grad,
        small[:, first : first + 4],
        small[:, first + 4],
        small[:, :size],
        small[:, first + 5],
        small[:, size : 2 * size],
        small[:, first + 6],
        small[:, first + 7],
        gain_grads[1],
        gate_w_grad,
        up_w_grad,
        down_grad,
    )


def aligned(
    tokens, cotangent, mix_gain, lru_in_weight, gelu_in_weight, out_weight, conv_weight, conv_bias,
    recurrence_weight, recurrence_bias, input_gate_weight, input_gate_bias, decay_param, mlp_gain,
    gate_weight, up_weight, down_weight,
):
    positions, width = tokens.shape[1:]
    rows = lru_in_weight.shape[0]
    shards = lax.axis_size("seq")
    channels = lru_in_weight.shape[1] // shards
    hidden_width = gate_weight.shape[1] // shards
    size = recurrence_weight.shape[1]

    groups = lax.axis_size("fsdp")
    resid_in = tokens.reshape(positions, width).astype(WIDE)
    grad_low = cotangent.reshape(positions, width)

    own_decay = decay_param.astype(WIDE)
    vecs = jnp.concatenate(
        [
            conv_weight.astype(WIDE).T,
            jnp.stack([conv_bias, recurrence_bias, input_gate_bias]).astype(WIDE),
            -RATE_SCALE * jax.nn.softplus(-own_decay)[None],
        ],
        axis=0,
    )
    gain_shard = jnp.pad(jnp.stack([mix_gain, mlp_gain]).astype(WIDE), ((0, 6), (0, 0)))
    tokens_low = tokens.reshape(positions, width)
    (
        normed, in_whole, ext, branch_pre, conv_low, recur_gate, input_gate, states, product, par, wr, wi,
        gains, glu_mine, out_whole, down_whole,
    ) = mix_in(
        tokens_low, lru_in_weight, gelu_in_weight, gate_weight, up_weight, out_weight, down_weight,
        recurrence_weight, input_gate_weight, vecs, gain_shard, shards, groups,
    )
    out_whole, down_whole = out_whole.reshape(-1, width), down_whole.reshape(-1, width)
    middle, middle_grad, mixed_low, mlp_sums, hidden, glu_grad, down_grad = feed(
        product, out_whole, glu_mine, down_whole, grad_low, tokens_low, gains, groups
    )
    down_grad = down_grad.reshape(groups, -1, width)
    (
        result, tokens_grad, glu_out, in_out, out_heard, small_heard, gain_out, unused, unused, down_heard,
    ) = back(
        mixed_low, hidden, down_whole, middle, middle_grad, tokens_low, gains, par, wr, wi,
        out_whole, in_whole, normed, product, ext, branch_pre, conv_low, recur_gate, input_gate, states,
        glu_grad, down_grad, mlp_sums, size,
    )
    small_rows = recurrence_weight.shape[0]
    gate_sum, up_sum, lru_sum, gelu_sum, out_sum, down_sum = settle(
        glu_out, in_out, out_heard, down_heard, down_grad
    )
    small = jnp.sum(small_heard, axis=0)
    gain_grads = jnp.sum(gain_out, axis=0)
    vector_sums = small[small_rows:, :small_rows]
    return (
        result.reshape(tokens.shape),
        tokens_grad.reshape(tokens.shape),
        gain_grads[0],
        lru_sum,
        gelu_sum,
        out_sum,
        vector_sums[:4].T,
        vector_sums[4],
        small[:small_rows, :size],
        vector_sums[5],
        small[:small_rows, size : 2 * size],
        vector_sums[6],
        vector_sums[7] * RATE_SCALE * jax.nn.sigmoid(-own_decay),
        gain_grads[1],
        gate_sum,
        up_sum,
        down_sum,
    )


def solution(mesh):
    shards, groups = mesh.shape["seq"], mesh.shape["fsdp"]

    def local(*arrays):
        rows, small_rows = arrays[3].shape[0], arrays[5].shape[0]
        simple = shards % 2 == 0 and rows % 16 == 0 and small_rows % 16 == 0
        simple = simple and arrays[0].shape[1] * shards % (8 * CHUNK) == 0
        return (aligned if simple else general)(*arrays)

    tokens = P("fsdp", "seq", None)
    vector = P(("seq", "fsdp"))
    matrix = P(("seq", "fsdp"), None)
    ranks = (1, 2, 2, 2, 2, 1, 2, 1, 2, 1, 1, 1, 2, 2, 2)
    specs = (tokens, tokens) + tuple(vector if rank == 1 else matrix for rank in ranks)
    return jax.shard_map(local, mesh=mesh, in_specs=specs, out_specs=specs, check_vma=False)
```

```python
import functools

import jax
import jax.numpy as jnp
from jax import lax
from jax.experimental import pallas as pl
from jax.experimental.pallas import tpu as pltpu
from jax.sharding import PartitionSpec as P

EPSILON = 1e-06
RATE_SCALE = 8.0
CHUNK = 128
EARLY = 2
LOW = jnp.bfloat16
WIDE = jnp.float32


def rms_scale(values, gain):
    scale = lax.rsqrt(jnp.mean(values * values, axis=-1, keepdims=True) + EPSILON)
    return values * scale * gain


def dot(left, right):
    return jnp.dot(left, right, preferred_element_type=WIDE)


def outer_sum(left, right):
    return lax.dot_general(left, right, (((0,), (0,)), ((), ())), preferred_element_type=WIDE)


def times_transpose(left, right):
    return lax.dot_general(left, right, (((1,), (1,)), ((), ())), preferred_element_type=WIDE)


def one_minus_exp(value):
    series = jnp.full_like(value, 1.0 / 40320.0)
    for bottom in (5040.0, 720.0, 120.0, 24.0, 6.0, 2.0, 1.0):
        series = 1.0 / bottom - value * series
    return jnp.where(value < 0.4, value * series, 1.0 - jnp.exp(-value))


def sigmoid(value):
    return 0.5 * jnp.tanh(0.5 * value) + 0.5


def lane_tiles(channels):
    return -(-channels // 128)


def put(tiles, rows, value):
    channels = value.shape[1]
    for n in range(lane_tiles(channels)):
        size = min(128, channels - n * 128)
        tiles[n, rows, 0:size] = value[:, n * 128 : n * 128 + size]


def get(tiles, rows, channels):
    return jnp.concatenate(
        [
            tiles[n, rows, 0 : min(128, channels - n * 128)]
            for n in range(lane_tiles(channels))
        ],
        axis=1,
    )


def scan_segments(step, count, tiles):
    def body(i, carried):
        return tuple(step(i, n, *carried[n]) for n in range(tiles))

    start = (jnp.zeros((8, 128), WIDE), jnp.ones((8, 128), WIDE))
    ends = lax.fori_loop(0, count, body, (start,) * tiles, unroll=4)
    return [jnp.concatenate([end[which] for end in ends], axis=1) for which in (0, 1)]


MESH = pl.DeviceIdType.MESH
VMEM_BYTES = 61 * 2**20
ANY = pl.BlockSpec(memory_space=pl.ANY)
HELD = pl.BlockSpec(memory_space=pltpu.VMEM)
ROOT = 0.7978845608028654
CUBE = 0.044715


def dma(*shape):
    return pltpu.SemaphoreType.DMA(shape)


def remote(src, dst, send, recv, axis, index):
    return pltpu.make_async_remote_copy(
        src_ref=src, dst_ref=dst, send_sem=send, recv_sem=recv,
        device_id={axis: index}, device_id_type=MESH,
    )


def gelu(value):
    return 0.5 * value * (1.0 + jnp.tanh(ROOT * (value + CUBE * value * value * value)))


def gelu_and_slope(value):
    square = value * value
    bent = jnp.tanh(ROOT * (value + CUBE * square * value))
    half = 0.5 * (1.0 + bent)
    slope = half + 0.5 * value * (1.0 - bent * bent) * (ROOT * (1.0 + 3.0 * CUBE * square))
    return value * half, slope


class Place:
    def __init__(self, shards, groups):
        self.shards, self.groups, self.line = shards, groups, shards // 2
        self.s, self.f = lax.axis_index("seq"), lax.axis_index("fsdp")
        self.z, self.c = self.s // 2, lax.rem(self.s, 2)
        self.sibling = 2 * self.z + 1 - self.c

    def nearest(self, n):
        chip = 0
        for z in range(self.line):
            for place, other in enumerate(sorted(range(self.line), key=lambda y: abs(y - z))):
                chip = jnp.where((self.z == z) & (n == place), other, chip)
        return chip

    def enter(self, seq=True, fsdp=True):
        barrier = pltpu.get_barrier_semaphore()
        met = 0
        for axis, mine, count, wanted in (
            ("seq", self.s, self.shards, seq), ("fsdp", self.f, self.groups, fsdp),
        ):
            for d in range(1, count if wanted else 1):
                pl.semaphore_signal(
                    barrier, inc=1, device_id={axis: lax.rem(mine + d, count)}, device_id_type=MESH
                )
                met += 1
        pl.semaphore_wait(barrier, met)


class Spread:
    def __init__(self, at, src, dst, send, recv, axis="fsdp"):
        self.at, self.src, self.dst, self.send, self.recv, self.axis = at, src, dst, send, recv, axis
        self.mine, self.count = (at.f, at.groups) if axis == "fsdp" else (at.s, at.shards)

    def copy(self, d):
        peer = lax.rem(self.mine + d, self.count)
        return remote(
            self.src(peer), self.dst(self.mine), self.send.at[d], self.recv.at[d], self.axis, peer
        )

    def start(self):
        for d in range(1, self.count):
            self.copy(d).start()

    def source(self, d):
        return lax.rem(self.mine + self.count - d, self.count)

    def arrive(self, d):
        origin = self.source(d)
        remote(
            self.src(origin), self.dst(origin), self.send.at[d], self.recv.at[d], self.axis, origin
        ).wait_recv()

    def sent(self):
        for d in range(1, self.count):
            self.copy(d).wait_send()

    def finish(self):
        for d in range(1, self.count):
            self.arrive(d)
        self.sent()


class LineGather:
    def __init__(self, at, src, buf, send, recv, pieces):
        self.at, self.src, self.buf, self.send, self.recv, self.pieces = at, src, buf, send, recv, pieces
        self.rows = buf.shape[1] // pieces

    def copy(self, slot, piece, kind, first=False):
        at = self.at
        rows = pl.ds(piece * self.rows, self.rows)
        there = self.buf.at[slot, rows]
        peer = (at.sibling, at.s + 2, at.s - 2)[kind]
        return remote(
            self.src.at[rows] if first else there, there,
            self.send.at[slot, piece, kind], self.recv.at[slot, piece], "seq", peer,
        )

    def start(self, first=0, last=None):
        at = self.at
        for piece in range(first, self.pieces if last is None else last):
            @pl.when(at.z + 1 < at.line)
            def _():
                self.copy(at.s, piece, 1, True).start()

            @pl.when(at.z > 0)
            def _():
                self.copy(at.s, piece, 2, True).start()

            self.copy(at.s, piece, 0, True).start()

    def arrive(self, chip, piece):
        at = self.at
        slot = 2 * chip + at.c
        self.copy(slot, piece, 0).wait_recv()

        @pl.when((chip < at.z) & (at.z + 1 < at.line))
        def _():
            self.copy(slot, piece, 1).start()

        @pl.when((chip > at.z) & (at.z > 0))
        def _():
            self.copy(slot, piece, 2).start()

        self.copy(slot, piece, 0).start()

    def settle(self, chip):
        for piece in range(self.pieces):
            self.copy(2 * chip + 1 - self.at.c, piece, 0).wait_recv()

    def pass_on(self, d):
        at = self.at
        for piece in range(self.pieces):
            for chip, known in ((at.z - d, at.z - d >= 0), (at.z + d, at.z + d < at.line)):
                @pl.when(known)
                def _():
                    self.arrive(chip, piece)

    def distances(self, body, beside=None):
        at = self.at

        @pl.loop(0, at.line)
        def _(n):
            @pl.when(n > 0)
            def _():
                self.pass_on(n)
                if beside is not None:
                    beside(n)

            chip = at.nearest(n)
            self.settle(chip)
            body(chip)

    def sent(self):
        at = self.at
        for chip in range(at.line):
            slot = 2 * chip + at.c
            for piece in range(self.pieces):
                self.copy(slot, piece, 0).wait_send()

                @pl.when((chip <= at.z) & (at.z + 1 < at.line))
                def _():
                    self.copy(slot, piece, 1).wait_send()

                @pl.when((chip >= at.z) & (at.z > 0))
                def _():
                    self.copy(slot, piece, 2).wait_send()


class LineScatter:
    def __init__(self, at, parts, heard, into, sems, pieces):
        self.at, self.parts, self.heard, self.into = at, parts, heard, into
        self.sib_send, self.sib_recv, self.send, self.recv = sems
        self.pieces = pieces
        self.rows = parts.shape[2] // pieces

    @staticmethod
    def scratch(line, rows, width, pieces):
        low = pltpu.VMEM((line, rows, width), LOW)
        return [
            pltpu.VMEM((line, 2, rows, width), LOW), low, low,
            dma(line), dma(line), dma(line, pieces), dma(line, pieces),
        ]

    def across(self, chip):
        return remote(
            self.parts.at[chip, 1 - self.at.c], self.heard.at[chip], self.sib_send.at[chip],
            self.sib_recv.at[chip], "seq", self.at.sibling,
        )

    def whole_way(self, chip, start):
        if self.at.line < 4:
            return False
        return jnp.abs(chip - start) == self.at.line - 1

    def joined(self, chip):
        at = self.at
        if at.line < 4:
            return False
        return ((at.z == 1) & (chip == at.line - 1)) | ((at.z == at.line - 2) & (chip == 0))

    def along(self, chip, piece):
        at = self.at
        rows = pl.ds(pl.multiple_of(piece * self.rows, self.rows), self.rows)
        target, slot = chip, at.z
        if at.line >= 4:
            stop = jnp.where(chip > at.z, at.z + 1, at.z - 1)
            target = jnp.where(self.whole_way(chip, at.z), stop, chip)
            slot = jnp.where(self.whole_way(chip, at.z), stop, at.z)
        return remote(
            self.parts.at[chip, 1 - at.c, rows], self.into.at[slot, rows], self.send.at[chip, piece],
            self.recv.at[slot, piece], "seq", 2 * target + at.c,
        )

    def landed(self, slot, piece):
        rows = pl.ds(pl.multiple_of(piece * self.rows, self.rows), self.rows)
        there = self.into.at[slot, rows]
        remote(
            there, there, self.recv.at[slot, piece], self.recv.at[slot, piece], "seq", self.at.sibling
        ).wait_recv()

    def add(self, chip, piece, extras, store):
        @pl.loop(0, self.rows // 16)
        def _(block):
            rows = pl.ds(pl.multiple_of(piece * self.rows + block * 16, 16), 16)
            total = self.parts[chip, self.at.c, rows, :].astype(WIDE) + self.heard[chip, rows, :].astype(WIDE)
            for known, slot in extras:
                here = self.into[slot, rows, :].astype(WIDE)
                total = total + (here if known is True else jnp.where(known, here, 0.0))
            store(rows, total)

    def store_out(self, chip):
        def store(rows, total):
            self.parts[chip, 1 - self.at.c, rows, :] = total.astype(LOW)

        return store

    def goes(self, chip):
        goes = chip != self.at.z
        return goes & jnp.logical_not(self.joined(chip)) if self.at.line >= 4 else goes

    def push(self, chip, first=0, last=None):
        @pl.when(self.goes(chip))
        def _():
            if first == 0:
                self.across(chip).wait()

            @pl.loop(first, self.pieces if last is None else last)
            def _(piece):
                self.add(chip, piece, [], self.store_out(chip))
                self.along(chip, piece).start()

    def join(self, first=0, last=None):
        at = self.at
        if at.line < 4:
            return

        @pl.when((at.z == 1) | (at.z == at.line - 2))
        def _():
            chip = jnp.where(at.z == 1, at.line - 1, 0)
            if first == 0:
                self.across(chip).wait()

            @pl.loop(first, self.pieces if last is None else last)
            def _(piece):
                self.landed(at.z, piece)
                self.add(chip, piece, [(True, at.z)], self.store_out(chip))
                self.along(chip, piece).start()

    def finish(self, store, first=0, last=None):
        at = self.at
        if first == 0:
            self.across(at.z).wait_recv()

        def known(chip):
            heard = chip != at.z
            return heard & jnp.logical_not(self.whole_way(chip, at.z)) if at.line >= 4 else heard

        @pl.loop(first, self.pieces if last is None else last)
        def _(piece):
            for chip in range(at.line):
                @pl.when(known(chip))
                def _():
                    self.landed(chip, piece)

            self.add(at.z, piece, [(known(chip), chip) for chip in range(at.line)], store)

    def sent(self):
        at = self.at
        self.across(at.z).wait_send()
        for chip in range(at.line):
            @pl.when(chip != at.z)
            def _():
                @pl.loop(0, self.pieces)
                def _(piece):
                    self.along(chip, piece).wait_send()


def normalise(source, gain, store, rows):
    @pl.loop(0, rows // 16)
    def _(block):
        here = pl.ds(pl.multiple_of(block * 16, 16), 16)
        values = source(here)
        scale = lax.rsqrt(jnp.mean(values * values, axis=-1, keepdims=True) + EPSILON)
        store(here, (values * scale * gain).astype(LOW))


def mixer_rows(positions):
    return [pl.ds(pl.multiple_of(n, CHUNK), CHUNK) for n in range(0, positions, CHUNK)]


def mix_in_kernel(
    tokens, lru_rows, gelu_rows, gate_rows, up_rows, out_shard, down_shard, gate_block, input_block,
    taps, biases, rates, both_gains,
    normed_far, in_far, ext_far, pre_far, conv_far, r_far, i_far, st_far,
    product_far, par_ref, wr_ref, wi_ref, gains, glu_mine, out_whole, down_whole,
    normed, in_whole, ext, pre_ref, conv_ref, r_ref, i_ref, st_ref, product_ref,
    in_shard, glu_shard, small, vecs, gain_shard, held, small_all, vecs_all, gain_all, factors, drive, prod,
    local_sems, tok_send, tok_recv, in_sems, in_xy_send, in_xy_recv, glu_sems, xy_sems, gain_sems, leave_sems,
):
    groups, shards = in_whole.shape[1], in_whole.shape[0]
    at = Place(shards, groups)
    s, f = at.s, at.f
    positions, channels = pre_ref.shape
    width = tokens.shape[1]
    rows = in_shard.shape[1]
    segment = positions // 8
    chunks = positions // CHUNK

    units = gate_rows.shape[1] // shards
    for shard in range(shards):
        part = slice(shard * units, (shard + 1) * units)
        glu_shard[shard, :, :units] = gate_rows[:, part]
        glu_shard[shard, :, units:] = up_rows[:, part]
        part = slice(shard * channels, (shard + 1) * channels)
        in_shard[shard, :, :channels] = lru_rows[:, part]
        in_shard[shard, :, channels:] = gelu_rows[:, part]
    size = gate_block.shape[1]
    small[:, :size] = gate_block[...]
    small[:, size:] = input_block[...]
    vecs[0:4, :] = taps[...].astype(WIDE)
    vecs[4:7, :] = biases[...].astype(WIDE)
    vecs[7:8, :] = rates[...]
    gain_shard[...] = jnp.zeros_like(gain_shard)
    gain_shard[0:2, :] = both_gains[...].astype(WIDE)
    leaving = [
        (normed, normed_far), (in_whole, in_far), (ext, ext_far), (pre_ref, pre_far), (conv_ref, conv_far),
        (r_ref, r_far), (i_ref, i_far), (st_ref, st_far), (product_ref, product_far),
    ]
    leaving = [pltpu.make_async_copy(a, b, leave_sems.at[n]) for n, (a, b) in enumerate(leaving)]
    keep = [
        (tokens, held.at[s]), (in_shard.at[s], in_whole.at[s, f]), (glu_shard.at[s], glu_mine.at[s]),
        (out_shard, out_whole.at[f]), (down_shard, down_whole.at[f]), (small, small_all.at[f]),
        (vecs, vecs_all.at[f]), (gain_shard, gain_all.at[s, f]),
    ]
    keep = [pltpu.make_async_copy(a, b, local_sems.at[n]) for n, (a, b) in enumerate(keep)]
    for copy in keep:
        copy.start()
    at.enter()

    def over_fsdp(src, dst, n):
        return Spread(at, lambda peer: src, lambda origin: dst.at[origin], xy_sems.at[n, 0], xy_sems.at[n, 1])

    gain_xy = Spread(
        at, lambda peer: gain_shard, lambda origin: gain_all.at[s, origin],
        xy_sems.at[0, 0], xy_sems.at[0, 1],
    )
    small_xy = over_fsdp(small, small_all, 1)
    vecs_xy = over_fsdp(vecs, vecs_all, 2)
    out_xy = over_fsdp(out_shard, out_whole, 3)
    down_xy = over_fsdp(down_shard, down_whole, 4)
    in_z = Spread(
        at, lambda peer: in_shard.at[peer], lambda origin: in_whole.at[origin, f],
        in_sems.at[0], in_sems.at[1], "seq",
    )
    glu_z = Spread(
        at, lambda peer: glu_shard.at[peer], lambda origin: glu_mine.at[origin],
        glu_sems.at[0], glu_sems.at[1], "seq",
    )
    gain_z = Spread(
        at, lambda peer: gain_all.at[s], lambda origin: gain_all.at[origin],
        gain_sems.at[0], gain_sems.at[1], "seq",
    )

    def in_xy(index):
        return Spread(
            at, lambda peer: in_whole.at[index, f], lambda origin: in_whole.at[index, origin],
            in_xy_send.at[index], in_xy_recv.at[index],
        )

    gather = LineGather(at, tokens, held, tok_send, tok_recv, tok_send.shape[1])
    gain_xy.start()
    in_z.start()
    keep[1].wait()
    in_xy(s).start()
    gather.start()
    vecs_xy.start()
    small_xy.start()
    keep[7].wait()
    gain_xy.finish()
    gain_z.start()
    for d in range(1, shards):
        in_z.arrive(d)
        in_xy(in_z.source(d)).start()
    out_xy.start()
    early = min(3, shards)
    for d in range(1, early):
        glu_z.copy(d).start()
    down_xy.start()
    gain_z.finish()
    for origin in range(shards):
        for other in range(groups):
            first = (origin * groups + other) * rows
            gains[:, first : first + rows] = gain_all[origin, other]
    keep[0].wait()

    def take(chip):
        for core in range(2):
            slot = 2 * chip + core

            def store(here, value):
                normed[slot, here, :] = value

            normalise(
                lambda here: held[slot, here, :].astype(WIDE), gains[0:1, :], store, tokens.shape[0]
            )

    def rest(n):
        @pl.when(n == at.line - 1)
        def _():
            for d in range(early, shards):
                glu_z.copy(d).start()

    gather.distances(take, rest)
    leaving[0].start()
    keep[6].wait()
    vecs_xy.finish()
    keep[5].wait()
    small_xy.finish()
    local = small.shape[0]
    wr_ref[...] = jnp.zeros_like(wr_ref)
    wi_ref[...] = jnp.zeros_like(wi_ref)
    flat = small_all[...].reshape(channels, 2 * size)
    for n in range(channels // size):
        block = slice(n * size, (n + 1) * size)
        wr_ref[block, block] = flat[block, :size]
        wi_ref[block, block] = flat[block, size:]
    for other in range(groups):
        par_ref[:, other * local : (other + 1) * local] = vecs_all[other]
    ext[0:8, :] = jnp.zeros((8, channels), WIDE)
    st_ref[0:8, :] = jnp.zeros((8, channels), WIDE)
    for index in range(shards):
        for d in range(1, groups):
            in_xy(index).arrive(d)
    leaving[1].start()
    @pl.loop(0, at.line)
    def _(chip):
        pair = normed[pl.ds(2 * chip, 2), :, :].reshape(2 * tokens.shape[0], width)
        both = dot(pair, in_whole[...].reshape(width, 2 * channels))
        base = pl.multiple_of(chip * 2 * tokens.shape[0], CHUNK)
        here = pl.ds(base, 2 * tokens.shape[0])
        ext[pl.ds(base + 8, 2 * tokens.shape[0]), :] = both[:, :channels].astype(LOW).astype(WIDE)
        pre_ref[here, :] = both[:, channels:]

    @pl.loop(0, chunks)
    def _(n):
        base = pl.multiple_of(n * CHUNK, CHUNK)
        here = pl.ds(base, CHUNK)
        block = ext[pl.ds(base, CHUNK + 8), :]
        conv = jnp.broadcast_to(par_ref[4:5, :], (CHUNK, channels))
        for k in range(4):
            conv = conv + par_ref[k : k + 1, :] * block[8 - k : 8 - k + CHUNK]
        conv_low = conv.astype(LOW)
        conv_ref[here, :] = conv_low
        r = jax.nn.sigmoid(dot(conv_low, wr_ref[...]) + par_ref[5:6, :])
        gate = jax.nn.sigmoid(dot(conv_low, wi_ref[...]) + par_ref[6:7, :])
        log_decay = r * par_ref[7:8, :]
        m = jnp.sqrt(one_minus_exp(-2.0 * log_decay))
        factor = jnp.exp(log_decay)
        r_ref[here, :] = r
        i_ref[here, :] = gate
        put(factors, here, factor)
        put(drive, here, m * gate * conv_low.astype(WIDE))

    for n in range(2, 7):
        leaving[n].start()

    def step(i, n, state, product):
        here = pl.ds(i, 8, stride=segment)
        factor = factors[n, here, :]
        state = factor * state + drive[n, here, :]
        product = factor * product
        drive[n, here, :] = state
        prod[n, here, :] = product
        return state, product

    state, product = scan_segments(step, segment, lane_tiles(channels))
    state, product = state[:, :channels], product[:, :channels]
    carry = jnp.zeros((1, channels), WIDE)
    for k in range(8):
        for part in range(segment // CHUNK):
            base = k * segment + part * CHUNK
            here = slice(base, base + CHUNK)
            states = get(drive, here, channels) + get(prod, here, channels) * carry
            st_ref[base + 8 : base + 8 + CHUNK, :] = states
            product_ref[here, :] = (
                states.astype(LOW).astype(WIDE) * gelu(pre_ref[here, :])
            ).astype(LOW)
        carry = state[k : k + 1] + product[k : k + 1] * carry

    leaving[7].start()
    leaving[8].start()
    glu_z.finish()
    out_xy.finish()
    down_xy.finish()
    gather.sent()
    in_z.sent()
    for index in range(shards):
        in_xy(index).sent()
    for n in (2, 3, 4):
        keep[n].wait()
    for copy in leaving:
        copy.wait()


def mix_in(
    tokens, lru_rows, gelu_rows, gate_rows, up_rows, out_shard, down_shard, gate_block, input_block,
    taps, biases, rates, both_gains, shards, groups,
):
    rows = lru_rows.shape[0]
    block, width = tokens.shape
    positions, channels = shards * block, lru_rows.shape[1] // shards
    both = 2 * channels
    in_shape = (shards, rows, both)
    glu_shape = (shards, rows, 2 * (gate_rows.shape[1] // shards))
    local = gate_block.shape[0]
    small_shape = (gate_block.shape[0], 2 * gate_block.shape[1])
    pieces = 2
    wide = jax.ShapeDtypeStruct((positions, channels), WIDE)
    low = jax.ShapeDtypeStruct((positions, channels), LOW)
    longer = jax.ShapeDtypeStruct((positions + 8, channels), WIDE)
    square = jax.ShapeDtypeStruct((channels, channels), LOW)
    saved = [
        jax.ShapeDtypeStruct((shards, block, width), LOW),
        jax.ShapeDtypeStruct((shards, groups, rows, both), LOW),
        longer, wide, low, wide, wide, longer,
        low,
    ]
    held = [
        jax.ShapeDtypeStruct((8, channels), WIDE), square, square, jax.ShapeDtypeStruct((8, width), WIDE),
    ]
    far = [
        jax.ShapeDtypeStruct(glu_shape, LOW),
        jax.ShapeDtypeStruct((groups,) + out_shard.shape, LOW),
        jax.ShapeDtypeStruct((groups,) + down_shard.shape, LOW),
    ]
    return pl.pallas_call(
        mix_in_kernel,
        out_shape=saved + held + far,
        in_specs=[HELD] * 13,
        out_specs=[ANY] * len(saved) + [HELD] * len(held) + [ANY] * len(far),
        scratch_shapes=[pltpu.VMEM(member.shape, member.dtype) for member in saved]
        + [
            pltpu.VMEM(in_shape, LOW), pltpu.VMEM(glu_shape, LOW), pltpu.VMEM(small_shape, LOW),
            pltpu.VMEM((8, local), WIDE), pltpu.VMEM((8, rows), WIDE),
            pltpu.VMEM((shards, block, width), LOW),
            pltpu.VMEM((groups,) + small_shape, LOW),
            pltpu.VMEM((groups, 8, local), WIDE),
            pltpu.VMEM((shards, groups, 8, rows), WIDE),
        ]
        + [pltpu.VMEM((lane_tiles(channels), positions, 128), WIDE)] * 3
        + [
            dma(8), dma(shards, pieces, 3), dma(shards, pieces), dma(2, shards), dma(shards, groups),
            dma(shards, groups), dma(2, shards), dma(5, 2, groups), dma(2, shards), dma(9),
        ],
        compiler_params=pltpu.CompilerParams(
            collective_id=1, has_side_effects=True, vmem_limit_bytes=VMEM_BYTES
        ),
        name="mix_in",
    )(
        tokens, lru_rows, gelu_rows, gate_rows, up_rows, out_shard, down_shard, gate_block, input_block,
        taps, biases, rates, both_gains,
    )


def feed_kernel(
    product_far, out_far, glu_mine, down_in, cotangent, tokens, gains,
    middle, middle_grad, mixed_low, gain_sums, hidden_far, glu_grad, down_grad, glu_first,
    product, out_whole, held, cots, glu, down, both, hidden, wide_pair, hidden_pair, normed2, staged, down_staged,
    parts, heard, into, sib_send, sib_recv, line_send, line_recv,
    local_sems, glu_send, glu_recv, two_send, two_recv, cot_send, cot_recv, stage_sems, first_sems,
):
    shards, groups = glu.shape[0], glu.shape[1]
    at = Place(shards, groups)
    s, f = at.s, at.f
    block, width = tokens.shape
    units = down.shape[0]
    pair = 2 * block

    keep = [(glu_mine, glu.at[:, f]), (down_in, down), (cotangent, cots.at[s])]
    keep += [(product_far, product), (out_far, out_whole)]
    keep = [pltpu.make_async_copy(a, b, local_sems.at[n]) for n, (a, b) in enumerate(keep)]
    for copy in keep:
        copy.start()
    at.enter()
    def glu_xy(index):
        return Spread(
            at, lambda peer: glu_mine.at[index], lambda origin: glu.at[index, origin],
            glu_send.at[index], glu_recv.at[index],
        )

    cot_z = LineGather(at, cotangent, cots, cot_send, cot_recv, cot_send.shape[1])
    two_z = LineGather(at, normed2, held, two_send, two_recv, two_send.shape[1])
    sums = LineScatter(
        at, parts, heard, into, (sib_send, sib_recv, line_send, line_recv), line_send.shape[1]
    )
    for index in range(shards):
        glu_xy(index).start()
    cot_z.start()

    def split(chip, columns, value, parts):
        parts[chip, :, :, columns] = value.astype(LOW).reshape(2, block, value.shape[1])

    def columns_of(j):
        return pl.ds(pl.multiple_of(j * 256, 256), 256)

    def pair_rows(chip):
        return pl.ds(pl.multiple_of(chip * pair, pair), pair)

    keep[3].wait()
    keep[4].wait()

    def project(chip):
        @pl.loop(0, width // 256)
        def _(j):
            value = dot(product[pair_rows(chip), :], out_whole[:, columns_of(j)])
            split(chip, columns_of(j), value, parts)

        sums.across(chip).start()

    for k in range(at.line // 2):
        project(at.line - 1 - k)
        project(k)
        sums.push(at.line - 1 - k, 0, 1)
        sums.push(k, 0, 1)
    for k in range(at.line // 2):
        sums.push(at.line - 1 - k, 1)
        sums.push(k, 1)
    sums.join(0, 1)
    cot_z.pass_on(1)

    def to_middle(here, total):
        values = total + tokens[here, :].astype(WIDE)
        middle[here, :] = values
        scale = lax.rsqrt(jnp.mean(values * values, axis=-1, keepdims=True) + EPSILON)
        normed2[here, :] = (values * scale * gains[1:2, :]).astype(LOW)

    sums.finish(to_middle, 0, 1)
    two_z.start(0, 1)
    cot_z.pass_on(2)
    sums.join(1)
    sums.finish(to_middle, 1)
    two_z.start(1)
    own_copy = pltpu.make_async_copy(normed2, held.at[s], local_sems.at[5])
    own_copy.start()
    keep[0].wait()
    keep[1].wait()
    keep[2].wait()
    sums.sent()
    own_copy.wait()
    for d in range(3, at.line):
        cot_z.pass_on(d)
    for index in range(shards):
        glu_xy(index).finish()

    def open_up(chip):
        rows = held[pl.ds(2 * chip, 2), :, :].reshape(pair, width)
        grads = cots[pl.ds(2 * chip, 2), :, :].reshape(pair, width)

        @pl.loop(0, 2 * units // 256)
        def _(j):
            wide_pair[:, columns_of(j)] = dot(
                rows, glu[:, :, :, columns_of(j)].reshape(width, 256)
            )

        @pl.loop(0, units // 256)
        def _(j):
            hidden_pair[:, columns_of(j)] = times_transpose(grads, down[columns_of(j), :])

        @pl.loop(0, pair // 16)
        def _(n):
            part = pl.ds(pl.multiple_of(n * 16, 16), 16)
            there = pl.ds(pl.multiple_of(chip * pair + n * 16, 16), 16)
            opened, slope = gelu_and_slope(wide_pair[part, :units])
            up = wide_pair[part, units:]
            grad = hidden_pair[part, :]
            hidden[there, :] = (opened * up).astype(LOW)
            both[there, :units] = (grad * up * slope).astype(LOW)
            both[there, units:] = (grad * opened).astype(LOW)

    def to_normed2(chip):
        @pl.loop(0, shards)
        def _(j):
            value = times_transpose(
                both[pair_rows(chip), :], glu[j].reshape(width // shards, 2 * units)
            )
            split(chip, columns_of(j), value, parts)

        sums.across(chip).start()

    cot_z.settle(at.z)
    two_z.settle(at.z)

    @pl.loop(1, at.line + 1)
    def _(n):
        chip = at.nearest(lax.rem(n, at.line))

        @pl.when(n < at.line)
        def _():
            two_z.pass_on(n)
            two_z.settle(chip)
            cot_z.settle(chip)

        open_up(chip)

        @pl.when(n > 1)
        def _():
            sums.push(at.nearest(n - 1))

        to_normed2(chip)

    hidden_leave = pltpu.make_async_copy(hidden, hidden_far, local_sems.at[6])
    hidden_leave.start()
    def glu_out(j):
        return pltpu.make_async_copy(
            staged.at[lax.rem(j, 2)], glu_grad.at[:, j], stage_sems.at[lax.rem(j, 2)]
        )

    def glu_sums(first, last):
        @pl.loop(first, last)
        def _(j):
            @pl.when(j >= first + 2)
            def _():
                glu_out(j - 2).wait()

            rows = held[:, :, columns_of(j)].reshape(shards * block, 256)
            staged[lax.rem(j, 2)] = outer_sum(rows, both[...]).astype(LOW).reshape(staged.shape[1:])
            glu_out(j).start()

        for j in range(max(last - 2, first), last):
            glu_out(j).wait()

    def down_out(j):
        return pltpu.make_async_copy(
            down_staged.at[lax.rem(j, 2)], down_grad.at[columns_of(j)], stage_sems.at[2 + lax.rem(j, 2)]
        )

    def down_sums():
        @pl.loop(0, units // 256)
        def _(j):
            @pl.when(j >= 2)
            def _():
                down_out(j - 2).wait()

            grads = cots[...].reshape(shards * block, width)
            down_staged[lax.rem(j, 2)] = outer_sum(hidden[:, columns_of(j)], grads).astype(LOW)
            down_out(j).start()

    early = glu_first.shape[1]
    glu_early = Spread(
        at, lambda peer: glu_grad.at[peer, pl.ds(0, early)], lambda origin: glu_first.at[origin],
        first_sems.at[0], first_sems.at[1],
    )
    glu_sums(0, early)
    glu_early.start()
    sums.join()
    down_sums()
    glu_sums(early, shards)
    gain_sums[...] = jnp.zeros_like(gain_sums)

    def back(here, grad):
        values = middle[here, :]
        scale = lax.rsqrt(jnp.mean(values * values, axis=-1, keepdims=True) + EPSILON)
        scaled = grad * gains[1:2, :]
        along = jnp.mean(scaled * values, axis=-1, keepdims=True)
        total = cots[at.s, here, :].astype(WIDE) + scale * scaled - values * (scale * scale * scale * along)
        middle_grad[here, :] = total
        mixed_low[here, :] = total.astype(LOW)
        gain_sums[0:1, :] += jnp.sum(grad * values * scale, axis=0, keepdims=True)

    sums.finish(back)
    for j in range(max(units // 256 - 2, 0), units // 256):
        down_out(j).wait()
    hidden_leave.wait()
    glu_early.finish()
    sums.sent()
    two_z.sent()
    cot_z.sent()


def feed(product, out_whole, glu_mine, down_whole, cotangent, tokens, gains, groups):
    shards, rows, both = glu_mine.shape
    block, width = tokens.shape
    units = both // 2
    line, pieces, thirds = shards // 2, 2, 2
    own = jax.ShapeDtypeStruct((block, width), WIDE)
    outs = [
        own, own, jax.ShapeDtypeStruct((block, width), LOW), jax.ShapeDtypeStruct((8, width), WIDE),
        jax.ShapeDtypeStruct((shards * block, units), LOW),
        jax.ShapeDtypeStruct((groups, shards, rows, both), LOW),
        jax.ShapeDtypeStruct((units, width), LOW),
        jax.ShapeDtypeStruct((groups, EARLY, rows, both), LOW),
    ]
    gathered = pltpu.VMEM((shards, block, width), LOW)
    return pl.pallas_call(
        feed_kernel,
        out_shape=outs,
        in_specs=[ANY] * 5 + [HELD] * 2,
        out_specs=[HELD] * 4 + [ANY] * 4,
        scratch_shapes=[
            pltpu.VMEM(product.shape, LOW), pltpu.VMEM(out_whole.shape, LOW),
            gathered, gathered,
            pltpu.VMEM((shards, groups, rows, both), LOW),
            pltpu.VMEM((units, width), LOW),
            pltpu.VMEM((shards * block, both), LOW),
            pltpu.VMEM((shards * block, units), LOW),
            pltpu.VMEM((2 * block, both), WIDE),
            pltpu.VMEM((2 * block, units), WIDE),
            pltpu.VMEM((block, width), LOW),
            pltpu.VMEM((2, groups, rows, both), LOW),
            pltpu.VMEM((2, 256, width), LOW),
        ]
        + LineScatter.scratch(line, block, width, thirds)
        + [
            dma(8), dma(shards, groups), dma(shards, groups), dma(shards, pieces, 3), dma(shards, pieces),
            dma(shards, pieces, 3), dma(shards, pieces), dma(4), dma(2, groups),
        ],
        compiler_params=pltpu.CompilerParams(
            collective_id=2, has_side_effects=True, vmem_limit_bytes=VMEM_BYTES
        ),
        name="feed",
    )(product, out_whole, glu_mine, down_whole, cotangent, tokens, gains)


def back_kernel(
    mixed, hidden_far, down_far, middle_far, middle_grad_far, tokens_far, gains, par_ref, wr_ref, wi_ref,
    out_far, in_far, normed_far, product_far, ext_far, pre_far, conv_far, r_far, i_far, st_far,
    glu_grad, glu_first, down_grad, mlp_parts,
    result, tokens_grad, glu_out, in_out, out_heard, small_heard, gain_out, glu_heard, in_grad, down_heard,
    middle, middle_grad, tokens, held, in_whole, out_whole, product, ext, pre, conv_ref, r_ref, i_ref, st_ref,
    both, pair_grad, staged, adj, totals_ref, wr_sum, wi_sum,
    out_sum, out_grad, small, gain_row, gain_parts, gain_heard, gain_sum, glu_parts, glu_sum, in_heard, in_sum,
    fed_parts, fed_heard, fed_into, fed_sib_send, fed_sib_recv, fed_send, fed_recv,
    parts, heard, into, sib_send, sib_recv, line_send, line_recv,
    local_sems, held_send, held_recv, glu_xy_sems, down_sems, stage_sems, in_xy_sems, out_sems,
    small_sems, gain_xy_sems, glu_sems, in_sems, gain_sems,
):
    shards, groups = in_whole.shape[0], in_whole.shape[1]
    at = Place(shards, groups)
    s, f = at.s, at.f
    block, width = tokens.shape
    positions, channels = product.shape
    rows = in_whole.shape[2]
    pair = 2 * block
    segment = positions // 8
    chunks = positions // CHUNK

    keep = [
        (mixed, held.at[s]), (out_far, out_whole), (pre_far, pre), (st_far, st_ref),
        (product_far, product), (r_far, r_ref), (i_far, i_ref), (conv_far, conv_ref),
        (ext_far, ext), (in_far, in_whole), (mixed, held.at[s]), (normed_far, held),
        (middle_far, middle), (middle_grad_far, middle_grad), (tokens_far, tokens),
    ]
    keep = [pltpu.make_async_copy(a, b, local_sems.at[n]) for n, (a, b) in enumerate(keep)]
    for copy in keep[:10] + keep[12:]:
        copy.start()
    at.enter()

    def over_fsdp(src, dst, sems):
        return Spread(
            at, lambda peer: src.at[peer], lambda origin: dst.at[origin], sems.at[0], sems.at[1]
        )

    def over_seq(src, dst, sems):
        return Spread(
            at, lambda peer: src.at[peer], lambda origin: dst.at[origin], sems.at[0], sems.at[1], "seq"
        )

    early = glu_first.shape[1]
    glu_xy = Spread(
        at, lambda peer: glu_grad.at[peer, pl.ds(early, shards - early)], lambda origin: glu_heard.at[origin],
        glu_xy_sems.at[0], glu_xy_sems.at[1],
    )
    in_xy = over_fsdp(in_grad, in_heard, in_xy_sems)
    out_xy = over_fsdp(out_grad, out_heard, out_sems)
    down_xy = over_fsdp(down_grad, down_heard, down_sems)
    small_xy = over_fsdp(small, small_heard, small_sems)
    gain_xy = over_fsdp(gain_parts, gain_heard, gain_xy_sems)
    glu_z = over_seq(glu_sum, glu_out, glu_sems)
    in_z = over_seq(in_sum, in_out, in_sems)
    gain_z = over_seq(gain_sum, gain_out, gain_sems)
    mixed_z = LineGather(at, mixed, held, held_send, held_recv, held_send.shape[1])
    fed = LineScatter(
        at, fed_parts, fed_heard, fed_into,
        (fed_sib_send, fed_sib_recv, fed_send, fed_recv), fed_send.shape[1],
    )
    sums = LineScatter(
        at, parts, heard, into, (sib_send, sib_recv, line_send, line_recv), line_send.shape[1]
    )
    mixed_z.start()
    glu_xy.start()
    out_sum[...] = jnp.zeros_like(out_sum)

    def columns_of(j):
        return pl.ds(pl.multiple_of(j * 256, 256), 256)

    def feed_out(hidden, down, sems):
        loads = [
            pltpu.make_async_copy(hidden_far, hidden, sems.at[0]),
            pltpu.make_async_copy(down_far, down, sems.at[1]),
        ]
        for load in loads:
            load.start()
        for load in loads:
            load.wait()

        def one(chip):
            @pl.loop(0, width // 256)
            def _(j):
                there = pl.ds(pl.multiple_of(chip * pair, pair), pair)
                value = dot(hidden[there, :], down[:, columns_of(j)])
                fed_parts[chip, :, :, columns_of(j)] = value.astype(LOW).reshape(2, block, 256)

            fed.across(chip).start()

        for k in range(at.line // 2):
            one(at.line - 1 - k)
            one(k)

    pl.run_scoped(
        feed_out, pltpu.VMEM(hidden_far.shape, LOW), pltpu.VMEM(down_far.shape, LOW), dma(2)
    )
    for n in (0, 1, 2, 3, 4):
        keep[n].wait()

    def mixed_back(chip):
        rows = held[pl.ds(2 * chip, 2), :, :].reshape(pair, width)
        pair_grad[...] = times_transpose(rows, out_whole[...])

        @pl.loop(0, pair // 64)
        def _(n):
            grad = pair_grad[pl.ds(pl.multiple_of(n * 64, 64), 64), :]
            base = pl.multiple_of(chip * pair + n * 64, 64)
            here = pl.ds(base, 64)
            opened, slope = gelu_and_slope(pre[here, :])
            states = st_ref[pl.ds(base + 8, 64), :].astype(LOW).astype(WIDE)
            put(adj, here, (grad * opened).astype(LOW).astype(WIDE))
            both[here, channels:] = (grad * states * slope).astype(LOW)

        there = pl.ds(pl.multiple_of(chip * pair, pair), pair)

        @pl.loop(0, width // 256)
        def _(j):
            part = held[pl.ds(2 * chip, 2), :, columns_of(j)].reshape(pair, 256)
            out_sum[:, columns_of(j)] += outer_sum(product[there, :], part)

    def fed_beside(n):
        @pl.when(n == 2)
        def _():
            @pl.loop(1, at.line)
            def _(far):
                fed.push(at.nearest(at.line - far))

    mixed_z.distances(mixed_back, fed_beside)
    def mix_back(factors, prod, cg, carries):
        keep[5].wait()

        @pl.loop(0, chunks)
        def _(n):
            here = pl.ds(pl.multiple_of(n * CHUNK, CHUNK), CHUNK)
            put(factors, here, jnp.exp(r_ref[here, :] * par_ref[7:8, :]))

        def step(j, n, flow, product):
            here = pl.ds(segment - 1 - j, 8, stride=segment)
            factor = factors[n, here, :]
            adjoint = adj[n, here, :] + flow
            adj[n, here, :] = adjoint
            prod[n, here, :] = product
            return factor * adjoint, factor * product

        flow, through = scan_segments(step, segment, lane_tiles(channels))
        flow, through = flow[:, :channels], through[:, :channels]
        carry = jnp.zeros((1, channels), WIDE)
        for k in range(7, -1, -1):
            carries[k : k + 1, :] = carry
            carry = flow[k : k + 1] + through[k : k + 1] * carry
        for n in (6, 7, 8):
            keep[n].wait()
        cg[pl.ds(positions, 8), :] = jnp.zeros((8, channels), WIDE)
        wr_sum[...] = jnp.zeros_like(wr_sum)
        wi_sum[...] = jnp.zeros_like(wi_sum)

        def grads(c, sums):
            base = pl.multiple_of(c * CHUNK, CHUNK)
            rows = pl.ds(base, CHUNK)
            adjoint = get(adj, rows, channels) + get(prod, rows, channels) * carries[pl.ds(base // segment, 1), :]
            before = st_ref[pl.ds(base, CHUNK + 8), :][7 : 7 + CHUNK]
            conv_low = conv_ref[rows, :]
            conv = conv_low.astype(WIDE)
            r = r_ref[rows, :]
            gate = i_ref[rows, :]
            factor = get(factors, rows, channels)
            m = jnp.sqrt(one_minus_exp(-2.0 * (r * par_ref[7:8, :])))
            driven = adjoint * gate
            by_log = adjoint * before * factor - driven * conv * factor * factor / m
            by_r = by_log * par_ref[7:8, :] * r * (1.0 - r)
            by_i = adjoint * m * conv * gate * (1.0 - gate)
            by_r_low = by_r.astype(LOW)
            by_i_low = by_i.astype(LOW)
            conv_grad = (
                driven * m
                + times_transpose(by_r_low, wr_ref[...])
                + times_transpose(by_i_low, wi_ref[...])
            )
            cg[rows, :] = conv_grad
            wr_sum[...] += outer_sum(conv_low, by_r_low)
            wi_sum[...] += outer_sum(conv_low, by_i_low)
            near = ext[pl.ds(base, CHUNK + 8), :]
            rows_of = [conv_grad * near[8 - k : 8 - k + CHUNK] for k in range(4)]
            rows_of += [conv_grad, by_r, by_i, by_log * r]
            return tuple(
                total + jnp.sum(member, axis=0, keepdims=True) for total, member in zip(sums, rows_of)
            )

        zero = jnp.zeros((1, channels), WIDE)
        totals = lax.fori_loop(0, chunks, grads, (zero,) * 8)
        for k in range(8):
            totals_ref[k : k + 1, :] = totals[k]
        @pl.loop(0, chunks)
        def _(c):
            base = pl.multiple_of(c * CHUNK, CHUNK)
            near = cg[pl.ds(base, CHUNK + 8), :]
            total = jnp.zeros((CHUNK, channels), WIDE)
            for k in range(4):
                total = total + par_ref[k : k + 1, :] * near[k : k + CHUNK]
            both[pl.ds(base, CHUNK), :channels] = total.astype(LOW)

    tiles = pltpu.VMEM((lane_tiles(channels), positions, 128), WIDE)
    pl.run_scoped(
        mix_back, tiles, tiles, pltpu.VMEM((positions + 8, channels), WIDE), pltpu.VMEM((8, channels), WIDE)
    )
    fed.join()
    keep[9].wait()

    def project(chip):
        rows = both[pl.ds(pl.multiple_of(chip * pair, pair), pair), :]

        @pl.loop(0, shards)
        def _(j):
            value = times_transpose(rows, in_whole[j].reshape(width // shards, 2 * channels))
            parts[chip, :, :, columns_of(j)] = value.astype(LOW).reshape(2, block, value.shape[1])

        sums.across(chip).start()

    for k in range(at.line // 2):
        project(at.line - 1 - k)
        project(k)
        sums.push(at.line - 1 - k)
        sums.push(k)
    mixed_z.sent()
    keep[11].start()
    local = small.shape[1] - 8
    size = small.shape[2] // 2
    for n in range(channels // size):
        part = slice(n * size, (n + 1) * size)
        wr_sum[part, :size] = wr_sum[part, part]
        wi_sum[part, :size] = wi_sum[part, part]
    for group in range(groups):
        part = slice(group * local, (group + 1) * local)
        small[group, :local, :size] = wr_sum[part, :size]
        small[group, :local, size:] = wi_sum[part, :size]
        for k in range(8):
            small[group, local + k : local + k + 1, :local] = totals_ref[k : k + 1, part]
    small_xy.start()
    keep[11].wait()

    def in_done(j):
        return pltpu.make_async_copy(
            staged.at[lax.rem(j, 2)], in_grad.at[:, j], stage_sems.at[lax.rem(j, 2)]
        )

    @pl.loop(0, shards)
    def _(j):
        @pl.when(j >= 2)
        def _():
            in_done(j - 2).wait()

        part = held[:, :, columns_of(j)].reshape(positions, 256)
        staged[lax.rem(j, 2)] = outer_sum(part, both[...]).astype(LOW).reshape(staged.shape[1:])
        in_done(j).start()

    for j in range(shards - 2, shards):
        in_done(j).wait()
    in_xy.start()
    in_own = pltpu.make_async_copy(in_grad.at[f], in_heard.at[f], local_sems.at[16])
    in_own.start()
    sums.join()
    glu_xy.finish()

    def glu_load(d, origin, first=False):
        peer = lax.rem(s + d, shards)
        half = lax.rem(d, 2)
        source = glu_first.at[origin, peer] if first else glu_heard.at[origin, peer - early]
        return pltpu.make_async_copy(
            source, glu_parts.at[half, origin], glu_sems.at[2 + half, origin]
        )

    def glu_load_own(d):
        peer = lax.rem(s + d, shards)
        half = lax.rem(d, 2)
        return pltpu.make_async_copy(
            glu_grad.at[f, peer], glu_parts.at[half, f], glu_sems.at[2 + half, f]
        )

    def glu_loads(d):
        glu_load_own(d).start()
        peer = lax.rem(s + d, shards)
        for first, known in ((True, peer < early), (False, peer >= early)):
            @pl.when(known)
            def _():
                for hop in range(1, groups):
                    glu_load(d, lax.rem(f + hop, groups), first).start()

    def add(parts, total, peer):
        @pl.loop(0, total.shape[1] // 16)
        def _(n):
            here = pl.ds(pl.multiple_of(n * 16, 16), 16)
            value = parts[0, here, :].astype(WIDE)
            for origin in range(1, groups):
                value = value + parts[origin, here, :].astype(WIDE)
            total[peer, here, :] = value.astype(total.dtype)

    glu_loads(1)

    @pl.loop(1, shards + 1)
    def _(d):
        @pl.when(d < shards)
        def _():
            glu_loads(d + 1)

        for origin in range(groups):
            pltpu.make_async_copy(
                glu_first.at[origin, 0], glu_parts.at[lax.rem(d, 2), origin],
                glu_sems.at[2 + lax.rem(d, 2), origin],
            ).wait()
        add(glu_parts.at[lax.rem(d, 2)], glu_sum, lax.rem(s + d, shards))

        @pl.when(d < shards)
        def _():
            glu_z.copy(d).start()

    glu_own = pltpu.make_async_copy(glu_sum.at[s], glu_out.at[s], local_sems.at[17])
    glu_own.start()
    out_grad[...] = out_sum[...].astype(LOW).reshape(out_grad.shape)
    out_xy.start()
    gain_row[...] = jnp.zeros_like(gain_row)

    for n in (12, 13, 14):
        keep[n].wait()

    def store_result(here, total):
        result[here, :] = (middle[here, :] + total).astype(LOW)

    fed.finish(store_result)

    def back(here, grad):
        values = tokens[here, :].astype(WIDE)
        scale = lax.rsqrt(jnp.mean(values * values, axis=-1, keepdims=True) + EPSILON)
        scaled = grad * gains[0:1, :]
        along = jnp.mean(scaled * values, axis=-1, keepdims=True)
        total = middle_grad[here, :] + scale * scaled - values * (scale * scale * scale * along)
        tokens_grad[here, :] = total.astype(LOW)
        gain_row[0:1, :] += jnp.sum(grad * values * scale, axis=0, keepdims=True)

    sums.finish(back)
    for group in range(groups):
        for shard in range(shards):
            first = (shard * groups + group) * rows
            gain_parts[group, shard, 0:1, :] = gain_row[0:1, first : first + rows]
            gain_parts[group, shard, 1:2, :] = mlp_parts[0:1, first : first + rows]
    gain_xy.start()
    in_own.wait()
    in_xy.finish()
    down_xy.start()

    @pl.loop(1, shards + 1)
    def _(d):
        peer = lax.rem(s + d, shards)
        add(in_heard.at[:, peer], in_sum, peer)

        @pl.when(d < shards)
        def _():
            in_z.copy(d).start()

    last = [
        pltpu.make_async_copy(in_sum.at[s], in_out.at[s], local_sems.at[18]),
        pltpu.make_async_copy(out_grad.at[f], out_heard.at[f], local_sems.at[19]),
        pltpu.make_async_copy(small.at[f], small_heard.at[f], local_sems.at[20]),
    ]
    for copy in last:
        copy.start()
    gain_xy.finish()
    total = gain_parts[f]
    for d in range(1, groups):
        total = total + gain_heard[lax.rem(f + d, groups)]
    gain_sum[...] = total
    gain_z.start()
    gain_own = pltpu.make_async_copy(gain_sum.at[s], gain_out.at[s], local_sems.at[21])
    gain_own.start()
    fed.sent()
    sums.sent()
    for spread in (small_xy, out_xy, down_xy, glu_z, gain_z, in_z):
        spread.finish()
    for copy in (glu_own, gain_own, *last):
        copy.wait()


def back(
    mixed, hidden, down_whole, middle, middle_grad, tokens, gains, par, wr, wi,
    out_whole, in_whole, normed, product, ext, pre, conv, r, i, st, glu_grad, glu_first, down_grad, mlp_sums, size,
):
    shards, groups, rows, both = in_whole.shape
    block, width = tokens.shape
    positions, channels = product.shape
    line, pieces, halves = shards // 2, 2, 2
    local = channels // groups
    short = jax.ShapeDtypeStruct((block, width), LOW)
    glu_shape = glu_grad.shape[1:]
    in_shape = (groups, shards, rows, both)
    outs = [
        short, short, jax.ShapeDtypeStruct(glu_shape, LOW), jax.ShapeDtypeStruct(in_shape[1:], LOW),
        jax.ShapeDtypeStruct((groups, local, width), LOW),
        jax.ShapeDtypeStruct((groups, local + 8, 2 * size), WIDE),
        jax.ShapeDtypeStruct((shards, 8, rows), WIDE),
        jax.ShapeDtypeStruct((groups, shards - glu_first.shape[1]) + glu_grad.shape[2:], LOW),
        jax.ShapeDtypeStruct(in_shape, LOW),
        jax.ShapeDtypeStruct(down_grad.shape, LOW),
    ]
    late = [middle, middle_grad, tokens]
    far = [out_whole, in_whole, normed, product, ext, pre, conv, r, i, st]
    near = [in_whole, out_whole, product, ext, pre, conv, r, i, st]
    return pl.pallas_call(
        back_kernel,
        out_shape=outs,
        in_specs=[ANY] * 6 + [HELD] * 4 + [ANY] * (len(far) + 3) + [HELD],
        out_specs=[HELD] * 2 + [ANY] * 8,
        scratch_shapes=[pltpu.VMEM(member.shape, member.dtype) for member in late]
        + [pltpu.VMEM((shards, block, width), LOW)]
        + [pltpu.VMEM(member.shape, member.dtype) for member in near]
        + [
            pltpu.VMEM((positions, 2 * channels), LOW),
            pltpu.VMEM((2 * block, channels), WIDE),
            pltpu.VMEM((2, groups, rows, both), LOW),
        ]
        + [pltpu.VMEM((lane_tiles(channels), positions, 128), WIDE), pltpu.VMEM((8, channels), WIDE)]
        + [pltpu.VMEM((channels, channels), WIDE)] * 2
        + [
            pltpu.VMEM((channels, width), WIDE),
            pltpu.VMEM((groups, local, width), LOW),
            pltpu.VMEM((groups, local + 8, 2 * size), WIDE),
            pltpu.VMEM((8, width), WIDE),
            pltpu.VMEM((groups, shards, 8, rows), WIDE),
            pltpu.VMEM((groups, shards, 8, rows), WIDE),
            pltpu.VMEM((shards, 8, rows), WIDE),
            pltpu.VMEM((2, groups) + glu_shape[1:], LOW),
            pltpu.VMEM(glu_shape, LOW),
            pltpu.VMEM(in_shape, LOW),
            pltpu.VMEM(in_shape[1:], LOW),
        ]
        + LineScatter.scratch(line, block, width, halves) * 2
        + [
            dma(22), dma(shards, pieces, 3), dma(shards, pieces), dma(2, groups), dma(2, groups), dma(2),
            dma(2, groups), dma(2, groups), dma(2, groups), dma(2, groups),
            dma(4, shards), dma(2, shards), dma(2, shards),
        ],
        compiler_params=pltpu.CompilerParams(
            collective_id=3, has_side_effects=True, vmem_limit_bytes=VMEM_BYTES
        ),
        name="back",
    )(
        mixed, hidden, down_whole, middle, middle_grad, tokens, gains, par, wr, wi, *far,
        glu_grad, glu_first, down_grad, mlp_sums,
    )


def settle_kernel(
    glu_far, ins_far, outs_far, down_heard, down_grad, result_far, tokens_far,
    result_out, tokens_out, gate_far, up_far, lru_far, gelu_far, out_far, down_far,
    result, tokens, glu, ins, outs, parts, gate_sum, up_sum, lru_sum, gelu_sum, out_sum, down_sum, sems, leave_sems,
):
    shards, rows, both = glu.shape
    groups = outs.shape[0]
    units, channels = both // 2, ins.shape[2] // 2
    f = lax.axis_index("fsdp")
    keep = [
        (glu_far, glu), (ins_far, ins), (outs_far, outs), (result_far, result), (tokens_far, tokens),
        (down_grad.at[f], parts.at[f]),
    ]
    for hop in range(1, groups):
        origin = lax.rem(f + hop, groups)
        keep.append((down_heard.at[origin], parts.at[origin]))
    keep = [pltpu.make_async_copy(a, b, sems.at[n]) for n, (a, b) in enumerate(keep)]
    for copy in keep:
        copy.start()
    leaving = [
        (gate_sum, gate_far), (up_sum, up_far), (lru_sum, lru_far), (gelu_sum, gelu_far),
        (out_sum, out_far), (down_sum, down_far), (result, result_out), (tokens, tokens_out),
    ]
    leaving = [pltpu.make_async_copy(a, b, leave_sems.at[n]) for n, (a, b) in enumerate(leaving)]
    keep[0].wait()
    for half, whole in enumerate((gate_sum, up_sum)):
        for shard in range(shards):
            part = slice(half * units, (half + 1) * units)
            whole[:, shard * units : (shard + 1) * units] = glu[shard, :, part].astype(WIDE)
        leaving[half].start()
    keep[1].wait()
    for half, whole in enumerate((lru_sum, gelu_sum)):
        for shard in range(shards):
            part = slice(half * channels, (half + 1) * channels)
            whole[:, shard * channels : (shard + 1) * channels] = ins[shard, :, part].astype(WIDE)
        leaving[2 + half].start()

    def add(terms, total):
        @pl.loop(0, total.shape[0] // 16)
        def _(n):
            here = pl.ds(pl.multiple_of(n * 16, 16), 16)
            value = terms[0, here, :].astype(WIDE)
            for origin in range(1, groups):
                value = value + terms[origin, here, :].astype(WIDE)
            total[here, :] = value

    for n in (3, 4):
        keep[n].wait()
        leaving[n + 3].start()
    keep[2].wait()
    add(outs, out_sum)
    leaving[4].start()
    for copy in keep[5:]:
        copy.wait()
    add(parts, down_sum)
    leaving[5].start()
    for copy in leaving:
        copy.wait()


def settle(glu, ins, outs, down_heard, down_grad, result, tokens):
    shards, rows, both = glu.shape
    groups, local, width = outs.shape
    units, channels = both // 2, ins.shape[2] // 2
    shapes = [(rows, shards * units)] * 2 + [(rows, shards * channels)] * 2
    shapes += [(local, width), down_grad.shape[1:]]
    return pl.pallas_call(
        settle_kernel,
        out_shape=[jax.ShapeDtypeStruct(result.shape, LOW)] * 2
        + [jax.ShapeDtypeStruct(shape, WIDE) for shape in shapes],
        in_specs=[ANY] * 7,
        out_specs=[ANY] * 8,
        scratch_shapes=[pltpu.VMEM(member.shape, LOW) for member in (result, tokens, glu, ins, outs, down_grad)]
        + [pltpu.VMEM(shape, WIDE) for shape in shapes]
        + [dma(groups + 5), dma(8)],
        compiler_params=pltpu.CompilerParams(vmem_limit_bytes=VMEM_BYTES),
        name="settle",
    )(glu, ins, outs, down_heard, down_grad, result, tokens)


def mixer_forward_kernel(
    x_ref, wr_ref, wi_ref, par_ref,
    conv_ref, r_ref, i_ref, f_ref, m_ref, st_ref,
    ext, factors, drive, prod,
):
    positions, channels = x_ref.shape
    segment = positions // 8
    chunks = positions // CHUNK
    ext[0:8, :] = jnp.zeros((8, channels), WIDE)
    st_ref[0:8, :] = jnp.zeros((8, channels), WIDE)

    @pl.loop(0, chunks)
    def _(c):
        base = pl.multiple_of(c * CHUNK, CHUNK)
        ext[pl.ds(base + 8, CHUNK), :] = x_ref[pl.ds(base, CHUNK), :].astype(WIDE)

    @pl.loop(0, chunks)
    def _(c):
        base = pl.multiple_of(c * CHUNK, CHUNK)
        rows = pl.ds(base, CHUNK)
        block = ext[pl.ds(base, CHUNK + 8), :]
        conv = jnp.broadcast_to(par_ref[4:5, :], (CHUNK, channels))
        for k in range(4):
            conv = conv + par_ref[k : k + 1, :] * block[8 - k : 8 - k + CHUNK]
        conv_low = conv.astype(LOW)
        conv_ref[rows, :] = conv_low
        r = jax.nn.sigmoid(dot(conv_low, wr_ref[...]) + par_ref[5:6, :])
        gate = jax.nn.sigmoid(dot(conv_low, wi_ref[...]) + par_ref[6:7, :])
        log_decay = r * par_ref[7:8, :]
        m = jnp.sqrt(one_minus_exp(-2.0 * log_decay))
        r_ref[rows, :] = r
        i_ref[rows, :] = gate
        factor = jnp.exp(log_decay)
        f_ref[rows, :] = factor
        m_ref[rows, :] = m
        put(factors, rows, factor)
        put(drive, rows, m * gate * conv_low.astype(WIDE))

    def step(i, n, state, product):
        rows = pl.ds(i, 8, stride=segment)
        factor = factors[n, rows, :]
        state = factor * state + drive[n, rows, :]
        product = factor * product
        drive[n, rows, :] = state
        prod[n, rows, :] = product
        return state, product

    state, product = scan_segments(step, segment, lane_tiles(channels))
    state, product = state[:, :channels], product[:, :channels]
    carry = jnp.zeros((1, channels), WIDE)
    for k in range(8):
        for part in range(segment // CHUNK):
            base = k * segment + part * CHUNK
            rows = slice(base, base + CHUNK)
            st_ref[base + 8 : base + 8 + CHUNK, :] = (
                get(drive, rows, channels) + get(prod, rows, channels) * carry
            )
        carry = state[k : k + 1] + product[k : k + 1] * carry


def mixer_backward_kernel(
    ds_ref, x_ref, conv_ref, r_ref, i_ref, f_ref, m_ref, st_ref, wr_ref, wi_ref, par_ref,
    xg_ref, wrg_ref, wig_ref, sums_ref,
    ext, factors, adj, prod, cg, carries, wr_sum, wi_sum,
):
    positions, channels = x_ref.shape
    segment = positions // 8
    chunks = positions // CHUNK
    ext[0:8, :] = jnp.zeros((8, channels), WIDE)
    cg[pl.ds(positions, 8), :] = jnp.zeros((8, channels), WIDE)
    wr_sum[...] = jnp.zeros_like(wr_sum)
    wi_sum[...] = jnp.zeros_like(wi_sum)

    @pl.loop(0, chunks)
    def _(c):
        base = pl.multiple_of(c * CHUNK, CHUNK)
        ext[pl.ds(base + 8, CHUNK), :] = x_ref[pl.ds(base, CHUNK), :].astype(WIDE)
        put(adj, pl.ds(base, CHUNK), ds_ref[pl.ds(base, CHUNK), :].astype(WIDE))
        put(factors, pl.ds(base, CHUNK), f_ref[pl.ds(base, CHUNK), :])

    def step(j, n, flow, product):
        rows = pl.ds(segment - 1 - j, 8, stride=segment)
        factor = factors[n, rows, :]
        adjoint = adj[n, rows, :] + flow
        adj[n, rows, :] = adjoint
        prod[n, rows, :] = product
        return factor * adjoint, factor * product

    flow, product = scan_segments(step, segment, lane_tiles(channels))
    flow, product = flow[:, :channels], product[:, :channels]
    carry = jnp.zeros((1, channels), WIDE)
    for k in range(7, -1, -1):
        carries[k : k + 1, :] = carry
        carry = flow[k : k + 1] + product[k : k + 1] * carry

    def grads(c, sums):
        base = pl.multiple_of(c * CHUNK, CHUNK)
        rows = pl.ds(base, CHUNK)
        adjoint = get(adj, rows, channels) + get(prod, rows, channels) * carries[pl.ds(base // segment, 1), :]
        before = st_ref[pl.ds(base, CHUNK + 8), :][7 : 7 + CHUNK]
        conv_low = conv_ref[rows, :]
        conv = conv_low.astype(WIDE)
        r = r_ref[rows, :]
        gate = i_ref[rows, :]
        factor = f_ref[rows, :]
        m = m_ref[rows, :]
        driven = adjoint * gate
        by_log = adjoint * before * factor - driven * conv * factor * factor / m
        by_r = by_log * par_ref[7:8, :] * r * (1.0 - r)
        by_i = adjoint * m * conv * gate * (1.0 - gate)
        by_r_low = by_r.astype(LOW)
        by_i_low = by_i.astype(LOW)
        conv_grad = (
            driven * m
            + times_transpose(by_r_low, wr_ref[...])
            + times_transpose(by_i_low, wi_ref[...])
        )
        cg[rows, :] = conv_grad
        wr_sum[...] += outer_sum(conv_low, by_r_low)
        wi_sum[...] += outer_sum(conv_low, by_i_low)
        block = ext[pl.ds(base, CHUNK + 8), :]
        rows_of = [conv_grad * block[8 - k : 8 - k + CHUNK] for k in range(4)]
        rows_of += [conv_grad, by_r, by_i, by_log * r]
        return tuple(
            total + jnp.sum(member, axis=0, keepdims=True) for total, member in zip(sums, rows_of)
        )

    zero = jnp.zeros((1, channels), WIDE)
    sums = lax.fori_loop(0, chunks, grads, (zero,) * 8)
    for k in range(8):
        sums_ref[k : k + 1, :] = sums[k]
    size = wrg_ref.shape[1]
    for n in range(channels // size):
        block = slice(n * size, (n + 1) * size)
        wrg_ref[block, :] = wr_sum[block, block]
        wig_ref[block, :] = wi_sum[block, block]

    @pl.loop(0, chunks)
    def _(c):
        base = pl.multiple_of(c * CHUNK, CHUNK)
        block = cg[pl.ds(base, CHUNK + 8), :]
        total = jnp.zeros((CHUNK, channels), WIDE)
        for k in range(4):
            total = total + par_ref[k : k + 1, :] * block[k : k + CHUNK]
        xg_ref[pl.ds(base, CHUNK), :] = total.astype(LOW)


def mixer_forward(x, wr, wi, par):
    positions, channels = x.shape
    wide = jax.ShapeDtypeStruct((positions, channels), WIDE)
    return pl.pallas_call(
        mixer_forward_kernel,
        out_shape=(
            jax.ShapeDtypeStruct((positions, channels), LOW), wide, wide, wide, wide,
            jax.ShapeDtypeStruct((positions + 8, channels), WIDE),
        ),
        scratch_shapes=[pltpu.VMEM((positions + 8, channels), WIDE)]
        + [pltpu.VMEM((lane_tiles(channels), positions, 128), WIDE)] * 3,
        compiler_params=pltpu.CompilerParams(vmem_limit_bytes=48 * 2**20),
        name="mixer_forward",
    )(x, wr, wi, par)


def mixer_backward(ds, x, saved, wr, wi, par, size):
    positions, channels = x.shape
    square = jax.ShapeDtypeStruct((channels, size), WIDE)
    return pl.pallas_call(
        mixer_backward_kernel,
        out_shape=(
            jax.ShapeDtypeStruct((positions, channels), LOW), square, square,
            jax.ShapeDtypeStruct((8, channels), WIDE),
        ),
        scratch_shapes=[pltpu.VMEM((positions + 8, channels), WIDE)]
        + [pltpu.VMEM((lane_tiles(channels), positions, 128), WIDE)] * 3
        + [pltpu.VMEM((positions + 8, channels), WIDE), pltpu.VMEM((8, channels), WIDE)]
        + [pltpu.VMEM((channels, channels), WIDE)] * 2,
        compiler_params=pltpu.CompilerParams(vmem_limit_bytes=48 * 2**20),
        name="mixer_backward",
    )(ds, x, *saved, wr, wi, par)


def gather_columns(weights):
    shards = lax.axis_size("seq")
    rows = weights[0].shape[0]
    widths = [member.shape[1] // shards for member in weights]
    stacked = jnp.concatenate(
        [member.reshape(rows, shards, width) for member, width in zip(weights, widths)], axis=2
    )
    mine = lax.all_to_all(stacked.transpose(1, 0, 2), "seq", split_axis=0, concat_axis=0)
    whole = lax.all_gather(mine, "fsdp", axis=1)
    return whole.reshape(-1, sum(widths))


def scatter_columns(grad, widths, rows):
    shards, groups = lax.axis_size("seq"), lax.axis_size("fsdp")
    parts = grad.astype(LOW).reshape(shards, groups, rows, sum(widths)).transpose(1, 0, 2, 3)
    mine = lax.psum_scatter(parts, "fsdp", scatter_dimension=0, tiled=False)
    swapped = lax.all_to_all(mine, "seq", split_axis=0, concat_axis=0).astype(WIDE)
    outs, first = [], 0
    for width in widths:
        outs.append(swapped[:, :, first : first + width].transpose(1, 0, 2).reshape(rows, -1))
        first += width
    return outs


def block_diagonal(weight, blocks):
    size = weight.shape[1]
    shaped = weight.reshape(blocks, size, size)
    full = jnp.zeros((blocks, size, blocks, size), weight.dtype)
    for n in range(blocks):
        full = full.at[n, :, n, :].set(shaped[n])
    return full.reshape(blocks * size, blocks * size)


def general(
    tokens, cotangent, mix_gain, lru_in_weight, gelu_in_weight, out_weight, conv_weight, conv_bias,
    recurrence_weight, recurrence_bias, input_gate_weight, input_gate_bias, decay_param, mlp_gain,
    gate_weight, up_weight, down_weight,
):
    positions, width = tokens.shape[1:]
    rows = lru_in_weight.shape[0]
    shards = lax.axis_size("seq")
    channels = lru_in_weight.shape[1] // shards
    hidden_width = gate_weight.shape[1] // shards
    size = recurrence_weight.shape[1]

    gains = lax.all_gather(
        jnp.stack([mix_gain, mlp_gain], axis=1), ("seq", "fsdp"), axis=0, tiled=True
    ).astype(WIDE)
    mix_scale, mlp_scale = gains[:, 0], gains[:, 1]
    in_whole = gather_columns([lru_in_weight, gelu_in_weight])
    lru_params = lax.all_gather(
        jnp.concatenate(
            [
                recurrence_weight, input_gate_weight, conv_weight, conv_bias[:, None],
                recurrence_bias[:, None], input_gate_bias[:, None], decay_param[:, None],
            ],
            axis=1,
        ),
        "fsdp", axis=0, tiled=True,
    )
    out_whole = lax.all_gather(out_weight, "fsdp", axis=0, tiled=True)
    glu_whole = gather_columns([gate_weight, up_weight])
    down_whole = lax.all_gather(down_weight, "fsdp", axis=0, tiled=True)

    wr = block_diagonal(lru_params[:, :size], channels // size)
    wi = block_diagonal(lru_params[:, size : 2 * size], channels // size)
    vectors = lru_params[:, 2 * size :].astype(WIDE).T
    decay = vectors[7]
    par = jnp.concatenate([vectors[:7], -RATE_SCALE * jax.nn.softplus(-decay)[None]], axis=0)

    resid_in = tokens.reshape(positions, width).astype(WIDE)
    grad_low = cotangent.reshape(positions, width)
    normed_low = rms_scale(resid_in, mix_scale).astype(LOW)
    normed_all = lax.all_gather(normed_low, "seq", axis=0, tiled=True)
    grad_all = lax.all_gather(grad_low, "seq", axis=0, tiled=True)
    branch_x = dot(normed_all, in_whole[:, :channels]).astype(LOW)
    branch_pre = dot(normed_all, in_whole[:, channels:])
    branch_y = jax.nn.gelu(branch_pre)

    saved = mixer_forward(branch_x, wr, wi, par)
    states_f = saved[5][8:].astype(LOW).astype(WIDE)
    product = (states_f * branch_y).astype(LOW)
    mixed = lax.psum_scatter(
        dot(product, out_whole).astype(LOW), "seq", scatter_dimension=0, tiled=True
    )
    middle = resid_in + mixed.astype(WIDE)
    normed2_low = rms_scale(middle, mlp_scale).astype(LOW)
    normed2_all = lax.all_gather(normed2_low, "seq", axis=0, tiled=True)
    gate_whole, up_whole = glu_whole[:, :hidden_width], glu_whole[:, hidden_width:]
    gate_val = dot(normed2_all, gate_whole)
    up_val = dot(normed2_all, up_whole)
    hidden = (jax.nn.gelu(gate_val) * up_val).astype(LOW)
    fed = lax.psum_scatter(
        dot(hidden, down_whole).astype(LOW), "seq", scatter_dimension=0, tiled=True
    )
    result = middle + fed.astype(WIDE)

    hidden_grad = times_transpose(grad_all, down_whole)
    unused, pull_glu = jax.vjp(lambda first, second: jax.nn.gelu(first) * second, gate_val, up_val)
    gate_grad, up_grad = pull_glu(hidden_grad)
    gate_low, up_low = gate_grad.astype(LOW), up_grad.astype(LOW)
    normed2_grad = lax.psum_scatter(
        (times_transpose(gate_low, gate_whole) + times_transpose(up_low, up_whole)).astype(LOW),
        "seq", scatter_dimension=0, tiled=True,
    ).astype(WIDE)
    unused, pull_norm2 = jax.vjp(rms_scale, middle, mlp_scale)
    middle_part, mlp_gain_grad = pull_norm2(normed2_grad)
    middle_grad = grad_low.astype(WIDE) + middle_part
    mixed_all = lax.all_gather(middle_grad.astype(LOW), "seq", axis=0, tiled=True)

    product_grad = times_transpose(mixed_all, out_whole)
    states_grad = (product_grad * branch_y).astype(LOW)
    unused, pull_gelu = jax.vjp(jax.nn.gelu, branch_pre)
    (pre_grad,) = pull_gelu(product_grad * states_f)
    pre_low = pre_grad.astype(LOW)
    x_low, wr_grad, wi_grad, sums = mixer_backward(states_grad, branch_x, saved, wr, wi, par, size)

    normed_grad = lax.psum_scatter(
        (
            times_transpose(x_low, in_whole[:, :channels])
            + times_transpose(pre_low, in_whole[:, channels:])
        ).astype(LOW),
        "seq", scatter_dimension=0, tiled=True,
    ).astype(WIDE)
    unused, pull_norm = jax.vjp(rms_scale, resid_in, mix_scale)
    input_part, mix_gain_grad = pull_norm(normed_grad)
    input_grad = middle_grad + input_part

    down_grad = lax.psum_scatter(
        outer_sum(hidden, grad_all).astype(LOW), "fsdp", scatter_dimension=0, tiled=True
    ).astype(WIDE)
    glu_grad = jnp.concatenate(
        [outer_sum(normed2_all, gate_low), outer_sum(normed2_all, up_low)], axis=1
    )
    gate_w_grad, up_w_grad = scatter_columns(glu_grad, [hidden_width] * 2, rows)
    out_grad = lax.psum_scatter(
        outer_sum(product, mixed_all).astype(LOW), "fsdp", scatter_dimension=0, tiled=True
    ).astype(WIDE)
    in_grad = jnp.concatenate(
        [outer_sum(normed_all, x_low), outer_sum(normed_all, pre_low)], axis=1
    )
    lru_in_grad, gelu_in_grad = scatter_columns(in_grad, [channels] * 2, rows)
    small = jnp.concatenate(
        [
            wr_grad, wi_grad, sums[:7].T,
            (sums[7] * RATE_SCALE * jax.nn.sigmoid(-decay))[:, None],
        ],
        axis=1,
    )
    small = lax.psum_scatter(
        small.reshape(lax.axis_size("fsdp"), -1, small.shape[1]),
        "fsdp", scatter_dimension=0, tiled=False,
    )
    gain_parts = jnp.stack([mix_gain_grad, mlp_gain_grad]).reshape(2, -1, rows).transpose(1, 0, 2)
    gain_grads = lax.psum_scatter(
        gain_parts, ("seq", "fsdp"), scatter_dimension=0, tiled=False
    )
    first = 2 * size
    return (
        result.astype(LOW).reshape(tokens.shape),
        input_grad.astype(LOW).reshape(tokens.shape),
        gain_grads[0],
        lru_in_grad,
        gelu_in_grad,
        out_grad,
        small[:, first : first + 4],
        small[:, first + 4],
        small[:, :size],
        small[:, first + 5],
        small[:, size : 2 * size],
        small[:, first + 6],
        small[:, first + 7],
        gain_grads[1],
        gate_w_grad,
        up_w_grad,
        down_grad,
    )


def aligned(
    tokens, cotangent, mix_gain, lru_in_weight, gelu_in_weight, out_weight, conv_weight, conv_bias,
    recurrence_weight, recurrence_bias, input_gate_weight, input_gate_bias, decay_param, mlp_gain,
    gate_weight, up_weight, down_weight,
):
    positions, width = tokens.shape[1:]
    rows = lru_in_weight.shape[0]
    shards = lax.axis_size("seq")
    channels = lru_in_weight.shape[1] // shards
    hidden_width = gate_weight.shape[1] // shards
    size = recurrence_weight.shape[1]

    groups = lax.axis_size("fsdp")
    resid_in = tokens.reshape(positions, width).astype(WIDE)
    grad_low = cotangent.reshape(positions, width)

    own_decay = decay_param.astype(WIDE)
    rates = -RATE_SCALE * jax.nn.softplus(-own_decay)[None]
    tokens_low = tokens.reshape(positions, width)
    (
        normed, in_whole, ext, branch_pre, conv_low, recur_gate, input_gate, states, product, par, wr, wi,
        gains, glu_mine, out_whole, down_whole,
    ) = mix_in(
        tokens_low, lru_in_weight, gelu_in_weight, gate_weight, up_weight, out_weight, down_weight,
        recurrence_weight, input_gate_weight, conv_weight.T,
        jnp.stack([conv_bias, recurrence_bias, input_gate_bias]), rates, jnp.stack([mix_gain, mlp_gain]),
        shards, groups,
    )
    out_whole, down_whole = out_whole.reshape(-1, width), down_whole.reshape(-1, width)
    middle, middle_grad, mixed_low, mlp_sums, hidden, glu_grad, down_grad, glu_first = feed(
        product, out_whole, glu_mine, down_whole, grad_low, tokens_low, gains, groups
    )
    down_grad = down_grad.reshape(groups, -1, width)
    (
        result, tokens_grad, glu_out, in_out, out_heard, small_heard, gain_out, unused, unused, down_heard,
    ) = back(
        mixed_low, hidden, down_whole, middle, middle_grad, tokens_low, gains, par, wr, wi,
        out_whole, in_whole, normed, product, ext, branch_pre, conv_low, recur_gate, input_gate, states,
        glu_grad, glu_first, down_grad, mlp_sums, size,
    )
    small_rows = recurrence_weight.shape[0]
    result, tokens_grad, gate_sum, up_sum, lru_sum, gelu_sum, out_sum, down_sum = settle(
        glu_out, in_out, out_heard, down_heard, down_grad, result, tokens_grad
    )
    small = jnp.sum(small_heard, axis=0)
    gain_grads = jnp.sum(gain_out, axis=0)
    vector_sums = small[small_rows:, :small_rows]
    return (
        result.reshape(tokens.shape),
        tokens_grad.reshape(tokens.shape),
        gain_grads[0],
        lru_sum,
        gelu_sum,
        out_sum,
        vector_sums[:4].T,
        vector_sums[4],
        small[:small_rows, :size],
        vector_sums[5],
        small[:small_rows, size : 2 * size],
        vector_sums[6],
        vector_sums[7] * RATE_SCALE * jax.nn.sigmoid(-own_decay),
        gain_grads[1],
        gate_sum,
        up_sum,
        down_sum,
    )


def solution(mesh):
    shards, groups = mesh.shape["seq"], mesh.shape["fsdp"]

    def local(*arrays):
        rows, small_rows = arrays[3].shape[0], arrays[5].shape[0]
        simple = shards % 2 == 0 and rows % 16 == 0 and small_rows % 16 == 0
        simple = simple and arrays[0].shape[1] * shards % (8 * CHUNK) == 0
        return (aligned if simple else general)(*arrays)

    tokens = P("fsdp", "seq", None)
    vector = P(("seq", "fsdp"))
    matrix = P(("seq", "fsdp"), None)
    ranks = (1, 2, 2, 2, 2, 1, 2, 1, 2, 1, 1, 1, 2, 2, 2)
    specs = (tokens, tokens) + tuple(vector if rank == 1 else matrix for rank in ranks)
    return jax.shard_map(local, mesh=mesh, in_specs=specs, out_specs=specs, check_vma=False)
```

```python
import functools

import jax
import jax.numpy as jnp
from jax import lax
from jax.experimental import pallas as pl
from jax.experimental.pallas import tpu as pltpu
from jax.sharding import PartitionSpec as P

EPSILON = 1e-06
RATE_SCALE = 8.0
CHUNK = 128
EARLY = 2
LOW = jnp.bfloat16
WIDE = jnp.float32


def rms_scale(values, gain):
    scale = lax.rsqrt(jnp.mean(values * values, axis=-1, keepdims=True) + EPSILON)
    return values * scale * gain


def dot(left, right):
    return jnp.dot(left, right, preferred_element_type=WIDE)


def outer_sum(left, right):
    return lax.dot_general(left, right, (((0,), (0,)), ((), ())), preferred_element_type=WIDE)


def times_transpose(left, right):
    return lax.dot_general(left, right, (((1,), (1,)), ((), ())), preferred_element_type=WIDE)


def one_minus_exp(value):
    series = jnp.full_like(value, 1.0 / 40320.0)
    for bottom in (5040.0, 720.0, 120.0, 24.0, 6.0, 2.0, 1.0):
        series = 1.0 / bottom - value * series
    return jnp.where(value < 0.4, value * series, 1.0 - jnp.exp(-value))


def sigmoid(value):
    return 0.5 * jnp.tanh(0.5 * value) + 0.5


def lane_tiles(channels):
    return -(-channels // 128)


def put(tiles, rows, value):
    channels = value.shape[1]
    for n in range(lane_tiles(channels)):
        size = min(128, channels - n * 128)
        tiles[n, rows, 0:size] = value[:, n * 128 : n * 128 + size]


def get(tiles, rows, channels):
    return jnp.concatenate(
        [
            tiles[n, rows, 0 : min(128, channels - n * 128)]
            for n in range(lane_tiles(channels))
        ],
        axis=1,
    )


def scan_segments(step, count, tiles):
    def body(i, carried):
        return tuple(step(i, n, *carried[n]) for n in range(tiles))

    start = (jnp.zeros((8, 128), WIDE), jnp.ones((8, 128), WIDE))
    ends = lax.fori_loop(0, count, body, (start,) * tiles, unroll=4)
    return [jnp.concatenate([end[which] for end in ends], axis=1) for which in (0, 1)]


MESH = pl.DeviceIdType.MESH
VMEM_BYTES = 61 * 2**20
ANY = pl.BlockSpec(memory_space=pl.ANY)
HELD = pl.BlockSpec(memory_space=pltpu.VMEM)
ROOT = 0.7978845608028654
CUBE = 0.044715


def dma(*shape):
    return pltpu.SemaphoreType.DMA(shape)


def remote(src, dst, send, recv, axis, index):
    return pltpu.make_async_remote_copy(
        src_ref=src, dst_ref=dst, send_sem=send, recv_sem=recv,
        device_id={axis: index}, device_id_type=MESH,
    )


def gelu(value):
    return 0.5 * value * (1.0 + jnp.tanh(ROOT * (value + CUBE * value * value * value)))


def gelu_and_slope(value):
    square = value * value
    bent = jnp.tanh(ROOT * (value + CUBE * square * value))
    half = 0.5 * (1.0 + bent)
    slope = half + 0.5 * value * (1.0 - bent * bent) * (ROOT * (1.0 + 3.0 * CUBE * square))
    return value * half, slope


class Place:
    def __init__(self, shards, groups):
        self.shards, self.groups, self.line = shards, groups, shards // 2
        self.s, self.f = lax.axis_index("seq"), lax.axis_index("fsdp")
        self.z, self.c = self.s // 2, lax.rem(self.s, 2)
        self.sibling = 2 * self.z + 1 - self.c

    def nearest(self, n):
        chip = 0
        for z in range(self.line):
            for place, other in enumerate(sorted(range(self.line), key=lambda y: abs(y - z))):
                chip = jnp.where((self.z == z) & (n == place), other, chip)
        return chip

    def enter(self, seq=True, fsdp=True):
        barrier = pltpu.get_barrier_semaphore()
        met = 0
        for axis, mine, count, wanted in (
            ("seq", self.s, self.shards, seq), ("fsdp", self.f, self.groups, fsdp),
        ):
            for d in range(1, count if wanted else 1):
                pl.semaphore_signal(
                    barrier, inc=1, device_id={axis: lax.rem(mine + d, count)}, device_id_type=MESH
                )
                met += 1
        pl.semaphore_wait(barrier, met)


class Spread:
    def __init__(self, at, src, dst, send, recv, axis="fsdp"):
        self.at, self.src, self.dst, self.send, self.recv, self.axis = at, src, dst, send, recv, axis
        self.mine, self.count = (at.f, at.groups) if axis == "fsdp" else (at.s, at.shards)

    def copy(self, d):
        peer = lax.rem(self.mine + d, self.count)
        return remote(
            self.src(peer), self.dst(self.mine), self.send.at[d], self.recv.at[d], self.axis, peer
        )

    def start(self):
        for d in range(1, self.count):
            self.copy(d).start()

    def source(self, d):
        return lax.rem(self.mine + self.count - d, self.count)

    def arrive(self, d):
        origin = self.source(d)
        remote(
            self.src(origin), self.dst(origin), self.send.at[d], self.recv.at[d], self.axis, origin
        ).wait_recv()

    def sent(self):
        for d in range(1, self.count):
            self.copy(d).wait_send()

    def finish(self):
        for d in range(1, self.count):
            self.arrive(d)
        self.sent()


class LineGather:
    def __init__(self, at, src, buf, send, recv, pieces):
        self.at, self.src, self.buf, self.send, self.recv, self.pieces = at, src, buf, send, recv, pieces
        self.rows = buf.shape[1] // pieces

    def copy(self, slot, piece, kind, first=False):
        at = self.at
        rows = pl.ds(piece * self.rows, self.rows)
        there = self.buf.at[slot, rows]
        peer = (at.sibling, at.s + 2, at.s - 2)[kind]
        return remote(
            self.src.at[rows] if first else there, there,
            self.send.at[slot, piece, kind], self.recv.at[slot, piece], "seq", peer,
        )

    def start(self, first=0, last=None):
        at = self.at
        for piece in range(first, self.pieces if last is None else last):
            @pl.when(at.z + 1 < at.line)
            def _():
                self.copy(at.s, piece, 1, True).start()

            @pl.when(at.z > 0)
            def _():
                self.copy(at.s, piece, 2, True).start()

            self.copy(at.s, piece, 0, True).start()

    def arrive(self, chip, piece):
        at = self.at
        slot = 2 * chip + at.c
        self.copy(slot, piece, 0).wait_recv()

        @pl.when((chip < at.z) & (at.z + 1 < at.line))
        def _():
            self.copy(slot, piece, 1).start()

        @pl.when((chip > at.z) & (at.z > 0))
        def _():
            self.copy(slot, piece, 2).start()

        self.copy(slot, piece, 0).start()

    def settle(self, chip):
        for piece in range(self.pieces):
            self.copy(2 * chip + 1 - self.at.c, piece, 0).wait_recv()

    def pass_on(self, d):
        at = self.at
        for piece in range(self.pieces):
            for chip, known in ((at.z - d, at.z - d >= 0), (at.z + d, at.z + d < at.line)):
                @pl.when(known)
                def _():
                    self.arrive(chip, piece)

    def distances(self, body, beside=None):
        at = self.at

        @pl.loop(0, at.line)
        def _(n):
            @pl.when(n > 0)
            def _():
                self.pass_on(n)
                if beside is not None:
                    beside(n)

            chip = at.nearest(n)
            self.settle(chip)
            body(chip)

    def sent(self):
        at = self.at
        for chip in range(at.line):
            slot = 2 * chip + at.c
            for piece in range(self.pieces):
                self.copy(slot, piece, 0).wait_send()

                @pl.when((chip <= at.z) & (at.z + 1 < at.line))
                def _():
                    self.copy(slot, piece, 1).wait_send()

                @pl.when((chip >= at.z) & (at.z > 0))
                def _():
                    self.copy(slot, piece, 2).wait_send()


class LineScatter:
    def __init__(self, at, parts, heard, into, sems, pieces):
        self.at, self.parts, self.heard, self.into = at, parts, heard, into
        self.sib_send, self.sib_recv, self.send, self.recv = sems
        self.pieces = pieces
        self.rows = parts.shape[2] // pieces

    @staticmethod
    def scratch(line, rows, width, pieces):
        low = pltpu.VMEM((line, rows, width), LOW)
        return [
            pltpu.VMEM((line, 2, rows, width), LOW), low, low,
            dma(line), dma(line), dma(line, pieces), dma(line, pieces),
        ]

    def across(self, chip):
        return remote(
            self.parts.at[chip, 1 - self.at.c], self.heard.at[chip], self.sib_send.at[chip],
            self.sib_recv.at[chip], "seq", self.at.sibling,
        )

    def whole_way(self, chip, start):
        if self.at.line < 4:
            return False
        return jnp.abs(chip - start) == self.at.line - 1

    def joined(self, chip):
        at = self.at
        if at.line < 4:
            return False
        return ((at.z == 1) & (chip == at.line - 1)) | ((at.z == at.line - 2) & (chip == 0))

    def along(self, chip, piece):
        at = self.at
        rows = pl.ds(pl.multiple_of(piece * self.rows, self.rows), self.rows)
        target, slot = chip, at.z
        if at.line >= 4:
            stop = jnp.where(chip > at.z, at.z + 1, at.z - 1)
            target = jnp.where(self.whole_way(chip, at.z), stop, chip)
            slot = jnp.where(self.whole_way(chip, at.z), stop, at.z)
        return remote(
            self.parts.at[chip, 1 - at.c, rows], self.into.at[slot, rows], self.send.at[chip, piece],
            self.recv.at[slot, piece], "seq", 2 * target + at.c,
        )

    def landed(self, slot, piece):
        rows = pl.ds(pl.multiple_of(piece * self.rows, self.rows), self.rows)
        there = self.into.at[slot, rows]
        remote(
            there, there, self.recv.at[slot, piece], self.recv.at[slot, piece], "seq", self.at.sibling
        ).wait_recv()

    def add(self, chip, piece, extras, store):
        @pl.loop(0, self.rows // 16)
        def _(block):
            rows = pl.ds(pl.multiple_of(piece * self.rows + block * 16, 16), 16)
            total = self.parts[chip, self.at.c, rows, :].astype(WIDE) + self.heard[chip, rows, :].astype(WIDE)
            for known, slot in extras:
                here = self.into[slot, rows, :].astype(WIDE)
                total = total + (here if known is True else jnp.where(known, here, 0.0))
            store(rows, total)

    def store_out(self, chip):
        def store(rows, total):
            self.parts[chip, 1 - self.at.c, rows, :] = total.astype(LOW)

        return store

    def goes(self, chip):
        goes = chip != self.at.z
        return goes & jnp.logical_not(self.joined(chip)) if self.at.line >= 4 else goes

    def push(self, chip, first=0, last=None):
        @pl.when(self.goes(chip))
        def _():
            if first == 0:
                self.across(chip).wait()

            @pl.loop(first, self.pieces if last is None else last)
            def _(piece):
                self.add(chip, piece, [], self.store_out(chip))
                self.along(chip, piece).start()

    def join(self, first=0, last=None):
        at = self.at
        if at.line < 4:
            return

        @pl.when((at.z == 1) | (at.z == at.line - 2))
        def _():
            chip = jnp.where(at.z == 1, at.line - 1, 0)
            if first == 0:
                self.across(chip).wait()

            @pl.loop(first, self.pieces if last is None else last)
            def _(piece):
                self.landed(at.z, piece)
                self.add(chip, piece, [(True, at.z)], self.store_out(chip))
                self.along(chip, piece).start()

    def finish(self, store, first=0, last=None):
        at = self.at
        if first == 0:
            self.across(at.z).wait_recv()

        def known(chip):
            heard = chip != at.z
            return heard & jnp.logical_not(self.whole_way(chip, at.z)) if at.line >= 4 else heard

        @pl.loop(first, self.pieces if last is None else last)
        def _(piece):
            for chip in range(at.line):
                @pl.when(known(chip))
                def _():
                    self.landed(chip, piece)

            self.add(at.z, piece, [(known(chip), chip) for chip in range(at.line)], store)

    def sent(self):
        at = self.at
        self.across(at.z).wait_send()
        for chip in range(at.line):
            @pl.when(chip != at.z)
            def _():
                @pl.loop(0, self.pieces)
                def _(piece):
                    self.along(chip, piece).wait_send()


def normalise(source, gain, store, rows):
    @pl.loop(0, rows // 16)
    def _(block):
        here = pl.ds(pl.multiple_of(block * 16, 16), 16)
        values = source(here)
        scale = lax.rsqrt(jnp.mean(values * values, axis=-1, keepdims=True) + EPSILON)
        store(here, (values * scale * gain).astype(LOW))


def mixer_rows(positions):
    return [pl.ds(pl.multiple_of(n, CHUNK), CHUNK) for n in range(0, positions, CHUNK)]


def mix_in_kernel(
    tokens, lru_rows, gelu_rows, gate_rows, up_rows, out_shard, down_shard, gate_block, input_block,
    taps, biases, rates, both_gains,
    normed_far, in_far, ext_far, pre_far, conv_far, r_far, i_far, st_far,
    product_far, par_ref, wr_ref, wi_ref, gains, glu_mine, out_whole, down_whole,
    normed, in_whole, ext, pre_ref, conv_ref, r_ref, i_ref, st_ref, product_ref,
    in_shard, glu_shard, small, vecs, gain_shard, held, small_all, vecs_all, gain_all, factors, drive, prod,
    local_sems, tok_send, tok_recv, in_sems, in_xy_send, in_xy_recv, glu_sems, xy_sems, gain_sems, leave_sems,
):
    groups, shards = in_whole.shape[1], in_whole.shape[0]
    at = Place(shards, groups)
    s, f = at.s, at.f
    positions, channels = pre_ref.shape
    width = tokens.shape[1]
    rows = in_shard.shape[1]
    segment = positions // 8
    chunks = positions // CHUNK

    units = gate_rows.shape[1] // shards
    for shard in range(shards):
        part = slice(shard * units, (shard + 1) * units)
        glu_shard[shard, :, :units] = gate_rows[:, part]
        glu_shard[shard, :, units:] = up_rows[:, part]
        part = slice(shard * channels, (shard + 1) * channels)
        in_shard[shard, :, :channels] = lru_rows[:, part]
        in_shard[shard, :, channels:] = gelu_rows[:, part]
    size = gate_block.shape[1]
    small[:, :size] = gate_block[...]
    small[:, size:] = input_block[...]
    vecs[0:4, :] = taps[...].astype(WIDE)
    vecs[4:7, :] = biases[...].astype(WIDE)
    vecs[7:8, :] = rates[...]
    gain_shard[...] = jnp.zeros_like(gain_shard)
    gain_shard[0:2, :] = both_gains[...].astype(WIDE)
    leaving = [
        (normed, normed_far), (in_whole, in_far), (ext, ext_far), (pre_ref, pre_far), (conv_ref, conv_far),
        (r_ref, r_far), (i_ref, i_far), (st_ref, st_far), (product_ref, product_far),
    ]
    leaving = [pltpu.make_async_copy(a, b, leave_sems.at[n]) for n, (a, b) in enumerate(leaving)]
    keep = [
        (tokens, held.at[s]), (in_shard.at[s], in_whole.at[s, f]), (glu_shard.at[s], glu_mine.at[s]),
        (out_shard, out_whole.at[f]), (down_shard, down_whole.at[f]), (small, small_all.at[f]),
        (vecs, vecs_all.at[f]), (gain_shard, gain_all.at[s, f]),
    ]
    keep = [pltpu.make_async_copy(a, b, local_sems.at[n]) for n, (a, b) in enumerate(keep)]
    for copy in keep:
        copy.start()
    at.enter()

    def over_fsdp(src, dst, n):
        return Spread(at, lambda peer: src, lambda origin: dst.at[origin], xy_sems.at[n, 0], xy_sems.at[n, 1])

    gain_xy = Spread(
        at, lambda peer: gain_shard, lambda origin: gain_all.at[s, origin],
        xy_sems.at[0, 0], xy_sems.at[0, 1],
    )
    small_xy = over_fsdp(small, small_all, 1)
    vecs_xy = over_fsdp(vecs, vecs_all, 2)
    out_xy = over_fsdp(out_shard, out_whole, 3)
    down_xy = over_fsdp(down_shard, down_whole, 4)
    in_z = Spread(
        at, lambda peer: in_shard.at[peer], lambda origin: in_whole.at[origin, f],
        in_sems.at[0], in_sems.at[1], "seq",
    )
    glu_z = Spread(
        at, lambda peer: glu_shard.at[peer], lambda origin: glu_mine.at[origin],
        glu_sems.at[0], glu_sems.at[1], "seq",
    )
    gain_z = Spread(
        at, lambda peer: gain_all.at[s], lambda origin: gain_all.at[origin],
        gain_sems.at[0], gain_sems.at[1], "seq",
    )

    def in_xy(index):
        return Spread(
            at, lambda peer: in_whole.at[index, f], lambda origin: in_whole.at[index, origin],
            in_xy_send.at[index], in_xy_recv.at[index],
        )

    gather = LineGather(at, tokens, held, tok_send, tok_recv, tok_send.shape[1])
    gain_xy.start()
    in_z.start()
    keep[1].wait()
    in_xy(s).start()
    gather.start()
    vecs_xy.start()
    small_xy.start()
    keep[7].wait()
    gain_xy.finish()
    gain_z.start()
    for d in range(1, shards):
        in_z.arrive(d)
        in_xy(in_z.source(d)).start()
    out_xy.start()
    early = min(3, shards)
    for d in range(1, early):
        glu_z.copy(d).start()
    down_xy.start()
    gain_z.finish()
    for origin in range(shards):
        for other in range(groups):
            first = (origin * groups + other) * rows
            gains[:, first : first + rows] = gain_all[origin, other]
    keep[0].wait()

    def take(chip):
        for core in range(2):
            slot = 2 * chip + core

            def store(here, value):
                normed[slot, here, :] = value

            normalise(
                lambda here: held[slot, here, :].astype(WIDE), gains[0:1, :], store, tokens.shape[0]
            )

    def rest(n):
        @pl.when(n == at.line - 1)
        def _():
            for d in range(early, shards):
                glu_z.copy(d).start()

    gather.distances(take, rest)
    leaving[0].start()
    keep[6].wait()
    vecs_xy.finish()
    keep[5].wait()
    small_xy.finish()
    local = small.shape[0]
    wr_ref[...] = jnp.zeros_like(wr_ref)
    wi_ref[...] = jnp.zeros_like(wi_ref)
    flat = small_all[...].reshape(channels, 2 * size)
    for n in range(channels // size):
        block = slice(n * size, (n + 1) * size)
        wr_ref[block, block] = flat[block, :size]
        wi_ref[block, block] = flat[block, size:]
    for other in range(groups):
        par_ref[:, other * local : (other + 1) * local] = vecs_all[other]
    ext[0:8, :] = jnp.zeros((8, channels), WIDE)
    st_ref[0:8, :] = jnp.zeros((8, channels), WIDE)
    for index in range(shards):
        for d in range(1, groups):
            in_xy(index).arrive(d)
    leaving[1].start()
    @pl.loop(0, at.line)
    def _(chip):
        pair = normed[pl.ds(2 * chip, 2), :, :].reshape(2 * tokens.shape[0], width)
        both = dot(pair, in_whole[...].reshape(width, 2 * channels))
        base = pl.multiple_of(chip * 2 * tokens.shape[0], CHUNK)
        here = pl.ds(base, 2 * tokens.shape[0])
        ext[pl.ds(base + 8, 2 * tokens.shape[0]), :] = both[:, :channels].astype(LOW).astype(WIDE)
        pre_ref[here, :] = both[:, channels:]

    @pl.loop(0, chunks)
    def _(n):
        base = pl.multiple_of(n * CHUNK, CHUNK)
        here = pl.ds(base, CHUNK)
        block = ext[pl.ds(base, CHUNK + 8), :]
        conv = jnp.broadcast_to(par_ref[4:5, :], (CHUNK, channels))
        for k in range(4):
            conv = conv + par_ref[k : k + 1, :] * block[8 - k : 8 - k + CHUNK]
        conv_low = conv.astype(LOW)
        conv_ref[here, :] = conv_low
        r = jax.nn.sigmoid(dot(conv_low, wr_ref[...]) + par_ref[5:6, :])
        gate = jax.nn.sigmoid(dot(conv_low, wi_ref[...]) + par_ref[6:7, :])
        log_decay = r * par_ref[7:8, :]
        m = jnp.sqrt(one_minus_exp(-2.0 * log_decay))
        factor = jnp.exp(log_decay)
        r_ref[here, :] = r
        i_ref[here, :] = gate
        put(factors, here, factor)
        put(drive, here, m * gate * conv_low.astype(WIDE))

    for n in range(2, 7):
        leaving[n].start()

    def step(i, n, state, product):
        here = pl.ds(i, 8, stride=segment)
        factor = factors[n, here, :]
        state = factor * state + drive[n, here, :]
        product = factor * product
        drive[n, here, :] = state
        prod[n, here, :] = product
        return state, product

    state, product = scan_segments(step, segment, lane_tiles(channels))
    state, product = state[:, :channels], product[:, :channels]
    carry = jnp.zeros((1, channels), WIDE)
    for k in range(8):
        for part in range(segment // CHUNK):
            base = k * segment + part * CHUNK
            here = slice(base, base + CHUNK)
            states = get(drive, here, channels) + get(prod, here, channels) * carry
            st_ref[base + 8 : base + 8 + CHUNK, :] = states
            product_ref[here, :] = (
                states.astype(LOW).astype(WIDE) * gelu(pre_ref[here, :])
            ).astype(LOW)
        carry = state[k : k + 1] + product[k : k + 1] * carry

    leaving[7].start()
    leaving[8].start()
    glu_z.finish()
    out_xy.finish()
    down_xy.finish()
    gather.sent()
    in_z.sent()
    for index in range(shards):
        in_xy(index).sent()
    for n in (2, 3, 4):
        keep[n].wait()
    for copy in leaving:
        copy.wait()


def mix_in(
    tokens, lru_rows, gelu_rows, gate_rows, up_rows, out_shard, down_shard, gate_block, input_block,
    taps, biases, rates, both_gains, shards, groups,
):
    rows = lru_rows.shape[0]
    block, width = tokens.shape
    positions, channels = shards * block, lru_rows.shape[1] // shards
    both = 2 * channels
    in_shape = (shards, rows, both)
    glu_shape = (shards, rows, 2 * (gate_rows.shape[1] // shards))
    local = gate_block.shape[0]
    small_shape = (gate_block.shape[0], 2 * gate_block.shape[1])
    pieces = 2
    wide = jax.ShapeDtypeStruct((positions, channels), WIDE)
    low = jax.ShapeDtypeStruct((positions, channels), LOW)
    longer = jax.ShapeDtypeStruct((positions + 8, channels), WIDE)
    square = jax.ShapeDtypeStruct((channels, channels), LOW)
    saved = [
        jax.ShapeDtypeStruct((shards, block, width), LOW),
        jax.ShapeDtypeStruct((shards, groups, rows, both), LOW),
        longer, wide, low, wide, wide, longer,
        low,
    ]
    held = [
        jax.ShapeDtypeStruct((8, channels), WIDE), square, square, jax.ShapeDtypeStruct((8, width), WIDE),
    ]
    far = [
        jax.ShapeDtypeStruct(glu_shape, LOW),
        jax.ShapeDtypeStruct((groups,) + out_shard.shape, LOW),
        jax.ShapeDtypeStruct((groups,) + down_shard.shape, LOW),
    ]
    return pl.pallas_call(
        mix_in_kernel,
        out_shape=saved + held + far,
        in_specs=[HELD] * 13,
        out_specs=[ANY] * len(saved) + [HELD] * len(held) + [ANY] * len(far),
        scratch_shapes=[pltpu.VMEM(member.shape, member.dtype) for member in saved]
        + [
            pltpu.VMEM(in_shape, LOW), pltpu.VMEM(glu_shape, LOW), pltpu.VMEM(small_shape, LOW),
            pltpu.VMEM((8, local), WIDE), pltpu.VMEM((8, rows), WIDE),
            pltpu.VMEM((shards, block, width), LOW),
            pltpu.VMEM((groups,) + small_shape, LOW),
            pltpu.VMEM((groups, 8, local), WIDE),
            pltpu.VMEM((shards, groups, 8, rows), WIDE),
        ]
        + [pltpu.VMEM((lane_tiles(channels), positions, 128), WIDE)] * 3
        + [
            dma(8), dma(shards, pieces, 3), dma(shards, pieces), dma(2, shards), dma(shards, groups),
            dma(shards, groups), dma(2, shards), dma(5, 2, groups), dma(2, shards), dma(9),
        ],
        compiler_params=pltpu.CompilerParams(
            collective_id=1, has_side_effects=True, vmem_limit_bytes=VMEM_BYTES
        ),
        name="mix_in",
    )(
        tokens, lru_rows, gelu_rows, gate_rows, up_rows, out_shard, down_shard, gate_block, input_block,
        taps, biases, rates, both_gains,
    )


def feed_kernel(
    product_far, out_far, glu_mine, down_in, cotangent, tokens, gains,
    middle, middle_grad, mixed_low, gain_sums, hidden_far, glu_grad, down_grad, glu_first,
    product, out_whole, held, cots, glu, down, both, hidden, wide_pair, hidden_pair, normed2, staged, down_staged,
    parts, heard, into, sib_send, sib_recv, line_send, line_recv,
    local_sems, glu_send, glu_recv, two_send, two_recv, cot_send, cot_recv, stage_sems, first_sems,
):
    shards, groups = glu.shape[0], glu.shape[1]
    at = Place(shards, groups)
    s, f = at.s, at.f
    block, width = tokens.shape
    units = down.shape[0]
    pair = 2 * block

    keep = [(glu_mine, glu.at[:, f]), (down_in, down), (cotangent, cots.at[s])]
    keep += [(product_far, product), (out_far, out_whole)]
    keep = [pltpu.make_async_copy(a, b, local_sems.at[n]) for n, (a, b) in enumerate(keep)]
    for copy in keep:
        copy.start()
    at.enter()
    def glu_xy(index):
        return Spread(
            at, lambda peer: glu_mine.at[index], lambda origin: glu.at[index, origin],
            glu_send.at[index], glu_recv.at[index],
        )

    cot_z = LineGather(at, cotangent, cots, cot_send, cot_recv, cot_send.shape[1])
    two_z = LineGather(at, normed2, held, two_send, two_recv, two_send.shape[1])
    sums = LineScatter(
        at, parts, heard, into, (sib_send, sib_recv, line_send, line_recv), line_send.shape[1]
    )
    for index in range(shards):
        glu_xy(index).start()
    cot_z.start()

    def split(chip, columns, value, parts):
        parts[chip, :, :, columns] = value.astype(LOW).reshape(2, block, value.shape[1])

    def columns_of(j):
        return pl.ds(pl.multiple_of(j * 256, 256), 256)

    def pair_rows(chip):
        return pl.ds(pl.multiple_of(chip * pair, pair), pair)

    keep[3].wait()
    keep[4].wait()

    def project(chip):
        @pl.loop(0, width // 256)
        def _(j):
            value = dot(product[pair_rows(chip), :], out_whole[:, columns_of(j)])
            split(chip, columns_of(j), value, parts)

        sums.across(chip).start()

    for k in range(at.line // 2):
        project(at.line - 1 - k)
        project(k)
        sums.push(at.line - 1 - k, 0, 1)
        sums.push(k, 0, 1)
    for k in range(at.line // 2):
        sums.push(at.line - 1 - k, 1)
        sums.push(k, 1)
    sums.join(0, 1)
    cot_z.pass_on(1)

    def to_middle(here, total):
        values = total + tokens[here, :].astype(WIDE)
        middle[here, :] = values
        scale = lax.rsqrt(jnp.mean(values * values, axis=-1, keepdims=True) + EPSILON)
        normed2[here, :] = (values * scale * gains[1:2, :]).astype(LOW)

    sums.finish(to_middle, 0, 1)
    two_z.start(0, 1)
    cot_z.pass_on(2)
    sums.join(1)
    sums.finish(to_middle, 1)
    two_z.start(1)
    own_copy = pltpu.make_async_copy(normed2, held.at[s], local_sems.at[5])
    own_copy.start()
    keep[0].wait()
    keep[1].wait()
    keep[2].wait()
    sums.sent()
    own_copy.wait()
    for d in range(3, at.line):
        cot_z.pass_on(d)
    for index in range(shards):
        glu_xy(index).finish()

    def open_up(chip):
        rows = held[pl.ds(2 * chip, 2), :, :].reshape(pair, width)
        grads = cots[pl.ds(2 * chip, 2), :, :].reshape(pair, width)

        @pl.loop(0, 2 * units // 256)
        def _(j):
            wide_pair[:, columns_of(j)] = dot(
                rows, glu[:, :, :, columns_of(j)].reshape(width, 256)
            )

        @pl.loop(0, units // 256)
        def _(j):
            hidden_pair[:, columns_of(j)] = times_transpose(grads, down[columns_of(j), :])

        @pl.loop(0, pair // 16)
        def _(n):
            part = pl.ds(pl.multiple_of(n * 16, 16), 16)
            there = pl.ds(pl.multiple_of(chip * pair + n * 16, 16), 16)
            opened, slope = gelu_and_slope(wide_pair[part, :units])
            up = wide_pair[part, units:]
            grad = hidden_pair[part, :]
            hidden[there, :] = (opened * up).astype(LOW)
            both[there, :units] = (grad * up * slope).astype(LOW)
            both[there, units:] = (grad * opened).astype(LOW)

    def to_normed2(chip):
        @pl.loop(0, shards)
        def _(j):
            value = times_transpose(
                both[pair_rows(chip), :], glu[j].reshape(width // shards, 2 * units)
            )
            split(chip, columns_of(j), value, parts)

        sums.across(chip).start()

    cot_z.settle(at.z)
    two_z.settle(at.z)

    @pl.loop(1, at.line + 1)
    def _(n):
        chip = at.nearest(lax.rem(n, at.line))

        @pl.when(n < at.line)
        def _():
            two_z.pass_on(n)
            two_z.settle(chip)
            cot_z.settle(chip)

        open_up(chip)

        @pl.when(n > 1)
        def _():
            sums.push(at.nearest(n - 1))

        to_normed2(chip)

    hidden_leave = pltpu.make_async_copy(hidden, hidden_far, local_sems.at[6])
    hidden_leave.start()
    def glu_out(j):
        return pltpu.make_async_copy(
            staged.at[lax.rem(j, 2)], glu_grad.at[:, j], stage_sems.at[lax.rem(j, 2)]
        )

    def glu_sums(first, last):
        @pl.loop(first, last)
        def _(j):
            @pl.when(j >= first + 2)
            def _():
                glu_out(j - 2).wait()

            rows = held[:, :, columns_of(j)].reshape(shards * block, 256)
            staged[lax.rem(j, 2)] = outer_sum(rows, both[...]).astype(LOW).reshape(staged.shape[1:])
            glu_out(j).start()

        for j in range(max(last - 2, first), last):
            glu_out(j).wait()

    def down_out(j):
        return pltpu.make_async_copy(
            down_staged.at[lax.rem(j, 2)], down_grad.at[columns_of(j)], stage_sems.at[2 + lax.rem(j, 2)]
        )

    def down_sums():
        @pl.loop(0, units // 256)
        def _(j):
            @pl.when(j >= 2)
            def _():
                down_out(j - 2).wait()

            grads = cots[...].reshape(shards * block, width)
            down_staged[lax.rem(j, 2)] = outer_sum(hidden[:, columns_of(j)], grads).astype(LOW)
            down_out(j).start()

    early = glu_first.shape[1]
    glu_early = Spread(
        at, lambda peer: glu_grad.at[peer, pl.ds(0, early)], lambda origin: glu_first.at[origin],
        first_sems.at[0], first_sems.at[1],
    )
    glu_sums(0, early)
    glu_early.start()
    sums.join()
    down_sums()
    glu_sums(early, shards)
    gain_sums[...] = jnp.zeros_like(gain_sums)

    def back(here, grad):
        values = middle[here, :]
        scale = lax.rsqrt(jnp.mean(values * values, axis=-1, keepdims=True) + EPSILON)
        scaled = grad * gains[1:2, :]
        along = jnp.mean(scaled * values, axis=-1, keepdims=True)
        total = cots[at.s, here, :].astype(WIDE) + scale * scaled - values * (scale * scale * scale * along)
        middle_grad[here, :] = total
        mixed_low[here, :] = total.astype(LOW)
        gain_sums[0:1, :] += jnp.sum(grad * values * scale, axis=0, keepdims=True)

    sums.finish(back)
    for j in range(max(units // 256 - 2, 0), units // 256):
        down_out(j).wait()
    hidden_leave.wait()
    glu_early.finish()
    sums.sent()
    two_z.sent()
    cot_z.sent()


def feed(product, out_whole, glu_mine, down_whole, cotangent, tokens, gains, groups):
    shards, rows, both = glu_mine.shape
    block, width = tokens.shape
    units = both // 2
    line, pieces, thirds = shards // 2, 2, 2
    own = jax.ShapeDtypeStruct((block, width), WIDE)
    outs = [
        own, own, jax.ShapeDtypeStruct((block, width), LOW), jax.ShapeDtypeStruct((8, width), WIDE),
        jax.ShapeDtypeStruct((shards * block, units), LOW),
        jax.ShapeDtypeStruct((groups, shards, rows, both), LOW),
        jax.ShapeDtypeStruct((units, width), LOW),
        jax.ShapeDtypeStruct((groups, EARLY, rows, both), LOW),
    ]
    gathered = pltpu.VMEM((shards, block, width), LOW)
    return pl.pallas_call(
        feed_kernel,
        out_shape=outs,
        in_specs=[ANY] * 5 + [HELD] * 2,
        out_specs=[HELD] * 4 + [ANY] * 4,
        scratch_shapes=[
            pltpu.VMEM(product.shape, LOW), pltpu.VMEM(out_whole.shape, LOW),
            gathered, gathered,
            pltpu.VMEM((shards, groups, rows, both), LOW),
            pltpu.VMEM((units, width), LOW),
            pltpu.VMEM((shards * block, both), LOW),
            pltpu.VMEM((shards * block, units), LOW),
            pltpu.VMEM((2 * block, both), WIDE),
            pltpu.VMEM((2 * block, units), WIDE),
            pltpu.VMEM((block, width), LOW),
            pltpu.VMEM((2, groups, rows, both), LOW),
            pltpu.VMEM((2, 256, width), LOW),
        ]
        + LineScatter.scratch(line, block, width, thirds)
        + [
            dma(8), dma(shards, groups), dma(shards, groups), dma(shards, pieces, 3), dma(shards, pieces),
            dma(shards, pieces, 3), dma(shards, pieces), dma(4), dma(2, groups),
        ],
        compiler_params=pltpu.CompilerParams(
            collective_id=2, has_side_effects=True, vmem_limit_bytes=VMEM_BYTES
        ),
        name="feed",
    )(product, out_whole, glu_mine, down_whole, cotangent, tokens, gains)


def back_kernel(
    mixed, hidden_far, down_far, middle_far, middle_grad_far, tokens_far, gains, par_ref, wr_ref, wi_ref,
    out_far, in_far, normed_far, product_far, ext_far, pre_far, conv_far, r_far, i_far, st_far,
    glu_grad, glu_first, down_grad, mlp_parts,
    result, tokens_grad, glu_out, in_out, out_heard, small_heard, gain_out, glu_heard, in_grad, down_heard,
    middle, middle_grad, tokens, held, in_whole, out_whole, product, ext, pre, conv_ref, r_ref, i_ref, st_ref,
    both, pair_grad, staged, adj, totals_ref, wr_sum, wi_sum,
    out_sum, out_grad, small, gain_row, gain_parts, gain_heard, gain_sum, glu_parts, glu_sum, in_heard, in_sum,
    fed_parts, fed_heard, fed_into, fed_sib_send, fed_sib_recv, fed_send, fed_recv,
    parts, heard, into, sib_send, sib_recv, line_send, line_recv,
    local_sems, held_send, held_recv, glu_xy_sems, down_sems, stage_sems, in_xy_sems, out_sems,
    small_sems, gain_xy_sems, glu_sems, in_sems, gain_sems,
):
    shards, groups = in_whole.shape[0], in_whole.shape[1]
    at = Place(shards, groups)
    s, f = at.s, at.f
    block, width = tokens.shape
    positions, channels = product.shape
    rows = in_whole.shape[2]
    pair = 2 * block
    segment = positions // 8
    chunks = positions // CHUNK

    keep = [
        (mixed, held.at[s]), (out_far, out_whole), (pre_far, pre), (st_far, st_ref),
        (product_far, product), (r_far, r_ref), (i_far, i_ref), (conv_far, conv_ref),
        (ext_far, ext), (in_far, in_whole), (mixed, held.at[s]), (normed_far, held),
        (middle_far, middle), (middle_grad_far, middle_grad), (tokens_far, tokens),
    ]
    keep = [pltpu.make_async_copy(a, b, local_sems.at[n]) for n, (a, b) in enumerate(keep)]
    for copy in keep[:10] + keep[12:]:
        copy.start()
    at.enter()

    def over_fsdp(src, dst, sems):
        return Spread(
            at, lambda peer: src.at[peer], lambda origin: dst.at[origin], sems.at[0], sems.at[1]
        )

    def over_seq(src, dst, sems):
        return Spread(
            at, lambda peer: src.at[peer], lambda origin: dst.at[origin], sems.at[0], sems.at[1], "seq"
        )

    early = glu_first.shape[1]
    glu_xy = Spread(
        at, lambda peer: glu_grad.at[peer, pl.ds(early, shards - early)], lambda origin: glu_heard.at[origin],
        glu_xy_sems.at[0], glu_xy_sems.at[1],
    )
    in_xy = over_fsdp(in_grad, in_heard, in_xy_sems)
    out_xy = over_fsdp(out_grad, out_heard, out_sems)
    down_xy = over_fsdp(down_grad, down_heard, down_sems)
    small_xy = over_fsdp(small, small_heard, small_sems)
    gain_xy = over_fsdp(gain_parts, gain_heard, gain_xy_sems)
    glu_z = over_seq(glu_sum, glu_out, glu_sems)
    in_z = over_seq(in_sum, in_out, in_sems)
    gain_z = over_seq(gain_sum, gain_out, gain_sems)
    mixed_z = LineGather(at, mixed, held, held_send, held_recv, held_send.shape[1])
    fed = LineScatter(
        at, fed_parts, fed_heard, fed_into,
        (fed_sib_send, fed_sib_recv, fed_send, fed_recv), fed_send.shape[1],
    )
    sums = LineScatter(
        at, parts, heard, into, (sib_send, sib_recv, line_send, line_recv), line_send.shape[1]
    )
    mixed_z.start()
    glu_xy.start()
    out_sum[...] = jnp.zeros_like(out_sum)

    def columns_of(j):
        return pl.ds(pl.multiple_of(j * 256, 256), 256)

    def feed_out(hidden, down, sems):
        loads = [
            pltpu.make_async_copy(hidden_far, hidden, sems.at[0]),
            pltpu.make_async_copy(down_far, down, sems.at[1]),
        ]
        for load in loads:
            load.start()
        for load in loads:
            load.wait()

        def one(chip):
            @pl.loop(0, width // 256)
            def _(j):
                there = pl.ds(pl.multiple_of(chip * pair, pair), pair)
                value = dot(hidden[there, :], down[:, columns_of(j)])
                fed_parts[chip, :, :, columns_of(j)] = value.astype(LOW).reshape(2, block, 256)

            fed.across(chip).start()

        for k in range(at.line // 2):
            one(at.line - 1 - k)
            one(k)

    pl.run_scoped(
        feed_out, pltpu.VMEM(hidden_far.shape, LOW), pltpu.VMEM(down_far.shape, LOW), dma(2)
    )
    for n in (0, 1, 2, 3, 4):
        keep[n].wait()

    def mixed_back(chip):
        rows = held[pl.ds(2 * chip, 2), :, :].reshape(pair, width)
        pair_grad[...] = times_transpose(rows, out_whole[...])

        @pl.loop(0, pair // 64)
        def _(n):
            grad = pair_grad[pl.ds(pl.multiple_of(n * 64, 64), 64), :]
            base = pl.multiple_of(chip * pair + n * 64, 64)
            here = pl.ds(base, 64)
            opened, slope = gelu_and_slope(pre[here, :])
            states = st_ref[pl.ds(base + 8, 64), :].astype(LOW).astype(WIDE)
            put(adj, here, (grad * opened).astype(LOW).astype(WIDE))
            both[here, channels:] = (grad * states * slope).astype(LOW)

        there = pl.ds(pl.multiple_of(chip * pair, pair), pair)

        @pl.loop(0, width // 256)
        def _(j):
            part = held[pl.ds(2 * chip, 2), :, columns_of(j)].reshape(pair, 256)
            out_sum[:, columns_of(j)] += outer_sum(product[there, :], part)

    def fed_beside(n):
        @pl.when(n == 2)
        def _():
            @pl.loop(1, at.line)
            def _(far):
                fed.push(at.nearest(at.line - far))

    mixed_z.distances(mixed_back, fed_beside)
    def mix_back(factors, prod, cg, carries):
        keep[5].wait()

        @pl.loop(0, chunks)
        def _(n):
            here = pl.ds(pl.multiple_of(n * CHUNK, CHUNK), CHUNK)
            put(factors, here, jnp.exp(r_ref[here, :] * par_ref[7:8, :]))

        def step(j, n, flow, product):
            here = pl.ds(segment - 1 - j, 8, stride=segment)
            factor = factors[n, here, :]
            adjoint = adj[n, here, :] + flow
            adj[n, here, :] = adjoint
            prod[n, here, :] = product
            return factor * adjoint, factor * product

        flow, through = scan_segments(step, segment, lane_tiles(channels))
        flow, through = flow[:, :channels], through[:, :channels]
        carry = jnp.zeros((1, channels), WIDE)
        for k in range(7, -1, -1):
            carries[k : k + 1, :] = carry
            carry = flow[k : k + 1] + through[k : k + 1] * carry
        for n in (6, 7, 8):
            keep[n].wait()
        cg[pl.ds(positions, 8), :] = jnp.zeros((8, channels), WIDE)
        wr_sum[...] = jnp.zeros_like(wr_sum)
        wi_sum[...] = jnp.zeros_like(wi_sum)

        def grads(c, sums):
            base = pl.multiple_of(c * CHUNK, CHUNK)
            rows = pl.ds(base, CHUNK)
            adjoint = get(adj, rows, channels) + get(prod, rows, channels) * carries[pl.ds(base // segment, 1), :]
            before = st_ref[pl.ds(base, CHUNK + 8), :][7 : 7 + CHUNK]
            conv_low = conv_ref[rows, :]
            conv = conv_low.astype(WIDE)
            r = r_ref[rows, :]
            gate = i_ref[rows, :]
            factor = get(factors, rows, channels)
            m = jnp.sqrt(one_minus_exp(-2.0 * (r * par_ref[7:8, :])))
            driven = adjoint * gate
            by_log = adjoint * before * factor - driven * conv * factor * factor / m
            by_r = by_log * par_ref[7:8, :] * r * (1.0 - r)
            by_i = adjoint * m * conv * gate * (1.0 - gate)
            by_r_low = by_r.astype(LOW)
            by_i_low = by_i.astype(LOW)
            conv_grad = (
                driven * m
                + times_transpose(by_r_low, wr_ref[...])
                + times_transpose(by_i_low, wi_ref[...])
            )
            cg[rows, :] = conv_grad
            wr_sum[...] += outer_sum(conv_low, by_r_low)
            wi_sum[...] += outer_sum(conv_low, by_i_low)
            near = ext[pl.ds(base, CHUNK + 8), :]
            rows_of = [conv_grad * near[8 - k : 8 - k + CHUNK] for k in range(4)]
            rows_of += [conv_grad, by_r, by_i, by_log * r]
            return tuple(
                total + jnp.sum(member, axis=0, keepdims=True) for total, member in zip(sums, rows_of)
            )

        zero = jnp.zeros((1, channels), WIDE)
        totals = lax.fori_loop(0, chunks, grads, (zero,) * 8)
        for k in range(8):
            totals_ref[k : k + 1, :] = totals[k]
        @pl.loop(0, chunks)
        def _(c):
            base = pl.multiple_of(c * CHUNK, CHUNK)
            near = cg[pl.ds(base, CHUNK + 8), :]
            total = jnp.zeros((CHUNK, channels), WIDE)
            for k in range(4):
                total = total + par_ref[k : k + 1, :] * near[k : k + CHUNK]
            both[pl.ds(base, CHUNK), :channels] = total.astype(LOW)

    tiles = pltpu.VMEM((lane_tiles(channels), positions, 128), WIDE)
    pl.run_scoped(
        mix_back, tiles, tiles, pltpu.VMEM((positions + 8, channels), WIDE), pltpu.VMEM((8, channels), WIDE)
    )
    fed.join()
    keep[9].wait()
    down_xy.start()

    def project(chip):
        rows = both[pl.ds(pl.multiple_of(chip * pair, pair), pair), :]

        @pl.loop(0, shards)
        def _(j):
            value = times_transpose(rows, in_whole[j].reshape(width // shards, 2 * channels))
            parts[chip, :, :, columns_of(j)] = value.astype(LOW).reshape(2, block, value.shape[1])

        sums.across(chip).start()

    for k in range(at.line // 2):
        project(at.line - 1 - k)
        project(k)
        sums.push(at.line - 1 - k)
        sums.push(k)
    mixed_z.sent()
    keep[11].start()
    local = small.shape[1] - 8
    size = small.shape[2] // 2
    for n in range(channels // size):
        part = slice(n * size, (n + 1) * size)
        wr_sum[part, :size] = wr_sum[part, part]
        wi_sum[part, :size] = wi_sum[part, part]
    for group in range(groups):
        part = slice(group * local, (group + 1) * local)
        small[group, :local, :size] = wr_sum[part, :size]
        small[group, :local, size:] = wi_sum[part, :size]
        for k in range(8):
            small[group, local + k : local + k + 1, :local] = totals_ref[k : k + 1, part]
    small_xy.start()
    keep[11].wait()

    def in_done(j):
        return pltpu.make_async_copy(
            staged.at[lax.rem(j, 2)], in_grad.at[:, j], stage_sems.at[lax.rem(j, 2)]
        )

    @pl.loop(0, shards)
    def _(j):
        @pl.when(j >= 2)
        def _():
            in_done(j - 2).wait()

        part = held[:, :, columns_of(j)].reshape(positions, 256)
        staged[lax.rem(j, 2)] = outer_sum(part, both[...]).astype(LOW).reshape(staged.shape[1:])
        in_done(j).start()

    for j in range(shards - 2, shards):
        in_done(j).wait()
    in_xy.start()
    in_own = pltpu.make_async_copy(in_grad.at[f], in_heard.at[f], local_sems.at[16])
    in_own.start()
    sums.join()
    glu_xy.finish()

    def glu_load(d, origin, first=False):
        peer = lax.rem(s + d, shards)
        half = lax.rem(d, 2)
        source = glu_first.at[origin, peer] if first else glu_heard.at[origin, peer - early]
        return pltpu.make_async_copy(
            source, glu_parts.at[half, origin], glu_sems.at[2 + half, origin]
        )

    def glu_load_own(d):
        peer = lax.rem(s + d, shards)
        half = lax.rem(d, 2)
        return pltpu.make_async_copy(
            glu_grad.at[f, peer], glu_parts.at[half, f], glu_sems.at[2 + half, f]
        )

    def glu_loads(d):
        glu_load_own(d).start()
        peer = lax.rem(s + d, shards)
        for first, known in ((True, peer < early), (False, peer >= early)):
            @pl.when(known)
            def _():
                for hop in range(1, groups):
                    glu_load(d, lax.rem(f + hop, groups), first).start()

    def add(parts, total, peer):
        @pl.loop(0, total.shape[1] // 16)
        def _(n):
            here = pl.ds(pl.multiple_of(n * 16, 16), 16)
            value = parts[0, here, :].astype(WIDE)
            for origin in range(1, groups):
                value = value + parts[origin, here, :].astype(WIDE)
            total[peer, here, :] = value.astype(total.dtype)

    glu_loads(1)

    @pl.loop(1, shards + 1)
    def _(d):
        @pl.when(d < shards)
        def _():
            glu_loads(d + 1)

        for origin in range(groups):
            pltpu.make_async_copy(
                glu_first.at[origin, 0], glu_parts.at[lax.rem(d, 2), origin],
                glu_sems.at[2 + lax.rem(d, 2), origin],
            ).wait()
        add(glu_parts.at[lax.rem(d, 2)], glu_sum, lax.rem(s + d, shards))

        @pl.when(d < shards)
        def _():
            glu_z.copy(d).start()

    glu_own = pltpu.make_async_copy(glu_sum.at[s], glu_out.at[s], local_sems.at[17])
    glu_own.start()
    out_grad[...] = out_sum[...].astype(LOW).reshape(out_grad.shape)
    out_xy.start()
    gain_row[...] = jnp.zeros_like(gain_row)

    for n in (12, 13, 14):
        keep[n].wait()

    def store_result(here, total):
        result[here, :] = (middle[here, :] + total).astype(LOW)

    fed.finish(store_result)

    def back(here, grad):
        values = tokens[here, :].astype(WIDE)
        scale = lax.rsqrt(jnp.mean(values * values, axis=-1, keepdims=True) + EPSILON)
        scaled = grad * gains[0:1, :]
        along = jnp.mean(scaled * values, axis=-1, keepdims=True)
        total = middle_grad[here, :] + scale * scaled - values * (scale * scale * scale * along)
        tokens_grad[here, :] = total.astype(LOW)
        gain_row[0:1, :] += jnp.sum(grad * values * scale, axis=0, keepdims=True)

    sums.finish(back)
    for group in range(groups):
        for shard in range(shards):
            first = (shard * groups + group) * rows
            gain_parts[group, shard, 0:1, :] = gain_row[0:1, first : first + rows]
            gain_parts[group, shard, 1:2, :] = mlp_parts[0:1, first : first + rows]
    gain_xy.start()
    in_own.wait()
    in_xy.finish()

    @pl.loop(1, shards + 1)
    def _(d):
        peer = lax.rem(s + d, shards)
        add(in_heard.at[:, peer], in_sum, peer)

        @pl.when(d < shards)
        def _():
            in_z.copy(d).start()

    last = [
        pltpu.make_async_copy(in_sum.at[s], in_out.at[s], local_sems.at[18]),
        pltpu.make_async_copy(out_grad.at[f], out_heard.at[f], local_sems.at[19]),
        pltpu.make_async_copy(small.at[f], small_heard.at[f], local_sems.at[20]),
    ]
    for copy in last:
        copy.start()
    gain_xy.finish()
    total = gain_parts[f]
    for d in range(1, groups):
        total = total + gain_heard[lax.rem(f + d, groups)]
    gain_sum[...] = total
    gain_z.start()
    gain_own = pltpu.make_async_copy(gain_sum.at[s], gain_out.at[s], local_sems.at[21])
    gain_own.start()
    fed.sent()
    sums.sent()
    for spread in (small_xy, out_xy, down_xy, glu_z, gain_z, in_z):
        spread.finish()
    for copy in (glu_own, gain_own, *last):
        copy.wait()


def back(
    mixed, hidden, down_whole, middle, middle_grad, tokens, gains, par, wr, wi,
    out_whole, in_whole, normed, product, ext, pre, conv, r, i, st, glu_grad, glu_first, down_grad, mlp_sums, size,
):
    shards, groups, rows, both = in_whole.shape
    block, width = tokens.shape
    positions, channels = product.shape
    line, pieces, halves = shards // 2, 2, 2
    local = channels // groups
    short = jax.ShapeDtypeStruct((block, width), LOW)
    glu_shape = glu_grad.shape[1:]
    in_shape = (groups, shards, rows, both)
    outs = [
        short, short, jax.ShapeDtypeStruct(glu_shape, LOW), jax.ShapeDtypeStruct(in_shape[1:], LOW),
        jax.ShapeDtypeStruct((groups, local, width), LOW),
        jax.ShapeDtypeStruct((groups, local + 8, 2 * size), WIDE),
        jax.ShapeDtypeStruct((shards, 8, rows), WIDE),
        jax.ShapeDtypeStruct((groups, shards - glu_first.shape[1]) + glu_grad.shape[2:], LOW),
        jax.ShapeDtypeStruct(in_shape, LOW),
        jax.ShapeDtypeStruct(down_grad.shape, LOW),
    ]
    late = [middle, middle_grad, tokens]
    far = [out_whole, in_whole, normed, product, ext, pre, conv, r, i, st]
    near = [in_whole, out_whole, product, ext, pre, conv, r, i, st]
    return pl.pallas_call(
        back_kernel,
        out_shape=outs,
        in_specs=[ANY] * 6 + [HELD] * 4 + [ANY] * (len(far) + 3) + [HELD],
        out_specs=[HELD] * 2 + [ANY] * 8,
        scratch_shapes=[pltpu.VMEM(member.shape, member.dtype) for member in late]
        + [pltpu.VMEM((shards, block, width), LOW)]
        + [pltpu.VMEM(member.shape, member.dtype) for member in near]
        + [
            pltpu.VMEM((positions, 2 * channels), LOW),
            pltpu.VMEM((2 * block, channels), WIDE),
            pltpu.VMEM((2, groups, rows, both), LOW),
        ]
        + [pltpu.VMEM((lane_tiles(channels), positions, 128), WIDE), pltpu.VMEM((8, channels), WIDE)]
        + [pltpu.VMEM((channels, channels), WIDE)] * 2
        + [
            pltpu.VMEM((channels, width), WIDE),
            pltpu.VMEM((groups, local, width), LOW),
            pltpu.VMEM((groups, local + 8, 2 * size), WIDE),
            pltpu.VMEM((8, width), WIDE),
            pltpu.VMEM((groups, shards, 8, rows), WIDE),
            pltpu.VMEM((groups, shards, 8, rows), WIDE),
            pltpu.VMEM((shards, 8, rows), WIDE),
            pltpu.VMEM((2, groups) + glu_shape[1:], LOW),
            pltpu.VMEM(glu_shape, LOW),
            pltpu.VMEM(in_shape, LOW),
            pltpu.VMEM(in_shape[1:], LOW),
        ]
        + LineScatter.scratch(line, block, width, halves) * 2
        + [
            dma(22), dma(shards, pieces, 3), dma(shards, pieces), dma(2, groups), dma(2, groups), dma(2),
            dma(2, groups), dma(2, groups), dma(2, groups), dma(2, groups),
            dma(4, shards), dma(2, shards), dma(2, shards),
        ],
        compiler_params=pltpu.CompilerParams(
            collective_id=3, has_side_effects=True, vmem_limit_bytes=VMEM_BYTES
        ),
        name="back",
    )(
        mixed, hidden, down_whole, middle, middle_grad, tokens, gains, par, wr, wi, *far,
        glu_grad, glu_first, down_grad, mlp_sums,
    )


def settle_kernel(
    glu_far, ins_far, outs_far, down_heard, down_grad, result_far, tokens_far,
    result_out, tokens_out, gate_far, up_far, lru_far, gelu_far, out_far, down_far,
    result, tokens, glu, ins, outs, parts, gate_sum, up_sum, lru_sum, gelu_sum, out_sum, down_sum, sems, leave_sems,
):
    shards, rows, both = glu.shape
    groups = outs.shape[0]
    units, channels = both // 2, ins.shape[2] // 2
    f = lax.axis_index("fsdp")
    keep = [
        (glu_far, glu), (ins_far, ins), (outs_far, outs), (result_far, result), (tokens_far, tokens),
        (down_grad.at[f], parts.at[f]),
    ]
    for hop in range(1, groups):
        origin = lax.rem(f + hop, groups)
        keep.append((down_heard.at[origin], parts.at[origin]))
    keep = [pltpu.make_async_copy(a, b, sems.at[n]) for n, (a, b) in enumerate(keep)]
    for copy in keep:
        copy.start()
    leaving = [
        (gate_sum, gate_far), (up_sum, up_far), (lru_sum, lru_far), (gelu_sum, gelu_far),
        (out_sum, out_far), (down_sum, down_far), (result, result_out), (tokens, tokens_out),
    ]
    leaving = [pltpu.make_async_copy(a, b, leave_sems.at[n]) for n, (a, b) in enumerate(leaving)]
    keep[0].wait()
    for half, whole in enumerate((gate_sum, up_sum)):
        for shard in range(shards):
            part = slice(half * units, (half + 1) * units)
            whole[:, shard * units : (shard + 1) * units] = glu[shard, :, part].astype(WIDE)
        leaving[half].start()
    keep[1].wait()
    for half, whole in enumerate((lru_sum, gelu_sum)):
        for shard in range(shards):
            part = slice(half * channels, (half + 1) * channels)
            whole[:, shard * channels : (shard + 1) * channels] = ins[shard, :, part].astype(WIDE)
        leaving[2 + half].start()

    def add(terms, total):
        @pl.loop(0, total.shape[0] // 16)
        def _(n):
            here = pl.ds(pl.multiple_of(n * 16, 16), 16)
            value = terms[0, here, :].astype(WIDE)
            for origin in range(1, groups):
                value = value + terms[origin, here, :].astype(WIDE)
            total[here, :] = value

    for n in (3, 4):
        keep[n].wait()
        leaving[n + 3].start()
    keep[2].wait()
    add(outs, out_sum)
    leaving[4].start()
    for copy in keep[5:]:
        copy.wait()
    add(parts, down_sum)
    leaving[5].start()
    for copy in leaving:
        copy.wait()


def settle(glu, ins, outs, down_heard, down_grad, result, tokens):
    shards, rows, both = glu.shape
    groups, local, width = outs.shape
    units, channels = both // 2, ins.shape[2] // 2
    shapes = [(rows, shards * units)] * 2 + [(rows, shards * channels)] * 2
    shapes += [(local, width), down_grad.shape[1:]]
    return pl.pallas_call(
        settle_kernel,
        out_shape=[jax.ShapeDtypeStruct(result.shape, LOW)] * 2
        + [jax.ShapeDtypeStruct(shape, WIDE) for shape in shapes],
        in_specs=[ANY] * 7,
        out_specs=[ANY] * 8,
        scratch_shapes=[pltpu.VMEM(member.shape, LOW) for member in (result, tokens, glu, ins, outs, down_grad)]
        + [pltpu.VMEM(shape, WIDE) for shape in shapes]
        + [dma(groups + 5), dma(8)],
        compiler_params=pltpu.CompilerParams(vmem_limit_bytes=VMEM_BYTES),
        name="settle",
    )(glu, ins, outs, down_heard, down_grad, result, tokens)


def mixer_forward_kernel(
    x_ref, wr_ref, wi_ref, par_ref,
    conv_ref, r_ref, i_ref, f_ref, m_ref, st_ref,
    ext, factors, drive, prod,
):
    positions, channels = x_ref.shape
    segment = positions // 8
    chunks = positions // CHUNK
    ext[0:8, :] = jnp.zeros((8, channels), WIDE)
    st_ref[0:8, :] = jnp.zeros((8, channels), WIDE)

    @pl.loop(0, chunks)
    def _(c):
        base = pl.multiple_of(c * CHUNK, CHUNK)
        ext[pl.ds(base + 8, CHUNK), :] = x_ref[pl.ds(base, CHUNK), :].astype(WIDE)

    @pl.loop(0, chunks)
    def _(c):
        base = pl.multiple_of(c * CHUNK, CHUNK)
        rows = pl.ds(base, CHUNK)
        block = ext[pl.ds(base, CHUNK + 8), :]
        conv = jnp.broadcast_to(par_ref[4:5, :], (CHUNK, channels))
        for k in range(4):
            conv = conv + par_ref[k : k + 1, :] * block[8 - k : 8 - k + CHUNK]
        conv_low = conv.astype(LOW)
        conv_ref[rows, :] = conv_low
        r = jax.nn.sigmoid(dot(conv_low, wr_ref[...]) + par_ref[5:6, :])
        gate = jax.nn.sigmoid(dot(conv_low, wi_ref[...]) + par_ref[6:7, :])
        log_decay = r * par_ref[7:8, :]
        m = jnp.sqrt(one_minus_exp(-2.0 * log_decay))
        r_ref[rows, :] = r
        i_ref[rows, :] = gate
        factor = jnp.exp(log_decay)
        f_ref[rows, :] = factor
        m_ref[rows, :] = m
        put(factors, rows, factor)
        put(drive, rows, m * gate * conv_low.astype(WIDE))

    def step(i, n, state, product):
        rows = pl.ds(i, 8, stride=segment)
        factor = factors[n, rows, :]
        state = factor * state + drive[n, rows, :]
        product = factor * product
        drive[n, rows, :] = state
        prod[n, rows, :] = product
        return state, product

    state, product = scan_segments(step, segment, lane_tiles(channels))
    state, product = state[:, :channels], product[:, :channels]
    carry = jnp.zeros((1, channels), WIDE)
    for k in range(8):
        for part in range(segment // CHUNK):
            base = k * segment + part * CHUNK
            rows = slice(base, base + CHUNK)
            st_ref[base + 8 : base + 8 + CHUNK, :] = (
                get(drive, rows, channels) + get(prod, rows, channels) * carry
            )
        carry = state[k : k + 1] + product[k : k + 1] * carry


def mixer_backward_kernel(
    ds_ref, x_ref, conv_ref, r_ref, i_ref, f_ref, m_ref, st_ref, wr_ref, wi_ref, par_ref,
    xg_ref, wrg_ref, wig_ref, sums_ref,
    ext, factors, adj, prod, cg, carries, wr_sum, wi_sum,
):
    positions, channels = x_ref.shape
    segment = positions // 8
    chunks = positions // CHUNK
    ext[0:8, :] = jnp.zeros((8, channels), WIDE)
    cg[pl.ds(positions, 8), :] = jnp.zeros((8, channels), WIDE)
    wr_sum[...] = jnp.zeros_like(wr_sum)
    wi_sum[...] = jnp.zeros_like(wi_sum)

    @pl.loop(0, chunks)
    def _(c):
        base = pl.multiple_of(c * CHUNK, CHUNK)
        ext[pl.ds(base + 8, CHUNK), :] = x_ref[pl.ds(base, CHUNK), :].astype(WIDE)
        put(adj, pl.ds(base, CHUNK), ds_ref[pl.ds(base, CHUNK), :].astype(WIDE))
        put(factors, pl.ds(base, CHUNK), f_ref[pl.ds(base, CHUNK), :])

    def step(j, n, flow, product):
        rows = pl.ds(segment - 1 - j, 8, stride=segment)
        factor = factors[n, rows, :]
        adjoint = adj[n, rows, :] + flow
        adj[n, rows, :] = adjoint
        prod[n, rows, :] = product
        return factor * adjoint, factor * product

    flow, product = scan_segments(step, segment, lane_tiles(channels))
    flow, product = flow[:, :channels], product[:, :channels]
    carry = jnp.zeros((1, channels), WIDE)
    for k in range(7, -1, -1):
        carries[k : k + 1, :] = carry
        carry = flow[k : k + 1] + product[k : k + 1] * carry

    def grads(c, sums):
        base = pl.multiple_of(c * CHUNK, CHUNK)
        rows = pl.ds(base, CHUNK)
        adjoint = get(adj, rows, channels) + get(prod, rows, channels) * carries[pl.ds(base // segment, 1), :]
        before = st_ref[pl.ds(base, CHUNK + 8), :][7 : 7 + CHUNK]
        conv_low = conv_ref[rows, :]
        conv = conv_low.astype(WIDE)
        r = r_ref[rows, :]
        gate = i_ref[rows, :]
        factor = f_ref[rows, :]
        m = m_ref[rows, :]
        driven = adjoint * gate
        by_log = adjoint * before * factor - driven * conv * factor * factor / m
        by_r = by_log * par_ref[7:8, :] * r * (1.0 - r)
        by_i = adjoint * m * conv * gate * (1.0 - gate)
        by_r_low = by_r.astype(LOW)
        by_i_low = by_i.astype(LOW)
        conv_grad = (
            driven * m
            + times_transpose(by_r_low, wr_ref[...])
            + times_transpose(by_i_low, wi_ref[...])
        )
        cg[rows, :] = conv_grad
        wr_sum[...] += outer_sum(conv_low, by_r_low)
        wi_sum[...] += outer_sum(conv_low, by_i_low)
        block = ext[pl.ds(base, CHUNK + 8), :]
        rows_of = [conv_grad * block[8 - k : 8 - k + CHUNK] for k in range(4)]
        rows_of += [conv_grad, by_r, by_i, by_log * r]
        return tuple(
            total + jnp.sum(member, axis=0, keepdims=True) for total, member in zip(sums, rows_of)
        )

    zero = jnp.zeros((1, channels), WIDE)
    sums = lax.fori_loop(0, chunks, grads, (zero,) * 8)
    for k in range(8):
        sums_ref[k : k + 1, :] = sums[k]
    size = wrg_ref.shape[1]
    for n in range(channels // size):
        block = slice(n * size, (n + 1) * size)
        wrg_ref[block, :] = wr_sum[block, block]
        wig_ref[block, :] = wi_sum[block, block]

    @pl.loop(0, chunks)
    def _(c):
        base = pl.multiple_of(c * CHUNK, CHUNK)
        block = cg[pl.ds(base, CHUNK + 8), :]
        total = jnp.zeros((CHUNK, channels), WIDE)
        for k in range(4):
            total = total + par_ref[k : k + 1, :] * block[k : k + CHUNK]
        xg_ref[pl.ds(base, CHUNK), :] = total.astype(LOW)


def mixer_forward(x, wr, wi, par):
    positions, channels = x.shape
    wide = jax.ShapeDtypeStruct((positions, channels), WIDE)
    return pl.pallas_call(
        mixer_forward_kernel,
        out_shape=(
            jax.ShapeDtypeStruct((positions, channels), LOW), wide, wide, wide, wide,
            jax.ShapeDtypeStruct((positions + 8, channels), WIDE),
        ),
        scratch_shapes=[pltpu.VMEM((positions + 8, channels), WIDE)]
        + [pltpu.VMEM((lane_tiles(channels), positions, 128), WIDE)] * 3,
        compiler_params=pltpu.CompilerParams(vmem_limit_bytes=48 * 2**20),
        name="mixer_forward",
    )(x, wr, wi, par)


def mixer_backward(ds, x, saved, wr, wi, par, size):
    positions, channels = x.shape
    square = jax.ShapeDtypeStruct((channels, size), WIDE)
    return pl.pallas_call(
        mixer_backward_kernel,
        out_shape=(
            jax.ShapeDtypeStruct((positions, channels), LOW), square, square,
            jax.ShapeDtypeStruct((8, channels), WIDE),
        ),
        scratch_shapes=[pltpu.VMEM((positions + 8, channels), WIDE)]
        + [pltpu.VMEM((lane_tiles(channels), positions, 128), WIDE)] * 3
        + [pltpu.VMEM((positions + 8, channels), WIDE), pltpu.VMEM((8, channels), WIDE)]
        + [pltpu.VMEM((channels, channels), WIDE)] * 2,
        compiler_params=pltpu.CompilerParams(vmem_limit_bytes=48 * 2**20),
        name="mixer_backward",
    )(ds, x, *saved, wr, wi, par)


def gather_columns(weights):
    shards = lax.axis_size("seq")
    rows = weights[0].shape[0]
    widths = [member.shape[1] // shards for member in weights]
    stacked = jnp.concatenate(
        [member.reshape(rows, shards, width) for member, width in zip(weights, widths)], axis=2
    )
    mine = lax.all_to_all(stacked.transpose(1, 0, 2), "seq", split_axis=0, concat_axis=0)
    whole = lax.all_gather(mine, "fsdp", axis=1)
    return whole.reshape(-1, sum(widths))


def scatter_columns(grad, widths, rows):
    shards, groups = lax.axis_size("seq"), lax.axis_size("fsdp")
    parts = grad.astype(LOW).reshape(shards, groups, rows, sum(widths)).transpose(1, 0, 2, 3)
    mine = lax.psum_scatter(parts, "fsdp", scatter_dimension=0, tiled=False)
    swapped = lax.all_to_all(mine, "seq", split_axis=0, concat_axis=0).astype(WIDE)
    outs, first = [], 0
    for width in widths:
        outs.append(swapped[:, :, first : first + width].transpose(1, 0, 2).reshape(rows, -1))
        first += width
    return outs


def block_diagonal(weight, blocks):
    size = weight.shape[1]
    shaped = weight.reshape(blocks, size, size)
    full = jnp.zeros((blocks, size, blocks, size), weight.dtype)
    for n in range(blocks):
        full = full.at[n, :, n, :].set(shaped[n])
    return full.reshape(blocks * size, blocks * size)


def general(
    tokens, cotangent, mix_gain, lru_in_weight, gelu_in_weight, out_weight, conv_weight, conv_bias,
    recurrence_weight, recurrence_bias, input_gate_weight, input_gate_bias, decay_param, mlp_gain,
    gate_weight, up_weight, down_weight,
):
    positions, width = tokens.shape[1:]
    rows = lru_in_weight.shape[0]
    shards = lax.axis_size("seq")
    channels = lru_in_weight.shape[1] // shards
    hidden_width = gate_weight.shape[1] // shards
    size = recurrence_weight.shape[1]

    gains = lax.all_gather(
        jnp.stack([mix_gain, mlp_gain], axis=1), ("seq", "fsdp"), axis=0, tiled=True
    ).astype(WIDE)
    mix_scale, mlp_scale = gains[:, 0], gains[:, 1]
    in_whole = gather_columns([lru_in_weight, gelu_in_weight])
    lru_params = lax.all_gather(
        jnp.concatenate(
            [
                recurrence_weight, input_gate_weight, conv_weight, conv_bias[:, None],
                recurrence_bias[:, None], input_gate_bias[:, None], decay_param[:, None],
            ],
            axis=1,
        ),
        "fsdp", axis=0, tiled=True,
    )
    out_whole = lax.all_gather(out_weight, "fsdp", axis=0, tiled=True)
    glu_whole = gather_columns([gate_weight, up_weight])
    down_whole = lax.all_gather(down_weight, "fsdp", axis=0, tiled=True)

    wr = block_diagonal(lru_params[:, :size], channels // size)
    wi = block_diagonal(lru_params[:, size : 2 * size], channels // size)
    vectors = lru_params[:, 2 * size :].astype(WIDE).T
    decay = vectors[7]
    par = jnp.concatenate([vectors[:7], -RATE_SCALE * jax.nn.softplus(-decay)[None]], axis=0)

    resid_in = tokens.reshape(positions, width).astype(WIDE)
    grad_low = cotangent.reshape(positions, width)
    normed_low = rms_scale(resid_in, mix_scale).astype(LOW)
    normed_all = lax.all_gather(normed_low, "seq", axis=0, tiled=True)
    grad_all = lax.all_gather(grad_low, "seq", axis=0, tiled=True)
    branch_x = dot(normed_all, in_whole[:, :channels]).astype(LOW)
    branch_pre = dot(normed_all, in_whole[:, channels:])
    branch_y = jax.nn.gelu(branch_pre)

    saved = mixer_forward(branch_x, wr, wi, par)
    states_f = saved[5][8:].astype(LOW).astype(WIDE)
    product = (states_f * branch_y).astype(LOW)
    mixed = lax.psum_scatter(
        dot(product, out_whole).astype(LOW), "seq", scatter_dimension=0, tiled=True
    )
    middle = resid_in + mixed.astype(WIDE)
    normed2_low = rms_scale(middle, mlp_scale).astype(LOW)
    normed2_all = lax.all_gather(normed2_low, "seq", axis=0, tiled=True)
    gate_whole, up_whole = glu_whole[:, :hidden_width], glu_whole[:, hidden_width:]
    gate_val = dot(normed2_all, gate_whole)
    up_val = dot(normed2_all, up_whole)
    hidden = (jax.nn.gelu(gate_val) * up_val).astype(LOW)
    fed = lax.psum_scatter(
        dot(hidden, down_whole).astype(LOW), "seq", scatter_dimension=0, tiled=True
    )
    result = middle + fed.astype(WIDE)

    hidden_grad = times_transpose(grad_all, down_whole)
    unused, pull_glu = jax.vjp(lambda first, second: jax.nn.gelu(first) * second, gate_val, up_val)
    gate_grad, up_grad = pull_glu(hidden_grad)
    gate_low, up_low = gate_grad.astype(LOW), up_grad.astype(LOW)
    normed2_grad = lax.psum_scatter(
        (times_transpose(gate_low, gate_whole) + times_transpose(up_low, up_whole)).astype(LOW),
        "seq", scatter_dimension=0, tiled=True,
    ).astype(WIDE)
    unused, pull_norm2 = jax.vjp(rms_scale, middle, mlp_scale)
    middle_part, mlp_gain_grad = pull_norm2(normed2_grad)
    middle_grad = grad_low.astype(WIDE) + middle_part
    mixed_all = lax.all_gather(middle_grad.astype(LOW), "seq", axis=0, tiled=True)

    product_grad = times_transpose(mixed_all, out_whole)
    states_grad = (product_grad * branch_y).astype(LOW)
    unused, pull_gelu = jax.vjp(jax.nn.gelu, branch_pre)
    (pre_grad,) = pull_gelu(product_grad * states_f)
    pre_low = pre_grad.astype(LOW)
    x_low, wr_grad, wi_grad, sums = mixer_backward(states_grad, branch_x, saved, wr, wi, par, size)

    normed_grad = lax.psum_scatter(
        (
            times_transpose(x_low, in_whole[:, :channels])
            + times_transpose(pre_low, in_whole[:, channels:])
        ).astype(LOW),
        "seq", scatter_dimension=0, tiled=True,
    ).astype(WIDE)
    unused, pull_norm = jax.vjp(rms_scale, resid_in, mix_scale)
    input_part, mix_gain_grad = pull_norm(normed_grad)
    input_grad = middle_grad + input_part

    down_grad = lax.psum_scatter(
        outer_sum(hidden, grad_all).astype(LOW), "fsdp", scatter_dimension=0, tiled=True
    ).astype(WIDE)
    glu_grad = jnp.concatenate(
        [outer_sum(normed2_all, gate_low), outer_sum(normed2_all, up_low)], axis=1
    )
    gate_w_grad, up_w_grad = scatter_columns(glu_grad, [hidden_width] * 2, rows)
    out_grad = lax.psum_scatter(
        outer_sum(product, mixed_all).astype(LOW), "fsdp", scatter_dimension=0, tiled=True
    ).astype(WIDE)
    in_grad = jnp.concatenate(
        [outer_sum(normed_all, x_low), outer_sum(normed_all, pre_low)], axis=1
    )
    lru_in_grad, gelu_in_grad = scatter_columns(in_grad, [channels] * 2, rows)
    small = jnp.concatenate(
        [
            wr_grad, wi_grad, sums[:7].T,
            (sums[7] * RATE_SCALE * jax.nn.sigmoid(-decay))[:, None],
        ],
        axis=1,
    )
    small = lax.psum_scatter(
        small.reshape(lax.axis_size("fsdp"), -1, small.shape[1]),
        "fsdp", scatter_dimension=0, tiled=False,
    )
    gain_parts = jnp.stack([mix_gain_grad, mlp_gain_grad]).reshape(2, -1, rows).transpose(1, 0, 2)
    gain_grads = lax.psum_scatter(
        gain_parts, ("seq", "fsdp"), scatter_dimension=0, tiled=False
    )
    first = 2 * size
    return (
        result.astype(LOW).reshape(tokens.shape),
        input_grad.astype(LOW).reshape(tokens.shape),
        gain_grads[0],
        lru_in_grad,
        gelu_in_grad,
        out_grad,
        small[:, first : first + 4],
        small[:, first + 4],
        small[:, :size],
        small[:, first + 5],
        small[:, size : 2 * size],
        small[:, first + 6],
        small[:, first + 7],
        gain_grads[1],
        gate_w_grad,
        up_w_grad,
        down_grad,
    )


def aligned(
    tokens, cotangent, mix_gain, lru_in_weight, gelu_in_weight, out_weight, conv_weight, conv_bias,
    recurrence_weight, recurrence_bias, input_gate_weight, input_gate_bias, decay_param, mlp_gain,
    gate_weight, up_weight, down_weight,
):
    positions, width = tokens.shape[1:]
    rows = lru_in_weight.shape[0]
    shards = lax.axis_size("seq")
    channels = lru_in_weight.shape[1] // shards
    hidden_width = gate_weight.shape[1] // shards
    size = recurrence_weight.shape[1]

    groups = lax.axis_size("fsdp")
    resid_in = tokens.reshape(positions, width).astype(WIDE)
    grad_low = cotangent.reshape(positions, width)

    own_decay = decay_param.astype(WIDE)
    rates = -RATE_SCALE * jax.nn.softplus(-own_decay)[None]
    tokens_low = tokens.reshape(positions, width)
    (
        normed, in_whole, ext, branch_pre, conv_low, recur_gate, input_gate, states, product, par, wr, wi,
        gains, glu_mine, out_whole, down_whole,
    ) = mix_in(
        tokens_low, lru_in_weight, gelu_in_weight, gate_weight, up_weight, out_weight, down_weight,
        recurrence_weight, input_gate_weight, conv_weight.T,
        jnp.stack([conv_bias, recurrence_bias, input_gate_bias]), rates, jnp.stack([mix_gain, mlp_gain]),
        shards, groups,
    )
    out_whole, down_whole = out_whole.reshape(-1, width), down_whole.reshape(-1, width)
    middle, middle_grad, mixed_low, mlp_sums, hidden, glu_grad, down_grad, glu_first = feed(
        product, out_whole, glu_mine, down_whole, grad_low, tokens_low, gains, groups
    )
    down_grad = down_grad.reshape(groups, -1, width)
    (
        result, tokens_grad, glu_out, in_out, out_heard, small_heard, gain_out, unused, unused, down_heard,
    ) = back(
        mixed_low, hidden, down_whole, middle, middle_grad, tokens_low, gains, par, wr, wi,
        out_whole, in_whole, normed, product, ext, branch_pre, conv_low, recur_gate, input_gate, states,
        glu_grad, glu_first, down_grad, mlp_sums, size,
    )
    small_rows = recurrence_weight.shape[0]
    result, tokens_grad, gate_sum, up_sum, lru_sum, gelu_sum, out_sum, down_sum = settle(
        glu_out, in_out, out_heard, down_heard, down_grad, result, tokens_grad
    )
    small = jnp.sum(small_heard, axis=0)
    gain_grads = jnp.sum(gain_out, axis=0)
    vector_sums = small[small_rows:, :small_rows]
    return (
        result.reshape(tokens.shape),
        tokens_grad.reshape(tokens.shape),
        gain_grads[0],
        lru_sum,
        gelu_sum,
        out_sum,
        vector_sums[:4].T,
        vector_sums[4],
        small[:small_rows, :size],
        vector_sums[5],
        small[:small_rows, size : 2 * size],
        vector_sums[6],
        vector_sums[7] * RATE_SCALE * jax.nn.sigmoid(-own_decay),
        gain_grads[1],
        gate_sum,
        up_sum,
        down_sum,
    )


def solution(mesh):
    shards, groups = mesh.shape["seq"], mesh.shape["fsdp"]

    def local(*arrays):
        rows, small_rows = arrays[3].shape[0], arrays[5].shape[0]
        simple = shards % 2 == 0 and rows % 16 == 0 and small_rows % 16 == 0
        simple = simple and arrays[0].shape[1] * shards % (8 * CHUNK) == 0
        return (aligned if simple else general)(*arrays)

    tokens = P("fsdp", "seq", None)
    vector = P(("seq", "fsdp"))
    matrix = P(("seq", "fsdp"), None)
    ranks = (1, 2, 2, 2, 2, 1, 2, 1, 2, 1, 1, 1, 2, 2, 2)
    specs = (tokens, tokens) + tuple(vector if rank == 1 else matrix for rank in ranks)
    return jax.shard_map(local, mesh=mesh, in_specs=specs, out_specs=specs, check_vma=False)
```

```python
import functools

import jax
import jax.numpy as jnp
from jax import lax
from jax.experimental import pallas as pl
from jax.experimental.pallas import tpu as pltpu
from jax.sharding import PartitionSpec as P

EPSILON = 1e-06
RATE_SCALE = 8.0
CHUNK = 128
EARLY = 2
LOW = jnp.bfloat16
WIDE = jnp.float32


def rms_scale(values, gain):
    scale = lax.rsqrt(jnp.mean(values * values, axis=-1, keepdims=True) + EPSILON)
    return values * scale * gain


def dot(left, right):
    return jnp.dot(left, right, preferred_element_type=WIDE)


def outer_sum(left, right):
    return lax.dot_general(left, right, (((0,), (0,)), ((), ())), preferred_element_type=WIDE)


def times_transpose(left, right):
    return lax.dot_general(left, right, (((1,), (1,)), ((), ())), preferred_element_type=WIDE)


def one_minus_exp(value):
    series = jnp.full_like(value, 1.0 / 40320.0)
    for bottom in (5040.0, 720.0, 120.0, 24.0, 6.0, 2.0, 1.0):
        series = 1.0 / bottom - value * series
    return jnp.where(value < 0.4, value * series, 1.0 - jnp.exp(-value))


def sigmoid(value):
    return 0.5 * jnp.tanh(0.5 * value) + 0.5


def lane_tiles(channels):
    return -(-channels // 128)


def put(tiles, rows, value):
    channels = value.shape[1]
    for n in range(lane_tiles(channels)):
        size = min(128, channels - n * 128)
        tiles[n, rows, 0:size] = value[:, n * 128 : n * 128 + size]


def get(tiles, rows, channels):
    return jnp.concatenate(
        [
            tiles[n, rows, 0 : min(128, channels - n * 128)]
            for n in range(lane_tiles(channels))
        ],
        axis=1,
    )


def scan_segments(step, count, tiles):
    def body(i, carried):
        return tuple(step(i, n, *carried[n]) for n in range(tiles))

    start = (jnp.zeros((8, 128), WIDE), jnp.ones((8, 128), WIDE))
    ends = lax.fori_loop(0, count, body, (start,) * tiles, unroll=4)
    return [jnp.concatenate([end[which] for end in ends], axis=1) for which in (0, 1)]


MESH = pl.DeviceIdType.MESH
VMEM_BYTES = 61 * 2**20
ANY = pl.BlockSpec(memory_space=pl.ANY)
HELD = pl.BlockSpec(memory_space=pltpu.VMEM)
ROOT = 0.7978845608028654
CUBE = 0.044715


def dma(*shape):
    return pltpu.SemaphoreType.DMA(shape)


def remote(src, dst, send, recv, axis, index):
    return pltpu.make_async_remote_copy(
        src_ref=src, dst_ref=dst, send_sem=send, recv_sem=recv,
        device_id={axis: index}, device_id_type=MESH,
    )


def gelu(value):
    return 0.5 * value * (1.0 + jnp.tanh(ROOT * (value + CUBE * value * value * value)))


def gelu_and_slope(value):
    square = value * value
    bent = jnp.tanh(ROOT * (value + CUBE * square * value))
    half = 0.5 * (1.0 + bent)
    slope = half + 0.5 * value * (1.0 - bent * bent) * (ROOT * (1.0 + 3.0 * CUBE * square))
    return value * half, slope


class Place:
    def __init__(self, shards, groups):
        self.shards, self.groups, self.line = shards, groups, shards // 2
        self.s, self.f = lax.axis_index("seq"), lax.axis_index("fsdp")
        self.z, self.c = self.s // 2, lax.rem(self.s, 2)
        self.sibling = 2 * self.z + 1 - self.c

    def nearest(self, n):
        chip = 0
        for z in range(self.line):
            for place, other in enumerate(sorted(range(self.line), key=lambda y: abs(y - z))):
                chip = jnp.where((self.z == z) & (n == place), other, chip)
        return chip

    def enter(self, seq=True, fsdp=True):
        barrier = pltpu.get_barrier_semaphore()
        met = 0
        for axis, mine, count, wanted in (
            ("seq", self.s, self.shards, seq), ("fsdp", self.f, self.groups, fsdp),
        ):
            for d in range(1, count if wanted else 1):
                pl.semaphore_signal(
                    barrier, inc=1, device_id={axis: lax.rem(mine + d, count)}, device_id_type=MESH
                )
                met += 1
        pl.semaphore_wait(barrier, met)


class Spread:
    def __init__(self, at, src, dst, send, recv, axis="fsdp"):
        self.at, self.src, self.dst, self.send, self.recv, self.axis = at, src, dst, send, recv, axis
        self.mine, self.count = (at.f, at.groups) if axis == "fsdp" else (at.s, at.shards)

    def copy(self, d):
        peer = lax.rem(self.mine + d, self.count)
        return remote(
            self.src(peer), self.dst(self.mine), self.send.at[d], self.recv.at[d], self.axis, peer
        )

    def start(self):
        for d in range(1, self.count):
            self.copy(d).start()

    def source(self, d):
        return lax.rem(self.mine + self.count - d, self.count)

    def arrive(self, d):
        origin = self.source(d)
        remote(
            self.src(origin), self.dst(origin), self.send.at[d], self.recv.at[d], self.axis, origin
        ).wait_recv()

    def sent(self):
        for d in range(1, self.count):
            self.copy(d).wait_send()

    def finish(self):
        for d in range(1, self.count):
            self.arrive(d)
        self.sent()


class LineGather:
    def __init__(self, at, src, buf, send, recv, pieces):
        self.at, self.src, self.buf, self.send, self.recv, self.pieces = at, src, buf, send, recv, pieces
        self.rows = buf.shape[1] // pieces

    def copy(self, slot, piece, kind, first=False):
        at = self.at
        rows = pl.ds(piece * self.rows, self.rows)
        there = self.buf.at[slot, rows]
        peer = (at.sibling, at.s + 2, at.s - 2)[kind]
        return remote(
            self.src.at[rows] if first else there, there,
            self.send.at[slot, piece, kind], self.recv.at[slot, piece], "seq", peer,
        )

    def start(self, first=0, last=None):
        at = self.at
        for piece in range(first, self.pieces if last is None else last):
            @pl.when(at.z + 1 < at.line)
            def _():
                self.copy(at.s, piece, 1, True).start()

            @pl.when(at.z > 0)
            def _():
                self.copy(at.s, piece, 2, True).start()

            self.copy(at.s, piece, 0, True).start()

    def arrive(self, chip, piece):
        at = self.at
        slot = 2 * chip + at.c
        self.copy(slot, piece, 0).wait_recv()

        @pl.when((chip < at.z) & (at.z + 1 < at.line))
        def _():
            self.copy(slot, piece, 1).start()

        @pl.when((chip > at.z) & (at.z > 0))
        def _():
            self.copy(slot, piece, 2).start()

        self.copy(slot, piece, 0).start()

    def settle(self, chip):
        for piece in range(self.pieces):
            self.copy(2 * chip + 1 - self.at.c, piece, 0).wait_recv()

    def pass_on(self, d):
        at = self.at
        for piece in range(self.pieces):
            for chip, known in ((at.z - d, at.z - d >= 0), (at.z + d, at.z + d < at.line)):
                @pl.when(known)
                def _():
                    self.arrive(chip, piece)

    def distances(self, body, beside=None):
        at = self.at

        @pl.loop(0, at.line)
        def _(n):
            @pl.when(n > 0)
            def _():
                self.pass_on(n)
                if beside is not None:
                    beside(n)

            chip = at.nearest(n)
            self.settle(chip)
            body(chip)

    def sent(self):
        at = self.at
        for chip in range(at.line):
            slot = 2 * chip + at.c
            for piece in range(self.pieces):
                self.copy(slot, piece, 0).wait_send()

                @pl.when((chip <= at.z) & (at.z + 1 < at.line))
                def _():
                    self.copy(slot, piece, 1).wait_send()

                @pl.when((chip >= at.z) & (at.z > 0))
                def _():
                    self.copy(slot, piece, 2).wait_send()


class LineScatter:
    def __init__(self, at, parts, heard, into, sems, pieces):
        self.at, self.parts, self.heard, self.into = at, parts, heard, into
        self.sib_send, self.sib_recv, self.send, self.recv = sems
        self.pieces = pieces
        self.rows = parts.shape[2] // pieces

    @staticmethod
    def scratch(line, rows, width, pieces):
        low = pltpu.VMEM((line, rows, width), LOW)
        return [
            pltpu.VMEM((line, 2, rows, width), LOW), low, low,
            dma(line), dma(line), dma(line, pieces), dma(line, pieces),
        ]

    def across(self, chip):
        return remote(
            self.parts.at[chip, 1 - self.at.c], self.heard.at[chip], self.sib_send.at[chip],
            self.sib_recv.at[chip], "seq", self.at.sibling,
        )

    def whole_way(self, chip, start):
        if self.at.line < 4:
            return False
        return jnp.abs(chip - start) == self.at.line - 1

    def joined(self, chip):
        at = self.at
        if at.line < 4:
            return False
        return ((at.z == 1) & (chip == at.line - 1)) | ((at.z == at.line - 2) & (chip == 0))

    def along(self, chip, piece):
        at = self.at
        rows = pl.ds(pl.multiple_of(piece * self.rows, self.rows), self.rows)
        target, slot = chip, at.z
        if at.line >= 4:
            stop = jnp.where(chip > at.z, at.z + 1, at.z - 1)
            target = jnp.where(self.whole_way(chip, at.z), stop, chip)
            slot = jnp.where(self.whole_way(chip, at.z), stop, at.z)
        return remote(
            self.parts.at[chip, 1 - at.c, rows], self.into.at[slot, rows], self.send.at[chip, piece],
            self.recv.at[slot, piece], "seq", 2 * target + at.c,
        )

    def landed(self, slot, piece):
        rows = pl.ds(pl.multiple_of(piece * self.rows, self.rows), self.rows)
        there = self.into.at[slot, rows]
        remote(
            there, there, self.recv.at[slot, piece], self.recv.at[slot, piece], "seq", self.at.sibling
        ).wait_recv()

    def add(self, chip, piece, extras, store):
        @pl.loop(0, self.rows // 16)
        def _(block):
            rows = pl.ds(pl.multiple_of(piece * self.rows + block * 16, 16), 16)
            total = self.parts[chip, self.at.c, rows, :].astype(WIDE) + self.heard[chip, rows, :].astype(WIDE)
            for known, slot in extras:
                here = self.into[slot, rows, :].astype(WIDE)
                total = total + (here if known is True else jnp.where(known, here, 0.0))
            store(rows, total)

    def store_out(self, chip):
        def store(rows, total):
            self.parts[chip, 1 - self.at.c, rows, :] = total.astype(LOW)

        return store

    def goes(self, chip):
        goes = chip != self.at.z
        return goes & jnp.logical_not(self.joined(chip)) if self.at.line >= 4 else goes

    def push(self, chip, first=0, last=None):
        @pl.when(self.goes(chip))
        def _():
            if first == 0:
                self.across(chip).wait()

            @pl.loop(first, self.pieces if last is None else last)
            def _(piece):
                self.add(chip, piece, [], self.store_out(chip))
                self.along(chip, piece).start()

    def join(self, first=0, last=None):
        at = self.at
        if at.line < 4:
            return

        @pl.when((at.z == 1) | (at.z == at.line - 2))
        def _():
            chip = jnp.where(at.z == 1, at.line - 1, 0)
            if first == 0:
                self.across(chip).wait()

            @pl.loop(first, self.pieces if last is None else last)
            def _(piece):
                self.landed(at.z, piece)
                self.add(chip, piece, [(True, at.z)], self.store_out(chip))
                self.along(chip, piece).start()

    def finish(self, store, first=0, last=None):
        at = self.at
        if first == 0:
            self.across(at.z).wait_recv()

        def known(chip):
            heard = chip != at.z
            return heard & jnp.logical_not(self.whole_way(chip, at.z)) if at.line >= 4 else heard

        @pl.loop(first, self.pieces if last is None else last)
        def _(piece):
            for chip in range(at.line):
                @pl.when(known(chip))
                def _():
                    self.landed(chip, piece)

            self.add(at.z, piece, [(known(chip), chip) for chip in range(at.line)], store)

    def sent(self):
        at = self.at
        self.across(at.z).wait_send()
        for chip in range(at.line):
            @pl.when(chip != at.z)
            def _():
                @pl.loop(0, self.pieces)
                def _(piece):
                    self.along(chip, piece).wait_send()


def normalise(source, gain, store, rows):
    @pl.loop(0, rows // 16)
    def _(block):
        here = pl.ds(pl.multiple_of(block * 16, 16), 16)
        values = source(here)
        scale = lax.rsqrt(jnp.mean(values * values, axis=-1, keepdims=True) + EPSILON)
        store(here, (values * scale * gain).astype(LOW))


def mixer_rows(positions):
    return [pl.ds(pl.multiple_of(n, CHUNK), CHUNK) for n in range(0, positions, CHUNK)]


def mix_in_kernel(
    tokens, lru_rows, gelu_rows, gate_rows, up_rows, out_shard, down_shard, gate_block, input_block,
    taps, biases, rates, both_gains,
    normed_far, in_far, ext_far, pre_far, conv_far, r_far, i_far, st_far,
    product_far, par_ref, wr_ref, wi_ref, gains, glu_mine, out_whole, down_whole,
    normed, in_whole, ext, pre_ref, conv_ref, r_ref, i_ref, st_ref, product_ref,
    in_shard, glu_shard, small, vecs, gain_shard, held, small_all, vecs_all, gain_all, factors, drive, prod,
    local_sems, tok_send, tok_recv, in_sems, in_xy_send, in_xy_recv, glu_sems, xy_sems, gain_sems, leave_sems,
):
    groups, shards = in_whole.shape[1], in_whole.shape[0]
    at = Place(shards, groups)
    s, f = at.s, at.f
    positions, channels = pre_ref.shape
    width = tokens.shape[1]
    rows = in_shard.shape[1]
    segment = positions // 8
    chunks = positions // CHUNK

    units = gate_rows.shape[1] // shards
    for shard in range(shards):
        part = slice(shard * units, (shard + 1) * units)
        glu_shard[shard, :, :units] = gate_rows[:, part]
        glu_shard[shard, :, units:] = up_rows[:, part]
        part = slice(shard * channels, (shard + 1) * channels)
        in_shard[shard, :, :channels] = lru_rows[:, part]
        in_shard[shard, :, channels:] = gelu_rows[:, part]
    size = gate_block.shape[1]
    small[:, :size] = gate_block[...]
    small[:, size:] = input_block[...]
    vecs[0:4, :] = taps[...].astype(WIDE)
    vecs[4:7, :] = biases[...].astype(WIDE)
    vecs[7:8, :] = rates[...]
    gain_shard[...] = jnp.zeros_like(gain_shard)
    gain_shard[0:2, :] = both_gains[...].astype(WIDE)
    leaving = [
        (normed, normed_far), (in_whole, in_far), (ext, ext_far), (pre_ref, pre_far), (conv_ref, conv_far),
        (r_ref, r_far), (i_ref, i_far), (st_ref, st_far), (product_ref, product_far),
    ]
    leaving = [pltpu.make_async_copy(a, b, leave_sems.at[n]) for n, (a, b) in enumerate(leaving)]
    keep = [
        (tokens, held.at[s]), (in_shard.at[s], in_whole.at[s, f]), (glu_shard.at[s], glu_mine.at[s]),
        (out_shard, out_whole.at[f]), (down_shard, down_whole.at[f]), (small, small_all.at[f]),
        (vecs, vecs_all.at[f]), (gain_shard, gain_all.at[s, f]),
    ]
    keep = [pltpu.make_async_copy(a, b, local_sems.at[n]) for n, (a, b) in enumerate(keep)]
    for copy in keep:
        copy.start()
    at.enter()

    def over_fsdp(src, dst, n):
        return Spread(at, lambda peer: src, lambda origin: dst.at[origin], xy_sems.at[n, 0], xy_sems.at[n, 1])

    gain_xy = Spread(
        at, lambda peer: gain_shard, lambda origin: gain_all.at[s, origin],
        xy_sems.at[0, 0], xy_sems.at[0, 1],
    )
    small_xy = over_fsdp(small, small_all, 1)
    vecs_xy = over_fsdp(vecs, vecs_all, 2)
    out_xy = over_fsdp(out_shard, out_whole, 3)
    down_xy = over_fsdp(down_shard, down_whole, 4)
    in_z = Spread(
        at, lambda peer: in_shard.at[peer], lambda origin: in_whole.at[origin, f],
        in_sems.at[0], in_sems.at[1], "seq",
    )
    glu_z = Spread(
        at, lambda peer: glu_shard.at[peer], lambda origin: glu_mine.at[origin],
        glu_sems.at[0], glu_sems.at[1], "seq",
    )
    gain_z = Spread(
        at, lambda peer: gain_all.at[s], lambda origin: gain_all.at[origin],
        gain_sems.at[0], gain_sems.at[1], "seq",
    )

    def in_xy(index):
        return Spread(
            at, lambda peer: in_whole.at[index, f], lambda origin: in_whole.at[index, origin],
            in_xy_send.at[index], in_xy_recv.at[index],
        )

    gather = LineGather(at, tokens, held, tok_send, tok_recv, tok_send.shape[1])
    gain_xy.start()
    in_z.start()
    keep[1].wait()
    in_xy(s).start()
    gather.start()
    vecs_xy.start()
    small_xy.start()
    keep[7].wait()
    gain_xy.finish()
    gain_z.start()
    for d in range(1, shards):
        in_z.arrive(d)
        in_xy(in_z.source(d)).start()
    out_xy.start()
    early = min(3, shards)
    for d in range(1, early):
        glu_z.copy(d).start()
    down_xy.start()
    gain_z.finish()
    for origin in range(shards):
        for other in range(groups):
            first = (origin * groups + other) * rows
            gains[:, first : first + rows] = gain_all[origin, other]
    keep[0].wait()

    def take(chip):
        for core in range(2):
            slot = 2 * chip + core

            def store(here, value):
                normed[slot, here, :] = value

            normalise(
                lambda here: held[slot, here, :].astype(WIDE), gains[0:1, :], store, tokens.shape[0]
            )

    def rest(n):
        @pl.when(n == at.line - 1)
        def _():
            for d in range(early, shards):
                glu_z.copy(d).start()

    gather.distances(take, rest)
    leaving[0].start()
    keep[6].wait()
    vecs_xy.finish()
    keep[5].wait()
    small_xy.finish()
    local = small.shape[0]
    wr_ref[...] = jnp.zeros_like(wr_ref)
    wi_ref[...] = jnp.zeros_like(wi_ref)
    flat = small_all[...].reshape(channels, 2 * size)
    for n in range(channels // size):
        block = slice(n * size, (n + 1) * size)
        wr_ref[block, block] = flat[block, :size]
        wi_ref[block, block] = flat[block, size:]
    for other in range(groups):
        par_ref[:, other * local : (other + 1) * local] = vecs_all[other]
    ext[0:8, :] = jnp.zeros((8, channels), WIDE)
    st_ref[0:8, :] = jnp.zeros((8, channels), WIDE)
    for index in range(shards):
        for d in range(1, groups):
            in_xy(index).arrive(d)
    leaving[1].start()
    @pl.loop(0, at.line)
    def _(chip):
        pair = normed[pl.ds(2 * chip, 2), :, :].reshape(2 * tokens.shape[0], width)
        both = dot(pair, in_whole[...].reshape(width, 2 * channels))
        base = pl.multiple_of(chip * 2 * tokens.shape[0], CHUNK)
        here = pl.ds(base, 2 * tokens.shape[0])
        ext[pl.ds(base + 8, 2 * tokens.shape[0]), :] = both[:, :channels].astype(LOW).astype(WIDE)
        pre_ref[here, :] = both[:, channels:]

    @pl.loop(0, chunks)
    def _(n):
        base = pl.multiple_of(n * CHUNK, CHUNK)
        here = pl.ds(base, CHUNK)
        block = ext[pl.ds(base, CHUNK + 8), :]
        conv = jnp.broadcast_to(par_ref[4:5, :], (CHUNK, channels))
        for k in range(4):
            conv = conv + par_ref[k : k + 1, :] * block[8 - k : 8 - k + CHUNK]
        conv_low = conv.astype(LOW)
        conv_ref[here, :] = conv_low
        r = jax.nn.sigmoid(dot(conv_low, wr_ref[...]) + par_ref[5:6, :])
        gate = jax.nn.sigmoid(dot(conv_low, wi_ref[...]) + par_ref[6:7, :])
        log_decay = r * par_ref[7:8, :]
        m = jnp.sqrt(one_minus_exp(-2.0 * log_decay))
        factor = jnp.exp(log_decay)
        r_ref[here, :] = r
        i_ref[here, :] = gate
        put(factors, here, factor)
        put(drive, here, m * gate * conv_low.astype(WIDE))

    for n in range(2, 7):
        leaving[n].start()

    def step(i, n, state, product):
        here = pl.ds(i, 8, stride=segment)
        factor = factors[n, here, :]
        state = factor * state + drive[n, here, :]
        product = factor * product
        drive[n, here, :] = state
        prod[n, here, :] = product
        return state, product

    state, product = scan_segments(step, segment, lane_tiles(channels))
    state, product = state[:, :channels], product[:, :channels]
    carry = jnp.zeros((1, channels), WIDE)
    for k in range(8):
        for part in range(segment // CHUNK):
            base = k * segment + part * CHUNK
            here = slice(base, base + CHUNK)
            states = get(drive, here, channels) + get(prod, here, channels) * carry
            st_ref[base + 8 : base + 8 + CHUNK, :] = states
            product_ref[here, :] = (
                states.astype(LOW).astype(WIDE) * gelu(pre_ref[here, :])
            ).astype(LOW)
        carry = state[k : k + 1] + product[k : k + 1] * carry

    leaving[7].start()
    leaving[8].start()
    glu_z.finish()
    out_xy.finish()
    down_xy.finish()
    gather.sent()
    in_z.sent()
    for index in range(shards):
        in_xy(index).sent()
    for n in (2, 3, 4):
        keep[n].wait()
    for copy in leaving:
        copy.wait()


def mix_in(
    tokens, lru_rows, gelu_rows, gate_rows, up_rows, out_shard, down_shard, gate_block, input_block,
    taps, biases, rates, both_gains, shards, groups,
):
    rows = lru_rows.shape[0]
    block, width = tokens.shape
    positions, channels = shards * block, lru_rows.shape[1] // shards
    both = 2 * channels
    in_shape = (shards, rows, both)
    glu_shape = (shards, rows, 2 * (gate_rows.shape[1] // shards))
    local = gate_block.shape[0]
    small_shape = (gate_block.shape[0], 2 * gate_block.shape[1])
    pieces = 2
    wide = jax.ShapeDtypeStruct((positions, channels), WIDE)
    low = jax.ShapeDtypeStruct((positions, channels), LOW)
    longer = jax.ShapeDtypeStruct((positions + 8, channels), WIDE)
    square = jax.ShapeDtypeStruct((channels, channels), LOW)
    saved = [
        jax.ShapeDtypeStruct((shards, block, width), LOW),
        jax.ShapeDtypeStruct((shards, groups, rows, both), LOW),
        longer, wide, low, wide, wide, longer,
        low,
    ]
    held = [
        jax.ShapeDtypeStruct((8, channels), WIDE), square, square, jax.ShapeDtypeStruct((8, width), WIDE),
    ]
    far = [
        jax.ShapeDtypeStruct(glu_shape, LOW),
        jax.ShapeDtypeStruct((groups,) + out_shard.shape, LOW),
        jax.ShapeDtypeStruct((groups,) + down_shard.shape, LOW),
    ]
    return pl.pallas_call(
        mix_in_kernel,
        out_shape=saved + held + far,
        in_specs=[HELD] * 13,
        out_specs=[ANY] * len(saved) + [HELD] * len(held) + [ANY] * len(far),
        scratch_shapes=[pltpu.VMEM(member.shape, member.dtype) for member in saved]
        + [
            pltpu.VMEM(in_shape, LOW), pltpu.VMEM(glu_shape, LOW), pltpu.VMEM(small_shape, LOW),
            pltpu.VMEM((8, local), WIDE), pltpu.VMEM((8, rows), WIDE),
            pltpu.VMEM((shards, block, width), LOW),
            pltpu.VMEM((groups,) + small_shape, LOW),
            pltpu.VMEM((groups, 8, local), WIDE),
            pltpu.VMEM((shards, groups, 8, rows), WIDE),
        ]
        + [pltpu.VMEM((lane_tiles(channels), positions, 128), WIDE)] * 3
        + [
            dma(8), dma(shards, pieces, 3), dma(shards, pieces), dma(2, shards), dma(shards, groups),
            dma(shards, groups), dma(2, shards), dma(5, 2, groups), dma(2, shards), dma(9),
        ],
        compiler_params=pltpu.CompilerParams(
            collective_id=1, has_side_effects=True, vmem_limit_bytes=VMEM_BYTES
        ),
        name="mix_in",
    )(
        tokens, lru_rows, gelu_rows, gate_rows, up_rows, out_shard, down_shard, gate_block, input_block,
        taps, biases, rates, both_gains,
    )


def feed_kernel(
    product_far, out_far, glu_mine, down_in, cotangent, tokens, gains,
    middle, middle_grad, mixed_low, gain_sums, hidden_far, glu_grad, down_grad, glu_first,
    product, out_whole, held, cots, glu, down, both, hidden, wide_pair, hidden_pair, normed2, staged, down_staged,
    parts, heard, into, sib_send, sib_recv, line_send, line_recv,
    local_sems, glu_send, glu_recv, two_send, two_recv, cot_send, cot_recv, stage_sems, first_sems,
):
    shards, groups = glu.shape[0], glu.shape[1]
    at = Place(shards, groups)
    s, f = at.s, at.f
    block, width = tokens.shape
    units = down.shape[0]
    pair = 2 * block

    keep = [(glu_mine, glu.at[:, f]), (down_in, down), (cotangent, cots.at[s])]
    keep += [(product_far, product), (out_far, out_whole)]
    keep = [pltpu.make_async_copy(a, b, local_sems.at[n]) for n, (a, b) in enumerate(keep)]
    for copy in keep:
        copy.start()
    at.enter()
    def glu_xy(index):
        return Spread(
            at, lambda peer: glu_mine.at[index], lambda origin: glu.at[index, origin],
            glu_send.at[index], glu_recv.at[index],
        )

    cot_z = LineGather(at, cotangent, cots, cot_send, cot_recv, cot_send.shape[1])
    two_z = LineGather(at, normed2, held, two_send, two_recv, two_send.shape[1])
    sums = LineScatter(
        at, parts, heard, into, (sib_send, sib_recv, line_send, line_recv), line_send.shape[1]
    )
    for index in range(shards):
        glu_xy(index).start()
    cot_z.start()

    def split(chip, columns, value, parts):
        parts[chip, :, :, columns] = value.astype(LOW).reshape(2, block, value.shape[1])

    def columns_of(j):
        return pl.ds(pl.multiple_of(j * 256, 256), 256)

    def pair_rows(chip):
        return pl.ds(pl.multiple_of(chip * pair, pair), pair)

    keep[3].wait()
    keep[4].wait()

    def project(chip):
        @pl.loop(0, width // 256)
        def _(j):
            value = dot(product[pair_rows(chip), :], out_whole[:, columns_of(j)])
            split(chip, columns_of(j), value, parts)

        sums.across(chip).start()

    for k in range(at.line // 2):
        project(at.line - 1 - k)
        project(k)
        sums.push(at.line - 1 - k, 0, 1)
        sums.push(k, 0, 1)
    for k in range(at.line // 2):
        sums.push(at.line - 1 - k, 1)
        sums.push(k, 1)
    sums.join(0, 1)
    cot_z.pass_on(1)

    def to_middle(here, total):
        values = total + tokens[here, :].astype(WIDE)
        middle[here, :] = values
        scale = lax.rsqrt(jnp.mean(values * values, axis=-1, keepdims=True) + EPSILON)
        normed2[here, :] = (values * scale * gains[1:2, :]).astype(LOW)

    sums.finish(to_middle, 0, 1)
    two_z.start(0, 1)
    cot_z.pass_on(2)
    sums.join(1)
    sums.finish(to_middle, 1)
    two_z.start(1)
    own_copy = pltpu.make_async_copy(normed2, held.at[s], local_sems.at[5])
    own_copy.start()
    keep[0].wait()
    keep[1].wait()
    keep[2].wait()
    sums.sent()
    own_copy.wait()
    for d in range(3, at.line):
        cot_z.pass_on(d)
    for index in range(shards):
        glu_xy(index).finish()

    def open_up(chip):
        rows = held[pl.ds(2 * chip, 2), :, :].reshape(pair, width)
        grads = cots[pl.ds(2 * chip, 2), :, :].reshape(pair, width)

        @pl.loop(0, 2 * units // 256)
        def _(j):
            wide_pair[:, columns_of(j)] = dot(
                rows, glu[:, :, :, columns_of(j)].reshape(width, 256)
            )

        @pl.loop(0, units // 256)
        def _(j):
            hidden_pair[:, columns_of(j)] = times_transpose(grads, down[columns_of(j), :])

        @pl.loop(0, pair // 16)
        def _(n):
            part = pl.ds(pl.multiple_of(n * 16, 16), 16)
            there = pl.ds(pl.multiple_of(chip * pair + n * 16, 16), 16)
            opened, slope = gelu_and_slope(wide_pair[part, :units])
            up = wide_pair[part, units:]
            grad = hidden_pair[part, :]
            hidden[there, :] = (opened * up).astype(LOW)
            both[there, :units] = (grad * up * slope).astype(LOW)
            both[there, units:] = (grad * opened).astype(LOW)

    def to_normed2(chip):
        @pl.loop(0, shards)
        def _(j):
            value = times_transpose(
                both[pair_rows(chip), :], glu[j].reshape(width // shards, 2 * units)
            )
            split(chip, columns_of(j), value, parts)

        sums.across(chip).start()

    cot_z.settle(at.z)
    two_z.settle(at.z)

    @pl.loop(1, at.line + 1)
    def _(n):
        chip = at.nearest(lax.rem(n, at.line))

        @pl.when(n < at.line)
        def _():
            two_z.pass_on(n)
            two_z.settle(chip)
            cot_z.settle(chip)

        open_up(chip)

        @pl.when(n > 1)
        def _():
            sums.push(at.nearest(n - 1))

        to_normed2(chip)

    hidden_leave = pltpu.make_async_copy(hidden, hidden_far, local_sems.at[6])
    hidden_leave.start()
    def glu_out(j):
        return pltpu.make_async_copy(
            staged.at[lax.rem(j, 2)], glu_grad.at[:, j], stage_sems.at[lax.rem(j, 2)]
        )

    def glu_sums(first, last):
        @pl.loop(first, last)
        def _(j):
            @pl.when(j >= first + 2)
            def _():
                glu_out(j - 2).wait()

            rows = held[:, :, columns_of(j)].reshape(shards * block, 256)
            staged[lax.rem(j, 2)] = outer_sum(rows, both[...]).astype(LOW).reshape(staged.shape[1:])
            glu_out(j).start()

        for j in range(max(last - 2, first), last):
            glu_out(j).wait()

    def down_out(j):
        return pltpu.make_async_copy(
            down_staged.at[lax.rem(j, 2)], down_grad.at[columns_of(j)], stage_sems.at[2 + lax.rem(j, 2)]
        )

    def down_sums():
        @pl.loop(0, units // 256)
        def _(j):
            @pl.when(j >= 2)
            def _():
                down_out(j - 2).wait()

            grads = cots[...].reshape(shards * block, width)
            down_staged[lax.rem(j, 2)] = outer_sum(hidden[:, columns_of(j)], grads).astype(LOW)
            down_out(j).start()

    early = glu_first.shape[1]
    glu_early = Spread(
        at, lambda peer: glu_grad.at[peer, pl.ds(0, early)], lambda origin: glu_first.at[origin],
        first_sems.at[0], first_sems.at[1],
    )
    glu_sums(0, early)
    glu_early.start()
    sums.join()
    down_sums()
    glu_sums(early, shards)
    gain_sums[...] = jnp.zeros_like(gain_sums)

    def back(here, grad):
        values = middle[here, :]
        scale = lax.rsqrt(jnp.mean(values * values, axis=-1, keepdims=True) + EPSILON)
        scaled = grad * gains[1:2, :]
        along = jnp.mean(scaled * values, axis=-1, keepdims=True)
        total = cots[at.s, here, :].astype(WIDE) + scale * scaled - values * (scale * scale * scale * along)
        middle_grad[here, :] = total
        mixed_low[here, :] = total.astype(LOW)
        gain_sums[0:1, :] += jnp.sum(grad * values * scale, axis=0, keepdims=True)

    sums.finish(back)
    for j in range(max(units // 256 - 2, 0), units // 256):
        down_out(j).wait()
    hidden_leave.wait()
    glu_early.finish()
    sums.sent()
    two_z.sent()
    cot_z.sent()


def feed(product, out_whole, glu_mine, down_whole, cotangent, tokens, gains, groups):
    shards, rows, both = glu_mine.shape
    block, width = tokens.shape
    units = both // 2
    line, pieces, thirds = shards // 2, 2, 2
    own = jax.ShapeDtypeStruct((block, width), WIDE)
    outs = [
        own, own, jax.ShapeDtypeStruct((block, width), LOW), jax.ShapeDtypeStruct((8, width), WIDE),
        jax.ShapeDtypeStruct((shards * block, units), LOW),
        jax.ShapeDtypeStruct((groups, shards, rows, both), LOW),
        jax.ShapeDtypeStruct((units, width), LOW),
        jax.ShapeDtypeStruct((groups, EARLY, rows, both), LOW),
    ]
    gathered = pltpu.VMEM((shards, block, width), LOW)
    return pl.pallas_call(
        feed_kernel,
        out_shape=outs,
        in_specs=[ANY] * 5 + [HELD] * 2,
        out_specs=[HELD] * 4 + [ANY] * 4,
        scratch_shapes=[
            pltpu.VMEM(product.shape, LOW), pltpu.VMEM(out_whole.shape, LOW),
            gathered, gathered,
            pltpu.VMEM((shards, groups, rows, both), LOW),
            pltpu.VMEM((units, width), LOW),
            pltpu.VMEM((shards * block, both), LOW),
            pltpu.VMEM((shards * block, units), LOW),
            pltpu.VMEM((2 * block, both), WIDE),
            pltpu.VMEM((2 * block, units), WIDE),
            pltpu.VMEM((block, width), LOW),
            pltpu.VMEM((2, groups, rows, both), LOW),
            pltpu.VMEM((2, 256, width), LOW),
        ]
        + LineScatter.scratch(line, block, width, thirds)
        + [
            dma(8), dma(shards, groups), dma(shards, groups), dma(shards, pieces, 3), dma(shards, pieces),
            dma(shards, pieces, 3), dma(shards, pieces), dma(4), dma(2, groups),
        ],
        compiler_params=pltpu.CompilerParams(
            collective_id=2, has_side_effects=True, vmem_limit_bytes=VMEM_BYTES
        ),
        name="feed",
    )(product, out_whole, glu_mine, down_whole, cotangent, tokens, gains)


def back_kernel(
    mixed, hidden_far, down_far, middle_far, middle_grad_far, tokens_far, gains, par_ref, wr_ref, wi_ref,
    out_far, in_far, normed_far, product_far, ext_far, pre_far, conv_far, r_far, i_far, st_far,
    glu_grad, glu_first, down_grad, mlp_parts,
    result, tokens_grad, glu_out, in_out, out_heard, small_heard, gain_out, glu_heard, in_grad, down_heard,
    middle, middle_grad, tokens, held, in_whole, out_whole, product, ext, pre, conv_ref, r_ref, i_ref, st_ref,
    both, pair_grad, staged, adj, totals_ref, wr_sum, wi_sum,
    out_sum, out_grad, small, gain_row, gain_parts, gain_heard, gain_sum, glu_parts, glu_sum, in_heard, in_sum,
    fed_parts, fed_heard, fed_into, fed_sib_send, fed_sib_recv, fed_send, fed_recv,
    parts, heard, into, sib_send, sib_recv, line_send, line_recv,
    local_sems, held_send, held_recv, glu_xy_sems, down_sems, stage_sems, in_xy_sems, out_sems,
    small_sems, gain_xy_sems, glu_sems, in_sems, gain_sems,
):
    shards, groups = in_whole.shape[0], in_whole.shape[1]
    at = Place(shards, groups)
    s, f = at.s, at.f
    block, width = tokens.shape
    positions, channels = product.shape
    rows = in_whole.shape[2]
    pair = 2 * block
    segment = positions // 8
    chunks = positions // CHUNK

    keep = [
        (mixed, held.at[s]), (out_far, out_whole), (pre_far, pre), (st_far, st_ref),
        (product_far, product), (r_far, r_ref), (i_far, i_ref), (conv_far, conv_ref),
        (ext_far, ext), (in_far, in_whole), (mixed, held.at[s]), (normed_far, held),
        (middle_far, middle), (middle_grad_far, middle_grad), (tokens_far, tokens),
    ]
    keep = [pltpu.make_async_copy(a, b, local_sems.at[n]) for n, (a, b) in enumerate(keep)]
    for copy in keep[:10] + keep[12:]:
        copy.start()
    at.enter()

    def over_fsdp(src, dst, sems):
        return Spread(
            at, lambda peer: src.at[peer], lambda origin: dst.at[origin], sems.at[0], sems.at[1]
        )

    def over_seq(src, dst, sems):
        return Spread(
            at, lambda peer: src.at[peer], lambda origin: dst.at[origin], sems.at[0], sems.at[1], "seq"
        )

    early = glu_first.shape[1]
    glu_xy = Spread(
        at, lambda peer: glu_grad.at[peer, pl.ds(early, shards - early)], lambda origin: glu_heard.at[origin],
        glu_xy_sems.at[0], glu_xy_sems.at[1],
    )
    in_xy = over_fsdp(in_grad, in_heard, in_xy_sems)
    out_xy = over_fsdp(out_grad, out_heard, out_sems)
    down_xy = over_fsdp(down_grad, down_heard, down_sems)
    small_xy = over_fsdp(small, small_heard, small_sems)
    gain_xy = over_fsdp(gain_parts, gain_heard, gain_xy_sems)
    glu_z = over_seq(glu_sum, glu_out, glu_sems)
    in_z = over_seq(in_sum, in_out, in_sems)
    gain_z = over_seq(gain_sum, gain_out, gain_sems)
    mixed_z = LineGather(at, mixed, held, held_send, held_recv, held_send.shape[1])
    fed = LineScatter(
        at, fed_parts, fed_heard, fed_into,
        (fed_sib_send, fed_sib_recv, fed_send, fed_recv), fed_send.shape[1],
    )
    sums = LineScatter(
        at, parts, heard, into, (sib_send, sib_recv, line_send, line_recv), line_send.shape[1]
    )
    mixed_z.start()
    glu_xy.start()
    out_sum[...] = jnp.zeros_like(out_sum)

    def columns_of(j):
        return pl.ds(pl.multiple_of(j * 256, 256), 256)

    def feed_out(hidden, down, sems):
        loads = [
            pltpu.make_async_copy(hidden_far, hidden, sems.at[0]),
            pltpu.make_async_copy(down_far, down, sems.at[1]),
        ]
        for load in loads:
            load.start()
        for load in loads:
            load.wait()

        def one(chip):
            @pl.loop(0, width // 256)
            def _(j):
                there = pl.ds(pl.multiple_of(chip * pair, pair), pair)
                value = dot(hidden[there, :], down[:, columns_of(j)])
                fed_parts[chip, :, :, columns_of(j)] = value.astype(LOW).reshape(2, block, 256)

            fed.across(chip).start()

        for k in range(at.line // 2):
            one(at.line - 1 - k)
            one(k)

    pl.run_scoped(
        feed_out, pltpu.VMEM(hidden_far.shape, LOW), pltpu.VMEM(down_far.shape, LOW), dma(2)
    )
    for n in (0, 1, 2, 3, 4):
        keep[n].wait()

    def mixed_back(chip):
        rows = held[pl.ds(2 * chip, 2), :, :].reshape(pair, width)
        pair_grad[...] = times_transpose(rows, out_whole[...])

        @pl.loop(0, pair // 64)
        def _(n):
            grad = pair_grad[pl.ds(pl.multiple_of(n * 64, 64), 64), :]
            base = pl.multiple_of(chip * pair + n * 64, 64)
            here = pl.ds(base, 64)
            opened, slope = gelu_and_slope(pre[here, :])
            states = st_ref[pl.ds(base + 8, 64), :].astype(LOW).astype(WIDE)
            put(adj, here, (grad * opened).astype(LOW).astype(WIDE))
            both[here, channels:] = (grad * states * slope).astype(LOW)

        there = pl.ds(pl.multiple_of(chip * pair, pair), pair)

        @pl.loop(0, width // 256)
        def _(j):
            part = held[pl.ds(2 * chip, 2), :, columns_of(j)].reshape(pair, 256)
            out_sum[:, columns_of(j)] += outer_sum(product[there, :], part)

    def fed_beside(n):
        @pl.when(n == 2)
        def _():
            @pl.loop(1, at.line)
            def _(far):
                fed.push(at.nearest(at.line - far))

    mixed_z.distances(mixed_back, fed_beside)
    def mix_back(factors, prod, cg, carries):
        keep[5].wait()

        @pl.loop(0, chunks)
        def _(n):
            here = pl.ds(pl.multiple_of(n * CHUNK, CHUNK), CHUNK)
            put(factors, here, jnp.exp(r_ref[here, :] * par_ref[7:8, :]))

        def step(j, n, flow, product):
            here = pl.ds(segment - 1 - j, 8, stride=segment)
            factor = factors[n, here, :]
            adjoint = adj[n, here, :] + flow
            adj[n, here, :] = adjoint
            prod[n, here, :] = product
            return factor * adjoint, factor * product

        flow, through = scan_segments(step, segment, lane_tiles(channels))
        flow, through = flow[:, :channels], through[:, :channels]
        carry = jnp.zeros((1, channels), WIDE)
        for k in range(7, -1, -1):
            carries[k : k + 1, :] = carry
            carry = flow[k : k + 1] + through[k : k + 1] * carry
        for n in (6, 7, 8):
            keep[n].wait()
        cg[pl.ds(positions, 8), :] = jnp.zeros((8, channels), WIDE)
        wr_sum[...] = jnp.zeros_like(wr_sum)
        wi_sum[...] = jnp.zeros_like(wi_sum)

        def grads(c, sums):
            base = pl.multiple_of(c * CHUNK, CHUNK)
            rows = pl.ds(base, CHUNK)
            adjoint = get(adj, rows, channels) + get(prod, rows, channels) * carries[pl.ds(base // segment, 1), :]
            before = st_ref[pl.ds(base, CHUNK + 8), :][7 : 7 + CHUNK]
            conv_low = conv_ref[rows, :]
            conv = conv_low.astype(WIDE)
            r = r_ref[rows, :]
            gate = i_ref[rows, :]
            factor = get(factors, rows, channels)
            m = jnp.sqrt(one_minus_exp(-2.0 * (r * par_ref[7:8, :])))
            driven = adjoint * gate
            by_log = adjoint * before * factor - driven * conv * factor * factor / m
            by_r = by_log * par_ref[7:8, :] * r * (1.0 - r)
            by_i = adjoint * m * conv * gate * (1.0 - gate)
            by_r_low = by_r.astype(LOW)
            by_i_low = by_i.astype(LOW)
            conv_grad = (
                driven * m
                + times_transpose(by_r_low, wr_ref[...])
                + times_transpose(by_i_low, wi_ref[...])
            )
            cg[rows, :] = conv_grad
            wr_sum[...] += outer_sum(conv_low, by_r_low)
            wi_sum[...] += outer_sum(conv_low, by_i_low)
            near = ext[pl.ds(base, CHUNK + 8), :]
            rows_of = [conv_grad * near[8 - k : 8 - k + CHUNK] for k in range(4)]
            rows_of += [conv_grad, by_r, by_i, by_log * r]
            return tuple(
                total + jnp.sum(member, axis=0, keepdims=True) for total, member in zip(sums, rows_of)
            )

        zero = jnp.zeros((1, channels), WIDE)
        totals = lax.fori_loop(0, chunks, grads, (zero,) * 8)
        for k in range(8):
            totals_ref[k : k + 1, :] = totals[k]
        @pl.loop(0, chunks)
        def _(c):
            base = pl.multiple_of(c * CHUNK, CHUNK)
            near = cg[pl.ds(base, CHUNK + 8), :]
            total = jnp.zeros((CHUNK, channels), WIDE)
            for k in range(4):
                total = total + par_ref[k : k + 1, :] * near[k : k + CHUNK]
            both[pl.ds(base, CHUNK), :channels] = total.astype(LOW)

    tiles = pltpu.VMEM((lane_tiles(channels), positions, 128), WIDE)
    pl.run_scoped(
        mix_back, tiles, tiles, pltpu.VMEM((positions + 8, channels), WIDE), pltpu.VMEM((8, channels), WIDE)
    )
    fed.join()
    keep[9].wait()
    down_xy.start()

    def project(chip):
        rows = both[pl.ds(pl.multiple_of(chip * pair, pair), pair), :]

        @pl.loop(0, shards)
        def _(j):
            value = times_transpose(rows, in_whole[j].reshape(width // shards, 2 * channels))
            parts[chip, :, :, columns_of(j)] = value.astype(LOW).reshape(2, block, value.shape[1])

        sums.across(chip).start()

    for k in range(at.line // 2):
        project(at.line - 1 - k)
        project(k)
        sums.push(at.line - 1 - k, 0, 1)
        sums.push(k, 0, 1)
    for k in range(at.line // 2):
        sums.push(at.line - 1 - k, 1)
        sums.push(k, 1)
    mixed_z.sent()
    keep[11].start()
    local = small.shape[1] - 8
    size = small.shape[2] // 2
    for n in range(channels // size):
        part = slice(n * size, (n + 1) * size)
        wr_sum[part, :size] = wr_sum[part, part]
        wi_sum[part, :size] = wi_sum[part, part]
    for group in range(groups):
        part = slice(group * local, (group + 1) * local)
        small[group, :local, :size] = wr_sum[part, :size]
        small[group, :local, size:] = wi_sum[part, :size]
        for k in range(8):
            small[group, local + k : local + k + 1, :local] = totals_ref[k : k + 1, part]
    small_xy.start()
    keep[11].wait()

    def in_done(j):
        return pltpu.make_async_copy(
            staged.at[lax.rem(j, 2)], in_grad.at[:, j], stage_sems.at[lax.rem(j, 2)]
        )

    @pl.loop(0, shards)
    def _(j):
        @pl.when(j >= 2)
        def _():
            in_done(j - 2).wait()

        part = held[:, :, columns_of(j)].reshape(positions, 256)
        staged[lax.rem(j, 2)] = outer_sum(part, both[...]).astype(LOW).reshape(staged.shape[1:])
        in_done(j).start()

    for j in range(shards - 2, shards):
        in_done(j).wait()
    in_xy.start()
    in_own = pltpu.make_async_copy(in_grad.at[f], in_heard.at[f], local_sems.at[16])
    in_own.start()
    sums.join()
    glu_xy.finish()

    def glu_load(d, origin, first=False):
        peer = lax.rem(s + d, shards)
        half = lax.rem(d, 2)
        source = glu_first.at[origin, peer] if first else glu_heard.at[origin, peer - early]
        return pltpu.make_async_copy(
            source, glu_parts.at[half, origin], glu_sems.at[2 + half, origin]
        )

    def glu_load_own(d):
        peer = lax.rem(s + d, shards)
        half = lax.rem(d, 2)
        return pltpu.make_async_copy(
            glu_grad.at[f, peer], glu_parts.at[half, f], glu_sems.at[2 + half, f]
        )

    def glu_loads(d):
        glu_load_own(d).start()
        peer = lax.rem(s + d, shards)
        for first, known in ((True, peer < early), (False, peer >= early)):
            @pl.when(known)
            def _():
                for hop in range(1, groups):
                    glu_load(d, lax.rem(f + hop, groups), first).start()

    def add(parts, total, peer):
        @pl.loop(0, total.shape[1] // 16)
        def _(n):
            here = pl.ds(pl.multiple_of(n * 16, 16), 16)
            value = parts[0, here, :].astype(WIDE)
            for origin in range(1, groups):
                value = value + parts[origin, here, :].astype(WIDE)
            total[peer, here, :] = value.astype(total.dtype)

    glu_loads(1)

    @pl.loop(1, shards + 1)
    def _(d):
        @pl.when(d < shards)
        def _():
            glu_loads(d + 1)

        for origin in range(groups):
            pltpu.make_async_copy(
                glu_first.at[origin, 0], glu_parts.at[lax.rem(d, 2), origin],
                glu_sems.at[2 + lax.rem(d, 2), origin],
            ).wait()
        add(glu_parts.at[lax.rem(d, 2)], glu_sum, lax.rem(s + d, shards))

        @pl.when(d < shards)
        def _():
            glu_z.copy(d).start()

    glu_own = pltpu.make_async_copy(glu_sum.at[s], glu_out.at[s], local_sems.at[17])
    glu_own.start()
    out_grad[...] = out_sum[...].astype(LOW).reshape(out_grad.shape)
    out_xy.start()
    gain_row[...] = jnp.zeros_like(gain_row)

    for n in (12, 13, 14):
        keep[n].wait()

    def store_result(here, total):
        result[here, :] = (middle[here, :] + total).astype(LOW)

    fed.finish(store_result)

    def back(here, grad):
        values = tokens[here, :].astype(WIDE)
        scale = lax.rsqrt(jnp.mean(values * values, axis=-1, keepdims=True) + EPSILON)
        scaled = grad * gains[0:1, :]
        along = jnp.mean(scaled * values, axis=-1, keepdims=True)
        total = middle_grad[here, :] + scale * scaled - values * (scale * scale * scale * along)
        tokens_grad[here, :] = total.astype(LOW)
        gain_row[0:1, :] += jnp.sum(grad * values * scale, axis=0, keepdims=True)

    sums.finish(back)
    for group in range(groups):
        for shard in range(shards):
            first = (shard * groups + group) * rows
            gain_parts[group, shard, 0:1, :] = gain_row[0:1, first : first + rows]
            gain_parts[group, shard, 1:2, :] = mlp_parts[0:1, first : first + rows]
    gain_xy.start()
    in_own.wait()
    in_xy.finish()

    @pl.loop(1, shards + 1)
    def _(d):
        peer = lax.rem(s + d, shards)
        add(in_heard.at[:, peer], in_sum, peer)

        @pl.when(d < shards)
        def _():
            in_z.copy(d).start()

    last = [
        pltpu.make_async_copy(in_sum.at[s], in_out.at[s], local_sems.at[18]),
        pltpu.make_async_copy(out_grad.at[f], out_heard.at[f], local_sems.at[19]),
        pltpu.make_async_copy(small.at[f], small_heard.at[f], local_sems.at[20]),
    ]
    for copy in last:
        copy.start()
    gain_xy.finish()
    total = gain_parts[f]
    for d in range(1, groups):
        total = total + gain_heard[lax.rem(f + d, groups)]
    gain_sum[...] = total
    gain_z.start()
    gain_own = pltpu.make_async_copy(gain_sum.at[s], gain_out.at[s], local_sems.at[21])
    gain_own.start()
    fed.sent()
    sums.sent()
    for spread in (small_xy, out_xy, down_xy, glu_z, gain_z, in_z):
        spread.finish()
    for copy in (glu_own, gain_own, *last):
        copy.wait()


def back(
    mixed, hidden, down_whole, middle, middle_grad, tokens, gains, par, wr, wi,
    out_whole, in_whole, normed, product, ext, pre, conv, r, i, st, glu_grad, glu_first, down_grad, mlp_sums, size,
):
    shards, groups, rows, both = in_whole.shape
    block, width = tokens.shape
    positions, channels = product.shape
    line, pieces, halves = shards // 2, 2, 2
    local = channels // groups
    short = jax.ShapeDtypeStruct((block, width), LOW)
    glu_shape = glu_grad.shape[1:]
    in_shape = (groups, shards, rows, both)
    outs = [
        short, short, jax.ShapeDtypeStruct(glu_shape, LOW), jax.ShapeDtypeStruct(in_shape[1:], LOW),
        jax.ShapeDtypeStruct((groups, local, width), LOW),
        jax.ShapeDtypeStruct((groups, local + 8, 2 * size), WIDE),
        jax.ShapeDtypeStruct((shards, 8, rows), WIDE),
        jax.ShapeDtypeStruct((groups, shards - glu_first.shape[1]) + glu_grad.shape[2:], LOW),
        jax.ShapeDtypeStruct(in_shape, LOW),
        jax.ShapeDtypeStruct(down_grad.shape, LOW),
    ]
    late = [middle, middle_grad, tokens]
    far = [out_whole, in_whole, normed, product, ext, pre, conv, r, i, st]
    near = [in_whole, out_whole, product, ext, pre, conv, r, i, st]
    return pl.pallas_call(
        back_kernel,
        out_shape=outs,
        in_specs=[ANY] * 6 + [HELD] * 4 + [ANY] * (len(far) + 3) + [HELD],
        out_specs=[HELD] * 2 + [ANY] * 8,
        scratch_shapes=[pltpu.VMEM(member.shape, member.dtype) for member in late]
        + [pltpu.VMEM((shards, block, width), LOW)]
        + [pltpu.VMEM(member.shape, member.dtype) for member in near]
        + [
            pltpu.VMEM((positions, 2 * channels), LOW),
            pltpu.VMEM((2 * block, channels), WIDE),
            pltpu.VMEM((2, groups, rows, both), LOW),
        ]
        + [pltpu.VMEM((lane_tiles(channels), positions, 128), WIDE), pltpu.VMEM((8, channels), WIDE)]
        + [pltpu.VMEM((channels, channels), WIDE)] * 2
        + [
            pltpu.VMEM((channels, width), WIDE),
            pltpu.VMEM((groups, local, width), LOW),
            pltpu.VMEM((groups, local + 8, 2 * size), WIDE),
            pltpu.VMEM((8, width), WIDE),
            pltpu.VMEM((groups, shards, 8, rows), WIDE),
            pltpu.VMEM((groups, shards, 8, rows), WIDE),
            pltpu.VMEM((shards, 8, rows), WIDE),
            pltpu.VMEM((2, groups) + glu_shape[1:], LOW),
            pltpu.VMEM(glu_shape, LOW),
            pltpu.VMEM(in_shape, LOW),
            pltpu.VMEM(in_shape[1:], LOW),
        ]
        + LineScatter.scratch(line, block, width, halves) * 2
        + [
            dma(22), dma(shards, pieces, 3), dma(shards, pieces), dma(2, groups), dma(2, groups), dma(2),
            dma(2, groups), dma(2, groups), dma(2, groups), dma(2, groups),
            dma(4, shards), dma(2, shards), dma(2, shards),
        ],
        compiler_params=pltpu.CompilerParams(
            collective_id=3, has_side_effects=True, vmem_limit_bytes=VMEM_BYTES
        ),
        name="back",
    )(
        mixed, hidden, down_whole, middle, middle_grad, tokens, gains, par, wr, wi, *far,
        glu_grad, glu_first, down_grad, mlp_sums,
    )


def settle_kernel(
    glu_far, ins_far, outs_far, down_heard, down_grad, result_far, tokens_far,
    result_out, tokens_out, gate_far, up_far, lru_far, gelu_far, out_far, down_far,
    result, tokens, glu, ins, outs, parts, gate_sum, up_sum, lru_sum, gelu_sum, out_sum, down_sum, sems, leave_sems,
):
    shards, rows, both = glu.shape
    groups = outs.shape[0]
    units, channels = both // 2, ins.shape[2] // 2
    f = lax.axis_index("fsdp")
    keep = [
        (glu_far, glu), (ins_far, ins), (outs_far, outs), (result_far, result), (tokens_far, tokens),
        (down_grad.at[f], parts.at[f]),
    ]
    for hop in range(1, groups):
        origin = lax.rem(f + hop, groups)
        keep.append((down_heard.at[origin], parts.at[origin]))
    keep = [pltpu.make_async_copy(a, b, sems.at[n]) for n, (a, b) in enumerate(keep)]
    for copy in keep:
        copy.start()
    leaving = [
        (gate_sum, gate_far), (up_sum, up_far), (lru_sum, lru_far), (gelu_sum, gelu_far),
        (out_sum, out_far), (down_sum, down_far), (result, result_out), (tokens, tokens_out),
    ]
    leaving = [pltpu.make_async_copy(a, b, leave_sems.at[n]) for n, (a, b) in enumerate(leaving)]
    keep[0].wait()
    for half, whole in enumerate((gate_sum, up_sum)):
        for shard in range(shards):
            part = slice(half * units, (half + 1) * units)
            whole[:, shard * units : (shard + 1) * units] = glu[shard, :, part].astype(WIDE)
        leaving[half].start()
    keep[1].wait()
    for half, whole in enumerate((lru_sum, gelu_sum)):
        for shard in range(shards):
            part = slice(half * channels, (half + 1) * channels)
            whole[:, shard * channels : (shard + 1) * channels] = ins[shard, :, part].astype(WIDE)
        leaving[2 + half].start()

    def add(terms, total):
        @pl.loop(0, total.shape[0] // 16)
        def _(n):
            here = pl.ds(pl.multiple_of(n * 16, 16), 16)
            value = terms[0, here, :].astype(WIDE)
            for origin in range(1, groups):
                value = value + terms[origin, here, :].astype(WIDE)
            total[here, :] = value

    for n in (3, 4):
        keep[n].wait()
        leaving[n + 3].start()
    keep[2].wait()
    add(outs, out_sum)
    leaving[4].start()
    for copy in keep[5:]:
        copy.wait()
    add(parts, down_sum)
    leaving[5].start()
    for copy in leaving:
        copy.wait()


def settle(glu, ins, outs, down_heard, down_grad, result, tokens):
    shards, rows, both = glu.shape
    groups, local, width = outs.shape
    units, channels = both // 2, ins.shape[2] // 2
    shapes = [(rows, shards * units)] * 2 + [(rows, shards * channels)] * 2
    shapes += [(local, width), down_grad.shape[1:]]
    return pl.pallas_call(
        settle_kernel,
        out_shape=[jax.ShapeDtypeStruct(result.shape, LOW)] * 2
        + [jax.ShapeDtypeStruct(shape, WIDE) for shape in shapes],
        in_specs=[ANY] * 7,
        out_specs=[ANY] * 8,
        scratch_shapes=[pltpu.VMEM(member.shape, LOW) for member in (result, tokens, glu, ins, outs, down_grad)]
        + [pltpu.VMEM(shape, WIDE) for shape in shapes]
        + [dma(groups + 5), dma(8)],
        compiler_params=pltpu.CompilerParams(vmem_limit_bytes=VMEM_BYTES),
        name="settle",
    )(glu, ins, outs, down_heard, down_grad, result, tokens)


def mixer_forward_kernel(
    x_ref, wr_ref, wi_ref, par_ref,
    conv_ref, r_ref, i_ref, f_ref, m_ref, st_ref,
    ext, factors, drive, prod,
):
    positions, channels = x_ref.shape
    segment = positions // 8
    chunks = positions // CHUNK
    ext[0:8, :] = jnp.zeros((8, channels), WIDE)
    st_ref[0:8, :] = jnp.zeros((8, channels), WIDE)

    @pl.loop(0, chunks)
    def _(c):
        base = pl.multiple_of(c * CHUNK, CHUNK)
        ext[pl.ds(base + 8, CHUNK), :] = x_ref[pl.ds(base, CHUNK), :].astype(WIDE)

    @pl.loop(0, chunks)
    def _(c):
        base = pl.multiple_of(c * CHUNK, CHUNK)
        rows = pl.ds(base, CHUNK)
        block = ext[pl.ds(base, CHUNK + 8), :]
        conv = jnp.broadcast_to(par_ref[4:5, :], (CHUNK, channels))
        for k in range(4):
            conv = conv + par_ref[k : k + 1, :] * block[8 - k : 8 - k + CHUNK]
        conv_low = conv.astype(LOW)
        conv_ref[rows, :] = conv_low
        r = jax.nn.sigmoid(dot(conv_low, wr_ref[...]) + par_ref[5:6, :])
        gate = jax.nn.sigmoid(dot(conv_low, wi_ref[...]) + par_ref[6:7, :])
        log_decay = r * par_ref[7:8, :]
        m = jnp.sqrt(one_minus_exp(-2.0 * log_decay))
        r_ref[rows, :] = r
        i_ref[rows, :] = gate
        factor = jnp.exp(log_decay)
        f_ref[rows, :] = factor
        m_ref[rows, :] = m
        put(factors, rows, factor)
        put(drive, rows, m * gate * conv_low.astype(WIDE))

    def step(i, n, state, product):
        rows = pl.ds(i, 8, stride=segment)
        factor = factors[n, rows, :]
        state = factor * state + drive[n, rows, :]
        product = factor * product
        drive[n, rows, :] = state
        prod[n, rows, :] = product
        return state, product

    state, product = scan_segments(step, segment, lane_tiles(channels))
    state, product = state[:, :channels], product[:, :channels]
    carry = jnp.zeros((1, channels), WIDE)
    for k in range(8):
        for part in range(segment // CHUNK):
            base = k * segment + part * CHUNK
            rows = slice(base, base + CHUNK)
            st_ref[base + 8 : base + 8 + CHUNK, :] = (
                get(drive, rows, channels) + get(prod, rows, channels) * carry
            )
        carry = state[k : k + 1] + product[k : k + 1] * carry


def mixer_backward_kernel(
    ds_ref, x_ref, conv_ref, r_ref, i_ref, f_ref, m_ref, st_ref, wr_ref, wi_ref, par_ref,
    xg_ref, wrg_ref, wig_ref, sums_ref,
    ext, factors, adj, prod, cg, carries, wr_sum, wi_sum,
):
    positions, channels = x_ref.shape
    segment = positions // 8
    chunks = positions // CHUNK
    ext[0:8, :] = jnp.zeros((8, channels), WIDE)
    cg[pl.ds(positions, 8), :] = jnp.zeros((8, channels), WIDE)
    wr_sum[...] = jnp.zeros_like(wr_sum)
    wi_sum[...] = jnp.zeros_like(wi_sum)

    @pl.loop(0, chunks)
    def _(c):
        base = pl.multiple_of(c * CHUNK, CHUNK)
        ext[pl.ds(base + 8, CHUNK), :] = x_ref[pl.ds(base, CHUNK), :].astype(WIDE)
        put(adj, pl.ds(base, CHUNK), ds_ref[pl.ds(base, CHUNK), :].astype(WIDE))
        put(factors, pl.ds(base, CHUNK), f_ref[pl.ds(base, CHUNK), :])

    def step(j, n, flow, product):
        rows = pl.ds(segment - 1 - j, 8, stride=segment)
        factor = factors[n, rows, :]
        adjoint = adj[n, rows, :] + flow
        adj[n, rows, :] = adjoint
        prod[n, rows, :] = product
        return factor * adjoint, factor * product

    flow, product = scan_segments(step, segment, lane_tiles(channels))
    flow, product = flow[:, :channels], product[:, :channels]
    carry = jnp.zeros((1, channels), WIDE)
    for k in range(7, -1, -1):
        carries[k : k + 1, :] = carry
        carry = flow[k : k + 1] + product[k : k + 1] * carry

    def grads(c, sums):
        base = pl.multiple_of(c * CHUNK, CHUNK)
        rows = pl.ds(base, CHUNK)
        adjoint = get(adj, rows, channels) + get(prod, rows, channels) * carries[pl.ds(base // segment, 1), :]
        before = st_ref[pl.ds(base, CHUNK + 8), :][7 : 7 + CHUNK]
        conv_low = conv_ref[rows, :]
        conv = conv_low.astype(WIDE)
        r = r_ref[rows, :]
        gate = i_ref[rows, :]
        factor = f_ref[rows, :]
        m = m_ref[rows, :]
        driven = adjoint * gate
        by_log = adjoint * before * factor - driven * conv * factor * factor / m
        by_r = by_log * par_ref[7:8, :] * r * (1.0 - r)
        by_i = adjoint * m * conv * gate * (1.0 - gate)
        by_r_low = by_r.astype(LOW)
        by_i_low = by_i.astype(LOW)
        conv_grad = (
            driven * m
            + times_transpose(by_r_low, wr_ref[...])
            + times_transpose(by_i_low, wi_ref[...])
        )
        cg[rows, :] = conv_grad
        wr_sum[...] += outer_sum(conv_low, by_r_low)
        wi_sum[...] += outer_sum(conv_low, by_i_low)
        block = ext[pl.ds(base, CHUNK + 8), :]
        rows_of = [conv_grad * block[8 - k : 8 - k + CHUNK] for k in range(4)]
        rows_of += [conv_grad, by_r, by_i, by_log * r]
        return tuple(
            total + jnp.sum(member, axis=0, keepdims=True) for total, member in zip(sums, rows_of)
        )

    zero = jnp.zeros((1, channels), WIDE)
    sums = lax.fori_loop(0, chunks, grads, (zero,) * 8)
    for k in range(8):
        sums_ref[k : k + 1, :] = sums[k]
    size = wrg_ref.shape[1]
    for n in range(channels // size):
        block = slice(n * size, (n + 1) * size)
        wrg_ref[block, :] = wr_sum[block, block]
        wig_ref[block, :] = wi_sum[block, block]

    @pl.loop(0, chunks)
    def _(c):
        base = pl.multiple_of(c * CHUNK, CHUNK)
        block = cg[pl.ds(base, CHUNK + 8), :]
        total = jnp.zeros((CHUNK, channels), WIDE)
        for k in range(4):
            total = total + par_ref[k : k + 1, :] * block[k : k + CHUNK]
        xg_ref[pl.ds(base, CHUNK), :] = total.astype(LOW)


def mixer_forward(x, wr, wi, par):
    positions, channels = x.shape
    wide = jax.ShapeDtypeStruct((positions, channels), WIDE)
    return pl.pallas_call(
        mixer_forward_kernel,
        out_shape=(
            jax.ShapeDtypeStruct((positions, channels), LOW), wide, wide, wide, wide,
            jax.ShapeDtypeStruct((positions + 8, channels), WIDE),
        ),
        scratch_shapes=[pltpu.VMEM((positions + 8, channels), WIDE)]
        + [pltpu.VMEM((lane_tiles(channels), positions, 128), WIDE)] * 3,
        compiler_params=pltpu.CompilerParams(vmem_limit_bytes=48 * 2**20),
        name="mixer_forward",
    )(x, wr, wi, par)


def mixer_backward(ds, x, saved, wr, wi, par, size):
    positions, channels = x.shape
    square = jax.ShapeDtypeStruct((channels, size), WIDE)
    return pl.pallas_call(
        mixer_backward_kernel,
        out_shape=(
            jax.ShapeDtypeStruct((positions, channels), LOW), square, square,
            jax.ShapeDtypeStruct((8, channels), WIDE),
        ),
        scratch_shapes=[pltpu.VMEM((positions + 8, channels), WIDE)]
        + [pltpu.VMEM((lane_tiles(channels), positions, 128), WIDE)] * 3
        + [pltpu.VMEM((positions + 8, channels), WIDE), pltpu.VMEM((8, channels), WIDE)]
        + [pltpu.VMEM((channels, channels), WIDE)] * 2,
        compiler_params=pltpu.CompilerParams(vmem_limit_bytes=48 * 2**20),
        name="mixer_backward",
    )(ds, x, *saved, wr, wi, par)


def gather_columns(weights):
    shards = lax.axis_size("seq")
    rows = weights[0].shape[0]
    widths = [member.shape[1] // shards for member in weights]
    stacked = jnp.concatenate(
        [member.reshape(rows, shards, width) for member, width in zip(weights, widths)], axis=2
    )
    mine = lax.all_to_all(stacked.transpose(1, 0, 2), "seq", split_axis=0, concat_axis=0)
    whole = lax.all_gather(mine, "fsdp", axis=1)
    return whole.reshape(-1, sum(widths))


def scatter_columns(grad, widths, rows):
    shards, groups = lax.axis_size("seq"), lax.axis_size("fsdp")
    parts = grad.astype(LOW).reshape(shards, groups, rows, sum(widths)).transpose(1, 0, 2, 3)
    mine = lax.psum_scatter(parts, "fsdp", scatter_dimension=0, tiled=False)
    swapped = lax.all_to_all(mine, "seq", split_axis=0, concat_axis=0).astype(WIDE)
    outs, first = [], 0
    for width in widths:
        outs.append(swapped[:, :, first : first + width].transpose(1, 0, 2).reshape(rows, -1))
        first += width
    return outs


def block_diagonal(weight, blocks):
    size = weight.shape[1]
    shaped = weight.reshape(blocks, size, size)
    full = jnp.zeros((blocks, size, blocks, size), weight.dtype)
    for n in range(blocks):
        full = full.at[n, :, n, :].set(shaped[n])
    return full.reshape(blocks * size, blocks * size)


def general(
    tokens, cotangent, mix_gain, lru_in_weight, gelu_in_weight, out_weight, conv_weight, conv_bias,
    recurrence_weight, recurrence_bias, input_gate_weight, input_gate_bias, decay_param, mlp_gain,
    gate_weight, up_weight, down_weight,
):
    positions, width = tokens.shape[1:]
    rows = lru_in_weight.shape[0]
    shards = lax.axis_size("seq")
    channels = lru_in_weight.shape[1] // shards
    hidden_width = gate_weight.shape[1] // shards
    size = recurrence_weight.shape[1]

    gains = lax.all_gather(
        jnp.stack([mix_gain, mlp_gain], axis=1), ("seq", "fsdp"), axis=0, tiled=True
    ).astype(WIDE)
    mix_scale, mlp_scale = gains[:, 0], gains[:, 1]
    in_whole = gather_columns([lru_in_weight, gelu_in_weight])
    lru_params = lax.all_gather(
        jnp.concatenate(
            [
                recurrence_weight, input_gate_weight, conv_weight, conv_bias[:, None],
                recurrence_bias[:, None], input_gate_bias[:, None], decay_param[:, None],
            ],
            axis=1,
        ),
        "fsdp", axis=0, tiled=True,
    )
    out_whole = lax.all_gather(out_weight, "fsdp", axis=0, tiled=True)
    glu_whole = gather_columns([gate_weight, up_weight])
    down_whole = lax.all_gather(down_weight, "fsdp", axis=0, tiled=True)

    wr = block_diagonal(lru_params[:, :size], channels // size)
    wi = block_diagonal(lru_params[:, size : 2 * size], channels // size)
    vectors = lru_params[:, 2 * size :].astype(WIDE).T
    decay = vectors[7]
    par = jnp.concatenate([vectors[:7], -RATE_SCALE * jax.nn.softplus(-decay)[None]], axis=0)

    resid_in = tokens.reshape(positions, width).astype(WIDE)
    grad_low = cotangent.reshape(positions, width)
    normed_low = rms_scale(resid_in, mix_scale).astype(LOW)
    normed_all = lax.all_gather(normed_low, "seq", axis=0, tiled=True)
    grad_all = lax.all_gather(grad_low, "seq", axis=0, tiled=True)
    branch_x = dot(normed_all, in_whole[:, :channels]).astype(LOW)
    branch_pre = dot(normed_all, in_whole[:, channels:])
    branch_y = jax.nn.gelu(branch_pre)

    saved = mixer_forward(branch_x, wr, wi, par)
    states_f = saved[5][8:].astype(LOW).astype(WIDE)
    product = (states_f * branch_y).astype(LOW)
    mixed = lax.psum_scatter(
        dot(product, out_whole).astype(LOW), "seq", scatter_dimension=0, tiled=True
    )
    middle = resid_in + mixed.astype(WIDE)
    normed2_low = rms_scale(middle, mlp_scale).astype(LOW)
    normed2_all = lax.all_gather(normed2_low, "seq", axis=0, tiled=True)
    gate_whole, up_whole = glu_whole[:, :hidden_width], glu_whole[:, hidden_width:]
    gate_val = dot(normed2_all, gate_whole)
    up_val = dot(normed2_all, up_whole)
    hidden = (jax.nn.gelu(gate_val) * up_val).astype(LOW)
    fed = lax.psum_scatter(
        dot(hidden, down_whole).astype(LOW), "seq", scatter_dimension=0, tiled=True
    )
    result = middle + fed.astype(WIDE)

    hidden_grad = times_transpose(grad_all, down_whole)
    unused, pull_glu = jax.vjp(lambda first, second: jax.nn.gelu(first) * second, gate_val, up_val)
    gate_grad, up_grad = pull_glu(hidden_grad)
    gate_low, up_low = gate_grad.astype(LOW), up_grad.astype(LOW)
    normed2_grad = lax.psum_scatter(
        (times_transpose(gate_low, gate_whole) + times_transpose(up_low, up_whole)).astype(LOW),
        "seq", scatter_dimension=0, tiled=True,
    ).astype(WIDE)
    unused, pull_norm2 = jax.vjp(rms_scale, middle, mlp_scale)
    middle_part, mlp_gain_grad = pull_norm2(normed2_grad)
    middle_grad = grad_low.astype(WIDE) + middle_part
    mixed_all = lax.all_gather(middle_grad.astype(LOW), "seq", axis=0, tiled=True)

    product_grad = times_transpose(mixed_all, out_whole)
    states_grad = (product_grad * branch_y).astype(LOW)
    unused, pull_gelu = jax.vjp(jax.nn.gelu, branch_pre)
    (pre_grad,) = pull_gelu(product_grad * states_f)
    pre_low = pre_grad.astype(LOW)
    x_low, wr_grad, wi_grad, sums = mixer_backward(states_grad, branch_x, saved, wr, wi, par, size)

    normed_grad = lax.psum_scatter(
        (
            times_transpose(x_low, in_whole[:, :channels])
            + times_transpose(pre_low, in_whole[:, channels:])
        ).astype(LOW),
        "seq", scatter_dimension=0, tiled=True,
    ).astype(WIDE)
    unused, pull_norm = jax.vjp(rms_scale, resid_in, mix_scale)
    input_part, mix_gain_grad = pull_norm(normed_grad)
    input_grad = middle_grad + input_part

    down_grad = lax.psum_scatter(
        outer_sum(hidden, grad_all).astype(LOW), "fsdp", scatter_dimension=0, tiled=True
    ).astype(WIDE)
    glu_grad = jnp.concatenate(
        [outer_sum(normed2_all, gate_low), outer_sum(normed2_all, up_low)], axis=1
    )
    gate_w_grad, up_w_grad = scatter_columns(glu_grad, [hidden_width] * 2, rows)
    out_grad = lax.psum_scatter(
        outer_sum(product, mixed_all).astype(LOW), "fsdp", scatter_dimension=0, tiled=True
    ).astype(WIDE)
    in_grad = jnp.concatenate(
        [outer_sum(normed_all, x_low), outer_sum(normed_all, pre_low)], axis=1
    )
    lru_in_grad, gelu_in_grad = scatter_columns(in_grad, [channels] * 2, rows)
    small = jnp.concatenate(
        [
            wr_grad, wi_grad, sums[:7].T,
            (sums[7] * RATE_SCALE * jax.nn.sigmoid(-decay))[:, None],
        ],
        axis=1,
    )
    small = lax.psum_scatter(
        small.reshape(lax.axis_size("fsdp"), -1, small.shape[1]),
        "fsdp", scatter_dimension=0, tiled=False,
    )
    gain_parts = jnp.stack([mix_gain_grad, mlp_gain_grad]).reshape(2, -1, rows).transpose(1, 0, 2)
    gain_grads = lax.psum_scatter(
        gain_parts, ("seq", "fsdp"), scatter_dimension=0, tiled=False
    )
    first = 2 * size
    return (
        result.astype(LOW).reshape(tokens.shape),
        input_grad.astype(LOW).reshape(tokens.shape),
        gain_grads[0],
        lru_in_grad,
        gelu_in_grad,
        out_grad,
        small[:, first : first + 4],
        small[:, first + 4],
        small[:, :size],
        small[:, first + 5],
        small[:, size : 2 * size],
        small[:, first + 6],
        small[:, first + 7],
        gain_grads[1],
        gate_w_grad,
        up_w_grad,
        down_grad,
    )


def aligned(
    tokens, cotangent, mix_gain, lru_in_weight, gelu_in_weight, out_weight, conv_weight, conv_bias,
    recurrence_weight, recurrence_bias, input_gate_weight, input_gate_bias, decay_param, mlp_gain,
    gate_weight, up_weight, down_weight,
):
    positions, width = tokens.shape[1:]
    rows = lru_in_weight.shape[0]
    shards = lax.axis_size("seq")
    channels = lru_in_weight.shape[1] // shards
    hidden_width = gate_weight.shape[1] // shards
    size = recurrence_weight.shape[1]

    groups = lax.axis_size("fsdp")
    resid_in = tokens.reshape(positions, width).astype(WIDE)
    grad_low = cotangent.reshape(positions, width)

    own_decay = decay_param.astype(WIDE)
    rates = -RATE_SCALE * jax.nn.softplus(-own_decay)[None]
    tokens_low = tokens.reshape(positions, width)
    (
        normed, in_whole, ext, branch_pre, conv_low, recur_gate, input_gate, states, product, par, wr, wi,
        gains, glu_mine, out_whole, down_whole,
    ) = mix_in(
        tokens_low, lru_in_weight, gelu_in_weight, gate_weight, up_weight, out_weight, down_weight,
        recurrence_weight, input_gate_weight, conv_weight.T,
        jnp.stack([conv_bias, recurrence_bias, input_gate_bias]), rates, jnp.stack([mix_gain, mlp_gain]),
        shards, groups,
    )
    out_whole, down_whole = out_whole.reshape(-1, width), down_whole.reshape(-1, width)
    middle, middle_grad, mixed_low, mlp_sums, hidden, glu_grad, down_grad, glu_first = feed(
        product, out_whole, glu_mine, down_whole, grad_low, tokens_low, gains, groups
    )
    down_grad = down_grad.reshape(groups, -1, width)
    (
        result, tokens_grad, glu_out, in_out, out_heard, small_heard, gain_out, unused, unused, down_heard,
    ) = back(
        mixed_low, hidden, down_whole, middle, middle_grad, tokens_low, gains, par, wr, wi,
        out_whole, in_whole, normed, product, ext, branch_pre, conv_low, recur_gate, input_gate, states,
        glu_grad, glu_first, down_grad, mlp_sums, size,
    )
    small_rows = recurrence_weight.shape[0]
    result, tokens_grad, gate_sum, up_sum, lru_sum, gelu_sum, out_sum, down_sum = settle(
        glu_out, in_out, out_heard, down_heard, down_grad, result, tokens_grad
    )
    small = jnp.sum(small_heard, axis=0)
    gain_grads = jnp.sum(gain_out, axis=0)
    vector_sums = small[small_rows:, :small_rows]
    return (
        result.reshape(tokens.shape),
        tokens_grad.reshape(tokens.shape),
        gain_grads[0],
        lru_sum,
        gelu_sum,
        out_sum,
        vector_sums[:4].T,
        vector_sums[4],
        small[:small_rows, :size],
        vector_sums[5],
        small[:small_rows, size : 2 * size],
        vector_sums[6],
        vector_sums[7] * RATE_SCALE * jax.nn.sigmoid(-own_decay),
        gain_grads[1],
        gate_sum,
        up_sum,
        down_sum,
    )


def solution(mesh):
    shards, groups = mesh.shape["seq"], mesh.shape["fsdp"]

    def local(*arrays):
        rows, small_rows = arrays[3].shape[0], arrays[5].shape[0]
        simple = shards % 2 == 0 and rows % 16 == 0 and small_rows % 16 == 0
        simple = simple and arrays[0].shape[1] * shards % (8 * CHUNK) == 0
        return (aligned if simple else general)(*arrays)

    tokens = P("fsdp", "seq", None)
    vector = P(("seq", "fsdp"))
    matrix = P(("seq", "fsdp"), None)
    ranks = (1, 2, 2, 2, 2, 1, 2, 1, 2, 1, 1, 1, 2, 2, 2)
    specs = (tokens, tokens) + tuple(vector if rank == 1 else matrix for rank in ranks)
    return jax.shard_map(local, mesh=mesh, in_specs=specs, out_specs=specs, check_vma=False)
```
